32 devices in a mesh: dp: 8 (over z, y), mp: 4 (over x, core).
Axes of the slice: x: 2, y: 2, z: 4, core: 2. Of those that a mesh axis runs over, the one named last changes fastest.
Arguments:
- latents: float32 [32, 4, 32, 32], P('dp'), may hold values from -6 to 6
- noise: float32 [32, 4, 32, 32], P('dp'), may hold values from -6 to 6
- timesteps: int32 [32], P('dp'), may hold values from 2 to 999, as said below
- labels: int32 [32], P('dp'), may hold values from 0 to 1000
- loss_weights: float32 [32], P('dp'), may hold values from 0.4 to 8
- slotted_block_weights: float32 [4, 72, 288, 288], P('mp', 'dp'), may hold values from -0.1875 to 0.1875
- statistics: float32 [4, 72, 2, 288, 288], P('mp', 'dp'), as said below
- slot_of_block: int32 [72], replicated, may hold values from 0 to 71, each once
- cond_tables: float32 [2425, 1152], P(None, 'dp'), may hold values from -4 to 4
- head_tables: float32 [1152, 2336], P('dp'), may hold values from -0.1875 to 0.1875
- slice_bias: float32 [4, 3456], P('mp'), may hold values from -1.2 to 1.2
- side_bias: float32 [8096], replicated, may hold values from -1.2 to 1.2
- cond_m: float32 [2425, 1152], P(None, 'dp'), may hold values from -0.0007377806 to 0.0007377806
- cond_v: float32 [2425, 1152], P(None, 'dp'), may hold values from 3.402001e-08 to 1.3608005e-07
- head_m: float32 [1152, 2336], P('dp'), may hold values from -0.0007377806 to 0.0007377806
- head_v: float32 [1152, 2336], P('dp'), may hold values from 3.402001e-08 to 1.3608005e-07
- slice_m: float32 [4, 3456], P('mp'), may hold values from -0.0029511224 to 0.0029511224
- slice_v: float32 [4, 3456], P('mp'), may hold values from 5.443202e-07 to 2.1772807e-06
- side_m: float32 [8096], replicated, may hold values from -0.0029511224 to 0.0029511224
- side_v: float32 [8096], replicated, may hold values from 5.443202e-07 to 2.1772807e-06
Outputs:
- loss_sum: float32 [], replicated
- weight_total: float32 [], replicated
- grad_norm: float32 [], replicated
- clipped_block_gradients: float32 [4, 72, 288, 288], P('mp', 'dp')
- new_statistics: float32 [4, 72, 2, 288, 288], P('mp', 'dp')
- new_blocks: float32 [4, 72, 288, 288], P('mp', 'dp')
- new_blocks_bf16: bfloat16 [4, 72, 288, 288], P('mp', 'dp')
- cond_first: float32 [2425, 1152], P(None, 'dp')
- cond_second: float32 [2425, 1152], P(None, 'dp')
- new_cond: float32 [2425, 1152], P(None, 'dp')
- new_cond_bf16: bfloat16 [2425, 1152], P(None, 'dp')
- head_first: float32 [1152, 2336], P('dp')
- head_second: float32 [1152, 2336], P('dp')
- new_head: float32 [1152, 2336], P('dp')
- new_head_bf16: bfloat16 [1152, 2336], P('dp')
- slice_first: float32 [4, 3456], P('mp')
- slice_second: float32 [4, 3456], P('mp')
- new_slice: float32 [4, 3456], P('mp')
- side_first: float32 [8096], replicated
- side_second: float32 [8096], replicated
- new_side: float32 [8096], replicated
The draws below stay inside these ranges and needn't reach their ends.
Inputs may be any that keep to these rules, and one draw needn't show every extreme that they name: `timesteps`: skewed towards high noise. Block b (b < 72) lies at slot slot_of_block[b], owned by the dp index slot_of_block[b] // 9. `statistics`: each statistic is symmetric positive definite.
All inputs are finite; a program needn't handle non-finite values.
Results may differ from the reference program's by a relative error of at most 0.0086.
Values may be sent and summed in bfloat16 or wider, within the bound.
A program may use at most 320 MiB of HBM per device.

```python
import math
import jax
import jax.numpy as jnp
from jax import lax

MODEL_WIDTH = 1152
HEADS = 16
HD = 72
FF = 4608
FREQ = 256
CLASSES = 1001
LATENT_SIDE = 32
PATCH_VALUES = 16
BLOCK_SIDE = 288
NEWTON = 6
STEP = 5
SAMP_DEV = 4
SAMPLES = 32
SEQ = 256
SBW = 3456
HTW = 2336
VBW = 8096
CONDROWS = 2425
SLOT_COUNT = 72
PARAMS = 29394464
N_DP = 8
N_MP = 4


def draw_timesteps(key, part):
    key = jax.random.fold_in(key, 11)
    leading_random_key, trailing_random_key = jax.random.split(key)
    left_ids = jax.random.randint(leading_random_key, (SAMPLES,), 0, 999)
    right_ids = jax.random.randint(trailing_random_key, (SAMPLES,), 0, 999)
    step_ids = 999 - left_ids * right_ids // 999
    position = jnp.arange(SAMPLES)
    step_ids = jnp.where(position == 0, 999, step_ids)
    return jnp.where(position == SAMPLES - 1, 2, step_ids).astype(jnp.int32)


def draw_loss_weights(key, part):
    key = jax.random.fold_in(key, 12)
    ramp = jnp.arange(SAMPLES).astype(jnp.float32) / max(SAMPLES - 1, 1)
    base = jax.random.uniform(key, (SAMPLES,), jnp.float32, 0.5, 1.5)
    return base * (1.0 + 2.0 * ramp)


def draw_statistics(key, part):
    key = jax.random.fold_in(key, 13)
    leading_random_key, trailing_random_key = jax.random.split(key)
    noise_level = BLOCK_SIDE / PARAMS
    diagonal_entries = noise_level * jnp.exp(jax.random.uniform(leading_random_key, (N_MP, SLOT_COUNT, 2, BLOCK_SIDE), jnp.float32, 0.0, 1.3862944))
    spread_values = jax.random.uniform(trailing_random_key, (N_MP, SLOT_COUNT, 2, BLOCK_SIDE, BLOCK_SIDE), jnp.float32, -1.0, 1.0)
    symmetric = (spread_values + jnp.swapaxes(spread_values, -1, -2)) * (0.25 * noise_level / BLOCK_SIDE)
    identity = jnp.eye(BLOCK_SIDE, dtype=jnp.float32)
    return symmetric * (1.0 - identity) + diagonal_entries[..., None] * identity


def draw_cond_tables(key, part):
    key = jax.random.fold_in(key, 14)
    rows_ids = jnp.arange(CONDROWS)
    scales = jnp.where(rows_ids < PATCH_VALUES, PATCH_VALUES ** (-0.5), jnp.where(rows_ids < PATCH_VALUES + FREQ, FREQ ** (-0.5), jnp.where(rows_ids < PATCH_VALUES + FREQ + MODEL_WIDTH, MODEL_WIDTH ** (-0.5), 0.5)))
    values = jnp.clip(jax.random.normal(key, (CONDROWS, MODEL_WIDTH), jnp.float32), -7.5, 7.5)
    return values * scales[:, None]


def plant(drawn, rng, least, high):
    dims = drawn.shape
    index_at = [jax.random.randint(jax.random.fold_in(rng, axis), (), 0, dims[axis]) for axis in range(len(dims))]
    drawn = drawn.at[tuple(index_at)].set(least)
    longest = dims.index(max(dims))
    index_at[longest] = (index_at[longest] + 1) % dims[longest]
    return drawn.at[tuple(index_at)].set(high)


def level_of(stream_key, extent, cuts, smallest, high):
    gain = 1.0
    for dim, shards_of in cuts:
        heights = jax.random.uniform(jax.random.fold_in(jax.random.fold_in(stream_key, 6), dim), (shards_of,), jnp.float32, smallest / len(cuts), high / len(cuts))
        gain = gain * jnp.repeat(jnp.exp(heights), extent[dim] // shards_of).reshape((-1,) + (1,) * (len(extent) - 1 - dim))
    return gain


def scatter_about(own_key, shape, deviation, limit, shards=(), held_as=jnp.bfloat16):
    entries = jax.random.normal(own_key, shape, jnp.float32) * deviation
    if len(shards) > 0:
        entries = level_of(own_key, shape, shards, -0.22, 0.18) * entries
    return jnp.clip(entries, min=-limit, max=limit).astype(held_as)


def setup_inputs(seed: int = 0) -> dict:
    splits = jax.random.split(jax.random.key(seed), 21)
    return {
        "latents": scatter_about(splits[0], (SAMPLES, 4, LATENT_SIDE, LATENT_SIDE), 1.0, 6.0, ((0, 8),), jnp.float32),
        "noise": scatter_about(splits[1], (SAMPLES, 4, LATENT_SIDE, LATENT_SIDE), 1.0, 6.0, ((0, 8),), jnp.float32),
        "timesteps": draw_timesteps(jax.random.fold_in(splits[20], 71), 0),
        "labels": plant(jax.random.randint(splits[3], (SAMPLES,), 0, CLASSES), jax.random.fold_in(splits[3], 1), 0, CLASSES - 1).astype(jnp.int32),
        "loss_weights": draw_loss_weights(jax.random.fold_in(splits[20], 71), 0),
        "slotted_block_weights": scatter_about(splits[5], (N_MP, SLOT_COUNT, BLOCK_SIDE, BLOCK_SIDE), MODEL_WIDTH ** -0.5, 0.1875, ((0, 4), (1, 8)), jnp.float32),
        "statistics": draw_statistics(jax.random.fold_in(splits[20], 71), 0),
        "slot_of_block": jax.random.permutation(splits[7], SLOT_COUNT).astype(jnp.int32),
        "cond_tables": draw_cond_tables(jax.random.fold_in(splits[20], 71), 0),
        "head_tables": scatter_about(splits[9], (MODEL_WIDTH, HTW), MODEL_WIDTH ** -0.5, 0.1875, ((0, 8),), jnp.float32),
        "slice_bias": scatter_about(splits[10], (N_MP, SBW), 0.2, 1.2, ((0, 4),), jnp.float32),
        "side_bias": scatter_about(splits[11], (VBW,), 0.2, 1.2, (), jnp.float32),
        "cond_m": scatter_about(splits[12], (CONDROWS, MODEL_WIDTH), (PARAMS ** -0.5), 0.0007377806, ((1, 8),), jnp.float32),
        "cond_v": jnp.clip(jnp.exp(math.log(1.3608004678644647e-07) - 1.3862944 * jax.random.uniform(splits[13], (CONDROWS, MODEL_WIDTH), jnp.float32) ** level_of(splits[13], (CONDROWS, MODEL_WIDTH), ((1, 8),), -0.2, 0.2)), 3.402001169661162e-08, 1.3608004678644647e-07),
        "head_m": scatter_about(splits[14], (MODEL_WIDTH, HTW), (PARAMS ** -0.5), 0.0007377806, ((0, 8),), jnp.float32),
        "head_v": jnp.clip(jnp.exp(math.log(1.3608004678644647e-07) - 1.3862944 * jax.random.uniform(splits[15], (MODEL_WIDTH, HTW), jnp.float32) ** level_of(splits[15], (MODEL_WIDTH, HTW), ((0, 8),), -0.2, 0.2)), 3.402001169661162e-08, 1.3608004678644647e-07),
        "slice_m": scatter_about(splits[16], (N_MP, SBW), (4.0 * PARAMS ** -0.5), 0.0029511224, ((0, 4),), jnp.float32),
        "slice_v": jnp.clip(jnp.exp(math.log(2.1772807485831436e-06) - 1.3862944 * jax.random.uniform(splits[17], (N_MP, SBW), jnp.float32) ** level_of(splits[17], (N_MP, SBW), ((0, 4),), -0.2, 0.2)), 5.443201871457859e-07, 2.1772807485831436e-06),
        "side_m": scatter_about(splits[18], (VBW,), (4.0 * PARAMS ** -0.5), 0.0029511224, (), jnp.float32),
        "side_v": jnp.clip(jnp.exp(jax.random.uniform(splits[19], (VBW,), jnp.float32, math.log(5.443201871457859e-07), math.log(2.1772807485831436e-06))), 5.443201871457859e-07, 2.1772807485831436e-06),
    }


exact_precision_flag = lax.Precision.HIGHEST
shampoo_rate = 0.5
adam_rate = 0.05
decay_rate = 0.01

@jax.custom_vjp
def lowered_values(v):
    return lax.optimization_barrier(v.astype(jnp.bfloat16)).astype(jnp.float32)

@jax.custom_vjp
def lowered_backward(v):
    return v

def low_keep(v):
    return (lowered_values(v), None)

def low_pass(kept, grad):
    return (grad,)

def back_keep(v):
    return (v, None)

def back_low(kept, grad):
    return (lowered_values(grad),)
lowered_values.defvjp(low_keep, low_pass)
lowered_backward.defvjp(back_keep, back_low)

def matmul(operand, other):
    return jnp.matmul(operand, other, precision=exact_precision_flag)

def swish_unit(inputs):
    return inputs / (1.0 + jnp.exp(-inputs))

def tanh_gelu_activation(inputs):
    return 0.5 * inputs * (1.0 + jnp.tanh(0.7978845608028654 * (inputs + 0.044715 * inputs * inputs * inputs)))

def layer_norm(inputs):
    centred = inputs - lax.optimization_barrier(jnp.mean(inputs, -1, keepdims=True))
    return centred * lax.rsqrt(lax.optimization_barrier(jnp.mean(centred * centred, -1, keepdims=True)) + 1e-06)

def coefficients(step_ids):
    grid = jnp.arange(1000).astype(jnp.float32)
    betas = 0.0001 + (0.02 - 0.0001) * grid / 999.0
    cumul = jnp.exp(jnp.cumsum(jnp.log(1.0 - betas)))
    before = jnp.concatenate([jnp.ones((1,), jnp.float32), cumul[:-1]])
    picked = (step_ids[:, None] == jnp.arange(1000, dtype=jnp.int32)[None, :]).astype(jnp.float32)
    beta_t = lax.optimization_barrier(jnp.sum(picked * betas[None, :], 1))
    cumul_t = lax.optimization_barrier(jnp.sum(picked * cumul[None, :], 1))
    before_t = lax.optimization_barrier(jnp.sum(picked * before[None, :], 1))
    keep_rate = jnp.sqrt(cumul_t)
    noise_rate = jnp.sqrt(1.0 - cumul_t)
    upper_log = jnp.log(beta_t)
    lower_log = jnp.log(beta_t * (1.0 - before_t) / (1.0 - cumul_t))
    mean_gap = beta_t * jnp.sqrt(before_t) / (1.0 - cumul_t) * jnp.sqrt(1.0 / cumul_t - 1.0)
    return (keep_rate, noise_rate, upper_log, lower_log, mean_gap)

def time_features(step_ids, feat_width):
    half_width = feat_width // 2
    frequencies = jnp.exp(-math.log(10000.0) * jnp.arange(half_width).astype(jnp.float32) / half_width)
    phases = step_ids.astype(jnp.float32)[:, None] * frequencies[None, :]
    return jnp.concatenate([jnp.cos(phases), jnp.sin(phases)], 1)

def position_embedding(grid_side, feat_width):
    quarter = feat_width // 4
    omegas = jnp.exp(-math.log(10000.0) * jnp.arange(quarter).astype(jnp.float32) / quarter)
    coords = jnp.arange(grid_side).astype(jnp.float32)
    angles = coords[:, None] * omegas[None, :]
    waves = jnp.concatenate([jnp.sin(angles), jnp.cos(angles)], 1)
    half_width = feat_width // 2
    rows_part = jnp.broadcast_to(waves[:, None, :], (grid_side, grid_side, half_width))
    cols_part = jnp.broadcast_to(waves[None, :, :], (grid_side, grid_side, half_width))
    return jnp.concatenate([rows_part, cols_part], 2).reshape(grid_side * grid_side, feat_width)

def patchify(latent):
    samples_n, channels, height, breadth = latent.shape
    shaped = latent.reshape(samples_n, channels, height // 2, 2, breadth // 2, 2).transpose(0, 2, 4, 3, 5, 1)
    return shaped.reshape(samples_n, height // 2 * (breadth // 2), 4 * channels)

def assemble(blocks, slot_of_block, first_block, row_count, col_count):
    picked = blocks[slot_of_block[first_block:first_block + row_count * col_count]]
    return picked.reshape(row_count, col_count, BLOCK_SIDE, BLOCK_SIDE).transpose(0, 2, 1, 3).reshape(row_count * BLOCK_SIDE, col_count * BLOCK_SIDE)

def split_blocks(matrix, row_count, col_count):
    return matrix.reshape(row_count, BLOCK_SIDE, col_count, BLOCK_SIDE).transpose(0, 2, 1, 3).reshape(row_count * col_count, BLOCK_SIDE, BLOCK_SIDE)

def loss_terms(result, frozen, target, weights, upper_log, lower_log, mean_gap):
    samples_n = result.shape[0]
    shaped = result.reshape(samples_n, -1, 4, 8)
    predicted = shaped[..., :4]
    var_raw = shaped[..., 4:]
    frozen_pred = frozen.reshape(samples_n, -1, 4, 8)[..., :4]
    upper = upper_log[:, None, None, None]
    lower = lower_log[:, None, None, None]
    squared = lax.optimization_barrier(jnp.mean((target - predicted) ** 2, axis=(1, 2, 3)))
    fraction = (var_raw + 1.0) / 2.0
    log_var = fraction * upper + (1.0 - fraction) * lower
    mean_diff = mean_gap[:, None, None, None] * (frozen_pred - target)
    diverge = 0.5 * (-1.0 + log_var - lower + jnp.exp(lower - log_var) + mean_diff * mean_diff * jnp.exp(-log_var))
    var_bound = lax.optimization_barrier(jnp.mean(diverge, axis=(1, 2, 3))) / math.log(2.0)
    return jnp.sum(weights * (squared + var_bound))

def inverse_root(matrix):
    size_b = matrix.shape[-1]
    identity = jnp.eye(size_b, dtype=jnp.float32)
    traces = jnp.trace(matrix, axis1=-2, axis2=-1)
    shifted = matrix + (0.0001 * traces / size_b)[..., None, None] * identity
    factor_z = 2.5 / jnp.sqrt(lax.optimization_barrier(jnp.sum(shifted * shifted, axis=(-2, -1))))
    contracted = shifted * factor_z[..., None, None]
    estimate = identity * jnp.sqrt(jnp.sqrt(factor_z))[..., None, None]
    for newton_step in range(NEWTON):
        factor = (5.0 * identity - contracted) / 4.0
        estimate = matmul(estimate, factor)
        factor_sq = matmul(factor, factor)
        contracted = matmul(matmul(factor_sq, factor_sq), contracted)
    return estimate

def adam_update(weight, gradient, moment_one, second):
    moment_one = 0.5 * moment_one + 0.5 * gradient
    second = 0.5 * second + 0.5 * gradient * gradient
    correct = 1.0 - 0.5 ** STEP
    updated = weight - adam_rate * (moment_one / correct / (jnp.sqrt(second / correct) + 1e-08) + decay_rate * weight)
    return (moment_one, second, updated)

def forward(params, latent_patches, time_freq, onehot):
    input_weight, output_weight, condition_vectors, head_condition_table, slice_bias_vector, side_bias_vector = params
    input_weight = lowered_values(input_weight)
    output_weight = lowered_values(output_weight)
    condition_vectors = lowered_values(condition_vectors)
    head_condition_table = lowered_values(head_condition_table)
    model_parallel_ways = input_weight.shape[0]
    query_width = HEADS * HD // model_parallel_ways
    feedforward_width = FF // model_parallel_ways
    adaptive_column = 3 * query_width + feedforward_width
    samples_n, seq_len = (latent_patches.shape[0], latent_patches.shape[1])
    t2_row = PATCH_VALUES + FREQ
    class_row = PATCH_VALUES + FREQ + MODEL_WIDTH
    initial_rows = lowered_backward(jnp.einsum('wne,et->wnt', lowered_values(latent_patches), condition_vectors[:PATCH_VALUES], precision=exact_precision_flag) + side_bias_vector[:MODEL_WIDTH] + position_embedding(LATENT_SIDE // 2, MODEL_WIDTH))
    first_t = lowered_backward(matmul(lowered_values(time_freq), condition_vectors[PATCH_VALUES:t2_row]) + side_bias_vector[MODEL_WIDTH:2 * MODEL_WIDTH])
    second_t = lowered_backward(matmul(lowered_values(swish_unit(first_t)), condition_vectors[t2_row:class_row]) + side_bias_vector[2 * MODEL_WIDTH:3 * MODEL_WIDTH])
    cond_vec = second_t + matmul(onehot, condition_vectors[class_row:])
    signal = lowered_values(swish_unit(cond_vec))
    modul = lowered_backward(jnp.einsum('sd,jde->sje', signal, input_weight[:, :, adaptive_column:], precision=exact_precision_flag) + slice_bias_vector[None, :, 2 * query_width + feedforward_width:])
    modul = modul.reshape(samples_n, 6 * MODEL_WIDTH)

    def modulation_part(position):
        return modul[:, None, position * MODEL_WIDTH:(position + 1) * MODEL_WIDTH]

    def heads_of(inputs):
        return inputs.reshape(samples_n, model_parallel_ways, seq_len, query_width // HD, HD)
    attention_input = lowered_values(layer_norm(initial_rows) * (1.0 + modulation_part(1)) + modulation_part(0))
    projected_output = jnp.einsum('vxo,poh->vpxh', attention_input, input_weight[:, :, :3 * query_width], precision=exact_precision_flag)
    queries = lowered_values(lowered_backward(projected_output[..., :query_width] + slice_bias_vector[None, :, None, :query_width]))
    key_heads = lowered_values(lowered_backward(projected_output[..., query_width:2 * query_width]))
    values = lowered_values(lowered_backward(projected_output[..., 2 * query_width:] + slice_bias_vector[None, :, None, query_width:2 * query_width]))
    scores = lowered_backward(jnp.einsum('sjlhe,sjmhe->sjhlm', heads_of(queries), heads_of(key_heads), precision=exact_precision_flag) * HD ** (-0.5))
    attn_probs = jax.nn.softmax(scores, axis=-1)
    merged_head_outputs = jnp.einsum('sjhlm,sjmhe->sjlhe', lowered_values(attn_probs), heads_of(values), precision=exact_precision_flag)
    merged_head_outputs = lowered_values(lowered_backward(merged_head_outputs.reshape(samples_n, model_parallel_ways, seq_len, query_width)))
    attention_output = lowered_backward(jnp.einsum('pgka,gaf->pkf', merged_head_outputs, output_weight[:, :query_width], precision=exact_precision_flag) + side_bias_vector[3 * MODEL_WIDTH:4 * MODEL_WIDTH])
    middle = initial_rows + modulation_part(2) * attention_output
    perceptron_input = lowered_values(layer_norm(middle) * (1.0 + modulation_part(4)) + modulation_part(3))
    hidden_activations = lowered_backward(jnp.einsum('pcx,rxt->prct', perceptron_input, input_weight[:, :, 3 * query_width:adaptive_column], precision=exact_precision_flag) + slice_bias_vector[None, :, None, 2 * query_width:2 * query_width + feedforward_width])
    branch_output = lowered_backward(jnp.einsum('kihw,iwc->khc', lowered_values(tanh_gelu_activation(hidden_activations)), output_weight[:, query_width:], precision=exact_precision_flag) + side_bias_vector[4 * MODEL_WIDTH:5 * MODEL_WIDTH])
    final_rows = middle + modulation_part(5) * branch_output
    final_mod = lowered_backward(matmul(signal, head_condition_table[:, :2 * MODEL_WIDTH]) + side_bias_vector[5 * MODEL_WIDTH:7 * MODEL_WIDTH])
    head_input = lowered_values(layer_norm(final_rows) * (1.0 + final_mod[:, None, MODEL_WIDTH:]) + final_mod[:, None, :MODEL_WIDTH])
    return lowered_backward(jnp.einsum('wjn,nk->wjk', head_input, head_condition_table[:, 2 * MODEL_WIDTH:], precision=exact_precision_flag) + side_bias_vector[7 * MODEL_WIDTH:])

def reference(latents, noise, timesteps, labels, loss_weights, slotted_block_weights, statistics, slot_of_block, cond_tables, head_tables, slice_bias, side_bias, cond_m, cond_v, head_m, head_v, slice_m, slice_v, side_m, side_v):
    model_parallel_ways = slotted_block_weights.shape[0]
    query_width = HEADS * HD // model_parallel_ways
    feedforward_width = FF // model_parallel_ways
    in_width = 3 * query_width + feedforward_width + 6 * MODEL_WIDTH // model_parallel_ways
    row_blocks = MODEL_WIDTH // BLOCK_SIDE
    col_blocks = in_width // BLOCK_SIDE
    out_blocks = (query_width + feedforward_width) // BLOCK_SIDE
    first_out = row_blocks * col_blocks
    occupied_blocks = first_out + out_blocks * row_blocks
    input_weight = jnp.stack([assemble(slotted_block_weights[part_j], slot_of_block, 0, row_blocks, col_blocks) for part_j in range(model_parallel_ways)])
    output_weight = jnp.stack([assemble(slotted_block_weights[part_j], slot_of_block, first_out, out_blocks, row_blocks) for part_j in range(model_parallel_ways)])
    params = (input_weight, output_weight, cond_tables, head_tables, slice_bias, side_bias)
    weight_sum = jnp.sum(loss_weights)
    grouped = tuple((source.reshape((N_DP, SAMP_DEV) + source.shape[1:]) for source in (latents, noise, timesteps, labels, loss_weights)))

    def one_group(running, group_data):
        gradients, loss_acc = running
        lat_group, noise_group, step_ids, label_ids, weights = group_data
        keep_rate, noise_rate, upper_log, lower_log, mean_gap = coefficients(step_ids)
        noisy_lat = keep_rate[:, None, None, None] * lat_group + noise_rate[:, None, None, None] * noise_group
        latent_patches = patchify(noisy_lat)
        target = patchify(noise_group).reshape(SAMP_DEV, SEQ, 4, 4)
        time_freq = time_features(step_ids, FREQ)
        onehot = (label_ids[:, None] == jnp.arange(CLASSES, dtype=jnp.int32)[None, :]).astype(jnp.float32)

        def model_fn(*tensors):
            return forward(tensors, latent_patches, time_freq, onehot)
        output, pull_back = jax.vjp(model_fn, *params)

        def objective(result):
            return loss_terms(result, output, target, weights, upper_log, lower_log, mean_gap)
        loss_part, loss_pull = jax.vjp(objective, output)
        seed_grad, = loss_pull(jnp.ones_like(loss_part) / weight_sum)
        split_pieces = pull_back(seed_grad)
        summed = tuple((before + addend for before, addend in zip(gradients, split_pieces)))
        return ((summed, loss_acc + loss_part), None)
    zero_filled = tuple((jnp.zeros_like(tensor) for tensor in params))
    (gradients, loss_sum), unused = lax.scan(one_group, (zero_filled, jnp.zeros((), jnp.float32)), grouped)
    g_in, g_out, g_cond, g_head, g_slice, g_side = gradients
    slot_total = slot_of_block.shape[0]
    split_pieces = jnp.stack([jnp.concatenate([split_blocks(g_in[part_j], row_blocks, col_blocks), split_blocks(g_out[part_j], out_blocks, row_blocks)], 0) for part_j in range(model_parallel_ways)])
    clipped_block_gradients = jnp.zeros((model_parallel_ways, slot_total, BLOCK_SIDE, BLOCK_SIDE), jnp.float32).at[:, slot_of_block[:occupied_blocks]].set(split_pieces)
    squares = jnp.sum(clipped_block_gradients * clipped_block_gradients) + jnp.sum(g_cond * g_cond) + jnp.sum(g_head * g_head) + jnp.sum(g_slice * g_slice) + jnp.sum(g_side * g_side)
    grad_norm = jnp.sqrt(squares)
    clip_factor = 1.0 / jnp.maximum(grad_norm, 1.0)
    clipped = clipped_block_gradients * clip_factor
    flipped = jnp.swapaxes(clipped, -1, -2)
    left_stat = 0.5 * statistics[:, :, 0] + 0.5 * matmul(clipped, flipped)
    right_stat = 0.5 * statistics[:, :, 1] + 0.5 * matmul(flipped, clipped)
    new_statistics = jnp.stack([left_stat, right_stat], 2)
    inverse_roots = inverse_root(new_statistics)
    direction = matmul(matmul(inverse_roots[:, :, 0], clipped), inverse_roots[:, :, 1])
    new_blocks = slotted_block_weights - shampoo_rate * (direction + decay_rate * slotted_block_weights)
    cond_one, cond_two, new_cond = adam_update(cond_tables, g_cond * clip_factor, cond_m, cond_v)
    head_one, head_two, new_head = adam_update(head_tables, g_head * clip_factor, head_m, head_v)
    slice_one, slice_two, new_slice = adam_update(slice_bias, g_slice * clip_factor, slice_m, slice_v)
    side_one, side_two, new_side = adam_update(side_bias, g_side * clip_factor, side_m, side_v)
    return (loss_sum, weight_sum, grad_norm, clipped, new_statistics, new_blocks, new_blocks.astype(jnp.bfloat16), cond_one, cond_two, new_cond, new_cond.astype(jnp.bfloat16), head_one, head_two, new_head, new_head.astype(jnp.bfloat16), slice_one, slice_two, new_slice, side_one, side_two, new_side)
```

```python
import math

import jax
import jax.numpy as jnp
from jax import lax
from jax.experimental import pallas as pl
from jax.experimental.pallas import tpu as pltpu
from jax.sharding import PartitionSpec as P

MODEL_WIDTH = 1152
HEADS = 16
HD = 72
FF = 4608
FREQ = 256
CLASSES = 1001
LATENT_SIDE = 32
PATCH_VALUES = 16
BLOCK_SIDE = 288
NEWTON = 6
STEP = 5
LANES = 256
TAIL = BLOCK_SIDE - LANES


exact_precision_flag = lax.Precision.HIGHEST
shampoo_rate = 0.5
adam_rate = 0.05
decay_rate = 0.01


def dense(operand, weight):
    return jnp.dot(operand, weight, preferred_element_type=jnp.float32)


def back_dense(gradient, weight):
    return jnp.einsum("...j,ij->...i", gradient, weight, preferred_element_type=jnp.float32)


def weight_grad(operand, gradient):
    return jnp.einsum("...i,...j->ij", operand, gradient, preferred_element_type=jnp.float32)


def total_of(inputs):
    return jnp.sum(inputs.astype(jnp.float32), axis=tuple(range(inputs.ndim - 1)))


def swish_unit(inputs):
    return inputs / (1.0 + jnp.exp(-inputs))


def swish_slope(inputs):
    sigmoid = 1.0 / (1.0 + jnp.exp(-inputs))
    return sigmoid * (1.0 + inputs * (1.0 - sigmoid))


def tanh_gelu_activation(inputs):
    return (
        0.5
        * inputs
        * (1.0 + jnp.tanh(0.7978845608028654 * (inputs + 0.044715 * inputs * inputs * inputs)))
    )


def gelu_slope(inputs):
    inner = jnp.tanh(0.7978845608028654 * (inputs + 0.044715 * inputs * inputs * inputs))
    return 0.5 * (1.0 + inner) + 0.5 * inputs * (1.0 - inner * inner) * 0.7978845608028654 * (
        1.0 + 3.0 * 0.044715 * inputs * inputs
    )


def layer_norm(inputs):
    centred = inputs - jnp.mean(inputs, -1, keepdims=True)
    inv_std = lax.rsqrt(jnp.mean(centred * centred, -1, keepdims=True) + 1e-06)
    return (centred * inv_std, inv_std)


def norm_back(gradient, normed, inv_std):
    return inv_std * (
        gradient
        - jnp.mean(gradient, -1, keepdims=True)
        - normed * jnp.mean(gradient * normed, -1, keepdims=True)
    )


def coefficients(step_ids):
    grid = jnp.arange(1000).astype(jnp.float32)
    betas = 0.0001 + (0.02 - 0.0001) * grid / 999.0
    logs = jnp.log(1.0 - betas)[None, :]
    index = jnp.arange(1000, dtype=jnp.int32)[None, :]
    beta_t = 0.0001 + (0.02 - 0.0001) * step_ids.astype(jnp.float32) / 999.0
    cumul_t = jnp.exp(jnp.sum(jnp.where(index <= step_ids[:, None], logs, 0.0), 1))
    before_t = jnp.exp(jnp.sum(jnp.where(index < step_ids[:, None], logs, 0.0), 1))
    keep_rate = jnp.sqrt(cumul_t)
    noise_rate = jnp.sqrt(1.0 - cumul_t)
    upper_log = jnp.log(beta_t)
    lower_log = jnp.log(beta_t * (1.0 - before_t) / (1.0 - cumul_t))
    mean_gap = beta_t * jnp.sqrt(before_t) / (1.0 - cumul_t) * jnp.sqrt(1.0 / cumul_t - 1.0)
    return (keep_rate, noise_rate, upper_log, lower_log, mean_gap)


def time_features(step_ids, feat_width):
    half_width = feat_width // 2
    frequencies = jnp.exp(
        -math.log(10000.0) * jnp.arange(half_width).astype(jnp.float32) / half_width
    )
    phases = step_ids.astype(jnp.float32)[:, None] * frequencies[None, :]
    return jnp.concatenate([jnp.cos(phases), jnp.sin(phases)], 1)


def position_embedding(grid_side, feat_width):
    quarter = feat_width // 4
    omegas = jnp.exp(-math.log(10000.0) * jnp.arange(quarter).astype(jnp.float32) / quarter)
    coords = jnp.arange(grid_side).astype(jnp.float32)
    angles = coords[:, None] * omegas[None, :]
    waves = jnp.concatenate([jnp.sin(angles), jnp.cos(angles)], 1)
    half_width = feat_width // 2
    rows_part = jnp.broadcast_to(waves[:, None, :], (grid_side, grid_side, half_width))
    cols_part = jnp.broadcast_to(waves[None, :, :], (grid_side, grid_side, half_width))
    return jnp.concatenate([rows_part, cols_part], 2).reshape(grid_side * grid_side, feat_width)


def patchify(latent):
    samples_n, channels, height, breadth = latent.shape
    shaped = latent.reshape(samples_n, channels, height // 2, 2, breadth // 2, 2).transpose(
        0, 2, 4, 3, 5, 1
    )
    return shaped.reshape(samples_n, height // 2 * (breadth // 2), 4 * channels)


PACK_ROWS = 656


def pack(x):
    quarter = BLOCK_SIDE // 4
    tail = x[:, LANES:].astype(jnp.float32)
    tail = jnp.concatenate([tail[i * quarter : (i + 1) * quarter] for i in range(4)], axis=1)
    fill = jnp.zeros((PACK_ROWS - 2 * BLOCK_SIDE - quarter, LANES // 2), jnp.float32)
    tail = jnp.concatenate([tail, fill], axis=0)
    half = LANES // 2
    return x[:, :half], x[:, half:LANES], tail.astype(x.dtype)


def unpack(x):
    side, quarter = BLOCK_SIDE, BLOCK_SIDE // 4
    tail = x[2 * side :].astype(jnp.float32)[:quarter]
    tail = jnp.concatenate([tail[:, i * TAIL : (i + 1) * TAIL] for i in range(4)], axis=0)
    main = jnp.concatenate([x[:side], x[side : 2 * side]], axis=1)
    return main, tail.astype(x.dtype)


def store_packed(ref, index, x):
    a, b, c = pack(x)
    side = BLOCK_SIDE
    ref[index + (slice(0, side),)] = a
    ref[index + (slice(side, 2 * side),)] = b
    ref[index + (slice(2 * side, PACK_ROWS),)] = c


def pack_blocks(blocks):
    count, side = blocks.shape[0], BLOCK_SIDE

    def body(x_ref, out_ref):
        store_packed(out_ref, (0,), x_ref[0].astype(jnp.bfloat16))

    return pl.pallas_call(
        body,
        grid=(count,),
        in_specs=[pl.BlockSpec((1, side, side), lambda i: (i, 0, 0))],
        out_specs=pl.BlockSpec((1, PACK_ROWS, LANES // 2), lambda i: (i, 0, 0)),
        out_shape=jax.ShapeDtypeStruct((count, PACK_ROWS, LANES // 2), jnp.bfloat16),
        name="pack_blocks",
    )(blocks)


def remote(source, target, send, receive, place):
    return pltpu.make_async_remote_copy(
        src_ref=source,
        dst_ref=target,
        send_sem=send,
        recv_sem=receive,
        device_id=place,
        device_id_type=pl.DeviceIdType.MESH,
    )


def signal_to(semaphore, place):
    pl.semaphore_signal(semaphore, inc=1, device_id=place, device_id_type=pl.DeviceIdType.MESH)


COLUMNS = 2
LAYERS = 4


def grid_place():
    me = lax.axis_index("dp")
    return me // COLUMNS, me % COLUMNS


def greet_neighbours(z, y):
    barrier = pltpu.get_barrier_semaphore()
    signal_to(barrier, {"dp": z * COLUMNS + 1 - y})

    @pl.when(z < LAYERS - 1)
    def _():
        signal_to(barrier, {"dp": (z + 1) * COLUMNS + y})

    @pl.when(z > 0)
    def _():
        signal_to(barrier, {"dp": (z - 1) * COLUMNS + y})

    pl.semaphore_wait(barrier, jnp.where((z > 0) & (z < LAYERS - 1), 3, 2))


def gather_body(x_ref, out_ref, local_sem, up_sem, down_sem, side_sem, recv_sem):
    count = x_ref.shape[0]
    z, y = grid_place()
    greet_neighbours(z, y)
    peer = {"dp": z * COLUMNS + 1 - y}
    above = {"dp": jnp.minimum(z + 1, LAYERS - 1) * COLUMNS + y}
    below = {"dp": jnp.maximum(z - 1, 0) * COLUMNS + y}

    def block(layer, column, k):
        return out_ref.at[(layer * COLUMNS + column) * count + k]

    def move(source, layer, k, send, place):
        return remote(
            source, block(layer, y, k), send.at[layer, k], recv_sem.at[layer, y, k], place
        )

    def arrival(layer, column, k):
        here = block(layer, column, k)
        return remote(here, here, side_sem.at[0, 0], recv_sem.at[layer, column, k], peer)

    def send_own(k, _):
        own = x_ref.at[k]

        @pl.when(z < LAYERS - 1)
        def _():
            move(own, z, k, up_sem, above).start()

        @pl.when(z > 0)
        def _():
            move(own, z, k, down_sem, below).start()

        move(own, z, k, side_sem, peer).start()
        pltpu.make_async_copy(own, block(z, y, k), local_sem.at[k]).start()
        return 0

    lax.fori_loop(0, count, send_own, 0)

    for hop in range(1, LAYERS):

        def pass_on(k, _):
            @pl.when(z >= hop)
            def _():
                layer = z - hop
                arrival(layer, y, k).wait_recv()

                @pl.when(z < LAYERS - 1)
                def _():
                    move(block(layer, y, k), layer, k, up_sem, above).start()

                move(block(layer, y, k), layer, k, side_sem, peer).start()

            @pl.when(z + hop < LAYERS)
            def _():
                layer = z + hop
                arrival(layer, y, k).wait_recv()

                @pl.when(z > 0)
                def _():
                    move(block(layer, y, k), layer, k, down_sem, below).start()

                move(block(layer, y, k), layer, k, side_sem, peer).start()

            return 0

        lax.fori_loop(0, count, pass_on, 0)

    def finish(k, _):
        pltpu.make_async_copy(x_ref.at[k], block(z, y, k), local_sem.at[k]).wait()
        for layer in range(LAYERS):
            arrival(layer, 1 - y, k).wait_recv()
            move(block(layer, y, k), layer, k, side_sem, peer).wait_send()

            @pl.when((z < LAYERS - 1) & (layer <= z))
            def _():
                move(block(layer, y, k), layer, k, up_sem, above).wait_send()

            @pl.when((z > 0) & (layer >= z))
            def _():
                move(block(layer, y, k), layer, k, down_sem, below).wait_send()

        return 0

    lax.fori_loop(0, count, finish, 0)


def gather_blocks(packed):
    ways = lax.axis_size("dp")
    if ways != COLUMNS * LAYERS:
        return lax.all_gather(packed, "dp", axis=0, tiled=True)
    count = packed.shape[0]
    dma = pltpu.SemaphoreType.DMA
    return pl.pallas_call(
        gather_body,
        in_specs=[pl.BlockSpec(memory_space=pl.ANY)],
        out_specs=pl.BlockSpec(memory_space=pl.ANY),
        out_shape=jax.ShapeDtypeStruct((count * ways,) + packed.shape[1:], packed.dtype),
        scratch_shapes=[
            dma((count,)),
            dma((LAYERS, count)),
            dma((LAYERS, count)),
            dma((LAYERS, count)),
            dma((LAYERS, COLUMNS, count)),
        ],
        compiler_params=pltpu.CompilerParams(collective_id=0, has_side_effects=True),
        name="gather_blocks",
    )(packed)


def reduce_body(
    x_ref, out_ref, side_buf, up_buf, down_buf, side_send, line_send, side_recv, up_recv, down_recv
):
    count = out_ref.shape[0]
    z, y = grid_place()
    greet_neighbours(z, y)
    peer = {"dp": z * COLUMNS + 1 - y}
    above = {"dp": jnp.minimum(z + 1, LAYERS - 1) * COLUMNS + y}
    below = {"dp": jnp.maximum(z - 1, 0) * COLUMNS + y}

    def across(layer, k):
        return remote(
            x_ref.at[(layer * COLUMNS + 1 - y) * count + k],
            side_buf.at[layer, k],
            side_send.at[layer, k],
            side_recv.at[layer, k],
            peer,
        )

    def upward(layer, k):
        return remote(
            side_buf.at[layer, k], up_buf.at[layer, k], line_send.at[layer, k], up_recv.at[layer, k], above
        )

    def downward(layer, k):
        return remote(
            side_buf.at[layer, k], down_buf.at[layer, k], line_send.at[layer, k], down_recv.at[layer, k], below
        )

    def pair_sum(layer, k):
        across(layer, k).wait_recv()
        own = x_ref[(layer * COLUMNS + y) * count + k].astype(jnp.float32)
        return own + side_buf[layer, k].astype(jnp.float32)

    for hop in range(LAYERS - 1, -1, -1):

        def start(k, _):
            @pl.when(z + hop < LAYERS)
            def _():
                across(z + hop, k).start()

            if hop > 0:

                @pl.when(z >= hop)
                def _():
                    across(z - hop, k).start()

            return 0

        lax.fori_loop(0, count, start, 0)

    for hop in range(LAYERS - 1, 0, -1):

        def step(k, _):
            @pl.when(z + hop < LAYERS)
            def _():
                layer = z + hop
                total = pair_sum(layer, k)

                @pl.when(z > 0)
                def _():
                    upward(layer, k).wait_recv()
                    side_buf[layer, k] = (total + up_buf[layer, k].astype(jnp.float32)).astype(
                        jnp.bfloat16
                    )

                @pl.when(z == 0)
                def _():
                    side_buf[layer, k] = total.astype(jnp.bfloat16)

                upward(layer, k).start()

            @pl.when(z >= hop)
            def _():
                layer = z - hop
                total = pair_sum(layer, k)

                @pl.when(z < LAYERS - 1)
                def _():
                    downward(layer, k).wait_recv()
                    side_buf[layer, k] = (total + down_buf[layer, k].astype(jnp.float32)).astype(
                        jnp.bfloat16
                    )

                @pl.when(z == LAYERS - 1)
                def _():
                    side_buf[layer, k] = total.astype(jnp.bfloat16)

                downward(layer, k).start()

            return 0

        lax.fori_loop(0, count, step, 0)

    def last(k, _):
        out_ref[k] = pair_sum(z, k)

        @pl.when(z > 0)
        def _():
            upward(z, k).wait_recv()
            out_ref[k] += up_buf[z, k].astype(jnp.float32)

        @pl.when(z < LAYERS - 1)
        def _():
            downward(z, k).wait_recv()
            out_ref[k] += down_buf[z, k].astype(jnp.float32)

        for layer in range(LAYERS):
            across(layer, k).wait_send()

            @pl.when(layer > z)
            def _():
                upward(layer, k).wait_send()

            @pl.when(layer < z)
            def _():
                downward(layer, k).wait_send()

        return 0

    lax.fori_loop(0, count, last, 0)


def reduce_blocks(slots):
    ways = lax.axis_size("dp")
    if ways != COLUMNS * LAYERS:
        return lax.psum_scatter(slots, "dp", scatter_dimension=0, tiled=True).astype(jnp.float32)
    count = slots.shape[0] // ways
    dma = pltpu.SemaphoreType.DMA
    landing = pltpu.VMEM((LAYERS, count) + slots.shape[1:], jnp.bfloat16)
    return pl.pallas_call(
        reduce_body,
        in_specs=[pl.BlockSpec(memory_space=pltpu.VMEM)],
        out_specs=pl.BlockSpec(memory_space=pltpu.VMEM),
        out_shape=jax.ShapeDtypeStruct((count,) + slots.shape[1:], jnp.float32),
        scratch_shapes=[landing] * 3 + [dma((LAYERS, count))] * 5,
        compiler_params=pltpu.CompilerParams(
            collective_id=1, has_side_effects=True, vmem_limit_bytes=52 * 2**20
        ),
        name="reduce_blocks",
    )(slots)


EVERY = ("dp", "mp")


def exchange(items, axes, number):
    mp, dp = lax.axis_size("mp"), lax.axis_size("dp")
    n = {"dp": dp, "mp": mp, EVERY: dp * mp}[axes]

    def place(i):
        return {"dp": i // mp, "mp": i % mp} if axes == EVERY else {axes: i}

    def row(i):
        return i // mp if axes == EVERY else i

    def body(*refs):
        m = len(items)
        sources, outs, send, receive = refs[:m], refs[m : 2 * m], refs[-2], refs[-1]
        me = lax.axis_index("dp") * mp + lax.axis_index("mp") if axes == EVERY else lax.axis_index(axes)
        barrier = pltpu.get_barrier_semaphore()

        def greet(i, _):
            signal_to(barrier, place(lax.rem(me + i, n)))
            return 0

        lax.fori_loop(1, n, greet, 0)
        pl.semaphore_wait(barrier, n - 1)

        def piece(j, to):
            return sources[j].at[row(to)] if items[j][1] == "scatter" else sources[j]

        def start(i, _):
            to = lax.rem(me + i, n)
            for j in range(m):
                remote(piece(j, to), outs[j].at[me], send.at[j, i], receive.at[j, me], place(to)).start()
            return 0

        lax.fori_loop(1, n, start, 0)
        for j in range(m):
            outs[j][me] = sources[j][row(me)] if items[j][1] == "scatter" else sources[j][...]

        def finish(i, _):
            to = lax.rem(me + i, n)
            for j in range(m):
                copy = remote(piece(j, to), outs[j].at[to], send.at[j, i], receive.at[j, to], place(to))
                copy.wait_recv()
                copy.wait_send()
            return 0

        lax.fori_loop(1, n, finish, 0)

    arrays = [a for a, _ in items]
    shapes = [
        jax.ShapeDtypeStruct((n,) + (a.shape[1:] if kind == "scatter" else a.shape), a.dtype)
        for a, kind in items
    ]
    vmem = pl.BlockSpec(memory_space=pltpu.VMEM)
    return pl.pallas_call(
        body,
        in_specs=[vmem] * len(arrays),
        out_specs=[vmem] * len(arrays),
        out_shape=shapes,
        scratch_shapes=[pltpu.SemaphoreType.DMA((len(arrays), n))] * 2,
        compiler_params=pltpu.CompilerParams(
            collective_id=number, has_side_effects=True, vmem_limit_bytes=40 * 2**20
        ),
        name=f"exchange_{number}",
    )(*arrays)


def assemble(blocks, slots, first, rows, cols):
    side = BLOCK_SIDE

    def body(ids, *refs):
        parts = [part for r in refs[:-1] for part in unpack(r[0])]
        refs[-1][...] = jnp.concatenate(parts, axis=1)

    def spec(c):
        return pl.BlockSpec(
            (1, PACK_ROWS, LANES // 2), lambda r, ids: (ids[first + r * cols + c], 0, 0)
        )

    return pl.pallas_call(
        body,
        grid_spec=pltpu.PrefetchScalarGridSpec(
            num_scalar_prefetch=1,
            grid=(rows,),
            in_specs=[spec(c) for c in range(cols)],
            out_specs=pl.BlockSpec((side, side * cols), lambda r, ids: (r, 0)),
        ),
        out_shape=jax.ShapeDtypeStruct((rows * side, cols * side), jnp.bfloat16),
        compiler_params=pltpu.CompilerParams(vmem_limit_bytes=40 * 2**20),
        cost_estimate=pl.CostEstimate(
            flops=0, bytes_accessed=4 * rows * cols * side * side, transcendentals=0
        ),
        name="assemble",
    )(slots, *([blocks] * cols))


def to_slots(g_in, g_out, slots, total):
    side = BLOCK_SIDE
    ri, ci = g_in.shape[0] // side, g_in.shape[1] // side
    ro, co = g_out.shape[0] // side, g_out.shape[1] // side
    steps = ri + ro

    def body(ids, gi, go, *rest):
        out, buf, sem = rest[-3:]
        s = pl.program_id(0)
        half = lax.rem(s, 2)

        def drain(which, count):
            for c in range(count):
                pltpu.make_async_copy(buf.at[which, c], out.at[0], sem.at[which, c]).wait()

        def send(source, count, base):
            for c in range(count):
                store_packed(buf, (half, c), source[:, c * side : (c + 1) * side])
                pltpu.make_async_copy(
                    buf.at[half, c], out.at[ids[base + c]], sem.at[half, c]
                ).start()

        @pl.when(jnp.logical_and(s >= 2, s - 2 < ri))
        def _():
            drain(half, ci)

        @pl.when(s - 2 >= ri)
        def _():
            drain(half, co)

        @pl.when(s < ri)
        def _():
            send(gi, ci, s * ci)

        @pl.when(s >= ri)
        def _():
            send(go, co, ri * ci + (s - ri) * co)

        @pl.when(s == steps - 1)
        def _():
            drain(1 - half, co)
            drain(half, co)

    extra, aliases = [], {}
    if total != ri * ci + ro * co:
        extra = [jnp.zeros((total, PACK_ROWS, LANES // 2), jnp.bfloat16)]
        aliases = {3: 0}
    return pl.pallas_call(
        body,
        grid_spec=pltpu.PrefetchScalarGridSpec(
            num_scalar_prefetch=1,
            grid=(steps,),
            in_specs=[
                pl.BlockSpec((side, ci * side), lambda s, ids: (jnp.minimum(s, ri - 1), 0)),
                pl.BlockSpec((side, co * side), lambda s, ids: (jnp.maximum(s - ri, 0), 0)),
            ]
            + [pl.BlockSpec(memory_space=pl.ANY)] * len(extra),
            out_specs=pl.BlockSpec(memory_space=pl.ANY),
            scratch_shapes=[
                pltpu.VMEM((2, max(ci, co), PACK_ROWS, LANES // 2), jnp.bfloat16),
                pltpu.SemaphoreType.DMA((2, max(ci, co))),
            ],
        ),
        out_shape=jax.ShapeDtypeStruct((total, PACK_ROWS, LANES // 2), jnp.bfloat16),
        compiler_params=pltpu.CompilerParams(vmem_limit_bytes=40 * 2**20),
        cost_estimate=pl.CostEstimate(
            flops=0, bytes_accessed=4 * (ri * ci + ro * co) * side * side, transcendentals=0
        ),
        input_output_aliases=aliases,
        name="to_slots",
    )(slots, g_in, g_out, *extra)


def loss_terms(result, frozen, target, weights, upper_log, lower_log, mean_gap):
    samples_n = result.shape[0]
    shaped = result.reshape(samples_n, -1, 4, 8)
    predicted = shaped[..., :4]
    var_raw = shaped[..., 4:]
    frozen_pred = frozen.reshape(samples_n, -1, 4, 8)[..., :4]
    upper = upper_log[:, None, None, None]
    lower = lower_log[:, None, None, None]
    squared = jnp.mean((target - predicted) ** 2, axis=(1, 2, 3))
    fraction = (var_raw + 1.0) / 2.0
    log_var = fraction * upper + (1.0 - fraction) * lower
    mean_diff = mean_gap[:, None, None, None] * (frozen_pred - target)
    diverge = 0.5 * (
        -1.0
        + log_var
        - lower
        + jnp.exp(lower - log_var)
        + mean_diff * mean_diff * jnp.exp(-log_var)
    )
    var_bound = jnp.mean(diverge, axis=(1, 2, 3)) / math.log(2.0)
    return jnp.sum(weights * (squared + var_bound))


def halves(x):
    high = x.astype(jnp.bfloat16)
    return high, (x - high.astype(jnp.float32)).astype(jnp.bfloat16)


def left_form(main, tail):
    mh, ml = halves(main)
    th, tl = halves(tail)
    return jnp.concatenate([mh, mh, ml, th, th, tl], axis=1)


def right_form(x):
    h, l = halves(x)
    return jnp.concatenate(
        [h[:LANES], l[:LANES], h[:LANES], h[LANES:], l[LANES:], h[LANES:]], axis=0
    )


def product(left, right):
    return jnp.dot(left, right, preferred_element_type=jnp.float32)


def symmetric_product(left, right_main, right_tail):
    main = product(left, right_main)
    corner = product(left[LANES:], right_tail)
    return main, jnp.concatenate([main[LANES:].T, corner], axis=0)


def inverse_roots(pairs, eye_main, eye_tail):
    contracted, scales = [], []
    for main, tail in pairs:
        trace = jnp.sum(main * eye_main) + jnp.sum(tail * eye_tail)
        shift = 0.0001 * trace / BLOCK_SIDE
        main = main + shift * eye_main
        tail = tail + shift * eye_tail
        square = jnp.sum(main * main, axis=(0, 1), keepdims=True) + jnp.sum(
            tail * tail, axis=(0, 1), keepdims=True
        )
        factor_z = 2.5 / jnp.sqrt(square)
        contracted.append((main * factor_z, tail * factor_z))
        scales.append(jnp.sqrt(jnp.sqrt(factor_z)))
    estimates = None
    for newton_step in range(NEWTON):
        more = newton_step < NEWTON - 1
        factors = [((5.0 * eye_main - m) * 0.25, (5.0 * eye_tail - t) * 0.25) for m, t in contracted]
        rights = [(right_form(m), right_form(t)) for m, t in factors]
        lefts = [left_form(m, t) for m, t in factors]
        if more:
            powers = [symmetric_product(l, *r) for l, r in zip(lefts, rights)]
        if estimates is None:
            estimates = [(m * s, t * s) for (m, t), s in zip(factors, scales)]
        else:
            estimates = [
                symmetric_product(left_form(*e), *r) for e, r in zip(estimates, rights)
            ]
        if more:
            powers = [
                symmetric_product(left_form(*q), right_form(q[0]), right_form(q[1])) for q in powers
            ]
            contracted = [
                symmetric_product(left_form(*q), right_form(m), right_form(t))
                for q, (m, t) in zip(powers, contracted)
            ]
    return estimates


def shampoo_body(clip_ref, g_ref, stat_ref, old_ref, clipped_ref, new_stat_ref, new_ref, low_ref):
    side = BLOCK_SIDE
    g_main, g_tail = unpack(g_ref[0] * clip_ref[0])
    clipped_ref[0, :, :LANES] = g_main
    clipped_ref[0, :, LANES:] = g_tail
    g = jnp.concatenate([g_main, g_tail], axis=1)

    def unit(width, offset):
        row = lax.broadcasted_iota(jnp.int32, (side, width), 0)
        col = lax.broadcasted_iota(jnp.int32, (side, width), 1) + offset
        return (row == col).astype(jnp.float32)

    eye_main, eye_tail = unit(LANES, 0), unit(TAIL, LANES)
    flipped = g.T
    g_right = (right_form(g[:, :LANES]), right_form(g[:, LANES:]))
    f_right = (right_form(flipped[:, :LANES]), right_form(flipped[:, LANES:]))
    g_left = left_form(g[:, :LANES], g[:, LANES:])
    f_left = left_form(flipped[:, :LANES], flipped[:, LANES:])
    pairs = []
    for k, (left, right) in enumerate(((g_left, f_right), (f_left, g_right))):
        main, tail = symmetric_product(left, *right)
        main = 0.5 * stat_ref[0, k, :, :LANES] + 0.5 * main
        tail = 0.5 * stat_ref[0, k, :, LANES:] + 0.5 * tail
        new_stat_ref[0, k, :, :LANES] = main
        new_stat_ref[0, k, :, LANES:] = tail
        pairs.append((main, tail))
    left_root, right_root = inverse_roots(pairs, eye_main, eye_tail)
    root_left = left_form(*left_root)
    half = left_form(product(root_left, g_right[0]), product(root_left, g_right[1]))
    for part, (a, b) in zip(right_root, ((0, LANES), (LANES, side))):
        direction = product(half, right_form(part))
        old = old_ref[0, :, a:b]
        new = old - shampoo_rate * (direction + decay_rate * old)
        new_ref[0, :, a:b] = new
        low_ref[0, :, a:b] = new.astype(jnp.bfloat16)


def shampoo(clip_factor, gradients, stats, old_blocks):
    count, side = gradients.shape[0], BLOCK_SIDE
    one = pl.BlockSpec((1, side, side), lambda i: (i, 0, 0))
    two = pl.BlockSpec((1, 2, side, side), lambda i: (i, 0, 0, 0))
    block = jax.ShapeDtypeStruct((count, side, side), jnp.float32)
    return pl.pallas_call(
        shampoo_body,
        grid=(count,),
        in_specs=[
            pl.BlockSpec(memory_space=pltpu.SMEM),
            pl.BlockSpec((1, PACK_ROWS, LANES // 2), lambda i: (i, 0, 0)),
            two,
            one,
        ],
        out_specs=[one, two, one, one],
        out_shape=[
            block,
            jax.ShapeDtypeStruct((count, 2, side, side), jnp.float32),
            block,
            jax.ShapeDtypeStruct((count, side, side), jnp.bfloat16),
        ],
        compiler_params=pltpu.CompilerParams(vmem_limit_bytes=56 * 2**20),
        cost_estimate=pl.CostEstimate(
            flops=count * 44 * 6 * side**3, bytes_accessed=count * 34 * side * side, transcendentals=0
        ),
        name="shampoo",
    )(clip_factor.reshape(1), gradients, stats, old_blocks)


def adam_update(weight, gradient, moment_one, second):
    moment_one = 0.5 * moment_one + 0.5 * gradient
    second = 0.5 * second + 0.5 * gradient * gradient
    correct = 1.0 - 0.5**STEP
    updated = weight - adam_rate * (
        moment_one / correct / (jnp.sqrt(second / correct) + 1e-08) + decay_rate * weight
    )
    return (moment_one, second, updated)


def per_device(
    latents,
    noise,
    timesteps,
    labels,
    loss_weights,
    slotted_block_weights,
    statistics,
    slot_of_block,
    cond_tables,
    head_tables,
    slice_bias,
    side_bias,
    cond_m,
    cond_v,
    head_m,
    head_v,
    slice_m,
    slice_v,
    side_m,
    side_v,
):
    bf16, f32 = jnp.bfloat16, jnp.float32
    width = MODEL_WIDTH
    mp, dp = lax.axis_size("mp"), lax.axis_size("dp")
    my_mp, my_dp = lax.axis_index("mp"), lax.axis_index("dp")
    query_width, ff_width, ada_width = HEADS * HD // mp, FF // mp, 6 * width // mp
    ada_column = 3 * query_width + ff_width
    row_blocks = width // BLOCK_SIDE
    col_blocks = (ada_column + ada_width) // BLOCK_SIDE
    out_blocks = (query_width + ff_width) // BLOCK_SIDE
    first_out = row_blocks * col_blocks
    t2_row = PATCH_VALUES + FREQ
    class_row = t2_row + width
    local_heads = query_width // HD
    score_scale = HD ** (-0.5)
    batch = latents.shape[0]
    own_n = batch // mp
    cols = cond_tables.shape[1]
    samples = batch * dp

    def own(x):
        return lax.dynamic_slice_in_dim(x, my_mp * own_n, own_n, 0)

    def my_cols(x):
        return lax.dynamic_slice_in_dim(x, my_dp * cols, cols, x.ndim - 1)

    def all_columns(x):
        return x.transpose(1, 0, 2).reshape(x.shape[1], -1)

    def by_columns(x):
        return x.reshape(x.shape[0], dp, cols).transpose(1, 0, 2)

    def reduce_rows(x):
        return lax.psum_scatter(
            x.astype(bf16), "mp", scatter_dimension=0, tiled=True
        ).astype(f32)

    def share_rows(x):
        return lax.all_gather(x, "mp", axis=0, tiled=True)

    blocks = gather_blocks(pack_blocks(slotted_block_weights[0]))

    cond_low, head_low = cond_tables.astype(bf16), head_tables.astype(bf16)
    facts, shared = exchange(
        [
            (jnp.stack([timesteps.astype(f32), labels.astype(f32), loss_weights], 1), "gather"),
            (jnp.concatenate([cond_low[:PATCH_VALUES].T, head_low[:, 2 * width :]], 1), "gather"),
        ],
        "dp",
        2,
    )
    facts, shared = facts.reshape(samples, 3), shared.reshape(width, -1)
    all_steps, all_labels = facts[:, 0].astype(jnp.int32), facts[:, 1].astype(jnp.int32)
    weight_total = jnp.sum(facts[:, 2])
    w_patch, w_head = shared[:, :PATCH_VALUES].T, shared[:, PATCH_VALUES:]
    time_freq = time_features(all_steps, FREQ).astype(bf16)
    onehot = all_labels[:, None] == jnp.arange(CLASSES, dtype=jnp.int32)[None, :]
    first_t = dense(time_freq, cond_low[PATCH_VALUES:t2_row]) + my_cols(side_bias[width : 2 * width])
    (first_s,) = exchange([(swish_unit(first_t).astype(bf16), "gather")], "dp", 3)
    first_s = all_columns(first_s)
    cond_vec = (
        dense(first_s, cond_low[t2_row:class_row])
        + my_cols(side_bias[2 * width : 3 * width])
        + dense(onehot.astype(bf16), cond_low[class_row:])
    )
    signal_cols = swish_unit(cond_vec).astype(bf16)
    signal, final_mod = exchange(
        [
            (signal_cols.reshape(dp, batch, cols), "scatter"),
            (dense(signal_cols, head_low[:, : 2 * width]).reshape(dp, batch, 2 * width), "scatter"),
        ],
        "dp",
        4,
    )
    signal = all_columns(signal)
    final_mod = own(jnp.sum(final_mod, 0) + side_bias[5 * width : 7 * width])

    w_in = assemble(blocks, slot_of_block, 0, row_blocks, col_blocks)
    w_out = assemble(blocks, slot_of_block, first_out, out_blocks, row_blocks)
    own_bias = slice_bias[0]
    modul = lax.all_gather(
        dense(signal, w_in[:, ada_column:]) + own_bias[2 * query_width + ff_width :],
        "mp",
        axis=1,
        tiled=True,
    )
    own_modul = own(modul)

    def part(position, source=own_modul):
        return source[:, None, position * width : (position + 1) * width]

    def heads_of(inputs):
        return inputs.reshape(batch, -1, local_heads, HD)

    keep_rate, noise_rate, upper_log, lower_log, mean_gap = coefficients(timesteps)
    noisy = keep_rate[:, None, None, None] * latents + noise_rate[:, None, None, None] * noise
    patches = patchify(noisy).astype(bf16)
    seq_len = patches.shape[1]
    initial = (
        dense(patches, w_patch) + side_bias[:width] + position_embedding(LATENT_SIDE // 2, width)
    )
    normed_all, inv_std_all = layer_norm(initial)
    attn_in = (normed_all * (1.0 + part(1, modul)) + part(0, modul)).astype(bf16)
    start, normed_a, inv_std_a = own(initial), own(normed_all), own(inv_std_all)
    own_patches = own(patches)
    target = patchify(own(noise)).reshape(own_n, seq_len, 4, 4)

    projected = dense(attn_in, w_in[:, : 3 * query_width])
    queries = heads_of((projected[..., :query_width] + own_bias[:query_width]).astype(bf16))
    keys = heads_of(projected[..., query_width : 2 * query_width].astype(bf16))
    values = heads_of(
        (projected[..., 2 * query_width :] + own_bias[query_width : 2 * query_width]).astype(bf16)
    )
    scores = (
        jnp.einsum("slhe,smhe->shlm", queries, keys, preferred_element_type=f32) * score_scale
    )
    row_peak = jnp.max(scores, -1, keepdims=True)
    shifted = jnp.exp(scores - row_peak)
    row_total = jnp.sum(shifted, -1, keepdims=True)
    probs = shifted / row_total
    log_total = row_peak + jnp.log(row_total)
    mixed = (
        jnp.einsum("shlm,smhe->slhe", probs.astype(bf16), values, preferred_element_type=f32)
        .reshape(batch, seq_len, query_width)
        .astype(bf16)
    )
    attn = reduce_rows(dense(mixed, w_out[:query_width])) + side_bias[3 * width : 4 * width]
    middle = start + part(2) * attn
    normed_m, inv_std_m = layer_norm(middle)
    mlp_in = share_rows((normed_m * (1.0 + part(4)) + part(3)).astype(bf16))
    hidden = (
        dense(mlp_in, w_in[:, 3 * query_width : ada_column])
        + own_bias[2 * query_width : 2 * query_width + ff_width]
    )
    active = tanh_gelu_activation(hidden).astype(bf16)
    branch = reduce_rows(dense(active, w_out[query_width:])) + side_bias[4 * width : 5 * width]
    final = middle + part(5) * branch
    normed_f, inv_std_f = layer_norm(final)
    fscale, fshift = final_mod[:, None, width:], final_mod[:, None, :width]
    head_in = (normed_f * (1.0 + fscale) + fshift).astype(bf16)
    output = dense(head_in, w_head) + side_bias[7 * width :]

    def objective(result):
        return loss_terms(
            result, output, target, own(loss_weights), own(upper_log), own(lower_log), own(mean_gap)
        )

    loss_part, loss_pull = jax.vjp(objective, output)
    (seed_grad,) = loss_pull(jnp.ones_like(loss_part) / weight_total)

    d_out = seed_grad.astype(bf16)
    d_headin = back_dense(d_out, w_head)
    d_final = norm_back(d_headin * (1.0 + fscale), normed_f, inv_std_f)
    d_fmod = jnp.concatenate([jnp.sum(d_headin, 1), jnp.sum(d_headin * normed_f, 1)], 1).astype(bf16)
    own_branch = (part(5) * d_final).astype(bf16)
    d_gate2 = jnp.sum(d_final * branch, 1)
    d_branch = share_rows(own_branch)
    g_down = weight_grad(active, d_branch).astype(bf16)
    d_active = back_dense(d_branch, w_out[query_width:])
    d_hidden = (d_active * gelu_slope(hidden)).astype(bf16)
    g_up = weight_grad(mlp_in, d_hidden).astype(bf16)
    d_mlpin = reduce_rows(back_dense(d_hidden, w_in[:, 3 * query_width : ada_column]))
    d_shift2 = jnp.sum(d_mlpin, 1)
    d_scale2 = jnp.sum(d_mlpin * normed_m, 1)
    d_middle = d_final + norm_back(d_mlpin * (1.0 + part(4)), normed_m, inv_std_m)
    own_attn = (part(2) * d_middle).astype(bf16)
    d_gate1 = jnp.sum(d_middle * attn, 1)
    d_attn = share_rows(own_attn)
    g_outp = weight_grad(mixed, d_attn).astype(bf16)
    d_mixed = heads_of(back_dense(d_attn, w_out[:query_width]).astype(bf16))
    probs = jnp.exp(
        jnp.einsum("slhe,smhe->shlm", queries, keys, preferred_element_type=f32) * score_scale
        - log_total
    )
    d_values = jnp.einsum(
        "shlm,slhe->smhe", probs.astype(bf16), d_mixed, preferred_element_type=f32
    ).astype(bf16)
    d_probs = jnp.einsum("slhe,smhe->shlm", d_mixed, values, preferred_element_type=f32)
    d_scores = (probs * (d_probs - jnp.sum(d_probs * probs, -1, keepdims=True))).astype(bf16)
    d_query = (
        jnp.einsum("shlm,smhe->slhe", d_scores, keys, preferred_element_type=f32) * score_scale
    ).astype(bf16)
    d_keys = (
        jnp.einsum("shlm,slhe->smhe", d_scores, queries, preferred_element_type=f32) * score_scale
    ).astype(bf16)
    flat_q = d_query.reshape(batch, seq_len, query_width)
    flat_v = d_values.reshape(batch, seq_len, query_width)
    d_proj = jnp.concatenate([flat_q, d_keys.reshape(batch, seq_len, query_width), flat_v], 2)
    g_qkv = weight_grad(attn_in, d_proj).astype(bf16)
    d_attnin = reduce_rows(back_dense(d_proj, w_in[:, : 3 * query_width]))
    d_shift1 = jnp.sum(d_attnin, 1)
    d_scale1 = jnp.sum(d_attnin * normed_a, 1)
    d_start = (
        d_middle + norm_back(d_attnin * (1.0 + part(1)), normed_a, inv_std_a)
    ).astype(bf16)
    d_mod_own = jnp.concatenate([d_shift1, d_scale1, d_gate1, d_shift2, d_scale2, d_gate2], 1)
    d_modul = lax.dynamic_slice_in_dim(
        share_rows(d_mod_own.astype(bf16)), my_mp * ada_width, ada_width, 1
    )
    g_ada = weight_grad(signal, d_modul).astype(bf16)

    slot_grad = to_slots(
        jnp.concatenate([g_qkv, g_up, g_ada], 1),
        jnp.concatenate([g_outp, g_down], 0),
        slot_of_block,
        slot_of_block.shape[0],
    )
    red_blocks = reduce_blocks(slot_grad)

    d_fmod_all, d_signal = exchange(
        [(d_fmod, "gather"), (by_columns(back_dense(d_modul, w_in[:, ada_column:])), "scatter")],
        EVERY,
        5,
    )
    d_fmod_all = d_fmod_all.reshape(samples, 2 * width)
    g_fada = weight_grad(signal_cols, d_fmod_all)
    d_signal = jnp.sum(d_signal.reshape(dp, mp, batch, cols), 1).reshape(samples, cols)
    d_signal = d_signal + back_dense(d_fmod_all, head_low[:, : 2 * width])
    d_cond = d_signal * swish_slope(cond_vec)
    d_second = d_cond.astype(bf16)
    g_second = weight_grad(first_s, d_second)
    g_class = jnp.einsum("sc,sd->cd", onehot.astype(f32), d_cond, precision=exact_precision_flag)
    small = jnp.concatenate(
        [weight_grad(own_patches, d_start), jnp.einsum("...i,...j->ij", d_out, head_in, preferred_element_type=f32)], 0
    )
    slice_part = jnp.concatenate(
        [total_of(flat_q), total_of(flat_v), total_of(d_hidden), total_of(d_modul)]
    )
    side_part = jnp.concatenate(
        [total_of(d_start), total_of(own_attn), total_of(own_branch), total_of(d_out), loss_part[None]]
    )
    bias_part = jnp.concatenate([slice_part, side_part])
    rows = -(-bias_part.shape[0] // 1024) * 8
    bias_part = jnp.pad(bias_part, (0, rows * 128 - bias_part.shape[0])).reshape(rows, 128)
    d_first, small, bias_part = exchange(
        [
            (by_columns(back_dense(d_second, cond_low[t2_row:class_row])), "scatter"),
            (by_columns(small), "scatter"),
            (bias_part, "gather"),
        ],
        "dp",
        6,
    )
    d_first = (jnp.sum(d_first, 0) * swish_slope(first_t)).astype(bf16)
    g_first = weight_grad(time_freq, d_first)
    bias_part = jnp.sum(bias_part, 0).reshape(-1)
    red_slice = bias_part[: slice_part.shape[0]]
    side_rows = bias_part[slice_part.shape[0] // 128 * 128 :].reshape(-1, 128)
    small, side_rows = exchange([(jnp.sum(small, 0), "gather"), (side_rows, "gather")], "mp", 7)
    small, side_sum = jnp.sum(small, 0), jnp.sum(side_rows, 0).reshape(-1)
    loss_sum = side_sum[side_part.shape[0] - 1]
    side_sum = side_sum[: side_part.shape[0] - 1]
    side_mod = total_of(d_fmod_all)
    red_cond = jnp.concatenate([small[:PATCH_VALUES], g_first, g_second, g_class], 0)
    red_head = jnp.concatenate([g_fada, small[PATCH_VALUES:].T], 1)
    side_cols = jnp.stack([total_of(d_first), total_of(d_second)])

    local_squares = (
        jnp.sum(red_blocks * red_blocks)
        + (jnp.sum(red_cond * red_cond) + jnp.sum(red_head * red_head) + jnp.sum(side_cols * side_cols)) / mp
        + jnp.sum(red_slice * red_slice) / dp
        + (jnp.sum(side_sum * side_sum) + jnp.sum(side_mod * side_mod)) / (dp * mp)
    )
    last = jnp.concatenate([side_cols, jnp.broadcast_to(local_squares, (2, 1))], 1)
    (last,) = exchange([(last, "gather")], EVERY, 8)
    grad_norm = jnp.sqrt(jnp.sum(last[:, 0, cols]))
    side_cols = last[:, :, :cols].reshape(dp, mp, 2, cols)[:, 0].transpose(1, 0, 2).reshape(2 * width)
    red_side = jnp.concatenate(
        [side_sum[:width], side_cols, side_sum[width : 3 * width], side_mod, side_sum[3 * width :]]
    )
    clip_factor = 1.0 / jnp.maximum(grad_norm, 1.0)
    clipped, new_stats, new_blocks, new_low = shampoo(
        clip_factor, red_blocks, statistics[0], slotted_block_weights[0]
    )
    cond_one, cond_two, new_cond = adam_update(cond_tables, red_cond * clip_factor, cond_m, cond_v)
    head_one, head_two, new_head = adam_update(head_tables, red_head * clip_factor, head_m, head_v)
    slice_one, slice_two, new_slice = adam_update(
        slice_bias[0], red_slice * clip_factor, slice_m[0], slice_v[0]
    )
    side_one, side_two, new_side = adam_update(side_bias, red_side * clip_factor, side_m, side_v)
    return (
        loss_sum,
        weight_total,
        grad_norm,
        clipped[None],
        new_stats[None],
        new_blocks[None],
        new_low[None],
        cond_one,
        cond_two,
        new_cond,
        new_cond.astype(bf16),
        head_one,
        head_two,
        new_head,
        new_head.astype(bf16),
        slice_one[None],
        slice_two[None],
        new_slice[None],
        side_one,
        side_two,
        new_side,
    )


def solution(mesh):
    return jax.shard_map(
        per_device,
        mesh=mesh,
        in_specs=(
            P("dp", None, None, None),
            P("dp", None, None, None),
            P("dp"),
            P("dp"),
            P("dp"),
            P("mp", "dp", None, None),
            P("mp", "dp", None, None, None),
            P(),
            P(None, "dp"),
            P("dp", None),
            P("mp", None),
            P(),
            P(None, "dp"),
            P(None, "dp"),
            P("dp", None),
            P("dp", None),
            P("mp", None),
            P("mp", None),
            P(),
            P(),
        ),
        out_specs=(
            P(),
            P(),
            P(),
            P("mp", "dp", None, None),
            P("mp", "dp", None, None, None),
            P("mp", "dp", None, None),
            P("mp", "dp", None, None),
            P(None, "dp"),
            P(None, "dp"),
            P(None, "dp"),
            P(None, "dp"),
            P("dp", None),
            P("dp", None),
            P("dp", None),
            P("dp", None),
            P("mp", None),
            P("mp", None),
            P("mp", None),
            P(),
            P(),
            P(),
        ),
        check_vma=False,
    )
```

```python
import math

import jax
import jax.numpy as jnp
from jax import lax
from jax.experimental import pallas as pl
from jax.experimental.pallas import tpu as pltpu
from jax.sharding import PartitionSpec as P

MODEL_WIDTH = 1152
HEADS = 16
HD = 72
FF = 4608
FREQ = 256
CLASSES = 1001
LATENT_SIDE = 32
PATCH_VALUES = 16
BLOCK_SIDE = 288
NEWTON = 6
STEP = 5
LANES = 256
TAIL = BLOCK_SIDE - LANES


exact_precision_flag = lax.Precision.HIGHEST
shampoo_rate = 0.5
adam_rate = 0.05
decay_rate = 0.01


def dense(operand, weight):
    return jnp.dot(operand, weight, preferred_element_type=jnp.float32)


def back_dense(gradient, weight):
    return jnp.einsum("...j,ij->...i", gradient, weight, preferred_element_type=jnp.float32)


def weight_grad(operand, gradient):
    return jnp.einsum("...i,...j->ij", operand, gradient, preferred_element_type=jnp.float32)


def total_of(inputs):
    return jnp.sum(inputs.astype(jnp.float32), axis=tuple(range(inputs.ndim - 1)))


def swish_unit(inputs):
    return inputs / (1.0 + jnp.exp(-inputs))


def swish_slope(inputs):
    sigmoid = 1.0 / (1.0 + jnp.exp(-inputs))
    return sigmoid * (1.0 + inputs * (1.0 - sigmoid))


def tanh_gelu_activation(inputs):
    return (
        0.5
        * inputs
        * (1.0 + jnp.tanh(0.7978845608028654 * (inputs + 0.044715 * inputs * inputs * inputs)))
    )


def gelu_slope(inputs):
    inner = jnp.tanh(0.7978845608028654 * (inputs + 0.044715 * inputs * inputs * inputs))
    return 0.5 * (1.0 + inner) + 0.5 * inputs * (1.0 - inner * inner) * 0.7978845608028654 * (
        1.0 + 3.0 * 0.044715 * inputs * inputs
    )


def layer_norm(inputs):
    centred = inputs - jnp.mean(inputs, -1, keepdims=True)
    inv_std = lax.rsqrt(jnp.mean(centred * centred, -1, keepdims=True) + 1e-06)
    return (centred * inv_std, inv_std)


def norm_back(gradient, normed, inv_std):
    return inv_std * (
        gradient
        - jnp.mean(gradient, -1, keepdims=True)
        - normed * jnp.mean(gradient * normed, -1, keepdims=True)
    )


def coefficients(step_ids):
    grid = jnp.arange(1000).astype(jnp.float32)
    betas = 0.0001 + (0.02 - 0.0001) * grid / 999.0
    logs = jnp.log(1.0 - betas)[None, :]
    index = jnp.arange(1000, dtype=jnp.int32)[None, :]
    beta_t = 0.0001 + (0.02 - 0.0001) * step_ids.astype(jnp.float32) / 999.0
    cumul_t = jnp.exp(jnp.sum(jnp.where(index <= step_ids[:, None], logs, 0.0), 1))
    before_t = jnp.exp(jnp.sum(jnp.where(index < step_ids[:, None], logs, 0.0), 1))
    keep_rate = jnp.sqrt(cumul_t)
    noise_rate = jnp.sqrt(1.0 - cumul_t)
    upper_log = jnp.log(beta_t)
    lower_log = jnp.log(beta_t * (1.0 - before_t) / (1.0 - cumul_t))
    mean_gap = beta_t * jnp.sqrt(before_t) / (1.0 - cumul_t) * jnp.sqrt(1.0 / cumul_t - 1.0)
    return (keep_rate, noise_rate, upper_log, lower_log, mean_gap)


def time_features(step_ids, feat_width):
    half_width = feat_width // 2
    frequencies = jnp.exp(
        -math.log(10000.0) * jnp.arange(half_width).astype(jnp.float32) / half_width
    )
    phases = step_ids.astype(jnp.float32)[:, None] * frequencies[None, :]
    return jnp.concatenate([jnp.cos(phases), jnp.sin(phases)], 1)


def position_embedding(grid_side, feat_width):
    quarter = feat_width // 4
    omegas = jnp.exp(-math.log(10000.0) * jnp.arange(quarter).astype(jnp.float32) / quarter)
    coords = jnp.arange(grid_side).astype(jnp.float32)
    angles = coords[:, None] * omegas[None, :]
    waves = jnp.concatenate([jnp.sin(angles), jnp.cos(angles)], 1)
    half_width = feat_width // 2
    rows_part = jnp.broadcast_to(waves[:, None, :], (grid_side, grid_side, half_width))
    cols_part = jnp.broadcast_to(waves[None, :, :], (grid_side, grid_side, half_width))
    return jnp.concatenate([rows_part, cols_part], 2).reshape(grid_side * grid_side, feat_width)


def patchify(latent):
    samples_n, channels, height, breadth = latent.shape
    shaped = latent.reshape(samples_n, channels, height // 2, 2, breadth // 2, 2).transpose(
        0, 2, 4, 3, 5, 1
    )
    return shaped.reshape(samples_n, height // 2 * (breadth // 2), 4 * channels)


PACK_ROWS = 656


def pack(x):
    quarter = BLOCK_SIDE // 4
    tail = x[:, LANES:].astype(jnp.float32)
    tail = jnp.concatenate([tail[i * quarter : (i + 1) * quarter] for i in range(4)], axis=1)
    fill = jnp.zeros((PACK_ROWS - 2 * BLOCK_SIDE - quarter, LANES // 2), jnp.float32)
    tail = jnp.concatenate([tail, fill], axis=0)
    half = LANES // 2
    return x[:, :half], x[:, half:LANES], tail.astype(x.dtype)


def unpack(x):
    side, quarter = BLOCK_SIDE, BLOCK_SIDE // 4
    tail = x[2 * side :].astype(jnp.float32)[:quarter]
    tail = jnp.concatenate([tail[:, i * TAIL : (i + 1) * TAIL] for i in range(4)], axis=0)
    main = jnp.concatenate([x[:side], x[side : 2 * side]], axis=1)
    return main, tail.astype(x.dtype)


def store_packed(ref, index, x):
    a, b, c = pack(x)
    side = BLOCK_SIDE
    ref[index + (slice(0, side),)] = a
    ref[index + (slice(side, 2 * side),)] = b
    ref[index + (slice(2 * side, PACK_ROWS),)] = c


def pack_blocks(blocks):
    count, side = blocks.shape[0], BLOCK_SIDE

    def body(x_ref, out_ref):
        store_packed(out_ref, (0,), x_ref[0].astype(jnp.bfloat16))

    return pl.pallas_call(
        body,
        grid=(count,),
        in_specs=[pl.BlockSpec((1, side, side), lambda i: (i, 0, 0))],
        out_specs=pl.BlockSpec((1, PACK_ROWS, LANES // 2), lambda i: (i, 0, 0)),
        out_shape=jax.ShapeDtypeStruct((count, PACK_ROWS, LANES // 2), jnp.bfloat16),
        name="pack_blocks",
    )(blocks)


def remote(source, target, send, receive, place):
    return pltpu.make_async_remote_copy(
        src_ref=source,
        dst_ref=target,
        send_sem=send,
        recv_sem=receive,
        device_id=place,
        device_id_type=pl.DeviceIdType.MESH,
    )


def signal_to(semaphore, place):
    pl.semaphore_signal(semaphore, inc=1, device_id=place, device_id_type=pl.DeviceIdType.MESH)


COLUMNS = 2
LAYERS = 4


def grid_place():
    me = lax.axis_index("dp")
    return me // COLUMNS, me % COLUMNS


def greet_neighbours(z, y):
    barrier = pltpu.get_barrier_semaphore()
    signal_to(barrier, {"dp": z * COLUMNS + 1 - y})

    @pl.when(z < LAYERS - 1)
    def _():
        signal_to(barrier, {"dp": (z + 1) * COLUMNS + y})

    @pl.when(z > 0)
    def _():
        signal_to(barrier, {"dp": (z - 1) * COLUMNS + y})

    pl.semaphore_wait(barrier, jnp.where((z > 0) & (z < LAYERS - 1), 3, 2))


def gather_body(x_ref, out_ref, local_sem, up_sem, down_sem, side_sem, recv_sem):
    count = x_ref.shape[0]
    z, y = grid_place()
    greet_neighbours(z, y)
    peer = {"dp": z * COLUMNS + 1 - y}
    above = {"dp": jnp.minimum(z + 1, LAYERS - 1) * COLUMNS + y}
    below = {"dp": jnp.maximum(z - 1, 0) * COLUMNS + y}

    def block(layer, column, k):
        return out_ref.at[(layer * COLUMNS + column) * count + k]

    def move(source, layer, k, send, place):
        return remote(
            source, block(layer, y, k), send.at[layer, k], recv_sem.at[layer, y, k], place
        )

    def arrival(layer, column, k):
        here = block(layer, column, k)
        return remote(here, here, side_sem.at[0, 0], recv_sem.at[layer, column, k], peer)

    def send_own(k, _):
        own = x_ref.at[k]

        @pl.when(z < LAYERS - 1)
        def _():
            move(own, z, k, up_sem, above).start()

        @pl.when(z > 0)
        def _():
            move(own, z, k, down_sem, below).start()

        move(own, z, k, side_sem, peer).start()
        pltpu.make_async_copy(own, block(z, y, k), local_sem.at[k]).start()
        return 0

    lax.fori_loop(0, count, send_own, 0)

    for hop in range(1, LAYERS):

        def pass_on(k, _):
            @pl.when(z >= hop)
            def _():
                layer = z - hop
                arrival(layer, y, k).wait_recv()

                @pl.when(z < LAYERS - 1)
                def _():
                    move(block(layer, y, k), layer, k, up_sem, above).start()

                move(block(layer, y, k), layer, k, side_sem, peer).start()

            @pl.when(z + hop < LAYERS)
            def _():
                layer = z + hop
                arrival(layer, y, k).wait_recv()

                @pl.when(z > 0)
                def _():
                    move(block(layer, y, k), layer, k, down_sem, below).start()

                move(block(layer, y, k), layer, k, side_sem, peer).start()

            return 0

        lax.fori_loop(0, count, pass_on, 0)

    def finish(k, _):
        pltpu.make_async_copy(x_ref.at[k], block(z, y, k), local_sem.at[k]).wait()
        for layer in range(LAYERS):
            arrival(layer, 1 - y, k).wait_recv()
            move(block(layer, y, k), layer, k, side_sem, peer).wait_send()

            @pl.when((z < LAYERS - 1) & (layer <= z))
            def _():
                move(block(layer, y, k), layer, k, up_sem, above).wait_send()

            @pl.when((z > 0) & (layer >= z))
            def _():
                move(block(layer, y, k), layer, k, down_sem, below).wait_send()

        return 0

    lax.fori_loop(0, count, finish, 0)


def gather_blocks(packed):
    ways = lax.axis_size("dp")
    if ways != COLUMNS * LAYERS:
        return lax.all_gather(packed, "dp", axis=0, tiled=True)
    count = packed.shape[0]
    dma = pltpu.SemaphoreType.DMA
    return pl.pallas_call(
        gather_body,
        in_specs=[pl.BlockSpec(memory_space=pl.ANY)],
        out_specs=pl.BlockSpec(memory_space=pl.ANY),
        out_shape=jax.ShapeDtypeStruct((count * ways,) + packed.shape[1:], packed.dtype),
        scratch_shapes=[
            dma((count,)),
            dma((LAYERS, count)),
            dma((LAYERS, count)),
            dma((LAYERS, count)),
            dma((LAYERS, COLUMNS, count)),
        ],
        compiler_params=pltpu.CompilerParams(collective_id=0, has_side_effects=True),
        name="gather_blocks",
    )(packed)


def reduce_body(
    x_ref, out_ref, side_buf, up_buf, down_buf, side_send, line_send, side_recv, up_recv, down_recv
):
    count = out_ref.shape[0]
    z, y = grid_place()
    greet_neighbours(z, y)
    peer = {"dp": z * COLUMNS + 1 - y}
    above = {"dp": jnp.minimum(z + 1, LAYERS - 1) * COLUMNS + y}
    below = {"dp": jnp.maximum(z - 1, 0) * COLUMNS + y}

    def across(layer, k):
        return remote(
            x_ref.at[(layer * COLUMNS + 1 - y) * count + k],
            side_buf.at[layer, k],
            side_send.at[layer, k],
            side_recv.at[layer, k],
            peer,
        )

    def upward(layer, k):
        return remote(
            side_buf.at[layer, k], up_buf.at[layer, k], line_send.at[layer, k], up_recv.at[layer, k], above
        )

    def downward(layer, k):
        return remote(
            side_buf.at[layer, k], down_buf.at[layer, k], line_send.at[layer, k], down_recv.at[layer, k], below
        )

    def pair_sum(layer, k):
        across(layer, k).wait_recv()
        own = x_ref[(layer * COLUMNS + y) * count + k].astype(jnp.float32)
        return own + side_buf[layer, k].astype(jnp.float32)

    for hop in range(LAYERS - 1, -1, -1):

        def start(k, _):
            @pl.when(z + hop < LAYERS)
            def _():
                across(z + hop, k).start()

            if hop > 0:

                @pl.when(z >= hop)
                def _():
                    across(z - hop, k).start()

            return 0

        lax.fori_loop(0, count, start, 0)

    for hop in range(LAYERS - 1, 0, -1):

        def step(k, _):
            @pl.when(z + hop < LAYERS)
            def _():
                layer = z + hop
                total = pair_sum(layer, k)

                @pl.when(z > 0)
                def _():
                    upward(layer, k).wait_recv()
                    side_buf[layer, k] = (total + up_buf[layer, k].astype(jnp.float32)).astype(
                        jnp.bfloat16
                    )

                @pl.when(z == 0)
                def _():
                    side_buf[layer, k] = total.astype(jnp.bfloat16)

                upward(layer, k).start()

            @pl.when(z >= hop)
            def _():
                layer = z - hop
                total = pair_sum(layer, k)

                @pl.when(z < LAYERS - 1)
                def _():
                    downward(layer, k).wait_recv()
                    side_buf[layer, k] = (total + down_buf[layer, k].astype(jnp.float32)).astype(
                        jnp.bfloat16
                    )

                @pl.when(z == LAYERS - 1)
                def _():
                    side_buf[layer, k] = total.astype(jnp.bfloat16)

                downward(layer, k).start()

            return 0

        lax.fori_loop(0, count, step, 0)

    def last(k, _):
        out_ref[k] = pair_sum(z, k)

        @pl.when(z > 0)
        def _():
            upward(z, k).wait_recv()
            out_ref[k] += up_buf[z, k].astype(jnp.float32)

        @pl.when(z < LAYERS - 1)
        def _():
            downward(z, k).wait_recv()
            out_ref[k] += down_buf[z, k].astype(jnp.float32)

        for layer in range(LAYERS):
            across(layer, k).wait_send()

            @pl.when(layer > z)
            def _():
                upward(layer, k).wait_send()

            @pl.when(layer < z)
            def _():
                downward(layer, k).wait_send()

        return 0

    lax.fori_loop(0, count, last, 0)


def reduce_blocks(slots):
    ways = lax.axis_size("dp")
    if ways != COLUMNS * LAYERS:
        return lax.psum_scatter(slots, "dp", scatter_dimension=0, tiled=True).astype(jnp.float32)
    count = slots.shape[0] // ways
    dma = pltpu.SemaphoreType.DMA
    landing = pltpu.VMEM((LAYERS, count) + slots.shape[1:], jnp.bfloat16)
    return pl.pallas_call(
        reduce_body,
        in_specs=[pl.BlockSpec(memory_space=pltpu.VMEM)],
        out_specs=pl.BlockSpec(memory_space=pltpu.VMEM),
        out_shape=jax.ShapeDtypeStruct((count,) + slots.shape[1:], jnp.float32),
        scratch_shapes=[landing] * 3 + [dma((LAYERS, count))] * 5,
        compiler_params=pltpu.CompilerParams(
            collective_id=1, has_side_effects=True, vmem_limit_bytes=52 * 2**20
        ),
        name="reduce_blocks",
    )(slots)


EVERY = ("dp", "mp")


def exchange(items, axes, number):
    mp, dp = lax.axis_size("mp"), lax.axis_size("dp")
    n = {"dp": dp, "mp": mp, EVERY: dp * mp}[axes]

    def place(i):
        return {"dp": i // mp, "mp": i % mp} if axes == EVERY else {axes: i}

    def row(i):
        return i // mp if axes == EVERY else i

    def body(*refs):
        m = len(items)
        sources, outs, send, receive = refs[:m], refs[m : 2 * m], refs[-2], refs[-1]
        me = lax.axis_index("dp") * mp + lax.axis_index("mp") if axes == EVERY else lax.axis_index(axes)
        barrier = pltpu.get_barrier_semaphore()

        def greet(i, _):
            signal_to(barrier, place(lax.rem(me + i, n)))
            return 0

        lax.fori_loop(1, n, greet, 0)
        pl.semaphore_wait(barrier, n - 1)

        def piece(j, to):
            return sources[j].at[row(to)] if items[j][1] == "scatter" else sources[j]

        def start(i, _):
            to = lax.rem(me + i, n)
            for j in range(m):
                remote(piece(j, to), outs[j].at[me], send.at[j, i], receive.at[j, me], place(to)).start()
            return 0

        lax.fori_loop(1, n, start, 0)
        for j in range(m):
            outs[j][me] = sources[j][row(me)] if items[j][1] == "scatter" else sources[j][...]

        def finish(i, _):
            to = lax.rem(me + i, n)
            for j in range(m):
                copy = remote(piece(j, to), outs[j].at[to], send.at[j, i], receive.at[j, to], place(to))
                copy.wait_recv()
                copy.wait_send()
            return 0

        lax.fori_loop(1, n, finish, 0)

    arrays = [a for a, _ in items]
    shapes = [
        jax.ShapeDtypeStruct((n,) + (a.shape[1:] if kind == "scatter" else a.shape), a.dtype)
        for a, kind in items
    ]
    vmem = pl.BlockSpec(memory_space=pltpu.VMEM)
    return pl.pallas_call(
        body,
        in_specs=[vmem] * len(arrays),
        out_specs=[vmem] * len(arrays),
        out_shape=shapes,
        scratch_shapes=[pltpu.SemaphoreType.DMA((len(arrays), n))] * 2,
        compiler_params=pltpu.CompilerParams(
            collective_id=number, has_side_effects=True, vmem_limit_bytes=40 * 2**20
        ),
        name=f"exchange_{number}",
    )(*arrays)


def assemble(blocks, slots, first, rows, widths):
    side, cols = BLOCK_SIDE, sum(widths)

    def body(ids, *refs):
        base = 0
        for out, width in zip(refs[cols:], widths):
            parts = [part for r in refs[base : base + width] for part in unpack(r[0])]
            out[...] = jnp.concatenate(parts, axis=1)
            base += width

    def spec(c):
        return pl.BlockSpec(
            (1, PACK_ROWS, LANES // 2), lambda r, ids: (ids[first + r * cols + c], 0, 0)
        )

    return pl.pallas_call(
        body,
        grid_spec=pltpu.PrefetchScalarGridSpec(
            num_scalar_prefetch=1,
            grid=(rows,),
            in_specs=[spec(c) for c in range(cols)],
            out_specs=[pl.BlockSpec((side, side * w), lambda r, ids: (r, 0)) for w in widths],
        ),
        out_shape=[jax.ShapeDtypeStruct((rows * side, w * side), jnp.bfloat16) for w in widths],
        compiler_params=pltpu.CompilerParams(vmem_limit_bytes=40 * 2**20),
        cost_estimate=pl.CostEstimate(
            flops=0, bytes_accessed=4 * rows * cols * side * side, transcendentals=0
        ),
        name="assemble",
    )(slots, *([blocks] * cols))


def to_slots(inner, outer, slots, total):
    side = BLOCK_SIDE
    ri, widths = inner[0].shape[0] // side, [g.shape[1] // side for g in inner]
    ci, co = sum(widths), outer[0].shape[1] // side
    heights = [g.shape[0] // side for g in outer]
    ro = sum(heights)
    steps = ri + ro
    n = len(inner) + len(outer)

    def body(ids, *refs):
        sources, (out, buf, sem) = refs[:n], refs[-3:]
        s = pl.program_id(0)
        half = lax.rem(s, 2)

        def drain(which, count):
            for c in range(count):
                pltpu.make_async_copy(buf.at[which, c], out.at[0], sem.at[which, c]).wait()

        def send(source, count, base, first=0):
            for c in range(count):
                store_packed(buf, (half, first + c), source[:, c * side : (c + 1) * side])
                pltpu.make_async_copy(
                    buf.at[half, first + c], out.at[ids[base + c]], sem.at[half, first + c]
                ).start()

        @pl.when(jnp.logical_and(s >= 2, s - 2 < ri))
        def _():
            drain(half, ci)

        @pl.when(s - 2 >= ri)
        def _():
            drain(half, co)

        @pl.when(s < ri)
        def _():
            first = 0
            for source, width in zip(sources, widths):
                send(source, width, s * ci + first, first)
                first += width

        base = ri
        for source, height in zip(sources[len(inner) :], heights):

            @pl.when(jnp.logical_and(s >= base, s < base + height))
            def _():
                send(source, co, ri * ci + (s - ri) * co)

            base += height

        @pl.when(s == steps - 1)
        def _():
            drain(1 - half, co)
            drain(half, co)

    extra, aliases = [], {}
    if total != ri * ci + ro * co:
        extra = [jnp.zeros((total, PACK_ROWS, LANES // 2), jnp.bfloat16)]
        aliases = {1 + n: 0}
    specs = [
        pl.BlockSpec((side, w * side), lambda s, ids: (jnp.minimum(s, ri - 1), 0)) for w in widths
    ]
    base = ri
    for height in heights:
        specs.append(
            pl.BlockSpec(
                (side, co * side),
                lambda s, ids, base=base, height=height: (jnp.clip(s - base, 0, height - 1), 0),
            )
        )
        base += height
    return pl.pallas_call(
        body,
        grid_spec=pltpu.PrefetchScalarGridSpec(
            num_scalar_prefetch=1,
            grid=(steps,),
            in_specs=specs + [pl.BlockSpec(memory_space=pl.ANY)] * len(extra),
            out_specs=pl.BlockSpec(memory_space=pl.ANY),
            scratch_shapes=[
                pltpu.VMEM((2, max(ci, co), PACK_ROWS, LANES // 2), jnp.bfloat16),
                pltpu.SemaphoreType.DMA((2, max(ci, co))),
            ],
        ),
        out_shape=jax.ShapeDtypeStruct((total, PACK_ROWS, LANES // 2), jnp.bfloat16),
        compiler_params=pltpu.CompilerParams(vmem_limit_bytes=40 * 2**20),
        cost_estimate=pl.CostEstimate(
            flops=0, bytes_accessed=4 * (ri * ci + ro * co) * side * side, transcendentals=0
        ),
        input_output_aliases=aliases,
        name="to_slots",
    )(slots, *inner, *outer, *extra)


CHUNK = 64


def mean_of(x):
    return jnp.sum(x, axis=-1, keepdims=True) * (1.0 / x.shape[-1])


def norm_rows(x):
    centred = x - mean_of(x)
    inv_std = lax.rsqrt(mean_of(centred * centred) + 1e-06)
    return centred * inv_std, inv_std


def norm_rows_back(gradient, normed, inv_std):
    return inv_std * (gradient - mean_of(gradient) - normed * mean_of(gradient * normed))


def column_sum(x):
    return jnp.sum(x, axis=0, keepdims=True)


def times(a, b):
    return jnp.dot(a, b, preferred_element_type=jnp.float32)


def times_flipped(a, b):
    return lax.dot_general(a, b, (((1,), (1,)), ((), ())), preferred_element_type=jnp.float32)


def stage(number, inputs, outputs, shared, make):
    rows, width = inputs[0].shape[1], MODEL_WIDTH
    pieces = rows // CHUNK
    n_in, n_out = len(inputs), len(outputs)

    def body(*refs):
        ins, outs = refs[:n_in], refs[n_in : n_in + n_out]
        rest = refs[n_in + n_out :]
        share = None
        if shared:
            share, rest = rest[0], rest[1:]
        a_out, a_in, b_out, b_in, c_out, c_in, total, near, far = rest
        me = lax.axis_index("mp")
        core = me + 1 - 2 * lax.rem(me, 2)
        across = lax.rem(me + 2, 4)
        other = lax.rem(core + 2, 4)
        to_core, to_across = {"mp": core}, {"mp": across}
        partial, own, after = make(ins, outs, share)
        barrier = pltpu.get_barrier_semaphore()
        signal_to(barrier, to_core)
        signal_to(barrier, to_across)
        pl.semaphore_wait(barrier, 2)

        copy_a = remote(a_out, a_in, near.at[0, 0], near.at[1, 0], to_core)
        copy_c = remote(c_out, c_in, near.at[0, 1], near.at[1, 1], to_core)

        def piece(i):
            return pl.ds(i * CHUNK, CHUNK)

        def copy_b(i):
            return remote(
                b_out.at[piece(i)], b_in.at[piece(i)], far.at[0, i], far.at[1, i], to_across
            )

        def share_far(group, i):
            part = share.at[group, piece(i)]
            return remote(part, part, far.at[2, i], far.at[3, i], to_across)

        def share_near(group, i):
            part = share.at[group, piece(i)]
            return remote(part, part, near.at[2, i], near.at[3, i], to_core)

        def pass_near(group, i):
            part = share.at[group, piece(i)]
            return remote(part, part, near.at[4, i], near.at[5, i], to_core)

        a_out[...] = partial(other).astype(jnp.bfloat16)
        copy_a.start()
        total[...] = partial(across)
        copy_a.wait_recv()
        for i in range(pieces):
            at = piece(i)
            b_out[at] = (total[at] + a_in[at].astype(jnp.float32)).astype(jnp.bfloat16)
            copy_b(i).start()
        c_out[...] = partial(core).astype(jnp.bfloat16)
        copy_c.start()
        total[...] = partial(me)
        copy_c.wait_recv()
        for i in range(pieces):
            at = piece(i)
            copy_b(i).wait_recv()
            result = own(
                i * CHUNK, total[at] + c_in[at].astype(jnp.float32) + b_in[at].astype(jnp.float32)
            )
            if shared:
                share[me, at] = result
                share_far(me, i).start()
                share_near(me, i).start()
        if shared:
            after(me)
            for i in range(pieces):
                share_near(core, i).wait_recv()
            after(core)
            for i in range(pieces):
                share_far(across, i).wait_recv()
                pass_near(across, i).start()
            after(across)
            for i in range(pieces):
                pass_near(other, i).wait_recv()
            after(other)
        copy_a.wait_send()
        copy_c.wait_send()
        for i in range(pieces):
            copy_b(i).wait_send()
            if shared:
                share_far(me, i).wait_send()
                share_near(me, i).wait_send()
                pass_near(across, i).wait_send()

    vmem = pl.BlockSpec(memory_space=pltpu.VMEM)
    out_shape = [jax.ShapeDtypeStruct(shape, dtype) for shape, dtype in outputs]
    if shared:
        out_shape.append(jax.ShapeDtypeStruct((4, rows, width), jnp.bfloat16))
    landing = pltpu.VMEM((rows, width), jnp.bfloat16)
    return pl.pallas_call(
        body,
        in_specs=[vmem] * n_in,
        out_specs=[vmem] * len(out_shape),
        out_shape=out_shape,
        scratch_shapes=[landing] * 6
        + [
            pltpu.VMEM((rows, width), jnp.float32),
            pltpu.SemaphoreType.DMA((6, max(pieces, 2))),
            pltpu.SemaphoreType.DMA((4, pieces)),
        ],
        compiler_params=pltpu.CompilerParams(
            collective_id=number, has_side_effects=True, vmem_limit_bytes=56 * 2**20
        ),
        name=f"stage_{number}",
    )(*inputs)


def attention_out_stage(mixed, w_o, w_up, start, rows, up_bias):
    n, width, f32 = mixed.shape[1], MODEL_WIDTH, jnp.float32

    def make(ins, outs, share):
        mixed_ref, w_o_ref, w_up_ref, start_ref, rows_ref, up_ref = ins
        attn_ref, middle_ref, hidden_ref, active_ref = outs

        def partial(group):
            return times(mixed_ref[group], w_o_ref[...])

        def own(at, total):
            at = slice(at, at + CHUNK)
            attn = total + rows_ref[0:1]
            middle = start_ref[at] + rows_ref[1:2] * attn
            attn_ref[at] = attn
            middle_ref[at] = middle
            normed, _ = norm_rows(middle)
            return (normed * (1.0 + rows_ref[2:3]) + rows_ref[3:4]).astype(jnp.bfloat16)

        def after(group):
            for at in range(0, n, CHUNK):
                at = slice(at, at + CHUNK)
                hidden = times(share[group, at], w_up_ref[...]) + up_ref[...]
                hidden_ref[group, at] = hidden
                active_ref[group, at] = tanh_gelu_activation(hidden).astype(jnp.bfloat16)

        return partial, own, after

    inner = w_up.shape[1]
    return stage(
        9,
        [mixed, w_o, w_up, start, rows, up_bias],
        [((n, width), f32), ((n, width), f32), ((4, n, inner), f32), ((4, n, inner), jnp.bfloat16)],
        True,
        make,
    )


def loss_stage(active, w_down, hidden, middle, rows, target, w_pred, w_raw, head_bias, facts):
    n, width, f32, bf16 = active.shape[1], MODEL_WIDTH, jnp.float32, jnp.bfloat16
    inner = active.shape[2]

    def make(ins, outs, share):
        active_ref, w_ref, hidden_ref, middle_ref, rows_ref, target_ref, wp_ref, wr_ref, bias_ref, facts_ref = ins
        d_final_ref, head_in_ref, d_pred_ref, d_raw_ref, sums_ref, loss_ref, d_hidden_ref, up_sum_ref = outs
        sums_ref[...] = jnp.zeros_like(sums_ref)
        loss_ref[...] = jnp.zeros_like(loss_ref)
        up_sum_ref[...] = jnp.zeros_like(up_sum_ref)

        def partial(group):
            return times(active_ref[group], w_ref[...])

        def own(at, total):
            at = slice(at, at + CHUNK)
            branch = total + rows_ref[0:1]
            gate, fscale = rows_ref[1:2], 1.0 + rows_ref[2:3]
            normed, inv_std = norm_rows(middle_ref[at] + gate * branch)
            head_in = (normed * fscale + rows_ref[3:4]).astype(bf16)
            head_in_ref[at] = head_in
            upper, lower, gap = facts_ref[0:1], facts_ref[1:2], facts_ref[2:3]
            weight, share_of = facts_ref[3:4], facts_ref[4:5]
            error = times(head_in, wp_ref[...]) + bias_ref[0:1] - target_ref[at]
            fraction = (times(head_in, wr_ref[...]) + bias_ref[1:2] + 1.0) / 2.0
            log_var = fraction * upper + (1.0 - fraction) * lower
            gap = gap * error
            ratio = jnp.exp(lower - log_var)
            spread = gap * gap * jnp.exp(-log_var)
            diverge = 0.5 * (-1.0 + log_var - lower + ratio + spread)
            cells = 1.0 / (n * error.shape[1])
            per_bit = cells / math.log(2.0)
            loss_ref[...] += weight * column_sum(error * error * cells + diverge * per_bit)
            d_pred = (share_of * (2.0 * cells) * error).astype(bf16)
            d_raw = (
                share_of * per_bit * 0.25 * (upper - lower) * (1.0 - ratio - spread)
            ).astype(bf16)
            d_pred_ref[at] = d_pred
            d_raw_ref[at] = d_raw
            d_head = times_flipped(d_pred, wp_ref[...]) + times_flipped(d_raw, wr_ref[...])
            d_final = norm_rows_back(d_head * fscale, normed, inv_std)
            d_final_ref[at] = d_final
            d_branch = (gate * d_final).astype(bf16)
            sums_ref[0:1] += column_sum(d_head)
            sums_ref[1:2] += column_sum(d_head * normed)
            sums_ref[2:3] += column_sum(d_final * branch)
            sums_ref[3:4] += column_sum(d_branch.astype(f32))
            return d_branch

        def after(group):
            for at in range(0, n, CHUNK):
                at = slice(at, at + CHUNK)
                d_active = times_flipped(share[group, at], w_ref[...])
                d_hidden = (d_active * gelu_slope(hidden_ref[group, at])).astype(bf16)
                d_hidden_ref[group, at] = d_hidden
                up_sum_ref[...] += column_sum(d_hidden.astype(f32))

        return partial, own, after

    half = w_pred.shape[1]
    return stage(
        10,
        [active, w_down, hidden, middle, rows, target, w_pred, w_raw, head_bias, facts],
        [
            ((n, width), f32),
            ((n, width), bf16),
            ((n, half), bf16),
            ((n, half), bf16),
            ((4, width), f32),
            ((1, half), f32),
            ((4, n, inner), bf16),
            ((1, inner), f32),
        ],
        True,
        make,
    )


def middle_back_stage(d_hidden, w_up, w_o, middle, d_final, attn, rows):
    n, width, f32, bf16 = d_hidden.shape[1], MODEL_WIDTH, jnp.float32, jnp.bfloat16

    def make(ins, outs, share):
        d_hidden_ref, w_up_ref, w_o_ref, middle_ref, d_final_ref, attn_ref, rows_ref = ins
        d_middle_ref, sums_ref, d_mixed_ref = outs
        sums_ref[...] = jnp.zeros_like(sums_ref)

        def partial(group):
            return times_flipped(d_hidden_ref[group], w_up_ref[...])

        def own(at, total):
            at = slice(at, at + CHUNK)
            normed, inv_std = norm_rows(middle_ref[at])
            d_middle = d_final_ref[at] + norm_rows_back(total * (1.0 + rows_ref[0:1]), normed, inv_std)
            d_middle_ref[at] = d_middle
            d_attn = (rows_ref[1:2] * d_middle).astype(bf16)
            sums_ref[0:1] += column_sum(total)
            sums_ref[1:2] += column_sum(total * normed)
            sums_ref[2:3] += column_sum(d_middle * attn_ref[at])
            sums_ref[3:4] += column_sum(d_attn.astype(f32))
            return d_attn

        def after(group):
            d_mixed_ref[group] = times_flipped(share[group], w_o_ref[...]).astype(bf16)

        return partial, own, after

    return stage(
        11,
        [d_hidden, w_up, w_o, middle, d_final, attn, rows],
        [((n, width), f32), ((4, width), f32), ((4, n, w_o.shape[0]), bf16)],
        True,
        make,
    )


def start_back_stage(d_proj, w_qkv, start, d_middle, rows):
    n, width, f32, bf16 = d_proj.shape[1], MODEL_WIDTH, jnp.float32, jnp.bfloat16

    def make(ins, outs, share):
        d_proj_ref, w_ref, start_ref, d_middle_ref, rows_ref = ins
        d_start_ref, sums_ref = outs
        sums_ref[...] = jnp.zeros_like(sums_ref)

        def partial(group):
            return times_flipped(d_proj_ref[group], w_ref[...])

        def own(at, total):
            at = slice(at, at + CHUNK)
            normed, inv_std = norm_rows(start_ref[at])
            d_start = d_middle_ref[at] + norm_rows_back(total * (1.0 + rows_ref[0:1]), normed, inv_std)
            d_start = d_start.astype(bf16)
            d_start_ref[at] = d_start
            sums_ref[0:1] += column_sum(total)
            sums_ref[1:2] += column_sum(total * normed)
            sums_ref[2:3] += column_sum(d_start.astype(f32))

        return partial, own, None

    return stage(
        12,
        [d_proj, w_qkv, start, d_middle, rows],
        [((n, width), bf16), ((3, width), f32)],
        False,
        make,
    )


def halves(x):
    high = x.astype(jnp.bfloat16)
    return high, (x - high.astype(jnp.float32)).astype(jnp.bfloat16)


def left_form(main, tail):
    mh, ml = halves(main)
    th, tl = halves(tail)
    return jnp.concatenate([mh, mh, ml, th, th, tl], axis=1)


def right_form(x):
    h, l = halves(x)
    return jnp.concatenate(
        [h[:LANES], l[:LANES], h[:LANES], h[LANES:], l[LANES:], h[LANES:]], axis=0
    )


def product(left, right):
    return jnp.dot(left, right, preferred_element_type=jnp.float32)


def symmetric_product(left, right_main, right_tail):
    main = product(left, right_main)
    corner = product(left[LANES:], right_tail)
    return main, jnp.concatenate([main[LANES:].T, corner], axis=0)


def inverse_roots(pairs, eye_main, eye_tail):
    contracted, scales = [], []
    for main, tail in pairs:
        trace = jnp.sum(main * eye_main) + jnp.sum(tail * eye_tail)
        shift = 0.0001 * trace / BLOCK_SIDE
        main = main + shift * eye_main
        tail = tail + shift * eye_tail
        square = jnp.sum(main * main, axis=(0, 1), keepdims=True) + jnp.sum(
            tail * tail, axis=(0, 1), keepdims=True
        )
        factor_z = 2.5 / jnp.sqrt(square)
        contracted.append((main * factor_z, tail * factor_z))
        scales.append(jnp.sqrt(jnp.sqrt(factor_z)))
    estimates = None
    for newton_step in range(NEWTON):
        more = newton_step < NEWTON - 1
        factors = [((5.0 * eye_main - m) * 0.25, (5.0 * eye_tail - t) * 0.25) for m, t in contracted]
        rights = [(right_form(m), right_form(t)) for m, t in factors]
        lefts = [left_form(m, t) for m, t in factors]
        if more:
            powers = [symmetric_product(l, *r) for l, r in zip(lefts, rights)]
        if estimates is None:
            estimates = [(m * s, t * s) for (m, t), s in zip(factors, scales)]
        else:
            estimates = [
                symmetric_product(left_form(*e), *r) for e, r in zip(estimates, rights)
            ]
        if more:
            powers = [
                symmetric_product(left_form(*q), right_form(q[0]), right_form(q[1])) for q in powers
            ]
            contracted = [
                symmetric_product(left_form(*q), right_form(m), right_form(t))
                for q, (m, t) in zip(powers, contracted)
            ]
    return estimates


def shampoo_body(clip_ref, g_ref, stat_ref, old_ref, clipped_ref, new_stat_ref, new_ref, low_ref):
    side = BLOCK_SIDE
    g_main, g_tail = unpack(g_ref[0] * clip_ref[0])
    clipped_ref[0, :, :LANES] = g_main
    clipped_ref[0, :, LANES:] = g_tail
    g = jnp.concatenate([g_main, g_tail], axis=1)

    def unit(width, offset):
        row = lax.broadcasted_iota(jnp.int32, (side, width), 0)
        col = lax.broadcasted_iota(jnp.int32, (side, width), 1) + offset
        return (row == col).astype(jnp.float32)

    eye_main, eye_tail = unit(LANES, 0), unit(TAIL, LANES)
    flipped = g.T
    g_right = (right_form(g[:, :LANES]), right_form(g[:, LANES:]))
    f_right = (right_form(flipped[:, :LANES]), right_form(flipped[:, LANES:]))
    g_left = left_form(g[:, :LANES], g[:, LANES:])
    f_left = left_form(flipped[:, :LANES], flipped[:, LANES:])
    pairs = []
    for k, (left, right) in enumerate(((g_left, f_right), (f_left, g_right))):
        main, tail = symmetric_product(left, *right)
        main = 0.5 * stat_ref[0, k, :, :LANES] + 0.5 * main
        tail = 0.5 * stat_ref[0, k, :, LANES:] + 0.5 * tail
        new_stat_ref[0, k, :, :LANES] = main
        new_stat_ref[0, k, :, LANES:] = tail
        pairs.append((main, tail))
    left_root, right_root = inverse_roots(pairs, eye_main, eye_tail)
    root_left = left_form(*left_root)
    half = left_form(product(root_left, g_right[0]), product(root_left, g_right[1]))
    for part, (a, b) in zip(right_root, ((0, LANES), (LANES, side))):
        direction = product(half, right_form(part))
        old = old_ref[0, :, a:b]
        new = old - shampoo_rate * (direction + decay_rate * old)
        new_ref[0, :, a:b] = new
        low_ref[0, :, a:b] = new.astype(jnp.bfloat16)


def shampoo(clip_factor, gradients, stats, old_blocks):
    count, side = gradients.shape[0], BLOCK_SIDE
    one = pl.BlockSpec((1, side, side), lambda i: (i, 0, 0))
    two = pl.BlockSpec((1, 2, side, side), lambda i: (i, 0, 0, 0))
    block = jax.ShapeDtypeStruct((count, side, side), jnp.float32)
    return pl.pallas_call(
        shampoo_body,
        grid=(count,),
        in_specs=[
            pl.BlockSpec(memory_space=pltpu.SMEM),
            pl.BlockSpec((1, PACK_ROWS, LANES // 2), lambda i: (i, 0, 0)),
            two,
            one,
        ],
        out_specs=[one, two, one, one],
        out_shape=[
            block,
            jax.ShapeDtypeStruct((count, 2, side, side), jnp.float32),
            block,
            jax.ShapeDtypeStruct((count, side, side), jnp.bfloat16),
        ],
        compiler_params=pltpu.CompilerParams(vmem_limit_bytes=56 * 2**20),
        cost_estimate=pl.CostEstimate(
            flops=count * 44 * 6 * side**3, bytes_accessed=count * 34 * side * side, transcendentals=0
        ),
        name="shampoo",
    )(clip_factor.reshape(1), gradients, stats, old_blocks)


def adam_update(weight, gradient, moment_one, second):
    moment_one = 0.5 * moment_one + 0.5 * gradient
    second = 0.5 * second + 0.5 * gradient * gradient
    correct = 1.0 - 0.5**STEP
    updated = weight - adam_rate * (
        moment_one / correct / (jnp.sqrt(second / correct) + 1e-08) + decay_rate * weight
    )
    return (moment_one, second, updated)


def per_device(
    latents,
    noise,
    timesteps,
    labels,
    loss_weights,
    slotted_block_weights,
    statistics,
    slot_of_block,
    cond_tables,
    head_tables,
    slice_bias,
    side_bias,
    cond_m,
    cond_v,
    head_m,
    head_v,
    slice_m,
    slice_v,
    side_m,
    side_v,
):
    bf16, f32 = jnp.bfloat16, jnp.float32
    width = MODEL_WIDTH
    mp, dp = lax.axis_size("mp"), lax.axis_size("dp")
    my_mp, my_dp = lax.axis_index("mp"), lax.axis_index("dp")
    query_width, ff_width, ada_width = HEADS * HD // mp, FF // mp, 6 * width // mp
    ada_column = 3 * query_width + ff_width
    row_blocks = width // BLOCK_SIDE
    col_blocks = (ada_column + ada_width) // BLOCK_SIDE
    out_blocks = (query_width + ff_width) // BLOCK_SIDE
    first_out = row_blocks * col_blocks
    t2_row = PATCH_VALUES + FREQ
    class_row = t2_row + width
    local_heads = query_width // HD
    score_scale = HD ** (-0.5)
    batch = latents.shape[0]
    own_n = batch // mp
    cols = cond_tables.shape[1]
    samples = batch * dp

    def own(x):
        return lax.dynamic_slice_in_dim(x, my_mp * own_n, own_n, 0)

    def my_cols(x):
        return lax.dynamic_slice_in_dim(x, my_dp * cols, cols, x.ndim - 1)

    def all_columns(x):
        return x.transpose(1, 0, 2).reshape(x.shape[1], -1)

    def by_columns(x):
        return x.reshape(x.shape[0], dp, cols).transpose(1, 0, 2)

    def share_rows(x):
        return lax.all_gather(x, "mp", axis=0, tiled=True)

    blocks = gather_blocks(pack_blocks(slotted_block_weights[0]))

    cond_low, head_low = cond_tables.astype(bf16), head_tables.astype(bf16)
    facts, shared = exchange(
        [
            (jnp.stack([timesteps.astype(f32), labels.astype(f32), loss_weights], 1), "gather"),
            (jnp.concatenate([cond_low[:PATCH_VALUES].T, head_low[:, 2 * width :]], 1), "gather"),
        ],
        "dp",
        2,
    )
    facts, shared = facts.reshape(samples, 3), shared.reshape(width, -1)
    all_steps, all_labels = facts[:, 0].astype(jnp.int32), facts[:, 1].astype(jnp.int32)
    weight_total = jnp.sum(facts[:, 2])
    w_patch, w_head = shared[:, :PATCH_VALUES].T, shared[:, PATCH_VALUES:]
    time_freq = time_features(all_steps, FREQ).astype(bf16)
    onehot = all_labels[:, None] == jnp.arange(CLASSES, dtype=jnp.int32)[None, :]
    first_t = dense(time_freq, cond_low[PATCH_VALUES:t2_row]) + my_cols(side_bias[width : 2 * width])
    (first_s,) = exchange([(swish_unit(first_t).astype(bf16), "gather")], "dp", 3)
    first_s = all_columns(first_s)
    cond_vec = (
        dense(first_s, cond_low[t2_row:class_row])
        + my_cols(side_bias[2 * width : 3 * width])
        + dense(onehot.astype(bf16), cond_low[class_row:])
    )
    signal_cols = swish_unit(cond_vec).astype(bf16)
    signal, final_mod = exchange(
        [
            (signal_cols.reshape(dp, batch, cols), "scatter"),
            (dense(signal_cols, head_low[:, : 2 * width]).reshape(dp, batch, 2 * width), "scatter"),
        ],
        "dp",
        4,
    )
    signal = all_columns(signal)
    final_mod = own(jnp.sum(final_mod, 0) + side_bias[5 * width : 7 * width])

    w_qkv, w_up, w_ada = assemble(
        blocks,
        slot_of_block,
        0,
        row_blocks,
        [3 * query_width // BLOCK_SIDE, ff_width // BLOCK_SIDE, ada_width // BLOCK_SIDE],
    )
    (w_o,) = assemble(blocks, slot_of_block, first_out, query_width // BLOCK_SIDE, [row_blocks])
    (w_down,) = assemble(
        blocks,
        slot_of_block,
        first_out + query_width // BLOCK_SIDE * row_blocks,
        ff_width // BLOCK_SIDE,
        [row_blocks],
    )
    own_bias = slice_bias[0]
    modul = lax.all_gather(
        dense(signal, w_ada) + own_bias[2 * query_width + ff_width :],
        "mp",
        axis=1,
        tiled=True,
    )
    own_modul = own(modul)

    def part(position):
        return modul[:, None, position * width : (position + 1) * width]

    def heads_of(inputs):
        return inputs.reshape(batch, -1, local_heads, HD)

    keep_rate, noise_rate, upper_log, lower_log, mean_gap = coefficients(timesteps)
    noisy = keep_rate[:, None, None, None] * latents + noise_rate[:, None, None, None] * noise
    patches = patchify(noisy).astype(bf16)
    seq_len = patches.shape[1]
    initial = (
        dense(patches, w_patch) + side_bias[:width] + position_embedding(LATENT_SIDE // 2, width)
    )
    normed_all, _ = layer_norm(initial)
    attn_in = (normed_all * (1.0 + part(1)) + part(0)).astype(bf16)
    start = own(initial)[0]
    own_patches = own(patches)
    target = patchify(own(noise))[0]

    projected = dense(attn_in, w_qkv)
    queries = heads_of((projected[..., :query_width] + own_bias[:query_width]).astype(bf16))
    keys = heads_of(projected[..., query_width : 2 * query_width].astype(bf16))
    values = heads_of(
        (projected[..., 2 * query_width :] + own_bias[query_width : 2 * query_width]).astype(bf16)
    )
    scores = (
        jnp.einsum("slhe,smhe->shlm", queries, keys, preferred_element_type=f32) * score_scale
    )
    row_peak = jnp.max(scores, -1, keepdims=True)
    shifted = jnp.exp(scores - row_peak)
    row_total = jnp.sum(shifted, -1, keepdims=True)
    probs = shifted / row_total
    log_total = row_peak + jnp.log(row_total)
    mixed = (
        jnp.einsum("shlm,smhe->slhe", probs.astype(bf16), values, preferred_element_type=f32)
        .reshape(batch, seq_len, query_width)
        .astype(bf16)
    )

    def rows_of(*rows):
        return jnp.concatenate([r.reshape(1, width) for r in rows], 0)

    shift1, scale1, gate1, shift2, scale2, gate2 = (own_modul[0, i * width : (i + 1) * width] for i in range(6))
    attn, middle, hidden, active, mlp_in = attention_out_stage(
        mixed,
        w_o,
        w_up,
        start,
        rows_of(side_bias[3 * width : 4 * width], gate1, scale2, shift2),
        own_bias[2 * query_width : 2 * query_width + ff_width].reshape(1, ff_width),
    )

    def halves_of(x):
        x = x.reshape(x.shape[:-1] + (4, 8))
        return x[..., :4].reshape(x.shape[:-2] + (16,)), x[..., 4:].reshape(x.shape[:-2] + (16,))

    w_pred, w_raw = halves_of(w_head)
    own_weight = own(loss_weights)
    facts = [own(upper_log), own(lower_log), own(mean_gap), own_weight, own_weight / weight_total]
    d_final, head_in, d_pred, d_raw, sums_f, loss_part, d_hidden, up_sum, d_branch = loss_stage(
        active,
        w_down,
        hidden,
        middle,
        rows_of(side_bias[4 * width : 5 * width], gate2, final_mod[0, width:], final_mod[0, :width]),
        target,
        w_pred,
        w_raw,
        jnp.stack(halves_of(side_bias[7 * width :])),
        jnp.broadcast_to(jnp.stack(facts), (5, 16)),
    )
    loss_part = jnp.sum(loss_part)
    d_fmod = sums_f[:2].reshape(1, 2 * width).astype(bf16)
    g_down = weight_grad(active, d_branch).astype(bf16)
    d_middle, sums_m, d_mixed, d_attn = middle_back_stage(
        d_hidden, w_up, w_o, middle, d_final, attn, rows_of(scale2, gate1)
    )
    g_up = weight_grad(mlp_in, d_hidden).astype(bf16)
    g_outp = weight_grad(mixed, d_attn).astype(bf16)
    d_mixed = heads_of(d_mixed)
    probs = jnp.exp(
        jnp.einsum("slhe,smhe->shlm", queries, keys, preferred_element_type=f32) * score_scale
        - log_total
    )
    d_values = jnp.einsum(
        "shlm,slhe->smhe", probs.astype(bf16), d_mixed, preferred_element_type=f32
    ).astype(bf16)
    d_probs = jnp.einsum("slhe,smhe->shlm", d_mixed, values, preferred_element_type=f32)
    d_scores = (probs * (d_probs - jnp.sum(d_probs * probs, -1, keepdims=True))).astype(bf16)
    d_query = (
        jnp.einsum("shlm,smhe->slhe", d_scores, keys, preferred_element_type=f32) * score_scale
    ).astype(bf16)
    d_keys = (
        jnp.einsum("shlm,slhe->smhe", d_scores, queries, preferred_element_type=f32) * score_scale
    ).astype(bf16)
    flat_q = d_query.reshape(batch, seq_len, query_width)
    flat_v = d_values.reshape(batch, seq_len, query_width)
    d_proj = jnp.concatenate([flat_q, d_keys.reshape(batch, seq_len, query_width), flat_v], 2)
    g_qkv = weight_grad(attn_in, d_proj).astype(bf16)
    d_start, sums_a = start_back_stage(d_proj, w_qkv, start, d_middle, scale1.reshape(1, width))
    d_mod_own = jnp.concatenate(
        [sums_a[0], sums_a[1], sums_m[2], sums_m[0], sums_m[1], sums_f[2]]
    ).reshape(1, 6 * width)
    d_modul = lax.dynamic_slice_in_dim(
        share_rows(d_mod_own.astype(bf16)), my_mp * ada_width, ada_width, 1
    )
    g_ada = weight_grad(signal, d_modul).astype(bf16)

    slot_grad = to_slots(
        [g_qkv, g_up, g_ada], [g_outp, g_down], slot_of_block, slot_of_block.shape[0]
    )
    red_blocks = reduce_blocks(slot_grad)

    d_fmod_all, d_signal = exchange(
        [(d_fmod, "gather"), (by_columns(back_dense(d_modul, w_ada)), "scatter")],
        EVERY,
        5,
    )
    d_fmod_all = d_fmod_all.reshape(samples, 2 * width)
    g_fada = weight_grad(signal_cols, d_fmod_all)
    d_signal = jnp.sum(d_signal.reshape(dp, mp, batch, cols), 1).reshape(samples, cols)
    d_signal = d_signal + back_dense(d_fmod_all, head_low[:, : 2 * width])
    d_cond = d_signal * swish_slope(cond_vec)
    d_second = d_cond.astype(bf16)
    g_second = weight_grad(first_s, d_second)
    g_class = jnp.einsum("sc,sd->cd", onehot.astype(f32), d_cond, precision=exact_precision_flag)

    def interleave(p, r):
        parts = [x.reshape(x.shape[:-1] + (4, 4)) for x in (p, r)]
        return jnp.concatenate(parts, -1).reshape(p.shape[:-1] + (32,))

    d_out = interleave(d_pred, d_raw)
    small = jnp.concatenate([weight_grad(own_patches[0], d_start), weight_grad(d_out, head_in)], 0)
    slice_part = jnp.concatenate([total_of(flat_q), total_of(flat_v), up_sum[0], total_of(d_modul)])
    side_part = jnp.concatenate([sums_a[2], sums_m[3], sums_f[3], total_of(d_out), loss_part[None]])
    bias_part = jnp.concatenate([slice_part, side_part])
    rows = -(-bias_part.shape[0] // 1024) * 8
    bias_part = jnp.pad(bias_part, (0, rows * 128 - bias_part.shape[0])).reshape(rows, 128)
    d_first, small, bias_part = exchange(
        [
            (by_columns(back_dense(d_second, cond_low[t2_row:class_row])), "scatter"),
            (by_columns(small), "scatter"),
            (bias_part, "gather"),
        ],
        "dp",
        6,
    )
    d_first = (jnp.sum(d_first, 0) * swish_slope(first_t)).astype(bf16)
    g_first = weight_grad(time_freq, d_first)
    bias_part = jnp.sum(bias_part, 0).reshape(-1)
    red_slice = bias_part[: slice_part.shape[0]]
    side_rows = bias_part[slice_part.shape[0] // 128 * 128 :].reshape(-1, 128)
    small, side_rows = exchange([(jnp.sum(small, 0), "gather"), (side_rows, "gather")], "mp", 7)
    small, side_sum = jnp.sum(small, 0), jnp.sum(side_rows, 0).reshape(-1)
    loss_sum = side_sum[side_part.shape[0] - 1]
    side_sum = side_sum[: side_part.shape[0] - 1]
    side_mod = total_of(d_fmod_all)
    red_cond = jnp.concatenate([small[:PATCH_VALUES], g_first, g_second, g_class], 0)
    red_head = jnp.concatenate([g_fada, small[PATCH_VALUES:].T], 1)
    side_cols = jnp.stack([total_of(d_first), total_of(d_second)])

    local_squares = (
        jnp.sum(red_blocks * red_blocks)
        + (jnp.sum(red_cond * red_cond) + jnp.sum(red_head * red_head) + jnp.sum(side_cols * side_cols)) / mp
        + jnp.sum(red_slice * red_slice) / dp
        + (jnp.sum(side_sum * side_sum) + jnp.sum(side_mod * side_mod)) / (dp * mp)
    )
    last = jnp.concatenate([side_cols, jnp.broadcast_to(local_squares, (2, 1))], 1)
    (last,) = exchange([(last, "gather")], EVERY, 8)
    grad_norm = jnp.sqrt(jnp.sum(last[:, 0, cols]))
    side_cols = last[:, :, :cols].reshape(dp, mp, 2, cols)[:, 0].transpose(1, 0, 2).reshape(2 * width)
    red_side = jnp.concatenate(
        [side_sum[:width], side_cols, side_sum[width : 3 * width], side_mod, side_sum[3 * width :]]
    )
    clip_factor = 1.0 / jnp.maximum(grad_norm, 1.0)
    clipped, new_stats, new_blocks, new_low = shampoo(
        clip_factor, red_blocks, statistics[0], slotted_block_weights[0]
    )
    cond_one, cond_two, new_cond = adam_update(cond_tables, red_cond * clip_factor, cond_m, cond_v)
    head_one, head_two, new_head = adam_update(head_tables, red_head * clip_factor, head_m, head_v)
    slice_one, slice_two, new_slice = adam_update(
        slice_bias[0], red_slice * clip_factor, slice_m[0], slice_v[0]
    )
    side_one, side_two, new_side = adam_update(side_bias, red_side * clip_factor, side_m, side_v)
    return (
        loss_sum,
        weight_total,
        grad_norm,
        clipped[None],
        new_stats[None],
        new_blocks[None],
        new_low[None],
        cond_one,
        cond_two,
        new_cond,
        new_cond.astype(bf16),
        head_one,
        head_two,
        new_head,
        new_head.astype(bf16),
        slice_one[None],
        slice_two[None],
        new_slice[None],
        side_one,
        side_two,
        new_side,
    )


def solution(mesh):
    return jax.shard_map(
        per_device,
        mesh=mesh,
        in_specs=(
            P("dp", None, None, None),
            P("dp", None, None, None),
            P("dp"),
            P("dp"),
            P("dp"),
            P("mp", "dp", None, None),
            P("mp", "dp", None, None, None),
            P(),
            P(None, "dp"),
            P("dp", None),
            P("mp", None),
            P(),
            P(None, "dp"),
            P(None, "dp"),
            P("dp", None),
            P("dp", None),
            P("mp", None),
            P("mp", None),
            P(),
            P(),
        ),
        out_specs=(
            P(),
            P(),
            P(),
            P("mp", "dp", None, None),
            P("mp", "dp", None, None, None),
            P("mp", "dp", None, None),
            P("mp", "dp", None, None),
            P(None, "dp"),
            P(None, "dp"),
            P(None, "dp"),
            P(None, "dp"),
            P("dp", None),
            P("dp", None),
            P("dp", None),
            P("dp", None),
            P("mp", None),
            P("mp", None),
            P("mp", None),
            P(),
            P(),
            P(),
        ),
        check_vma=False,
    )
```

```python
import math

import jax
import jax.numpy as jnp
from jax import lax
from jax.experimental import pallas as pl
from jax.experimental.pallas import tpu as pltpu
from jax.sharding import PartitionSpec as P

MODEL_WIDTH = 1152
HEADS = 16
HD = 72
FF = 4608
FREQ = 256
CLASSES = 1001
LATENT_SIDE = 32
PATCH_VALUES = 16
BLOCK_SIDE = 288
NEWTON = 6
STEP = 5
LANES = 256
TAIL = BLOCK_SIDE - LANES


exact_precision_flag = lax.Precision.HIGHEST
shampoo_rate = 0.5
adam_rate = 0.05
decay_rate = 0.01


def dense(operand, weight):
    return jnp.dot(operand, weight, preferred_element_type=jnp.float32)


def back_dense(gradient, weight):
    return jnp.einsum("...j,ij->...i", gradient, weight, preferred_element_type=jnp.float32)


def weight_grad(operand, gradient):
    return jnp.einsum("...i,...j->ij", operand, gradient, preferred_element_type=jnp.float32)


def total_of(inputs):
    return jnp.sum(inputs.astype(jnp.float32), axis=tuple(range(inputs.ndim - 1)))


def swish_unit(inputs):
    return inputs / (1.0 + jnp.exp(-inputs))


def swish_slope(inputs):
    sigmoid = 1.0 / (1.0 + jnp.exp(-inputs))
    return sigmoid * (1.0 + inputs * (1.0 - sigmoid))


def tanh_gelu_activation(inputs):
    return (
        0.5
        * inputs
        * (1.0 + jnp.tanh(0.7978845608028654 * (inputs + 0.044715 * inputs * inputs * inputs)))
    )


def gelu_slope(inputs):
    inner = jnp.tanh(0.7978845608028654 * (inputs + 0.044715 * inputs * inputs * inputs))
    return 0.5 * (1.0 + inner) + 0.5 * inputs * (1.0 - inner * inner) * 0.7978845608028654 * (
        1.0 + 3.0 * 0.044715 * inputs * inputs
    )


def layer_norm(inputs):
    centred = inputs - jnp.mean(inputs, -1, keepdims=True)
    inv_std = lax.rsqrt(jnp.mean(centred * centred, -1, keepdims=True) + 1e-06)
    return (centred * inv_std, inv_std)


def norm_back(gradient, normed, inv_std):
    return inv_std * (
        gradient
        - jnp.mean(gradient, -1, keepdims=True)
        - normed * jnp.mean(gradient * normed, -1, keepdims=True)
    )


def coefficients(step_ids):
    grid = jnp.arange(1000).astype(jnp.float32)
    betas = 0.0001 + (0.02 - 0.0001) * grid / 999.0
    logs = jnp.log(1.0 - betas)[None, :]
    index = jnp.arange(1000, dtype=jnp.int32)[None, :]
    beta_t = 0.0001 + (0.02 - 0.0001) * step_ids.astype(jnp.float32) / 999.0
    cumul_t = jnp.exp(jnp.sum(jnp.where(index <= step_ids[:, None], logs, 0.0), 1))
    before_t = jnp.exp(jnp.sum(jnp.where(index < step_ids[:, None], logs, 0.0), 1))
    keep_rate = jnp.sqrt(cumul_t)
    noise_rate = jnp.sqrt(1.0 - cumul_t)
    upper_log = jnp.log(beta_t)
    lower_log = jnp.log(beta_t * (1.0 - before_t) / (1.0 - cumul_t))
    mean_gap = beta_t * jnp.sqrt(before_t) / (1.0 - cumul_t) * jnp.sqrt(1.0 / cumul_t - 1.0)
    return (keep_rate, noise_rate, upper_log, lower_log, mean_gap)


def time_features(step_ids, feat_width):
    half_width = feat_width // 2
    frequencies = jnp.exp(
        -math.log(10000.0) * jnp.arange(half_width).astype(jnp.float32) / half_width
    )
    phases = step_ids.astype(jnp.float32)[:, None] * frequencies[None, :]
    return jnp.concatenate([jnp.cos(phases), jnp.sin(phases)], 1)


def position_embedding(grid_side, feat_width):
    quarter = feat_width // 4
    omegas = jnp.exp(-math.log(10000.0) * jnp.arange(quarter).astype(jnp.float32) / quarter)
    coords = jnp.arange(grid_side).astype(jnp.float32)
    angles = coords[:, None] * omegas[None, :]
    waves = jnp.concatenate([jnp.sin(angles), jnp.cos(angles)], 1)
    half_width = feat_width // 2
    rows_part = jnp.broadcast_to(waves[:, None, :], (grid_side, grid_side, half_width))
    cols_part = jnp.broadcast_to(waves[None, :, :], (grid_side, grid_side, half_width))
    return jnp.concatenate([rows_part, cols_part], 2).reshape(grid_side * grid_side, feat_width)


def patchify(latent):
    samples_n, channels, height, breadth = latent.shape
    shaped = latent.reshape(samples_n, channels, height // 2, 2, breadth // 2, 2).transpose(
        0, 2, 4, 3, 5, 1
    )
    return shaped.reshape(samples_n, height // 2 * (breadth // 2), 4 * channels)


PACK_ROWS = 656


def pack(x):
    quarter = BLOCK_SIDE // 4
    tail = x[:, LANES:].astype(jnp.float32)
    tail = jnp.concatenate([tail[i * quarter : (i + 1) * quarter] for i in range(4)], axis=1)
    fill = jnp.zeros((PACK_ROWS - 2 * BLOCK_SIDE - quarter, LANES // 2), jnp.float32)
    tail = jnp.concatenate([tail, fill], axis=0)
    half = LANES // 2
    return x[:, :half], x[:, half:LANES], tail.astype(x.dtype)


def unpack(x):
    side, quarter = BLOCK_SIDE, BLOCK_SIDE // 4
    tail = x[2 * side :].astype(jnp.float32)[:quarter]
    tail = jnp.concatenate([tail[:, i * TAIL : (i + 1) * TAIL] for i in range(4)], axis=0)
    main = jnp.concatenate([x[:side], x[side : 2 * side]], axis=1)
    return main, tail.astype(x.dtype)


def store_packed(ref, index, x):
    a, b, c = pack(x)
    side = BLOCK_SIDE
    ref[index + (slice(0, side),)] = a
    ref[index + (slice(side, 2 * side),)] = b
    ref[index + (slice(2 * side, PACK_ROWS),)] = c


def pack_blocks(blocks):
    count, side = blocks.shape[0], BLOCK_SIDE

    def body(x_ref, out_ref):
        store_packed(out_ref, (0,), x_ref[0].astype(jnp.bfloat16))

    return pl.pallas_call(
        body,
        grid=(count,),
        in_specs=[pl.BlockSpec((1, side, side), lambda i: (i, 0, 0))],
        out_specs=pl.BlockSpec((1, PACK_ROWS, LANES // 2), lambda i: (i, 0, 0)),
        out_shape=jax.ShapeDtypeStruct((count, PACK_ROWS, LANES // 2), jnp.bfloat16),
        name="pack_blocks",
    )(blocks)


def remote(source, target, send, receive, place):
    return pltpu.make_async_remote_copy(
        src_ref=source,
        dst_ref=target,
        send_sem=send,
        recv_sem=receive,
        device_id=place,
        device_id_type=pl.DeviceIdType.MESH,
    )


def signal_to(semaphore, place):
    pl.semaphore_signal(semaphore, inc=1, device_id=place, device_id_type=pl.DeviceIdType.MESH)


COLUMNS = 2
LAYERS = 4


def grid_place():
    me = lax.axis_index("dp")
    return me // COLUMNS, me % COLUMNS


EVERY = ("dp", "mp")


def exchange(items, axes, number):
    mp, dp = lax.axis_size("mp"), lax.axis_size("dp")
    n = {"dp": dp, "mp": mp, EVERY: dp * mp}[axes]

    def place(i):
        return {"dp": i // mp, "mp": i % mp} if axes == EVERY else {axes: i}

    def row(i):
        return i // mp if axes == EVERY else i

    def body(*refs):
        m = len(items)
        sources, outs, send, receive = refs[:m], refs[m : 2 * m], refs[-2], refs[-1]
        me = lax.axis_index("dp") * mp + lax.axis_index("mp") if axes == EVERY else lax.axis_index(axes)
        barrier = pltpu.get_barrier_semaphore()

        def greet(i, _):
            signal_to(barrier, place(lax.rem(me + i, n)))
            return 0

        lax.fori_loop(1, n, greet, 0)
        pl.semaphore_wait(barrier, n - 1)

        def piece(j, to):
            return sources[j].at[row(to)] if items[j][1] == "scatter" else sources[j]

        def start(i, _):
            to = lax.rem(me + i, n)
            for j in range(m):
                remote(piece(j, to), outs[j].at[me], send.at[j, i], receive.at[j, me], place(to)).start()
            return 0

        lax.fori_loop(1, n, start, 0)
        for j in range(m):
            outs[j][me] = sources[j][row(me)] if items[j][1] == "scatter" else sources[j][...]

        def finish(i, _):
            to = lax.rem(me + i, n)
            for j in range(m):
                copy = remote(piece(j, to), outs[j].at[to], send.at[j, i], receive.at[j, to], place(to))
                copy.wait_recv()
                copy.wait_send()
            return 0

        lax.fori_loop(1, n, finish, 0)

    arrays = [a for a, _ in items]
    shapes = [
        jax.ShapeDtypeStruct((n,) + (a.shape[1:] if kind == "scatter" else a.shape), a.dtype)
        for a, kind in items
    ]
    vmem = pl.BlockSpec(memory_space=pltpu.VMEM)
    return pl.pallas_call(
        body,
        in_specs=[vmem] * len(arrays),
        out_specs=[vmem] * len(arrays),
        out_shape=shapes,
        scratch_shapes=[pltpu.SemaphoreType.DMA((len(arrays), n))] * 2,
        compiler_params=pltpu.CompilerParams(
            collective_id=number, has_side_effects=True, vmem_limit_bytes=40 * 2**20
        ),
        name=f"exchange_{number}",
    )(*arrays)


def assemble(blocks, slots, first, rows, widths):
    side, cols = BLOCK_SIDE, sum(widths)

    def body(ids, *refs):
        base = 0
        for out, width in zip(refs[cols:], widths):
            parts = [part for r in refs[base : base + width] for part in unpack(r[0])]
            out[...] = jnp.concatenate(parts, axis=1)
            base += width

    def spec(c):
        return pl.BlockSpec(
            (1, PACK_ROWS, LANES // 2), lambda r, ids: (ids[first + r * cols + c], 0, 0)
        )

    return pl.pallas_call(
        body,
        grid_spec=pltpu.PrefetchScalarGridSpec(
            num_scalar_prefetch=1,
            grid=(rows,),
            in_specs=[spec(c) for c in range(cols)],
            out_specs=[pl.BlockSpec((side, side * w), lambda r, ids: (r, 0)) for w in widths],
        ),
        out_shape=[jax.ShapeDtypeStruct((rows * side, w * side), jnp.bfloat16) for w in widths],
        compiler_params=pltpu.CompilerParams(vmem_limit_bytes=40 * 2**20),
        cost_estimate=pl.CostEstimate(
            flops=0, bytes_accessed=4 * rows * cols * side * side, transcendentals=0
        ),
        name="assemble",
    )(slots, *([blocks] * cols))


def to_slots(inner, signal, d_modul, lower, slots, total):
    side = BLOCK_SIDE
    ri, widths = inner[0].shape[0] // side, [g.shape[1] // side for g in inner]
    wide = d_modul.shape[1] // side
    ci, co = sum(widths) + wide, lower[0].shape[1] // side
    heights = [g.shape[0] // side for g in lower]
    ro = sum(heights)
    steps = ri + ro
    n = len(inner) + 2 + len(lower)
    batch = signal.shape[0]
    signal = signal.reshape(batch, ri, side).transpose(1, 0, 2)

    def body(ids, *refs):
        sources, (out, buf, sem) = refs[:n], refs[-3:]
        s = pl.program_id(0)
        half = lax.rem(s, 2)

        def drain(which, count):
            for c in range(count):
                pltpu.make_async_copy(buf.at[which, c], out.at[0], sem.at[which, c]).wait()

        def send(source, count, base, first=0):
            for c in range(count):
                store_packed(buf, (half, first + c), source[:, c * side : (c + 1) * side])
                pltpu.make_async_copy(
                    buf.at[half, first + c], out.at[ids[base + c]], sem.at[half, first + c]
                ).start()

        @pl.when(jnp.logical_and(s >= 2, s - 2 < ri))
        def _():
            drain(half, ci)

        @pl.when(s - 2 >= ri)
        def _():
            drain(half, co)

        @pl.when(s < ri)
        def _():
            first = 0
            for source, width in zip(sources, widths):
                send(source, width, s * ci + first, first)
                first += width
            send(outer(refs[len(inner)][0], refs[len(inner) + 1][...]).astype(jnp.bfloat16), wide, s * ci + first, first)

        base = ri
        for source, height in zip(sources[len(inner) + 2 :], heights):

            @pl.when(jnp.logical_and(s >= base, s < base + height))
            def _():
                send(source, co, ri * ci + (s - ri) * co)

            base += height

        @pl.when(s == steps - 1)
        def _():
            drain(1 - half, co)
            drain(half, co)

    extra, aliases = [], {}
    if total != ri * ci + ro * co:
        extra = [jnp.zeros((total, PACK_ROWS, LANES // 2), jnp.bfloat16)]
        aliases = {1 + n: 0}
    specs = [
        pl.BlockSpec((side, w * side), lambda s, ids: (jnp.minimum(s, ri - 1), 0)) for w in widths
    ]
    specs += [
        pl.BlockSpec((1, batch, side), lambda s, ids: (jnp.minimum(s, ri - 1), 0, 0)),
        pl.BlockSpec(d_modul.shape, lambda s, ids: (0, 0)),
    ]
    base = ri
    for height in heights:
        specs.append(
            pl.BlockSpec(
                (side, co * side),
                lambda s, ids, base=base, height=height: (jnp.clip(s - base, 0, height - 1), 0),
            )
        )
        base += height
    return pl.pallas_call(
        body,
        grid_spec=pltpu.PrefetchScalarGridSpec(
            num_scalar_prefetch=1,
            grid=(steps,),
            in_specs=specs + [pl.BlockSpec(memory_space=pl.ANY)] * len(extra),
            out_specs=pl.BlockSpec(memory_space=pl.ANY),
            scratch_shapes=[
                pltpu.VMEM((2, max(ci, co), PACK_ROWS, LANES // 2), jnp.bfloat16),
                pltpu.SemaphoreType.DMA((2, max(ci, co))),
            ],
        ),
        out_shape=jax.ShapeDtypeStruct((total, PACK_ROWS, LANES // 2), jnp.bfloat16),
        compiler_params=pltpu.CompilerParams(vmem_limit_bytes=40 * 2**20),
        cost_estimate=pl.CostEstimate(
            flops=0, bytes_accessed=4 * (ri * ci + ro * co) * side * side, transcendentals=0
        ),
        input_output_aliases=aliases,
        name="to_slots",
    )(slots, *inner, signal, d_modul, *lower, *extra)


CHUNK = 64


def mean_of(x):
    return jnp.sum(x, axis=-1, keepdims=True) * (1.0 / x.shape[-1])


def norm_rows(x):
    centred = x - mean_of(x)
    inv_std = lax.rsqrt(mean_of(centred * centred) + 1e-06)
    return centred * inv_std, inv_std


def norm_rows_back(gradient, normed, inv_std):
    return inv_std * (gradient - mean_of(gradient) - normed * mean_of(gradient * normed))


def column_sum(x):
    return jnp.sum(x, axis=0, keepdims=True)


def times(a, b):
    return jnp.dot(a, b, preferred_element_type=jnp.float32)


def times_flipped(a, b):
    return lax.dot_general(a, b, (((1,), (1,)), ((), ())), preferred_element_type=jnp.float32)


def stage(number, inputs, outputs, shared, make):
    rows, width = inputs[0].shape[1], MODEL_WIDTH
    pieces = rows // CHUNK
    n_in, n_out = len(inputs), len(outputs)

    def body(*refs):
        ins, outs = refs[:n_in], refs[n_in : n_in + n_out]
        rest = refs[n_in + n_out :]
        share = None
        if shared:
            share, rest = rest[0], rest[1:]
        a_out, a_in, b_out, b_in, c_out, c_in, total, near, far = rest
        me = lax.axis_index("mp")
        core = me + 1 - 2 * lax.rem(me, 2)
        across = lax.rem(me + 2, 4)
        other = lax.rem(core + 2, 4)
        to_core, to_across = {"mp": core}, {"mp": across}
        partial, own, after = make(ins, outs, share)
        barrier = pltpu.get_barrier_semaphore()
        signal_to(barrier, to_core)
        signal_to(barrier, to_across)
        pl.semaphore_wait(barrier, 2)

        copy_a = remote(a_out, a_in, near.at[0, 0], near.at[1, 0], to_core)
        copy_c = remote(c_out, c_in, near.at[0, 1], near.at[1, 1], to_core)

        def piece(i):
            return pl.ds(i * CHUNK, CHUNK)

        def copy_b(i):
            return remote(
                b_out.at[piece(i)], b_in.at[piece(i)], far.at[0, i], far.at[1, i], to_across
            )

        def share_far(group, i):
            part = share.at[group, piece(i)]
            return remote(part, part, far.at[2, i], far.at[3, i], to_across)

        def share_near(group, i):
            part = share.at[group, piece(i)]
            return remote(part, part, near.at[2, i], near.at[3, i], to_core)

        def pass_near(group, i):
            part = share.at[group, piece(i)]
            return remote(part, part, near.at[4, i], near.at[5, i], to_core)

        a_out[...] = partial(other).astype(jnp.bfloat16)
        copy_a.start()
        total[...] = partial(across)
        copy_a.wait_recv()
        for i in range(pieces):
            at = piece(i)
            b_out[at] = (total[at] + a_in[at].astype(jnp.float32)).astype(jnp.bfloat16)
            copy_b(i).start()
        c_out[...] = partial(core).astype(jnp.bfloat16)
        copy_c.start()
        total[...] = partial(me)
        copy_c.wait_recv()
        for i in range(pieces):
            at = piece(i)
            copy_b(i).wait_recv()
            result = own(
                i * CHUNK, total[at] + c_in[at].astype(jnp.float32) + b_in[at].astype(jnp.float32)
            )
            if shared:
                share[me, at] = result
                share_far(me, i).start()
                share_near(me, i).start()
        if shared:
            after(me)
            for i in range(pieces):
                share_near(core, i).wait_recv()
            after(core)
            for i in range(pieces):
                share_far(across, i).wait_recv()
                pass_near(across, i).start()
            after(across)
            for i in range(pieces):
                pass_near(other, i).wait_recv()
            after(other)
        copy_a.wait_send()
        copy_c.wait_send()
        for i in range(pieces):
            copy_b(i).wait_send()
            if shared:
                share_far(me, i).wait_send()
                share_near(me, i).wait_send()
                pass_near(across, i).wait_send()

    vmem = pl.BlockSpec(memory_space=pltpu.VMEM)
    out_shape = [jax.ShapeDtypeStruct(shape, dtype) for shape, dtype in outputs]
    if shared:
        out_shape.append(jax.ShapeDtypeStruct((4, rows, width), jnp.bfloat16))
    landing = pltpu.VMEM((rows, width), jnp.bfloat16)
    return pl.pallas_call(
        body,
        in_specs=[vmem] * n_in,
        out_specs=[vmem] * len(out_shape),
        out_shape=out_shape,
        scratch_shapes=[landing] * 6
        + [
            pltpu.VMEM((rows, width), jnp.float32),
            pltpu.SemaphoreType.DMA((6, max(pieces, 2))),
            pltpu.SemaphoreType.DMA((4, pieces)),
        ],
        compiler_params=pltpu.CompilerParams(
            collective_id=number, has_side_effects=True, vmem_limit_bytes=56 * 2**20
        ),
        name=f"stage_{number}",
    )(*inputs)


def attention_out_stage(mixed, w_o, w_up, start, rows, up_bias):
    n, width, f32 = mixed.shape[1], MODEL_WIDTH, jnp.float32

    def make(ins, outs, share):
        mixed_ref, w_o_ref, w_up_ref, start_ref, rows_ref, up_ref = ins
        attn_ref, middle_ref, hidden_ref, active_ref = outs

        def partial(group):
            return times(mixed_ref[group], w_o_ref[...])

        def own(at, total):
            at = slice(at, at + CHUNK)
            attn = total + rows_ref[0:1]
            middle = start_ref[at] + rows_ref[1:2] * attn
            attn_ref[at] = attn
            middle_ref[at] = middle
            normed, _ = norm_rows(middle)
            return (normed * (1.0 + rows_ref[2:3]) + rows_ref[3:4]).astype(jnp.bfloat16)

        def after(group):
            for at in range(0, n, CHUNK):
                at = slice(at, at + CHUNK)
                hidden = times(share[group, at], w_up_ref[...]) + up_ref[...]
                hidden_ref[group, at] = hidden
                active_ref[group, at] = tanh_gelu_activation(hidden).astype(jnp.bfloat16)

        return partial, own, after

    inner = w_up.shape[1]
    return stage(
        9,
        [mixed, w_o, w_up, start, rows, up_bias],
        [((n, width), f32), ((n, width), f32), ((4, n, inner), f32), ((4, n, inner), jnp.bfloat16)],
        True,
        make,
    )


def loss_stage(active, w_down, hidden, middle, rows, target, w_pred, w_raw, head_bias, facts):
    n, width, f32, bf16 = active.shape[1], MODEL_WIDTH, jnp.float32, jnp.bfloat16
    inner = active.shape[2]

    def make(ins, outs, share):
        active_ref, w_ref, hidden_ref, middle_ref, rows_ref, target_ref, wp_ref, wr_ref, bias_ref, facts_ref = ins
        d_final_ref, head_in_ref, d_pred_ref, d_raw_ref, sums_ref, loss_ref, d_hidden_ref, up_sum_ref = outs
        sums_ref[...] = jnp.zeros_like(sums_ref)
        loss_ref[...] = jnp.zeros_like(loss_ref)
        up_sum_ref[...] = jnp.zeros_like(up_sum_ref)

        def partial(group):
            return times(active_ref[group], w_ref[...])

        def own(at, total):
            at = slice(at, at + CHUNK)
            branch = total + rows_ref[0:1]
            gate, fscale = rows_ref[1:2], 1.0 + rows_ref[2:3]
            normed, inv_std = norm_rows(middle_ref[at] + gate * branch)
            head_in = (normed * fscale + rows_ref[3:4]).astype(bf16)
            head_in_ref[at] = head_in
            upper, lower, gap = facts_ref[0:1], facts_ref[1:2], facts_ref[2:3]
            weight, share_of = facts_ref[3:4], facts_ref[4:5]
            error = times(head_in, wp_ref[...]) + bias_ref[0:1] - target_ref[at]
            fraction = (times(head_in, wr_ref[...]) + bias_ref[1:2] + 1.0) / 2.0
            log_var = fraction * upper + (1.0 - fraction) * lower
            gap = gap * error
            ratio = jnp.exp(lower - log_var)
            spread = gap * gap * jnp.exp(-log_var)
            diverge = 0.5 * (-1.0 + log_var - lower + ratio + spread)
            cells = 1.0 / (n * error.shape[1])
            per_bit = cells / math.log(2.0)
            loss_ref[...] += weight * column_sum(error * error * cells + diverge * per_bit)
            d_pred = (share_of * (2.0 * cells) * error).astype(bf16)
            d_raw = (
                share_of * per_bit * 0.25 * (upper - lower) * (1.0 - ratio - spread)
            ).astype(bf16)
            d_pred_ref[at] = d_pred
            d_raw_ref[at] = d_raw
            d_head = times_flipped(d_pred, wp_ref[...]) + times_flipped(d_raw, wr_ref[...])
            d_final = norm_rows_back(d_head * fscale, normed, inv_std)
            d_final_ref[at] = d_final
            d_branch = (gate * d_final).astype(bf16)
            sums_ref[0:1] += column_sum(d_head)
            sums_ref[1:2] += column_sum(d_head * normed)
            sums_ref[2:3] += column_sum(d_final * branch)
            sums_ref[3:4] += column_sum(d_branch.astype(f32))
            return d_branch

        def after(group):
            for at in range(0, n, CHUNK):
                at = slice(at, at + CHUNK)
                d_active = times_flipped(share[group, at], w_ref[...])
                d_hidden = (d_active * gelu_slope(hidden_ref[group, at])).astype(bf16)
                d_hidden_ref[group, at] = d_hidden
                up_sum_ref[...] += column_sum(d_hidden.astype(f32))

        return partial, own, after

    half = w_pred.shape[1]
    return stage(
        10,
        [active, w_down, hidden, middle, rows, target, w_pred, w_raw, head_bias, facts],
        [
            ((n, width), f32),
            ((n, width), bf16),
            ((n, half), bf16),
            ((n, half), bf16),
            ((4, width), f32),
            ((1, half), f32),
            ((4, n, inner), bf16),
            ((1, inner), f32),
        ],
        True,
        make,
    )


def middle_back_stage(d_hidden, w_up, w_o, middle, d_final, attn, rows):
    n, width, f32, bf16 = d_hidden.shape[1], MODEL_WIDTH, jnp.float32, jnp.bfloat16

    def make(ins, outs, share):
        d_hidden_ref, w_up_ref, w_o_ref, middle_ref, d_final_ref, attn_ref, rows_ref = ins
        d_middle_ref, sums_ref, d_mixed_ref = outs
        sums_ref[...] = jnp.zeros_like(sums_ref)

        def partial(group):
            return times_flipped(d_hidden_ref[group], w_up_ref[...])

        def own(at, total):
            at = slice(at, at + CHUNK)
            normed, inv_std = norm_rows(middle_ref[at])
            d_middle = d_final_ref[at] + norm_rows_back(total * (1.0 + rows_ref[0:1]), normed, inv_std)
            d_middle_ref[at] = d_middle
            d_attn = (rows_ref[1:2] * d_middle).astype(bf16)
            sums_ref[0:1] += column_sum(total)
            sums_ref[1:2] += column_sum(total * normed)
            sums_ref[2:3] += column_sum(d_middle * attn_ref[at])
            sums_ref[3:4] += column_sum(d_attn.astype(f32))
            return d_attn

        def after(group):
            d_mixed_ref[group] = times_flipped(share[group], w_o_ref[...]).astype(bf16)

        return partial, own, after

    return stage(
        11,
        [d_hidden, w_up, w_o, middle, d_final, attn, rows],
        [((n, width), f32), ((4, width), f32), ((4, n, w_o.shape[0]), bf16)],
        True,
        make,
    )


def start_back_stage(d_proj, w_qkv, start, d_middle, rows):
    n, width, f32, bf16 = d_proj.shape[1], MODEL_WIDTH, jnp.float32, jnp.bfloat16

    def make(ins, outs, share):
        d_proj_ref, w_ref, start_ref, d_middle_ref, rows_ref = ins
        d_start_ref, sums_ref = outs
        sums_ref[...] = jnp.zeros_like(sums_ref)

        def partial(group):
            return times_flipped(d_proj_ref[group], w_ref[...])

        def own(at, total):
            at = slice(at, at + CHUNK)
            normed, inv_std = norm_rows(start_ref[at])
            d_start = d_middle_ref[at] + norm_rows_back(total * (1.0 + rows_ref[0:1]), normed, inv_std)
            d_start = d_start.astype(bf16)
            d_start_ref[at] = d_start
            sums_ref[0:1] += column_sum(total)
            sums_ref[1:2] += column_sum(total * normed)
            sums_ref[2:3] += column_sum(d_start.astype(f32))

        return partial, own, None

    return stage(
        12,
        [d_proj, w_qkv, start, d_middle, rows],
        [((n, width), bf16), ((3, width), f32)],
        False,
        make,
    )


CROSS_LATE = 1


class Push:
    def __init__(self, source, landing, send, receive, n, me, place, row=None):
        self.source, self.landing, self.send, self.receive = source, landing, send, receive
        self.n, self.me, self.place, self.row = n, me, place, row

    def _copy(self, i, sender, to):
        source = self.source if self.row is None else self.source.at[self.row(to)]
        return remote(
            source, self.landing.at[sender], self.send.at[i], self.receive.at[sender], self.place(to)
        )

    def start(self):
        def one(i, _):
            self._copy(i, self.me, lax.rem(self.me + i, self.n)).start()
            return 0

        lax.fori_loop(1, self.n, one, 0)
        own = self.source[...] if self.row is None else self.source[self.row(self.me)]
        self.landing[self.me] = own

    def wait(self):
        def one(i, _):
            to = lax.rem(self.me + i, self.n)
            copy = self._copy(i, to, to)
            copy.wait_recv()
            copy.wait_send()
            return 0

        lax.fori_loop(1, self.n, one, 0)


def head_body(
    x_ref, tf_ref, facts_ref, shared_ref, w1_ref, w2_ref, class_ref, fada_ref, b1_ref, b2_ref,
    out_ref, tf_all, facts_all, shared_all, first_t_ref, first_s_all, cond_ref, signal_ref,
    signal_all, mod_ref,
    packed, tf_land, first_s, signal_own, mod_own, mod_land, local_sem, up_sem, down_sem, side_sem,
    up_other, down_other, recv_sem, send, receive,
):
    count, ways, f32, bf16 = x_ref.shape[0], LAYERS * COLUMNS, jnp.float32, jnp.bfloat16
    batch, cols = tf_ref.shape[0], shared_ref.shape[0]
    late = count - CROSS_LATE
    z, y = grid_place()
    me = lax.axis_index("dp")

    def place(i):
        return {"dp": i}

    barrier = pltpu.get_barrier_semaphore()

    def greet(i, _):
        signal_to(barrier, place(lax.rem(me + i, ways)))
        return 0

    lax.fori_loop(1, ways, greet, 0)
    pl.semaphore_wait(barrier, ways - 1)

    def push(j, source, landing, row=None):
        return Push(source, landing, send.at[j], receive.at[j], ways, me, place, row)

    first = [
        push(0, tf_ref, tf_land),
        push(1, facts_ref, facts_all),
        push(2, shared_ref, shared_all),
    ]
    for p in first:
        p.start()

    peer = {"dp": z * COLUMNS + 1 - y}
    above = {"dp": jnp.minimum(z + 1, LAYERS - 1) * COLUMNS + y}
    below = {"dp": jnp.maximum(z - 1, 0) * COLUMNS + y}

    def block(layer, column, k):
        return out_ref.at[(layer * COLUMNS + column) * count + k]

    def move(source, layer, k, sem, to):
        return remote(source, block(layer, y, k), sem.at[layer, k], recv_sem.at[layer, y, k], to)

    def move_other(layer, k, sem, to):
        here = block(layer, 1 - y, k)
        return remote(here, here, sem.at[layer, k - late], recv_sem.at[layer, 1 - y, k], to)

    def arrival(layer, column, k):
        here = block(layer, column, k)
        return remote(here, here, side_sem.at[0, 0], recv_sem.at[layer, column, k], peer)

    def send_own(i, _):
        k = count - 1 - i
        store_packed(packed, (k,), x_ref[k].astype(bf16))
        own = packed.at[k]
        move(own, z, k, side_sem, peer).start()

        @pl.when(z < LAYERS - 1)
        def _():
            move(own, z, k, up_sem, above).start()

        @pl.when(z > 0)
        def _():
            move(own, z, k, down_sem, below).start()

        pltpu.make_async_copy(own, block(z, y, k), local_sem.at[k]).start()
        return 0

    lax.fori_loop(0, count, send_own, 0)

    for p in first:
        p.wait()
    for i in range(ways):
        tf_all[i * batch : (i + 1) * batch] = tf_land[i]
    first_t = times(tf_all[...].astype(bf16), w1_ref[...]) + b1_ref[...]
    first_t_ref[...] = first_t
    first_s[...] = swish_unit(first_t).astype(bf16)
    second = push(3, first_s, first_s_all)
    second.start()

    for k in range(late, count):
        arrival(z, 1 - y, k).wait_recv()

        @pl.when(z < LAYERS - 1)
        def _():
            move_other(z, k, up_other, above).start()

        @pl.when(z > 0)
        def _():
            move_other(z, k, down_other, below).start()

    def run_hop(hop):
        def pass_on(i, _):
            k = count - 1 - i

            @pl.when(z >= hop)
            def _():
                layer = z - hop
                arrival(layer, y, k).wait_recv()

                @pl.when(z < LAYERS - 1)
                def _():
                    move(block(layer, y, k), layer, k, up_sem, above).start()

                @pl.when(k < late)
                def _():
                    move(block(layer, y, k), layer, k, side_sem, peer).start()

            @pl.when(z + hop < LAYERS)
            def _():
                layer = z + hop
                arrival(layer, y, k).wait_recv()

                @pl.when(z > 0)
                def _():
                    move(block(layer, y, k), layer, k, down_sem, below).start()

                @pl.when(k < late)
                def _():
                    move(block(layer, y, k), layer, k, side_sem, peer).start()

            return 0

        lax.fori_loop(0, count, pass_on, 0)
        for k in range(late, count):

            @pl.when(z >= hop)
            def _():
                layer = z - hop
                arrival(layer, 1 - y, k).wait_recv()

                @pl.when(z < LAYERS - 1)
                def _():
                    move_other(layer, k, up_other, above).start()

            @pl.when(z + hop < LAYERS)
            def _():
                layer = z + hop
                arrival(layer, 1 - y, k).wait_recv()

                @pl.when(z > 0)
                def _():
                    move_other(layer, k, down_other, below).start()

    run_hop(1)
    second.wait()
    cond = b2_ref[...]
    for i in range(ways):
        cond = cond + times(first_s_all[i], w2_ref[i * cols : (i + 1) * cols])
        row = lax.broadcasted_iota(jnp.int32, (batch, class_ref.shape[0]), 1)
        hot = (row == facts_all[i][:, 0:1].astype(jnp.int32)).astype(bf16)
        cond_ref[i * batch : (i + 1) * batch] = times(hot, class_ref[...])
    cond = cond + cond_ref[...]
    cond_ref[...] = cond
    signal = swish_unit(cond).astype(bf16)
    signal_ref[...] = signal
    mod = times(signal, fada_ref[...])
    signal = signal.astype(f32)
    for i in range(ways):
        signal_own[i] = signal[i * batch : (i + 1) * batch]
        mod_own[i] = mod[i * batch : (i + 1) * batch]
    third = [
        push(4, signal_own, signal_all, lambda to: to),
        push(5, mod_own, mod_land, lambda to: to),
    ]
    for p in third:
        p.start()
    run_hop(2)
    for p in third:
        p.wait()
    mod_ref[...] = jnp.sum(mod_land[...], axis=0)
    run_hop(3)

    def finish(k, _):
        pltpu.make_async_copy(packed.at[k], block(z, y, k), local_sem.at[k]).wait()
        for layer in range(LAYERS):

            @pl.when(k < late)
            def _():
                arrival(layer, 1 - y, k).wait_recv()

            @pl.when((k < late) | (layer == z))
            def _():
                move(block(layer, y, k), layer, k, side_sem, peer).wait_send()

            @pl.when((z < LAYERS - 1) & (layer <= z))
            def _():
                move(block(layer, y, k), layer, k, up_sem, above).wait_send()

            @pl.when((z > 0) & (layer >= z))
            def _():
                move(block(layer, y, k), layer, k, down_sem, below).wait_send()

        return 0

    lax.fori_loop(0, count, finish, 0)
    for k in range(late, count):
        for layer in range(LAYERS):

            @pl.when((z < LAYERS - 1) & (layer <= z))
            def _():
                move_other(layer, k, up_other, above).wait_send()

            @pl.when((z > 0) & (layer >= z))
            def _():
                move_other(layer, k, down_other, below).wait_send()


def head(blocks, time_freq, facts, shared, w1, w2, w_class, w_fada, b1, b2):
    ways, f32, bf16 = LAYERS * COLUMNS, jnp.float32, jnp.bfloat16
    count, side = blocks.shape[0], BLOCK_SIDE
    batch, cols, rows = time_freq.shape[0], shared.shape[0], time_freq.shape[0] * ways
    fada = w_fada.shape[1]
    dma = pltpu.SemaphoreType.DMA
    vmem, anywhere = pl.BlockSpec(memory_space=pltpu.VMEM), pl.BlockSpec(memory_space=pl.ANY)
    shape = jax.ShapeDtypeStruct
    return pl.pallas_call(
        head_body,
        in_specs=[vmem] * 10,
        out_specs=[anywhere] + [vmem] * 9,
        out_shape=[
            shape((count * ways, PACK_ROWS, LANES // 2), bf16),
            shape((rows, time_freq.shape[1]), f32),
            shape((ways,) + facts.shape, f32),
            shape((ways,) + shared.shape, bf16),
            shape((rows, cols), f32),
            shape((ways, rows, cols), bf16),
            shape((rows, cols), f32),
            shape((rows, cols), bf16),
            shape((ways, batch, cols), f32),
            shape((batch, fada), f32),
        ],
        scratch_shapes=[
            pltpu.VMEM((count, PACK_ROWS, LANES // 2), bf16),
            pltpu.VMEM((ways,) + time_freq.shape, f32),
            pltpu.VMEM((rows, cols), bf16),
            pltpu.VMEM((ways, batch, cols), f32),
            pltpu.VMEM((ways, batch, fada), f32),
            pltpu.VMEM((ways, batch, fada), f32),
            dma((count,)),
            dma((LAYERS, count)),
            dma((LAYERS, count)),
            dma((LAYERS, count)),
            dma((LAYERS, CROSS_LATE)),
            dma((LAYERS, CROSS_LATE)),
            dma((LAYERS, COLUMNS, count)),
            dma((6, ways)),
            dma((6, ways)),
        ],
        compiler_params=pltpu.CompilerParams(
            collective_id=0, has_side_effects=True, vmem_limit_bytes=48 * 2**20
        ),
        name="head",
    )(blocks, time_freq, facts, shared, w1, w2, w_class, w_fada, b1, b2)


def outer(a, b):
    return lax.dot_general(a, b, (((0,), (0,)), ((), ())), preferred_element_type=jnp.float32)


def tail_body(
    x_ref, fmod_ref, dsig_ref, small_ref, bias_ref, fada_ref, w2_ref, cond_ref, first_t_ref,
    signal_ref, first_s_ref, tf_ref, facts_ref,
    out_ref, g_cond_ref, g_head_ref, slice_ref, side_ref, mod_sum_ref, last_all,
    side_buf, up_buf, down_buf, other_buf, up_other, down_other, fmod_land, dsig_land, small_land,
    bias_land, dsig_all, first_own, first_land, small_own, small_mp, side_own, side_mp, fmod_all, last_own,
    hot_buf,
    side_send, line_send, side_recv, up_recv, down_recv, other_send, other_up, other_down,
    send_all, recv_all, send_dp, recv_dp, send_mp, recv_mp,
):
    f32, bf16 = jnp.float32, jnp.bfloat16
    count, ways, mp = out_ref.shape[0], LAYERS * COLUMNS, lax.axis_size("mp")
    batch, cols = dsig_ref.shape[1], dsig_ref.shape[2]
    everyone = ways * mp
    late = count - CROSS_LATE
    z, y = grid_place()
    my_dp, my_mp = lax.axis_index("dp"), lax.axis_index("mp")
    me = my_dp * mp + my_mp

    def place_all(i):
        return {"dp": i // mp, "mp": lax.rem(i, mp)}

    barrier = pltpu.get_barrier_semaphore()

    def greet(i, _):
        signal_to(barrier, place_all(lax.rem(me + i, everyone)))
        return 0

    lax.fori_loop(1, everyone, greet, 0)
    pl.semaphore_wait(barrier, everyone - 1)

    def push_all(j, source, landing, row=None):
        return Push(source, landing, send_all.at[j], recv_all.at[j], everyone, me, place_all, row)

    def push_dp(j, source, landing, row=None):
        return Push(
            source, landing, send_dp.at[j], recv_dp.at[j], ways, my_dp, lambda i: {"dp": i}, row
        )

    def push_mp(j, source, landing):
        return Push(source, landing, send_mp.at[j], recv_mp.at[j], mp, my_mp, lambda i: {"mp": i})

    first = [
        push_all(0, fmod_ref, fmod_land),
        push_all(1, dsig_ref, dsig_land, lambda to: to // mp),
    ]
    second = [push_dp(0, small_ref, small_land, lambda to: to), push_dp(1, bias_ref, bias_land)]
    for p in first + second:
        p.start()

    peer = {"dp": z * COLUMNS + 1 - y}
    above = {"dp": jnp.minimum(z + 1, LAYERS - 1) * COLUMNS + y}
    below = {"dp": jnp.maximum(z - 1, 0) * COLUMNS + y}

    def slot(layer, column, k):
        return (layer * COLUMNS + column) * count + k

    def across(layer, k):
        return remote(
            x_ref.at[slot(layer, 1 - y, k)],
            side_buf.at[layer, k],
            side_send.at[layer, k],
            side_recv.at[layer, k],
            peer,
        )

    def cross_late(k):
        return remote(
            other_buf.at[z, k - late],
            side_buf.at[z, k],
            side_send.at[z, k],
            side_recv.at[z, k],
            peer,
        )

    def upward(layer, k):
        return remote(
            side_buf.at[layer, k], up_buf.at[layer, k], line_send.at[layer, k], up_recv.at[layer, k], above
        )

    def downward(layer, k):
        return remote(
            side_buf.at[layer, k], down_buf.at[layer, k], line_send.at[layer, k], down_recv.at[layer, k], below
        )

    def upward_other(layer, k):
        j = k - late
        return remote(
            other_buf.at[layer, j], up_other.at[layer, j], other_send.at[layer, j], other_up.at[layer, j], above
        )

    def downward_other(layer, k):
        j = k - late
        return remote(
            other_buf.at[layer, j], down_other.at[layer, j], other_send.at[layer, j], other_down.at[layer, j], below
        )

    def own_part(layer, k):
        return x_ref[slot(layer, y, k)].astype(f32)

    def pair_sum(layer, k):
        across(layer, k).wait_recv()
        return own_part(layer, k) + side_buf[layer, k].astype(f32)

    for hop in range(LAYERS - 1, -1, -1):

        def begin(k, _):
            @pl.when(z + hop < LAYERS)
            def _():
                across(z + hop, k).start()

            if hop > 0:

                @pl.when(z >= hop)
                def _():
                    across(z - hop, k).start()

            return 0

        lax.fori_loop(0, late, begin, 0)

    def along(total, stage_ref, layer, k, copy, landed, begins):
        @pl.when(jnp.logical_not(begins))
        def _():
            copy(layer, k).wait_recv()
            stage_ref[...] = (total + landed[...].astype(f32)).astype(bf16)

        @pl.when(begins)
        def _():
            stage_ref[...] = total.astype(bf16)

        copy(layer, k).start()

    bottom, top = z == 0, z == LAYERS - 1

    def run_hop(hop):
        for k in range(late, count):
            j = k - late

            @pl.when(z + hop < LAYERS)
            def _():
                layer = z + hop
                along(
                    own_part(layer, k), side_buf.at[layer, k], layer, k, upward, up_buf.at[layer, k], bottom
                )
                along(
                    x_ref[slot(layer, 1 - y, k)].astype(f32),
                    other_buf.at[layer, j], layer, k, upward_other, up_other.at[layer, j], bottom,
                )

            @pl.when(z >= hop)
            def _():
                layer = z - hop
                along(
                    own_part(layer, k), side_buf.at[layer, k], layer, k, downward, down_buf.at[layer, k], top
                )
                along(
                    x_ref[slot(layer, 1 - y, k)].astype(f32),
                    other_buf.at[layer, j], layer, k, downward_other, down_other.at[layer, j], top,
                )

        def step(k, _):
            @pl.when(z + hop < LAYERS)
            def _():
                layer = z + hop
                along(
                    pair_sum(layer, k), side_buf.at[layer, k], layer, k, upward, up_buf.at[layer, k], bottom
                )

            @pl.when(z >= hop)
            def _():
                layer = z - hop
                along(
                    pair_sum(layer, k), side_buf.at[layer, k], layer, k, downward, down_buf.at[layer, k], top
                )

            return 0

        lax.fori_loop(0, late, step, 0)

    run_hop(3)

    for p in first:
        p.wait()
    for i in range(everyone):
        fmod_all[i : i + 1] = fmod_land[i]
    for i in range(ways):
        dsig_all[i * batch : (i + 1) * batch] = jnp.sum(dsig_land[i * mp : (i + 1) * mp], axis=0)
    d_fmod = fmod_all[...].astype(bf16)
    d_signal = dsig_all[...] + times_flipped(d_fmod, fada_ref[...])
    d_cond = d_signal * swish_slope(cond_ref[...])
    d_second = d_cond.astype(bf16)
    back = times_flipped(d_second, w2_ref[...])
    for i in range(ways):
        first_own[i] = back[:, i * cols : (i + 1) * cols]
    for p in second:
        p.wait()
    third = push_dp(2, first_own, first_land, lambda to: to)

    def square(x):
        return jnp.sum(jnp.sum(x * x, axis=1, keepdims=True), axis=0, keepdims=True)

    third.start()
    shared_squares = jnp.zeros((1, 1), f32)
    g_fada = outer(signal_ref[...], d_fmod)
    g_head_ref[:, : g_fada.shape[1]] = g_fada
    shared_squares += square(g_fada)
    mod_sum = column_sum(fmod_all[...])
    mod_sum_ref[...] = mod_sum
    t2_row = PATCH_VALUES + FREQ
    class_row = t2_row + MODEL_WIDTH
    for i in range(ways):
        g = outer(first_s_ref[i], d_second)
        g_cond_ref[t2_row + i * cols : t2_row + (i + 1) * cols] = g
        shared_squares += square(g)
    for i in range(ways):
        row = lax.broadcasted_iota(jnp.int32, (batch, hot_buf.shape[1]), 1)
        hot = (row == facts_ref[i][:, 0:1].astype(jnp.int32)).astype(f32)
        hot_buf[i * batch : (i + 1) * batch] = hot
    hot = hot_buf[...].astype(bf16)
    high = d_cond.astype(bf16)
    rest = d_cond - high.astype(f32)
    mid = rest.astype(bf16)
    low = (rest - mid.astype(f32)).astype(bf16)
    g_class = outer(hot, high) + outer(hot, mid) + outer(hot, low)
    g_cond_ref[class_row:] = g_class[:CLASSES]
    shared_squares += square(g_class)
    run_hop(2)
    third.wait()
    d_first = (jnp.sum(first_land[...], axis=0) * swish_slope(first_t_ref[...])).astype(bf16)
    g_first = outer(tf_ref[...].astype(bf16), d_first)
    g_cond_ref[PATCH_VALUES:t2_row] = g_first
    shared_squares += square(g_first)
    small_own[...] = jnp.sum(small_land[...], axis=0)
    bias = jnp.sum(bias_land[...], axis=0)
    slice_rows = slice_ref.shape[0]
    slice_ref[...] = bias[:slice_rows]
    slice_squares = square(bias[:slice_rows])
    side_own[...] = bias[slice_rows:]
    fourth = [push_mp(0, small_own, small_mp), push_mp(1, side_own, side_mp)]
    for p in fourth:
        p.start()
    run_hop(1)
    for p in fourth:
        p.wait()
    small = jnp.sum(small_mp[...], axis=0)
    g_cond_ref[:PATCH_VALUES] = small[:PATCH_VALUES]
    g_head_ref[:, g_head_ref.shape[1] - (small.shape[0] - PATCH_VALUES) :] = small[PATCH_VALUES:].T
    shared_squares += square(small)
    side = jnp.sum(side_mp[...], axis=0)
    side_ref[...] = side
    every_squares = square(side[: side.shape[0] - 8]) + square(mod_sum)
    column_sums = [column_sum(d_first.astype(f32)), column_sum(d_second.astype(f32))]
    for s in column_sums:
        shared_squares += square(s)
    squares = shared_squares / mp + slice_squares / ways + every_squares / (ways * mp)

    for k in range(late, count):
        j = k - late
        other_buf[z, j] = x_ref[slot(z, 1 - y, k)]

        @pl.when(z > 0)
        def _():
            upward_other(z, k).wait_recv()
            other_buf[z, j] = (other_buf[z, j].astype(f32) + up_other[z, j].astype(f32)).astype(bf16)

        @pl.when(z < LAYERS - 1)
        def _():
            downward_other(z, k).wait_recv()
            other_buf[z, j] = (other_buf[z, j].astype(f32) + down_other[z, j].astype(f32)).astype(bf16)

        cross_late(k).start()

    last_own[...] = jnp.zeros_like(last_own)

    def final(k, _):
        out_ref[k] = pair_sum(z, k)

        @pl.when(z > 0)
        def _():
            upward(z, k).wait_recv()
            out_ref[k] += up_buf[z, k].astype(f32)

        @pl.when(z < LAYERS - 1)
        def _():
            downward(z, k).wait_recv()
            out_ref[k] += down_buf[z, k].astype(f32)

        total = out_ref[k]
        last_own[2:3, :128] += column_sum(total * total)
        return 0

    lax.fori_loop(0, count, final, 0)
    squares += jnp.sum(last_own[2:3, :128], axis=1, keepdims=True)
    last_own[0:1, :cols] = column_sums[0]
    last_own[1:2, :cols] = column_sums[1]
    last_own[2:3, :128] = jnp.broadcast_to(squares, (1, 128))
    fifth = push_all(2, last_own, last_all)
    fifth.start()

    def sent(k, _):
        for layer in range(LAYERS):

            @pl.when(k < late)
            def _():
                across(layer, k).wait_send()

            @pl.when(layer > z)
            def _():
                upward(layer, k).wait_send()

            @pl.when(layer < z)
            def _():
                downward(layer, k).wait_send()

        return 0

    lax.fori_loop(0, count, sent, 0)
    for k in range(late, count):
        cross_late(k).wait_send()
        for layer in range(LAYERS):

            @pl.when(layer > z)
            def _():
                upward_other(layer, k).wait_send()

            @pl.when(layer < z)
            def _():
                downward_other(layer, k).wait_send()

    fifth.wait()


def tail(slots, d_fmod, d_signal, small, bias, w_fada, w2, cond, first_t, signal, first_s, tf, facts, slice_rows):
    ways, mp, f32, bf16 = LAYERS * COLUMNS, lax.axis_size("mp"), jnp.float32, jnp.bfloat16
    count, packed = slots.shape[0] // ways, slots.shape[1:]
    batch, cols = d_signal.shape[1:]
    rows, fada = batch * ways, w_fada.shape[1]
    side_rows = bias.shape[0] - slice_rows
    dma, vmem = pltpu.SemaphoreType.DMA, pl.BlockSpec(memory_space=pltpu.VMEM)
    shape, scratch = jax.ShapeDtypeStruct, pltpu.VMEM
    landing = scratch((LAYERS, count) + packed, bf16)
    few = scratch((LAYERS, CROSS_LATE) + packed, bf16)
    out_shape = [
        shape((count,) + packed, f32),
        shape((PATCH_VALUES + FREQ + MODEL_WIDTH + CLASSES, cols), f32),
        shape((cols, fada + small.shape[1] - PATCH_VALUES), f32),
        shape((slice_rows, 128), f32),
        shape((side_rows, 128), f32),
        shape((1, fada), f32),
        shape((ways * mp, 8, LANES), f32),
    ]
    return pl.pallas_call(
        tail_body,
        in_specs=[vmem] * 13,
        out_specs=[vmem] * len(out_shape),
        out_shape=out_shape,
        scratch_shapes=[landing] * 3
        + [few] * 3
        + [
            scratch((ways * mp, 1, fada), f32),
            scratch((ways * mp, batch, cols), f32),
            scratch(small.shape, f32),
            scratch((ways,) + bias.shape, f32),
            scratch((rows, cols), f32),
            scratch((ways, rows, cols), f32),
            scratch((ways, rows, cols), f32),
            scratch(small.shape[1:], f32),
            scratch((mp,) + small.shape[1:], f32),
            scratch((side_rows, 128), f32),
            scratch((mp, side_rows, 128), f32),
            scratch((rows, fada), f32),
            scratch((8, LANES), f32),
            scratch((rows, 1024), f32),
        ]
        + [dma((LAYERS, count))] * 5
        + [dma((LAYERS, CROSS_LATE))] * 3
        + [dma((3, ways * mp))] * 2
        + [dma((3, ways))] * 2
        + [dma((2, mp))] * 2,
        compiler_params=pltpu.CompilerParams(
            collective_id=1, has_side_effects=True, vmem_limit_bytes=58 * 2**20
        ),
        name="tail",
    )(slots, d_fmod, d_signal, small, bias, w_fada, w2, cond, first_t, signal, first_s, tf, facts)


def halves(x):
    high = x.astype(jnp.bfloat16)
    return high, (x - high.astype(jnp.float32)).astype(jnp.bfloat16)


def left_form(main, tail):
    mh, ml = halves(main)
    th, tl = halves(tail)
    return jnp.concatenate([mh, mh, ml, th, th, tl], axis=1)


def right_form(x):
    h, l = halves(x)
    return jnp.concatenate(
        [h[:LANES], l[:LANES], h[:LANES], h[LANES:], l[LANES:], h[LANES:]], axis=0
    )


def product(left, right):
    return jnp.dot(left, right, preferred_element_type=jnp.float32)


def symmetric_product(left, right_main, right_tail):
    main = product(left, right_main)
    corner = product(left[LANES:], right_tail)
    return main, jnp.concatenate([main[LANES:].T, corner], axis=0)


def inverse_roots(pairs, eye_main, eye_tail):
    contracted, scales = [], []
    for main, tail in pairs:
        trace = jnp.sum(main * eye_main) + jnp.sum(tail * eye_tail)
        shift = 0.0001 * trace / BLOCK_SIDE
        main = main + shift * eye_main
        tail = tail + shift * eye_tail
        square = jnp.sum(main * main, axis=(0, 1), keepdims=True) + jnp.sum(
            tail * tail, axis=(0, 1), keepdims=True
        )
        factor_z = 2.5 / jnp.sqrt(square)
        contracted.append((main * factor_z, tail * factor_z))
        scales.append(jnp.sqrt(jnp.sqrt(factor_z)))
    estimates = None
    for newton_step in range(NEWTON):
        more = newton_step < NEWTON - 1
        factors = [((5.0 * eye_main - m) * 0.25, (5.0 * eye_tail - t) * 0.25) for m, t in contracted]
        rights = [(right_form(m), right_form(t)) for m, t in factors]
        lefts = [left_form(m, t) for m, t in factors]
        if more:
            powers = [symmetric_product(l, *r) for l, r in zip(lefts, rights)]
        if estimates is None:
            estimates = [(m * s, t * s) for (m, t), s in zip(factors, scales)]
        else:
            estimates = [
                symmetric_product(left_form(*e), *r) for e, r in zip(estimates, rights)
            ]
        if more:
            powers = [
                symmetric_product(left_form(*q), right_form(q[0]), right_form(q[1])) for q in powers
            ]
            contracted = [
                symmetric_product(left_form(*q), right_form(m), right_form(t))
                for q, (m, t) in zip(powers, contracted)
            ]
    return estimates


def shampoo_body(clip_ref, g_ref, stat_ref, old_ref, clipped_ref, new_stat_ref, new_ref, low_ref):
    side = BLOCK_SIDE

    def unit(width, offset):
        row = lax.broadcasted_iota(jnp.int32, (side, width), 0)
        col = lax.broadcasted_iota(jnp.int32, (side, width), 1) + offset
        return (row == col).astype(jnp.float32)

    eye_main, eye_tail = unit(LANES, 0), unit(TAIL, LANES)
    pairs, g_rights = [], []
    for j in range(g_ref.shape[0]):
        g_main, g_tail = unpack(g_ref[j] * clip_ref[0])
        clipped_ref[j, :, :LANES] = g_main
        clipped_ref[j, :, LANES:] = g_tail
        flipped = jnp.concatenate([g_main, g_tail], axis=1).T
        g_right = (right_form(g_main), right_form(g_tail))
        f_right = (right_form(flipped[:, :LANES]), right_form(flipped[:, LANES:]))
        g_left = left_form(g_main, g_tail)
        f_left = left_form(flipped[:, :LANES], flipped[:, LANES:])
        g_rights.append(g_right)
        for k, (left, right) in enumerate(((g_left, f_right), (f_left, g_right))):
            main, tail = symmetric_product(left, *right)
            main = 0.5 * stat_ref[j, k, :, :LANES] + 0.5 * main
            tail = 0.5 * stat_ref[j, k, :, LANES:] + 0.5 * tail
            new_stat_ref[j, k, :, :LANES] = main
            new_stat_ref[j, k, :, LANES:] = tail
            pairs.append((main, tail))
    roots = inverse_roots(pairs, eye_main, eye_tail)
    for j, g_right in enumerate(g_rights):
        root_left = left_form(*roots[2 * j])
        half = left_form(product(root_left, g_right[0]), product(root_left, g_right[1]))
        for part, (a, b) in zip(roots[2 * j + 1], ((0, LANES), (LANES, side))):
            direction = product(half, right_form(part))
            old = old_ref[j, :, a:b]
            new = old - shampoo_rate * (direction + decay_rate * old)
            new_ref[j, :, a:b] = new
            low_ref[j, :, a:b] = new.astype(jnp.bfloat16)


def shampoo(clip_factor, gradients, stats, old_blocks):
    count, side = gradients.shape[0], BLOCK_SIDE
    group = next(g for g in (3, 2, 1) if count % g == 0)
    one = pl.BlockSpec((group, side, side), lambda i: (i, 0, 0))
    two = pl.BlockSpec((group, 2, side, side), lambda i: (i, 0, 0, 0))
    block = jax.ShapeDtypeStruct((count, side, side), jnp.float32)
    return pl.pallas_call(
        shampoo_body,
        grid=(count // group,),
        in_specs=[
            pl.BlockSpec(memory_space=pltpu.SMEM),
            pl.BlockSpec((group, PACK_ROWS, LANES // 2), lambda i: (i, 0, 0)),
            two,
            one,
        ],
        out_specs=[one, two, one, one],
        out_shape=[
            block,
            jax.ShapeDtypeStruct((count, 2, side, side), jnp.float32),
            block,
            jax.ShapeDtypeStruct((count, side, side), jnp.bfloat16),
        ],
        compiler_params=pltpu.CompilerParams(vmem_limit_bytes=60 * 2**20),
        cost_estimate=pl.CostEstimate(
            flops=count * 44 * 6 * side**3, bytes_accessed=count * 34 * side * side, transcendentals=0
        ),
        name="shampoo",
    )(clip_factor.reshape(1), gradients, stats, old_blocks)


def adam_update(weight, gradient, moment_one, second):
    moment_one = 0.5 * moment_one + 0.5 * gradient
    second = 0.5 * second + 0.5 * gradient * gradient
    correct = 1.0 - 0.5**STEP
    updated = weight - adam_rate * (
        moment_one / correct / (jnp.sqrt(second / correct) + 1e-08) + decay_rate * weight
    )
    return (moment_one, second, updated)


def per_device(
    latents,
    noise,
    timesteps,
    labels,
    loss_weights,
    slotted_block_weights,
    statistics,
    slot_of_block,
    cond_tables,
    head_tables,
    slice_bias,
    side_bias,
    cond_m,
    cond_v,
    head_m,
    head_v,
    slice_m,
    slice_v,
    side_m,
    side_v,
):
    bf16, f32 = jnp.bfloat16, jnp.float32
    width = MODEL_WIDTH
    mp, dp = lax.axis_size("mp"), lax.axis_size("dp")
    my_mp, my_dp = lax.axis_index("mp"), lax.axis_index("dp")
    query_width, ff_width, ada_width = HEADS * HD // mp, FF // mp, 6 * width // mp
    ada_column = 3 * query_width + ff_width
    row_blocks = width // BLOCK_SIDE
    col_blocks = (ada_column + ada_width) // BLOCK_SIDE
    out_blocks = (query_width + ff_width) // BLOCK_SIDE
    first_out = row_blocks * col_blocks
    t2_row = PATCH_VALUES + FREQ
    class_row = t2_row + width
    local_heads = query_width // HD
    score_scale = HD ** (-0.5)
    batch = latents.shape[0]
    own_n = batch // mp
    cols = cond_tables.shape[1]
    samples = batch * dp

    def own(x):
        return lax.dynamic_slice_in_dim(x, my_mp * own_n, own_n, 0)

    def my_cols(x):
        return lax.dynamic_slice_in_dim(x, my_dp * cols, cols, x.ndim - 1)

    def all_columns(x):
        return x.transpose(1, 0, 2).reshape(x.shape[1], -1)

    def by_columns(x):
        return x.reshape(x.shape[0], dp, cols).transpose(1, 0, 2)

    def share_rows(x):
        return lax.all_gather(x, "mp", axis=0, tiled=True)

    tuned = dp == COLUMNS * LAYERS
    cond_low, head_low = cond_tables.astype(bf16), head_tables.astype(bf16)
    w_first, w_second = cond_low[PATCH_VALUES:t2_row], cond_low[t2_row:class_row]
    w_class = jnp.pad(cond_low[class_row:], ((0, 1024 - CLASSES), (0, 0)))
    w_fada = head_low[:, : 2 * width]
    b_first = my_cols(side_bias[width : 2 * width])
    b_second = my_cols(side_bias[2 * width : 3 * width])
    time_freq = time_features(timesteps, FREQ).astype(bf16).astype(f32)
    facts = jnp.pad(jnp.stack([labels.astype(f32), loss_weights], 1), ((0, 0), (0, 126)))
    shared = jnp.concatenate([cond_low[:PATCH_VALUES].T, head_low[:, 2 * width :]], 1)
    if tuned:
        (
            blocks, time_freq, facts, shared, first_t, first_s, cond_vec, signal_cols, signal, final_mod,
        ) = head(
            slotted_block_weights[0], time_freq, facts, shared, w_first, w_second, w_class, w_fada,
            b_first[None], b_second[None],
        )
    else:
        blocks = lax.all_gather(pack_blocks(slotted_block_weights[0]), "dp", axis=0, tiled=True)
        time_freq, facts, shared = exchange(
            [(time_freq, "gather"), (facts, "gather"), (shared, "gather")], "dp", 2
        )
        time_freq = time_freq.reshape(samples, FREQ)
        first_t = dense(time_freq.astype(bf16), w_first) + b_first
        (first_s,) = exchange([(swish_unit(first_t).astype(bf16), "gather")], "dp", 3)
        labels_all = facts[:, :, 0].reshape(samples, 1).astype(jnp.int32)
        onehot = labels_all == jnp.arange(1024, dtype=jnp.int32)[None, :]
        cond_vec = (
            dense(all_columns(first_s), w_second) + b_second + dense(onehot.astype(bf16), w_class)
        )
        signal_cols = swish_unit(cond_vec).astype(bf16)
        signal, final_mod = exchange(
            [
                (signal_cols.astype(f32).reshape(dp, batch, cols), "scatter"),
                (dense(signal_cols, w_fada).reshape(dp, batch, 2 * width), "scatter"),
            ],
            "dp",
            4,
        )
        final_mod = jnp.sum(final_mod, 0)
    weight_total = jnp.sum(facts[:, :, 1])
    shared = shared.reshape(width, -1)
    w_patch, w_head = shared[:, :PATCH_VALUES].T, shared[:, PATCH_VALUES:]
    signal = all_columns(signal).astype(bf16)
    final_mod = own(final_mod + side_bias[5 * width : 7 * width])

    w_qkv, w_up, w_ada = assemble(
        blocks,
        slot_of_block,
        0,
        row_blocks,
        [3 * query_width // BLOCK_SIDE, ff_width // BLOCK_SIDE, ada_width // BLOCK_SIDE],
    )
    (w_o,) = assemble(blocks, slot_of_block, first_out, query_width // BLOCK_SIDE, [row_blocks])
    (w_down,) = assemble(
        blocks,
        slot_of_block,
        first_out + query_width // BLOCK_SIDE * row_blocks,
        ff_width // BLOCK_SIDE,
        [row_blocks],
    )
    own_bias = slice_bias[0]
    modul = lax.all_gather(
        dense(signal, w_ada) + own_bias[2 * query_width + ff_width :],
        "mp",
        axis=1,
        tiled=True,
    )
    own_modul = own(modul)

    def part(position):
        return modul[:, None, position * width : (position + 1) * width]

    def heads_of(inputs):
        return inputs.reshape(batch, -1, local_heads, HD)

    keep_rate, noise_rate, upper_log, lower_log, mean_gap = coefficients(timesteps)
    noisy = keep_rate[:, None, None, None] * latents + noise_rate[:, None, None, None] * noise
    patches = patchify(noisy).astype(bf16)
    seq_len = patches.shape[1]
    initial = (
        dense(patches, w_patch) + side_bias[:width] + position_embedding(LATENT_SIDE // 2, width)
    )
    normed_all, _ = layer_norm(initial)
    attn_in = (normed_all * (1.0 + part(1)) + part(0)).astype(bf16)
    start = own(initial)[0]
    own_patches = own(patches)
    target = patchify(own(noise))[0]

    projected = dense(attn_in, w_qkv)
    queries = heads_of((projected[..., :query_width] + own_bias[:query_width]).astype(bf16))
    keys = heads_of(projected[..., query_width : 2 * query_width].astype(bf16))
    values = heads_of(
        (projected[..., 2 * query_width :] + own_bias[query_width : 2 * query_width]).astype(bf16)
    )
    scores = (
        jnp.einsum("slhe,smhe->shlm", queries, keys, preferred_element_type=f32) * score_scale
    )
    row_peak = jnp.max(scores, -1, keepdims=True)
    shifted = jnp.exp(scores - row_peak)
    row_total = jnp.sum(shifted, -1, keepdims=True)
    probs = shifted / row_total
    log_total = row_peak + jnp.log(row_total)
    mixed = (
        jnp.einsum("shlm,smhe->slhe", probs.astype(bf16), values, preferred_element_type=f32)
        .reshape(batch, seq_len, query_width)
        .astype(bf16)
    )

    def rows_of(*rows):
        return jnp.concatenate([r.reshape(1, width) for r in rows], 0)

    shift1, scale1, gate1, shift2, scale2, gate2 = (own_modul[0, i * width : (i + 1) * width] for i in range(6))
    attn, middle, hidden, active, mlp_in = attention_out_stage(
        mixed,
        w_o,
        w_up,
        start,
        rows_of(side_bias[3 * width : 4 * width], gate1, scale2, shift2),
        own_bias[2 * query_width : 2 * query_width + ff_width].reshape(1, ff_width),
    )

    def halves_of(x):
        x = x.reshape(x.shape[:-1] + (4, 8))
        return x[..., :4].reshape(x.shape[:-2] + (16,)), x[..., 4:].reshape(x.shape[:-2] + (16,))

    w_pred, w_raw = halves_of(w_head)
    own_weight = own(loss_weights)
    loss_facts = [own(upper_log), own(lower_log), own(mean_gap), own_weight, own_weight / weight_total]
    d_final, head_in, d_pred, d_raw, sums_f, loss_part, d_hidden, up_sum, d_branch = loss_stage(
        active,
        w_down,
        hidden,
        middle,
        rows_of(side_bias[4 * width : 5 * width], gate2, final_mod[0, width:], final_mod[0, :width]),
        target,
        w_pred,
        w_raw,
        jnp.stack(halves_of(side_bias[7 * width :])),
        jnp.broadcast_to(jnp.stack(loss_facts), (5, 16)),
    )
    loss_part = jnp.sum(loss_part)
    d_fmod = sums_f[:2].reshape(1, 2 * width).astype(bf16)
    g_down = weight_grad(active, d_branch).astype(bf16)
    d_middle, sums_m, d_mixed, d_attn = middle_back_stage(
        d_hidden, w_up, w_o, middle, d_final, attn, rows_of(scale2, gate1)
    )
    g_up = weight_grad(mlp_in, d_hidden).astype(bf16)
    g_outp = weight_grad(mixed, d_attn).astype(bf16)
    d_mixed = heads_of(d_mixed)
    probs = jnp.exp(
        jnp.einsum("slhe,smhe->shlm", queries, keys, preferred_element_type=f32) * score_scale
        - log_total
    )
    d_values = jnp.einsum(
        "shlm,slhe->smhe", probs.astype(bf16), d_mixed, preferred_element_type=f32
    ).astype(bf16)
    d_probs = jnp.einsum("slhe,smhe->shlm", d_mixed, values, preferred_element_type=f32)
    d_scores = (probs * (d_probs - jnp.sum(d_probs * probs, -1, keepdims=True))).astype(bf16)
    d_query = (
        jnp.einsum("shlm,smhe->slhe", d_scores, keys, preferred_element_type=f32) * score_scale
    ).astype(bf16)
    d_keys = (
        jnp.einsum("shlm,slhe->smhe", d_scores, queries, preferred_element_type=f32) * score_scale
    ).astype(bf16)
    flat_q = d_query.reshape(batch, seq_len, query_width)
    flat_v = d_values.reshape(batch, seq_len, query_width)
    d_proj = jnp.concatenate([flat_q, d_keys.reshape(batch, seq_len, query_width), flat_v], 2)
    g_qkv = weight_grad(attn_in, d_proj).astype(bf16)
    d_start, sums_a = start_back_stage(d_proj, w_qkv, start, d_middle, scale1.reshape(1, width))
    d_mod_own = jnp.concatenate(
        [sums_a[0], sums_a[1], sums_m[2], sums_m[0], sums_m[1], sums_f[2]]
    ).reshape(1, 6 * width)
    d_modul = lax.dynamic_slice_in_dim(
        share_rows(d_mod_own.astype(bf16)), my_mp * ada_width, ada_width, 1
    )

    slot_grad = to_slots(
        [g_qkv, g_up], signal, d_modul, [g_outp, g_down], slot_of_block, slot_of_block.shape[0]
    )
    d_signal = by_columns(back_dense(d_modul, w_ada))

    def interleave(p, r):
        parts = [x.reshape(x.shape[:-1] + (4, 4)) for x in (p, r)]
        return jnp.concatenate(parts, -1).reshape(p.shape[:-1] + (32,))

    def lanes(x, rows):
        return jnp.pad(x, (0, rows * 128 - x.shape[0])).reshape(rows, 128)

    d_out = interleave(d_pred, d_raw)
    small = by_columns(
        jnp.concatenate([weight_grad(own_patches[0], d_start), weight_grad(d_out, head_in)], 0)
    )
    slice_part = jnp.concatenate([total_of(flat_q), total_of(flat_v), up_sum[0], total_of(d_modul)])
    side_part = jnp.concatenate([sums_a[2], sums_m[3], sums_f[3], total_of(d_out)])
    slice_rows, side_rows = (-(-x.shape[0] // 1024) * 8 for x in (slice_part, side_part))
    bias_part = jnp.concatenate(
        [lanes(slice_part, slice_rows), lanes(side_part, side_rows), lanes(loss_part[None], 8)], 0
    )
    if tuned:
        red_blocks, red_cond, red_head, red_slice, side_sum, side_mod, last = tail(
            slot_grad, d_fmod.astype(f32), d_signal, small, bias_part, w_fada, w_second, cond_vec,
            first_t, signal_cols, first_s, time_freq, facts, slice_rows,
        )
    else:
        red_blocks = lax.psum_scatter(slot_grad, "dp", scatter_dimension=0, tiled=True).astype(f32)
        d_fmod_all, d_signal = exchange(
            [(d_fmod.astype(f32), "gather"), (d_signal, "scatter")], EVERY, 5
        )
        d_fmod_all = d_fmod_all.reshape(samples, 2 * width).astype(bf16)
        d_signal = jnp.sum(d_signal.reshape(dp, mp, batch, cols), 1).reshape(samples, cols)
        d_signal = d_signal + back_dense(d_fmod_all, w_fada)
        d_cond = d_signal * swish_slope(cond_vec)
        d_second = d_cond.astype(bf16)
        d_first, small, bias_part = exchange(
            [
                (by_columns(back_dense(d_second, w_second)), "scatter"),
                (small, "scatter"),
                (bias_part, "gather"),
            ],
            "dp",
            6,
        )
        d_first = (jnp.sum(d_first, 0) * swish_slope(first_t)).astype(bf16)
        bias_part = jnp.sum(bias_part, 0)
        red_slice = bias_part[:slice_rows]
        small, side_sum = exchange(
            [(jnp.sum(small, 0), "gather"), (bias_part[slice_rows:], "gather")], "mp", 7
        )
        small, side_sum = jnp.sum(small, 0), jnp.sum(side_sum, 0)
        side_mod = total_of(d_fmod_all)
        g_class = jnp.einsum(
            "sc,sd->cd", onehot[:, :CLASSES].astype(f32), d_cond, precision=exact_precision_flag
        )
        red_cond = jnp.concatenate(
            [
                small[:PATCH_VALUES],
                weight_grad(time_freq.astype(bf16), d_first),
                weight_grad(all_columns(first_s), d_second),
                g_class,
            ],
            0,
        )
        red_head = jnp.concatenate([weight_grad(signal_cols, d_fmod_all), small[PATCH_VALUES:].T], 1)
        side_cols = jnp.stack([total_of(d_first), total_of(d_second)])
        local_squares = (
            jnp.sum(red_blocks * red_blocks)
            + (
                jnp.sum(red_cond * red_cond)
                + jnp.sum(red_head * red_head)
                + jnp.sum(side_cols * side_cols)
            )
            / mp
            + jnp.sum(red_slice * red_slice) / dp
            + (jnp.sum(side_sum[:-8] * side_sum[:-8]) + jnp.sum(side_mod * side_mod)) / (dp * mp)
        )
        last = jnp.pad(side_cols, ((0, 6), (0, LANES - cols)))
        last = jnp.where(jnp.arange(8)[:, None] == 2, local_squares, last)
        (last,) = exchange([(last, "gather")], EVERY, 8)
    grad_norm = jnp.sqrt(jnp.sum(last[:, 2, 0]))
    loss_sum = side_sum[side_rows, 0]
    side_sum = side_sum[:side_rows].reshape(-1)[: side_part.shape[0]]
    red_slice = red_slice.reshape(-1)[: slice_part.shape[0]]
    side_cols = last[:, :2, :cols].reshape(dp, mp, 2, cols)[:, 0].transpose(1, 0, 2).reshape(2 * width)
    red_side = jnp.concatenate(
        [
            side_sum[:width],
            side_cols,
            side_sum[width : 3 * width],
            side_mod.reshape(2 * width),
            side_sum[3 * width :],
        ]
    )
    clip_factor = 1.0 / jnp.maximum(grad_norm, 1.0)
    clipped, new_stats, new_blocks, new_low = shampoo(
        clip_factor, red_blocks, statistics[0], slotted_block_weights[0]
    )
    cond_one, cond_two, new_cond = adam_update(cond_tables, red_cond * clip_factor, cond_m, cond_v)
    head_one, head_two, new_head = adam_update(head_tables, red_head * clip_factor, head_m, head_v)
    slice_one, slice_two, new_slice = adam_update(
        slice_bias[0], red_slice * clip_factor, slice_m[0], slice_v[0]
    )
    side_one, side_two, new_side = adam_update(side_bias, red_side * clip_factor, side_m, side_v)
    return (
        loss_sum,
        weight_total,
        grad_norm,
        clipped[None],
        new_stats[None],
        new_blocks[None],
        new_low[None],
        cond_one,
        cond_two,
        new_cond,
        new_cond.astype(bf16),
        head_one,
        head_two,
        new_head,
        new_head.astype(bf16),
        slice_one[None],
        slice_two[None],
        new_slice[None],
        side_one,
        side_two,
        new_side,
    )


def solution(mesh):
    return jax.shard_map(
        per_device,
        mesh=mesh,
        in_specs=(
            P("dp", None, None, None),
            P("dp", None, None, None),
            P("dp"),
            P("dp"),
            P("dp"),
            P("mp", "dp", None, None),
            P("mp", "dp", None, None, None),
            P(),
            P(None, "dp"),
            P("dp", None),
            P("mp", None),
            P(),
            P(None, "dp"),
            P(None, "dp"),
            P("dp", None),
            P("dp", None),
            P("mp", None),
            P("mp", None),
            P(),
            P(),
        ),
        out_specs=(
            P(),
            P(),
            P(),
            P("mp", "dp", None, None),
            P("mp", "dp", None, None, None),
            P("mp", "dp", None, None),
            P("mp", "dp", None, None),
            P(None, "dp"),
            P(None, "dp"),
            P(None, "dp"),
            P(None, "dp"),
            P("dp", None),
            P("dp", None),
            P("dp", None),
            P("dp", None),
            P("mp", None),
            P("mp", None),
            P("mp", None),
            P(),
            P(),
            P(),
        ),
        check_vma=False,
    )
```

```python
import math

import jax
import jax.numpy as jnp
from jax import lax
from jax.experimental import pallas as pl
from jax.experimental.pallas import tpu as pltpu
from jax.sharding import PartitionSpec as P

MODEL_WIDTH = 1152
HEADS = 16
HD = 72
FF = 4608
FREQ = 256
CLASSES = 1001
LATENT_SIDE = 32
PATCH_VALUES = 16
BLOCK_SIDE = 288
NEWTON = 6
STEP = 5
LANES = 256
TAIL = BLOCK_SIDE - LANES


exact_precision_flag = lax.Precision.HIGHEST
shampoo_rate = 0.5
adam_rate = 0.05
decay_rate = 0.01


def dense(operand, weight):
    return jnp.dot(operand, weight, preferred_element_type=jnp.float32)


def back_dense(gradient, weight):
    return jnp.einsum("...j,ij->...i", gradient, weight, preferred_element_type=jnp.float32)


def weight_grad(operand, gradient):
    return jnp.einsum("...i,...j->ij", operand, gradient, preferred_element_type=jnp.float32)


def total_of(inputs):
    return jnp.sum(inputs.astype(jnp.float32), axis=tuple(range(inputs.ndim - 1)))


def swish_unit(inputs):
    return inputs / (1.0 + jnp.exp(-inputs))


def swish_slope(inputs):
    sigmoid = 1.0 / (1.0 + jnp.exp(-inputs))
    return sigmoid * (1.0 + inputs * (1.0 - sigmoid))


def tanh_gelu_activation(inputs):
    return (
        0.5
        * inputs
        * (1.0 + jnp.tanh(0.7978845608028654 * (inputs + 0.044715 * inputs * inputs * inputs)))
    )


def gelu_slope(inputs):
    inner = jnp.tanh(0.7978845608028654 * (inputs + 0.044715 * inputs * inputs * inputs))
    return 0.5 * (1.0 + inner) + 0.5 * inputs * (1.0 - inner * inner) * 0.7978845608028654 * (
        1.0 + 3.0 * 0.044715 * inputs * inputs
    )


def layer_norm(inputs):
    centred = inputs - jnp.mean(inputs, -1, keepdims=True)
    inv_std = lax.rsqrt(jnp.mean(centred * centred, -1, keepdims=True) + 1e-06)
    return (centred * inv_std, inv_std)


def norm_back(gradient, normed, inv_std):
    return inv_std * (
        gradient
        - jnp.mean(gradient, -1, keepdims=True)
        - normed * jnp.mean(gradient * normed, -1, keepdims=True)
    )


def coefficients(step_ids):
    grid = jnp.arange(1000).astype(jnp.float32)
    betas = 0.0001 + (0.02 - 0.0001) * grid / 999.0
    logs = jnp.log(1.0 - betas)[None, :]
    index = jnp.arange(1000, dtype=jnp.int32)[None, :]
    beta_t = 0.0001 + (0.02 - 0.0001) * step_ids.astype(jnp.float32) / 999.0
    cumul_t = jnp.exp(jnp.sum(jnp.where(index <= step_ids[:, None], logs, 0.0), 1))
    before_t = jnp.exp(jnp.sum(jnp.where(index < step_ids[:, None], logs, 0.0), 1))
    keep_rate = jnp.sqrt(cumul_t)
    noise_rate = jnp.sqrt(1.0 - cumul_t)
    upper_log = jnp.log(beta_t)
    lower_log = jnp.log(beta_t * (1.0 - before_t) / (1.0 - cumul_t))
    mean_gap = beta_t * jnp.sqrt(before_t) / (1.0 - cumul_t) * jnp.sqrt(1.0 / cumul_t - 1.0)
    return (keep_rate, noise_rate, upper_log, lower_log, mean_gap)


def time_features(step_ids, feat_width):
    half_width = feat_width // 2
    frequencies = jnp.exp(
        -math.log(10000.0) * jnp.arange(half_width).astype(jnp.float32) / half_width
    )
    phases = step_ids.astype(jnp.float32)[:, None] * frequencies[None, :]
    return jnp.concatenate([jnp.cos(phases), jnp.sin(phases)], 1)


def position_embedding(grid_side, feat_width):
    quarter = feat_width // 4
    omegas = jnp.exp(-math.log(10000.0) * jnp.arange(quarter).astype(jnp.float32) / quarter)
    coords = jnp.arange(grid_side).astype(jnp.float32)
    angles = coords[:, None] * omegas[None, :]
    waves = jnp.concatenate([jnp.sin(angles), jnp.cos(angles)], 1)
    half_width = feat_width // 2
    rows_part = jnp.broadcast_to(waves[:, None, :], (grid_side, grid_side, half_width))
    cols_part = jnp.broadcast_to(waves[None, :, :], (grid_side, grid_side, half_width))
    return jnp.concatenate([rows_part, cols_part], 2).reshape(grid_side * grid_side, feat_width)


def patchify(latent):
    samples_n, channels, height, breadth = latent.shape
    shaped = latent.reshape(samples_n, channels, height // 2, 2, breadth // 2, 2).transpose(
        0, 2, 4, 3, 5, 1
    )
    return shaped.reshape(samples_n, height // 2 * (breadth // 2), 4 * channels)


PACK_ROWS = 656
SPLIT = 1


def pack(x):
    quarter = BLOCK_SIDE // 4
    tail = x[:, LANES:].astype(jnp.float32)
    tail = jnp.concatenate([tail[i * quarter : (i + 1) * quarter] for i in range(4)], axis=1)
    fill = jnp.zeros((PACK_ROWS - 2 * BLOCK_SIDE - quarter, LANES // 2), jnp.float32)
    tail = jnp.concatenate([tail, fill], axis=0)
    half = LANES // 2
    return x[:, :half], x[:, half:LANES], tail.astype(x.dtype)


def unpack(x):
    side, quarter = BLOCK_SIDE, BLOCK_SIDE // 4
    tail = x[2 * side :].astype(jnp.float32)[:quarter]
    tail = jnp.concatenate([tail[:, i * TAIL : (i + 1) * TAIL] for i in range(4)], axis=0)
    main = jnp.concatenate([x[:side], x[side : 2 * side]], axis=1)
    return main, tail.astype(x.dtype)


def store_packed(ref, index, x):
    a, b, c = pack(x)
    side = BLOCK_SIDE
    ref[index + (slice(0, side),)] = a
    ref[index + (slice(side, 2 * side),)] = b
    ref[index + (slice(2 * side, PACK_ROWS),)] = c


def store_pieces(ref, first, x):
    rows = [part for part in pack(x)]
    size, at, piece = PACK_ROWS // SPLIT, 0, 0
    for part in rows:
        done = 0
        while done < part.shape[0]:
            step = min(size - at, part.shape[0] - done)
            ref[first + piece, at : at + step] = part[done : done + step]
            done, at = done + step, at + step
            if at == size:
                piece, at = piece + 1, 0


def pack_blocks(blocks):
    count, side = blocks.shape[0], BLOCK_SIDE

    def body(x_ref, out_ref):
        store_packed(out_ref, (0,), x_ref[0].astype(jnp.bfloat16))

    return pl.pallas_call(
        body,
        grid=(count,),
        in_specs=[pl.BlockSpec((1, side, side), lambda i: (i, 0, 0))],
        out_specs=pl.BlockSpec((1, PACK_ROWS, LANES // 2), lambda i: (i, 0, 0)),
        out_shape=jax.ShapeDtypeStruct((count, PACK_ROWS, LANES // 2), jnp.bfloat16),
        name="pack_blocks",
    )(blocks)


def remote(source, target, send, receive, place):
    return pltpu.make_async_remote_copy(
        src_ref=source,
        dst_ref=target,
        send_sem=send,
        recv_sem=receive,
        device_id=place,
        device_id_type=pl.DeviceIdType.MESH,
    )


def signal_to(semaphore, place):
    pl.semaphore_signal(semaphore, inc=1, device_id=place, device_id_type=pl.DeviceIdType.MESH)


COLUMNS = 2
LAYERS = 4


def grid_place():
    me = lax.axis_index("dp")
    return me // COLUMNS, me % COLUMNS


EVERY = ("dp", "mp")


def exchange(items, axes, number):
    mp, dp = lax.axis_size("mp"), lax.axis_size("dp")
    n = {"dp": dp, "mp": mp, EVERY: dp * mp}[axes]

    def place(i):
        return {"dp": i // mp, "mp": i % mp} if axes == EVERY else {axes: i}

    def row(i):
        return i // mp if axes == EVERY else i

    def body(*refs):
        m = len(items)
        sources, outs, send, receive = refs[:m], refs[m : 2 * m], refs[-2], refs[-1]
        me = lax.axis_index("dp") * mp + lax.axis_index("mp") if axes == EVERY else lax.axis_index(axes)
        barrier = pltpu.get_barrier_semaphore()

        def greet(i, _):
            signal_to(barrier, place(lax.rem(me + i, n)))
            return 0

        lax.fori_loop(1, n, greet, 0)
        pl.semaphore_wait(barrier, n - 1)

        def piece(j, to):
            return sources[j].at[row(to)] if items[j][1] == "scatter" else sources[j]

        def start(i, _):
            to = lax.rem(me + i, n)
            for j in range(m):
                remote(piece(j, to), outs[j].at[me], send.at[j, i], receive.at[j, me], place(to)).start()
            return 0

        lax.fori_loop(1, n, start, 0)
        for j in range(m):
            outs[j][me] = sources[j][row(me)] if items[j][1] == "scatter" else sources[j][...]

        def finish(i, _):
            to = lax.rem(me + i, n)
            for j in range(m):
                copy = remote(piece(j, to), outs[j].at[to], send.at[j, i], receive.at[j, to], place(to))
                copy.wait_recv()
                copy.wait_send()
            return 0

        lax.fori_loop(1, n, finish, 0)

    arrays = [a for a, _ in items]
    shapes = [
        jax.ShapeDtypeStruct((n,) + (a.shape[1:] if kind == "scatter" else a.shape), a.dtype)
        for a, kind in items
    ]
    vmem = pl.BlockSpec(memory_space=pltpu.VMEM)
    return pl.pallas_call(
        body,
        in_specs=[vmem] * len(arrays),
        out_specs=[vmem] * len(arrays),
        out_shape=shapes,
        scratch_shapes=[pltpu.SemaphoreType.DMA((len(arrays), n))] * 2,
        compiler_params=pltpu.CompilerParams(
            collective_id=number, has_side_effects=True, vmem_limit_bytes=40 * 2**20
        ),
        name=f"exchange_{number}",
    )(*arrays)


def assemble(blocks, slots, first, rows, widths):
    side, cols = BLOCK_SIDE, sum(widths)

    def body(ids, *refs):
        base = 0
        for out, width in zip(refs[cols:], widths):
            parts = [part for r in refs[base : base + width] for part in unpack(r[0])]
            out[...] = jnp.concatenate(parts, axis=1)
            base += width

    def spec(c):
        return pl.BlockSpec(
            (1, PACK_ROWS, LANES // 2), lambda r, ids: (ids[first + r * cols + c], 0, 0)
        )

    return pl.pallas_call(
        body,
        grid_spec=pltpu.PrefetchScalarGridSpec(
            num_scalar_prefetch=1,
            grid=(rows,),
            in_specs=[spec(c) for c in range(cols)],
            out_specs=[pl.BlockSpec((side, side * w), lambda r, ids: (r, 0)) for w in widths],
        ),
        out_shape=[jax.ShapeDtypeStruct((rows * side, w * side), jnp.bfloat16) for w in widths],
        compiler_params=pltpu.CompilerParams(vmem_limit_bytes=40 * 2**20),
        cost_estimate=pl.CostEstimate(
            flops=0, bytes_accessed=4 * rows * cols * side * side, transcendentals=0
        ),
        name="assemble",
    )(slots, *([blocks] * cols))


def to_slots(inner, signal, d_modul, lower, slots, total):
    side = BLOCK_SIDE
    ri, widths = inner[0].shape[0] // side, [g.shape[1] // side for g in inner]
    wide = d_modul.shape[1] // side
    ci, co = sum(widths) + wide, lower[0].shape[1] // side
    heights = [g.shape[0] // side for g in lower]
    ro = sum(heights)
    steps = ri + ro
    n = len(inner) + 2 + len(lower)
    batch = signal.shape[0]
    signal = signal.reshape(batch, ri, side).transpose(1, 0, 2)

    def body(ids, *refs):
        sources, (out, buf, sem) = refs[:n], refs[-3:]
        s = pl.program_id(0)
        half = lax.rem(s, 2)

        def drain(which, count):
            for c in range(count):
                pltpu.make_async_copy(buf.at[which, c], out.at[0], sem.at[which, c]).wait()

        def send(source, count, base, first=0):
            for c in range(count):
                store_packed(buf, (half, first + c), source[:, c * side : (c + 1) * side])
                pltpu.make_async_copy(
                    buf.at[half, first + c], out.at[ids[base + c]], sem.at[half, first + c]
                ).start()

        @pl.when(jnp.logical_and(s >= 2, s - 2 < ri))
        def _():
            drain(half, ci)

        @pl.when(s - 2 >= ri)
        def _():
            drain(half, co)

        @pl.when(s < ri)
        def _():
            first = 0
            for source, width in zip(sources, widths):
                send(source, width, s * ci + first, first)
                first += width
            send(outer(refs[len(inner)][0], refs[len(inner) + 1][...]).astype(jnp.bfloat16), wide, s * ci + first, first)

        base = ri
        for source, height in zip(sources[len(inner) + 2 :], heights):

            @pl.when(jnp.logical_and(s >= base, s < base + height))
            def _():
                send(source, co, ri * ci + (s - ri) * co)

            base += height

        @pl.when(s == steps - 1)
        def _():
            drain(1 - half, co)
            drain(half, co)

    extra, aliases = [], {}
    if total != ri * ci + ro * co:
        extra = [jnp.zeros((total, PACK_ROWS, LANES // 2), jnp.bfloat16)]
        aliases = {1 + n: 0}
    specs = [
        pl.BlockSpec((side, w * side), lambda s, ids: (jnp.minimum(s, ri - 1), 0)) for w in widths
    ]
    specs += [
        pl.BlockSpec((1, batch, side), lambda s, ids: (jnp.minimum(s, ri - 1), 0, 0)),
        pl.BlockSpec(d_modul.shape, lambda s, ids: (0, 0)),
    ]
    base = ri
    for height in heights:
        specs.append(
            pl.BlockSpec(
                (side, co * side),
                lambda s, ids, base=base, height=height: (jnp.clip(s - base, 0, height - 1), 0),
            )
        )
        base += height
    return pl.pallas_call(
        body,
        grid_spec=pltpu.PrefetchScalarGridSpec(
            num_scalar_prefetch=1,
            grid=(steps,),
            in_specs=specs + [pl.BlockSpec(memory_space=pl.ANY)] * len(extra),
            out_specs=pl.BlockSpec(memory_space=pl.ANY),
            scratch_shapes=[
                pltpu.VMEM((2, max(ci, co), PACK_ROWS, LANES // 2), jnp.bfloat16),
                pltpu.SemaphoreType.DMA((2, max(ci, co))),
            ],
        ),
        out_shape=jax.ShapeDtypeStruct((total, PACK_ROWS, LANES // 2), jnp.bfloat16),
        compiler_params=pltpu.CompilerParams(vmem_limit_bytes=40 * 2**20),
        cost_estimate=pl.CostEstimate(
            flops=0, bytes_accessed=4 * (ri * ci + ro * co) * side * side, transcendentals=0
        ),
        input_output_aliases=aliases,
        name="to_slots",
    )(slots, *inner, signal, d_modul, *lower, *extra)


CHUNK = 64


def mean_of(x):
    return jnp.sum(x, axis=-1, keepdims=True) * (1.0 / x.shape[-1])


def norm_rows(x):
    centred = x - mean_of(x)
    inv_std = lax.rsqrt(mean_of(centred * centred) + 1e-06)
    return centred * inv_std, inv_std


def norm_rows_back(gradient, normed, inv_std):
    return inv_std * (gradient - mean_of(gradient) - normed * mean_of(gradient * normed))


def column_sum(x):
    return jnp.sum(x, axis=0, keepdims=True)


def times(a, b):
    return jnp.dot(a, b, preferred_element_type=jnp.float32)


def times_flipped(a, b):
    return lax.dot_general(a, b, (((1,), (1,)), ((), ())), preferred_element_type=jnp.float32)


def stage(number, inputs, outputs, shared, make):
    rows, width = inputs[0].shape[1], MODEL_WIDTH
    pieces = rows // CHUNK
    n_in, n_out = len(inputs), len(outputs)

    def body(*refs):
        ins, outs = refs[:n_in], refs[n_in : n_in + n_out]
        rest = refs[n_in + n_out :]
        share = None
        if shared:
            share, rest = rest[0], rest[1:]
        a_out, a_in, b_out, b_in, c_out, c_in, total, near, far = rest
        me = lax.axis_index("mp")
        core = me + 1 - 2 * lax.rem(me, 2)
        across = lax.rem(me + 2, 4)
        other = lax.rem(core + 2, 4)
        to_core, to_across = {"mp": core}, {"mp": across}
        partial, own, after = make(ins, outs, share)
        barrier = pltpu.get_barrier_semaphore()
        signal_to(barrier, to_core)
        signal_to(barrier, to_across)
        pl.semaphore_wait(barrier, 2)

        copy_a = remote(a_out, a_in, near.at[0, 0], near.at[1, 0], to_core)
        copy_c = remote(c_out, c_in, near.at[0, 1], near.at[1, 1], to_core)

        def piece(i):
            return pl.ds(i * CHUNK, CHUNK)

        def copy_b(i):
            return remote(
                b_out.at[piece(i)], b_in.at[piece(i)], far.at[0, i], far.at[1, i], to_across
            )

        def share_far(group, i):
            part = share.at[group, piece(i)]
            return remote(part, part, far.at[2, i], far.at[3, i], to_across)

        def share_near(group, i):
            part = share.at[group, piece(i)]
            return remote(part, part, near.at[2, i], near.at[3, i], to_core)

        def pass_near(group, i):
            part = share.at[group, piece(i)]
            return remote(part, part, near.at[4, i], near.at[5, i], to_core)

        a_out[...] = partial(other).astype(jnp.bfloat16)
        copy_a.start()
        total[...] = partial(across)
        copy_a.wait_recv()
        for i in range(pieces):
            at = piece(i)
            b_out[at] = (total[at] + a_in[at].astype(jnp.float32)).astype(jnp.bfloat16)
            copy_b(i).start()
        c_out[...] = partial(core).astype(jnp.bfloat16)
        copy_c.start()
        total[...] = partial(me)
        copy_c.wait_recv()
        for i in range(pieces):
            at = piece(i)
            copy_b(i).wait_recv()
            result = own(
                i * CHUNK, total[at] + c_in[at].astype(jnp.float32) + b_in[at].astype(jnp.float32)
            )
            if shared:
                share[me, at] = result
                share_far(me, i).start()
                share_near(me, i).start()
        if shared:
            after(me)
            for i in range(pieces):
                share_near(core, i).wait_recv()
            after(core)
            for i in range(pieces):
                share_far(across, i).wait_recv()
                pass_near(across, i).start()
            after(across)
            for i in range(pieces):
                pass_near(other, i).wait_recv()
            after(other)
        copy_a.wait_send()
        copy_c.wait_send()
        for i in range(pieces):
            copy_b(i).wait_send()
            if shared:
                share_far(me, i).wait_send()
                share_near(me, i).wait_send()
                pass_near(across, i).wait_send()

    vmem = pl.BlockSpec(memory_space=pltpu.VMEM)
    out_shape = [jax.ShapeDtypeStruct(shape, dtype) for shape, dtype in outputs]
    if shared:
        out_shape.append(jax.ShapeDtypeStruct((4, rows, width), jnp.bfloat16))
    landing = pltpu.VMEM((rows, width), jnp.bfloat16)
    return pl.pallas_call(
        body,
        in_specs=[vmem] * n_in,
        out_specs=[vmem] * len(out_shape),
        out_shape=out_shape,
        scratch_shapes=[landing] * 6
        + [
            pltpu.VMEM((rows, width), jnp.float32),
            pltpu.SemaphoreType.DMA((6, max(pieces, 2))),
            pltpu.SemaphoreType.DMA((4, pieces)),
        ],
        compiler_params=pltpu.CompilerParams(
            collective_id=number, has_side_effects=True, vmem_limit_bytes=56 * 2**20
        ),
        name=f"stage_{number}",
    )(*inputs)


def attention_out_stage(mixed, w_o, w_up, start, rows, up_bias):
    n, width, f32 = mixed.shape[1], MODEL_WIDTH, jnp.float32

    def make(ins, outs, share):
        mixed_ref, w_o_ref, w_up_ref, start_ref, rows_ref, up_ref = ins
        attn_ref, middle_ref, hidden_ref, active_ref = outs

        def partial(group):
            return times(mixed_ref[group], w_o_ref[...])

        def own(at, total):
            at = slice(at, at + CHUNK)
            attn = total + rows_ref[0:1]
            middle = start_ref[at] + rows_ref[1:2] * attn
            attn_ref[at] = attn
            middle_ref[at] = middle
            normed, _ = norm_rows(middle)
            return (normed * (1.0 + rows_ref[2:3]) + rows_ref[3:4]).astype(jnp.bfloat16)

        def after(group):
            for at in range(0, n, CHUNK):
                at = slice(at, at + CHUNK)
                hidden = times(share[group, at], w_up_ref[...]) + up_ref[...]
                hidden_ref[group, at] = hidden
                active_ref[group, at] = tanh_gelu_activation(hidden).astype(jnp.bfloat16)

        return partial, own, after

    inner = w_up.shape[1]
    return stage(
        9,
        [mixed, w_o, w_up, start, rows, up_bias],
        [((n, width), f32), ((n, width), f32), ((4, n, inner), f32), ((4, n, inner), jnp.bfloat16)],
        True,
        make,
    )


def loss_stage(active, w_down, hidden, middle, rows, target, w_pred, w_raw, head_bias, facts):
    n, width, f32, bf16 = active.shape[1], MODEL_WIDTH, jnp.float32, jnp.bfloat16
    inner = active.shape[2]

    def make(ins, outs, share):
        active_ref, w_ref, hidden_ref, middle_ref, rows_ref, target_ref, wp_ref, wr_ref, bias_ref, facts_ref = ins
        d_final_ref, head_in_ref, d_pred_ref, d_raw_ref, sums_ref, loss_ref, d_hidden_ref, up_sum_ref = outs
        sums_ref[...] = jnp.zeros_like(sums_ref)
        loss_ref[...] = jnp.zeros_like(loss_ref)
        up_sum_ref[...] = jnp.zeros_like(up_sum_ref)

        def partial(group):
            return times(active_ref[group], w_ref[...])

        def own(at, total):
            at = slice(at, at + CHUNK)
            branch = total + rows_ref[0:1]
            gate, fscale = rows_ref[1:2], 1.0 + rows_ref[2:3]
            normed, inv_std = norm_rows(middle_ref[at] + gate * branch)
            head_in = (normed * fscale + rows_ref[3:4]).astype(bf16)
            head_in_ref[at] = head_in
            upper, lower, gap = facts_ref[0:1], facts_ref[1:2], facts_ref[2:3]
            weight, share_of = facts_ref[3:4], facts_ref[4:5]
            error = times(head_in, wp_ref[...]) + bias_ref[0:1] - target_ref[at]
            fraction = (times(head_in, wr_ref[...]) + bias_ref[1:2] + 1.0) / 2.0
            log_var = fraction * upper + (1.0 - fraction) * lower
            gap = gap * error
            ratio = jnp.exp(lower - log_var)
            spread = gap * gap * jnp.exp(-log_var)
            diverge = 0.5 * (-1.0 + log_var - lower + ratio + spread)
            cells = 1.0 / (n * error.shape[1])
            per_bit = cells / math.log(2.0)
            loss_ref[...] += weight * column_sum(error * error * cells + diverge * per_bit)
            d_pred = (share_of * (2.0 * cells) * error).astype(bf16)
            d_raw = (
                share_of * per_bit * 0.25 * (upper - lower) * (1.0 - ratio - spread)
            ).astype(bf16)
            d_pred_ref[at] = d_pred
            d_raw_ref[at] = d_raw
            d_head = times_flipped(d_pred, wp_ref[...]) + times_flipped(d_raw, wr_ref[...])
            d_final = norm_rows_back(d_head * fscale, normed, inv_std)
            d_final_ref[at] = d_final
            d_branch = (gate * d_final).astype(bf16)
            sums_ref[0:1] += column_sum(d_head)
            sums_ref[1:2] += column_sum(d_head * normed)
            sums_ref[2:3] += column_sum(d_final * branch)
            sums_ref[3:4] += column_sum(d_branch.astype(f32))
            return d_branch

        def after(group):
            for at in range(0, n, CHUNK):
                at = slice(at, at + CHUNK)
                d_active = times_flipped(share[group, at], w_ref[...])
                d_hidden = (d_active * gelu_slope(hidden_ref[group, at])).astype(bf16)
                d_hidden_ref[group, at] = d_hidden
                up_sum_ref[...] += column_sum(d_hidden.astype(f32))

        return partial, own, after

    half = w_pred.shape[1]
    return stage(
        10,
        [active, w_down, hidden, middle, rows, target, w_pred, w_raw, head_bias, facts],
        [
            ((n, width), f32),
            ((n, width), bf16),
            ((n, half), bf16),
            ((n, half), bf16),
            ((4, width), f32),
            ((1, half), f32),
            ((4, n, inner), bf16),
            ((1, inner), f32),
        ],
        True,
        make,
    )


def middle_back_stage(d_hidden, w_up, w_o, middle, d_final, attn, rows):
    n, width, f32, bf16 = d_hidden.shape[1], MODEL_WIDTH, jnp.float32, jnp.bfloat16

    def make(ins, outs, share):
        d_hidden_ref, w_up_ref, w_o_ref, middle_ref, d_final_ref, attn_ref, rows_ref = ins
        d_middle_ref, sums_ref, d_mixed_ref = outs
        sums_ref[...] = jnp.zeros_like(sums_ref)

        def partial(group):
            return times_flipped(d_hidden_ref[group], w_up_ref[...])

        def own(at, total):
            at = slice(at, at + CHUNK)
            normed, inv_std = norm_rows(middle_ref[at])
            d_middle = d_final_ref[at] + norm_rows_back(total * (1.0 + rows_ref[0:1]), normed, inv_std)
            d_middle_ref[at] = d_middle
            d_attn = (rows_ref[1:2] * d_middle).astype(bf16)
            sums_ref[0:1] += column_sum(total)
            sums_ref[1:2] += column_sum(total * normed)
            sums_ref[2:3] += column_sum(d_middle * attn_ref[at])
            sums_ref[3:4] += column_sum(d_attn.astype(f32))
            return d_attn

        def after(group):
            d_mixed_ref[group] = times_flipped(share[group], w_o_ref[...]).astype(bf16)

        return partial, own, after

    return stage(
        11,
        [d_hidden, w_up, w_o, middle, d_final, attn, rows],
        [((n, width), f32), ((4, width), f32), ((4, n, w_o.shape[0]), bf16)],
        True,
        make,
    )


def start_back_stage(d_proj, w_qkv, start, d_middle, rows):
    n, width, f32, bf16 = d_proj.shape[1], MODEL_WIDTH, jnp.float32, jnp.bfloat16

    def make(ins, outs, share):
        d_proj_ref, w_ref, start_ref, d_middle_ref, rows_ref = ins
        d_start_ref, sums_ref = outs
        sums_ref[...] = jnp.zeros_like(sums_ref)

        def partial(group):
            return times_flipped(d_proj_ref[group], w_ref[...])

        def own(at, total):
            at = slice(at, at + CHUNK)
            normed, inv_std = norm_rows(start_ref[at])
            d_start = d_middle_ref[at] + norm_rows_back(total * (1.0 + rows_ref[0:1]), normed, inv_std)
            d_start = d_start.astype(bf16)
            d_start_ref[at] = d_start
            sums_ref[0:1] += column_sum(total)
            sums_ref[1:2] += column_sum(total * normed)
            sums_ref[2:3] += column_sum(d_start.astype(f32))

        return partial, own, None

    return stage(
        12,
        [d_proj, w_qkv, start, d_middle, rows],
        [((n, width), bf16), ((3, width), f32)],
        False,
        make,
    )


AHEAD = 4
CROSS_LATE = 1


class Push:
    def __init__(self, source, landing, send, receive, n, me, place, row=None):
        self.source, self.landing, self.send, self.receive = source, landing, send, receive
        self.n, self.me, self.place, self.row = n, me, place, row

    def _copy(self, i, sender, to):
        source = self.source if self.row is None else self.source.at[self.row(to)]
        return remote(
            source, self.landing.at[sender], self.send.at[i], self.receive.at[sender], self.place(to)
        )

    def start(self):
        def one(i, _):
            self._copy(i, self.me, lax.rem(self.me + i, self.n)).start()
            return 0

        lax.fori_loop(1, self.n, one, 0)
        own = self.source[...] if self.row is None else self.source[self.row(self.me)]
        self.landing[self.me] = own

    def wait(self):
        def one(i, _):
            to = lax.rem(self.me + i, self.n)
            copy = self._copy(i, to, to)
            copy.wait_recv()
            copy.wait_send()
            return 0

        lax.fori_loop(1, self.n, one, 0)


def in_parts(first, last, step, between):
    for at, work in between:
        lax.fori_loop(first, at, step, 0)
        work()
        first = at
    lax.fori_loop(first, last, step, 0)


def head_body(
    x_ref, tf_ref, facts_ref, shared_ref, tables_ref, fada_ref, b1_ref, b2_ref,
    out_ref, tf_all, facts_all, shared_all, first_t_ref, first_s_ref, cond_ref, signal_ref,
    signal_all, mod_ref,
    packed, tf_land, hot_buf, first_s, first_s_all, signal_own, mod_own, mod_land, local_sem, up_sem, down_sem, side_sem,
    up_other, down_other, recv_sem, send, receive,
):
    count, ways, f32, bf16 = packed.shape[0], LAYERS * COLUMNS, jnp.float32, jnp.bfloat16
    batch, cols = mod_ref.shape[0], tables_ref.shape[0]
    late = count - CROSS_LATE
    z, y = grid_place()
    me = lax.axis_index("dp")

    def place(i):
        return {"dp": i}

    barrier = pltpu.get_barrier_semaphore()

    def greet(i, _):
        signal_to(barrier, place(lax.rem(me + i, ways)))
        return 0

    lax.fori_loop(1, ways, greet, 0)
    pl.semaphore_wait(barrier, ways - 1)

    def push(j, source, landing, row=None):
        return Push(source, landing, send.at[j], receive.at[j], ways, me, place, row)

    first = [
        push(0, tf_ref, tf_land),
        push(1, facts_ref, facts_all),
        push(2, shared_ref, shared_all),
    ]
    for p in first:
        p.start()

    peer = {"dp": z * COLUMNS + 1 - y}
    above = {"dp": jnp.minimum(z + 1, LAYERS - 1) * COLUMNS + y}
    below = {"dp": jnp.maximum(z - 1, 0) * COLUMNS + y}

    def block(layer, column, k):
        return out_ref.at[(layer * COLUMNS + column) * count + k]

    def move(source, layer, k, sem, to):
        return remote(source, block(layer, y, k), sem.at[layer, k], recv_sem.at[layer, y, k], to)

    def move_other(layer, k, sem, to):
        here = block(layer, 1 - y, k)
        return remote(here, here, sem.at[layer, k - late], recv_sem.at[layer, 1 - y, k], to)

    def arrival(layer, column, k):
        here = block(layer, column, k)
        return remote(here, here, side_sem.at[0, 0], recv_sem.at[layer, column, k], peer)

    def send_own(i, _):
        base = count - SPLIT * (i + 1)
        store_pieces(packed, base, x_ref[x_ref.shape[0] - 1 - i].astype(bf16))
        for j in range(SPLIT - 1, -1, -1):
            k = base + j
            own = packed.at[k]
            move(own, z, k, side_sem, peer).start()

            @pl.when(z < LAYERS - 1)
            def _():
                move(own, z, k, up_sem, above).start()

            @pl.when(z > 0)
            def _():
                move(own, z, k, down_sem, below).start()

            pltpu.make_async_copy(own, block(z, y, k), local_sem.at[k]).start()
        return 0

    def pass_own(k):
        arrival(z, 1 - y, k).wait_recv()

        @pl.when(z < LAYERS - 1)
        def _():
            move_other(z, k, up_other, above).start()

        @pl.when(z > 0)
        def _():
            move_other(z, k, down_other, below).start()

    def run_hop(hop):
        def pass_on(i, _):
            k = count - 1 - i

            @pl.when(z >= hop)
            def _():
                layer = z - hop
                arrival(layer, y, k).wait_recv()

                @pl.when(z < LAYERS - 1)
                def _():
                    move(block(layer, y, k), layer, k, up_sem, above).start()

                @pl.when(k < late)
                def _():
                    move(block(layer, y, k), layer, k, side_sem, peer).start()

            @pl.when(z + hop < LAYERS)
            def _():
                layer = z + hop
                arrival(layer, y, k).wait_recv()

                @pl.when(z > 0)
                def _():
                    move(block(layer, y, k), layer, k, down_sem, below).start()

                @pl.when(k < late)
                def _():
                    move(block(layer, y, k), layer, k, side_sem, peer).start()

            return 0

        lax.fori_loop(0, count, pass_on, 0)
        for k in range(late, count):

            @pl.when(z >= hop)
            def _():
                layer = z - hop
                arrival(layer, 1 - y, k).wait_recv()

                @pl.when(z < LAYERS - 1)
                def _():
                    move_other(layer, k, up_other, above).start()

            @pl.when(z + hop < LAYERS)
            def _():
                layer = z + hop
                arrival(layer, 1 - y, k).wait_recv()

                @pl.when(z > 0)
                def _():
                    move_other(layer, k, down_other, below).start()

    t2_row = PATCH_VALUES + FREQ
    class_row = t2_row + MODEL_WIDTH
    second = push(3, first_s, first_s_all)
    third = [
        push(4, signal_own, signal_all, lambda to: to),
        push(5, mod_own, mod_land, lambda to: to),
    ]

    def first_row():
        for p in first:
            p.wait()
        for i in range(ways):
            tf_all[i * batch : (i + 1) * batch] = tf_land[i][:batch]
        first_t = times_flipped(tf_all[...].astype(bf16), tables_ref[:, PATCH_VALUES:t2_row]) + b1_ref[...]
        first_t_ref[...] = first_t
        first_s[:, :cols] = swish_unit(first_t).astype(bf16)
        second.start()

    def class_part():
        for i in range(ways):
            row = lax.broadcasted_iota(jnp.int32, (batch, CLASSES), 1)
            hot = (row == facts_all[i][:batch, 0:1].astype(jnp.int32)).astype(f32)
            hot_buf[i * batch : (i + 1) * batch] = hot
        cond_ref[...] = (
            times_flipped(hot_buf[...].astype(bf16), tables_ref[:, class_row:]) + b2_ref[...]
        )

    def second_row():
        second.wait()
        first_s_ref[...] = jnp.concatenate([first_s_all[i][:, :cols] for i in range(ways)], axis=1)
        cond = cond_ref[...] + times_flipped(first_s_ref[...], tables_ref[:, t2_row:class_row])
        cond_ref[...] = cond
        signal = swish_unit(cond).astype(bf16)
        signal_ref[...] = signal
        signal = signal.astype(f32)
        for i in range(ways):
            signal_own[i, :batch, :cols] = signal[i * batch : (i + 1) * batch]
        third[0].start()

    def modulation():
        mod = times(signal_ref[...], fada_ref[...])
        half = mod.shape[1] // 2
        for i in range(ways):
            mod_own[i, :batch] = mod[i * batch : (i + 1) * batch, :half]
            mod_own[i, batch:] = mod[i * batch : (i + 1) * batch, half:]
        third[1].start()

    own_count = x_ref.shape[0]
    third_of = -(-own_count // 3)
    in_parts(0, own_count, send_own, [(third_of, first_row), (2 * third_of, class_part)])
    second_row()
    modulation()
    for k in range(late, count):
        pass_own(k)
    run_hop(1)
    run_hop(2)
    for p in third:
        p.wait()
    mod = jnp.sum(mod_land[...], axis=0)
    mod_ref[...] = jnp.concatenate([mod[:batch], mod[batch:]], axis=1)
    run_hop(3)

    def finish(k, _):
        pltpu.make_async_copy(packed.at[k], block(z, y, k), local_sem.at[k]).wait()
        for layer in range(LAYERS):

            @pl.when(k < late)
            def _():
                arrival(layer, 1 - y, k).wait_recv()

            @pl.when((k < late) | (layer == z))
            def _():
                move(block(layer, y, k), layer, k, side_sem, peer).wait_send()

            @pl.when((z < LAYERS - 1) & (layer <= z))
            def _():
                move(block(layer, y, k), layer, k, up_sem, above).wait_send()

            @pl.when((z > 0) & (layer >= z))
            def _():
                move(block(layer, y, k), layer, k, down_sem, below).wait_send()

        return 0

    lax.fori_loop(0, count, finish, 0)
    for k in range(late, count):
        for layer in range(LAYERS):

            @pl.when((z < LAYERS - 1) & (layer <= z))
            def _():
                move_other(layer, k, up_other, above).wait_send()

            @pl.when((z > 0) & (layer >= z))
            def _():
                move_other(layer, k, down_other, below).wait_send()


def head(blocks, time_freq, facts, shared, tables, w_fada, b1, b2):
    ways, f32, bf16 = LAYERS * COLUMNS, jnp.float32, jnp.bfloat16
    count = blocks.shape[0] * SPLIT
    batch, cols, rows = time_freq.shape[0], tables.shape[0], time_freq.shape[0] * ways
    fada = w_fada.shape[1]
    piece = (PACK_ROWS // SPLIT, LANES // 2)
    time_freq = jnp.pad(time_freq, ((0, 8 - batch), (0, 0)))
    facts = jnp.pad(facts, ((0, 8 - batch), (0, 0)))
    shared = jnp.pad(shared.T, ((0, 0), (0, LANES - cols)))
    dma = pltpu.SemaphoreType.DMA
    vmem, anywhere = pl.BlockSpec(memory_space=pltpu.VMEM), pl.BlockSpec(memory_space=pl.ANY)
    shape = jax.ShapeDtypeStruct
    out = pl.pallas_call(
        head_body,
        in_specs=[vmem] * 8,
        out_specs=[anywhere] + [vmem] * 9,
        out_shape=[
            shape((count * ways,) + piece, bf16),
            shape((rows, time_freq.shape[1]), f32),
            shape((ways,) + facts.shape, f32),
            shape((ways,) + shared.shape, bf16),
            shape((rows, cols), f32),
            shape((rows, ways * cols), bf16),
            shape((rows, cols), f32),
            shape((rows, cols), bf16),
            shape((ways, 8, LANES), f32),
            shape((batch, fada), f32),
        ],
        scratch_shapes=[
            pltpu.VMEM((count,) + piece, bf16),
            pltpu.VMEM((ways,) + time_freq.shape, f32),
            pltpu.VMEM((rows, CLASSES), f32),
            pltpu.VMEM((rows, LANES), bf16),
            pltpu.VMEM((ways, rows, LANES), bf16),
            pltpu.VMEM((ways, 8, LANES), f32),
            pltpu.VMEM((ways, 2 * batch, fada // 2), f32),
            pltpu.VMEM((ways, 2 * batch, fada // 2), f32),
            dma((count,)),
            dma((LAYERS, count)),
            dma((LAYERS, count)),
            dma((LAYERS, count)),
            dma((LAYERS, CROSS_LATE)),
            dma((LAYERS, CROSS_LATE)),
            dma((LAYERS, COLUMNS, count)),
            dma((6, ways)),
            dma((6, ways)),
        ],
        compiler_params=pltpu.CompilerParams(
            collective_id=0, has_side_effects=True, vmem_limit_bytes=48 * 2**20
        ),
        name="head",
    )(blocks, time_freq, facts, shared, tables, w_fada, b1, b2)
    blocks, time_freq, facts, shared, first_t, first_s, cond, signal, signal_all, mod = out
    blocks = blocks.reshape(-1, PACK_ROWS, LANES // 2)
    return (
        blocks, time_freq, facts[:, :batch], shared[:, :, :cols].transpose(0, 2, 1), first_t, first_s, cond, signal,
        signal_all[:, :batch, :cols], mod,
    )


def outer(a, b):
    return lax.dot_general(a, b, (((0,), (0,)), ((), ())), preferred_element_type=jnp.float32)


def tail_body(
    x_ref, early_ref, small_ref, bias_ref, fada_ref, tables_ref, cond_ref, first_t_ref,
    signal_ref, first_s_ref, tf_ref, facts_ref,
    out_ref, g_cond_ref, g_head_ref, slice_ref, side_ref, mod_sum_ref, columns_all, last_all,
    side_buf, up_buf, down_buf, other_buf, up_other, down_other, early_land, small_land,
    bias_land, dsig_all, first_own, first_land, small_own, small_mp, side_own, side_mp, fmod_all, columns_own,
    last_own, hot_buf,
    side_send, line_send, side_recv, up_recv, down_recv, other_send, other_up, other_down,
    send_all, recv_all, send_dp, recv_dp, send_mp, recv_mp,
):
    f32, bf16 = jnp.float32, jnp.bfloat16
    count, ways, mp = out_ref.shape[0], LAYERS * COLUMNS, lax.axis_size("mp")
    batch, cols = facts_ref.shape[1], tables_ref.shape[0]
    everyone = ways * mp
    late = count - CROSS_LATE
    z, y = grid_place()
    my_dp, my_mp = lax.axis_index("dp"), lax.axis_index("mp")
    me = my_dp * mp + my_mp

    def place_all(i):
        return {"dp": i // mp, "mp": lax.rem(i, mp)}

    barrier = pltpu.get_barrier_semaphore()

    def greet(i, _):
        signal_to(barrier, place_all(lax.rem(me + i, everyone)))
        return 0

    lax.fori_loop(1, everyone, greet, 0)
    pl.semaphore_wait(barrier, everyone - 1)

    def push_all(j, source, landing, row=None):
        return Push(source, landing, send_all.at[j], recv_all.at[j], everyone, me, place_all, row)

    def push_dp(j, source, landing, row=None):
        return Push(
            source, landing, send_dp.at[j], recv_dp.at[j], ways, my_dp, lambda i: {"dp": i}, row
        )

    def push_mp(j, source, landing):
        return Push(source, landing, send_mp.at[j], recv_mp.at[j], mp, my_mp, lambda i: {"mp": i})

    first = [push_all(0, early_ref, early_land, lambda to: to // mp)]
    second = [push_dp(0, small_ref, small_land, lambda to: to), push_dp(1, bias_ref, bias_land)]
    third = push_dp(2, first_own, first_land, lambda to: to)
    fifth = push_dp(3, columns_own, columns_all)
    fourth = [push_mp(0, small_own, small_mp), push_mp(1, side_own, side_mp)]

    peer = {"dp": z * COLUMNS + 1 - y}
    above = {"dp": jnp.minimum(z + 1, LAYERS - 1) * COLUMNS + y}
    below = {"dp": jnp.maximum(z - 1, 0) * COLUMNS + y}

    def slot(layer, column, k):
        return (layer * COLUMNS + column) * count + k

    def across(layer, k):
        return remote(
            x_ref.at[slot(layer, 1 - y, k)],
            side_buf.at[layer, k],
            side_send.at[layer, k],
            side_recv.at[layer, k],
            peer,
        )

    def cross_late(k):
        return remote(
            other_buf.at[z, k - late],
            side_buf.at[z, k],
            side_send.at[z, k],
            side_recv.at[z, k],
            peer,
        )

    def upward(layer, k):
        return remote(
            side_buf.at[layer, k], up_buf.at[layer, k], line_send.at[layer, k], up_recv.at[layer, k], above
        )

    def downward(layer, k):
        return remote(
            side_buf.at[layer, k], down_buf.at[layer, k], line_send.at[layer, k], down_recv.at[layer, k], below
        )

    def upward_other(layer, k):
        j = k - late
        return remote(
            other_buf.at[layer, j], up_other.at[layer, j], other_send.at[layer, j], other_up.at[layer, j], above
        )

    def downward_other(layer, k):
        j = k - late
        return remote(
            other_buf.at[layer, j], down_other.at[layer, j], other_send.at[layer, j], other_down.at[layer, j], below
        )

    def own_part(layer, k):
        return x_ref[slot(layer, y, k)].astype(f32)

    def pair_sum(layer, k):
        across(layer, k).wait_recv()
        return own_part(layer, k) + side_buf[layer, k].astype(f32)

    at_end = (z == 0) | (z == LAYERS - 1)

    def turn(t):
        part, within = t // late, lax.rem(t, late)
        end_layer = jnp.where(z == 0, LAYERS - 1 - part, part)
        pair = t - late
        near = jnp.where(lax.rem(pair, 2) == 0, z + 1, z - 1)
        inner_layer = jnp.where(part == 0, jnp.where(z == 1, LAYERS - 1, 0), jnp.where(part == 3, z, near))
        inner_k = jnp.where((part == 0) | (part == 3), within, pair // 2)
        return jnp.where(at_end, end_layer, inner_layer), jnp.where(at_end, within, inner_k)

    def issue(t):
        @pl.when(t < LAYERS * late)
        def _():
            across(*turn(t)).start()

    for t in range(AHEAD):
        issue(jnp.int32(t))
    for p in first + second:
        p.start()

    def along(total, stage_ref, layer, k, copy, landed, begins):
        @pl.when(jnp.logical_not(begins))
        def _():
            copy(layer, k).wait_recv()
            stage_ref[...] = (total + landed[...].astype(f32)).astype(bf16)

        @pl.when(begins)
        def _():
            stage_ref[...] = total.astype(bf16)

        copy(layer, k).start()

    bottom, top = z == 0, z == LAYERS - 1

    def run_late(hop):
        for k in range(late, count):
            j = k - late

            @pl.when(z + hop < LAYERS)
            def _():
                layer = z + hop
                along(
                    own_part(layer, k), side_buf.at[layer, k], layer, k, upward, up_buf.at[layer, k], bottom
                )
                along(
                    x_ref[slot(layer, 1 - y, k)].astype(f32),
                    other_buf.at[layer, j], layer, k, upward_other, up_other.at[layer, j], bottom,
                )

            @pl.when(z >= hop)
            def _():
                layer = z - hop
                along(
                    own_part(layer, k), side_buf.at[layer, k], layer, k, downward, down_buf.at[layer, k], top
                )
                along(
                    x_ref[slot(layer, 1 - y, k)].astype(f32),
                    other_buf.at[layer, j], layer, k, downward_other, down_other.at[layer, j], top,
                )

    def step(t, _):
        issue(t + AHEAD)
        layer, k = turn(t)

        @pl.when(layer > z)
        def _():
            along(
                pair_sum(layer, k), side_buf.at[layer, k], layer, k, upward, up_buf.at[layer, k], bottom
            )

        @pl.when(layer < z)
        def _():
            along(
                pair_sum(layer, k), side_buf.at[layer, k], layer, k, downward, down_buf.at[layer, k], top
            )

        return 0

    t2_row = PATCH_VALUES + FREQ
    class_row = t2_row + MODEL_WIDTH
    held = {"shared": jnp.zeros((1, 1), f32)}

    def square(x):
        return jnp.sum(jnp.sum(x * x, axis=1, keepdims=True), axis=0, keepdims=True)

    def add_shared(x):
        held["shared"] = held["shared"] + square(x)

    def signal_back():
        for p in first:
            p.wait()
        lines = fmod_all.shape[1] // 128
        for i in range(everyone):
            here = early_land[i].astype(f32)
            for j in range(lines):
                fmod_all[i : i + 1, j * 128 : (j + 1) * 128] = here[j : j + 1]
        for i in range(ways):
            here = early_land[i * mp].astype(f32)[24:]
            for j in range(1, mp):
                here = here + early_land[i * mp + j].astype(f32)[24:]
            dsig_all[i * batch : (i + 1) * batch, :128] = here[:batch]
            dsig_all[i * batch : (i + 1) * batch, 128:] = here[batch:]
        d_signal = dsig_all[:, :cols] + times_flipped(fmod_all[...].astype(bf16), fada_ref[...])
        held["d_cond"] = d_signal * swish_slope(cond_ref[...])
        held["d_second"] = held["d_cond"].astype(bf16)

    def second_back():
        back = times(held["d_second"], tables_ref[:, t2_row:class_row])
        for i in range(ways):
            first_own[i, :, :cols] = back[:, i * cols : (i + 1) * cols].astype(bf16)
        third.start()

    def bias_sums():
        for p in second:
            p.wait()
        small_own[...] = jnp.sum(small_land[...].astype(f32), axis=0)
        bias = jnp.sum(bias_land[...].astype(f32), axis=0)
        slice_rows = slice_ref.shape[0]
        slice_ref[...] = bias[:slice_rows]
        held["slice"] = square(bias[:slice_rows])
        side_own[...] = bias[slice_rows:]
        for p in fourth:
            p.start()

    def fada_gradient():
        g_fada = outer(signal_ref[...], fmod_all[...].astype(bf16))
        g_head_ref[:, : g_fada.shape[1]] = g_fada
        add_shared(g_fada)
        held["mod"] = column_sum(fmod_all[...])
        mod_sum_ref[...] = held["mod"]

    def second_gradient():
        held["g_second"] = outer(held["d_second"], first_s_ref[...])
        add_shared(held["g_second"])

    def class_gradient():
        for i in range(ways):
            row = lax.broadcasted_iota(jnp.int32, (batch, CLASSES), 1)
            hot = (row == facts_ref[i][:, 0:1].astype(jnp.int32)).astype(f32)
            hot_buf[i * batch : (i + 1) * batch] = hot
        hot = hot_buf[...].astype(bf16)
        high = held["d_cond"].astype(bf16)
        rest = held["d_cond"] - high.astype(f32)
        mid = rest.astype(bf16)
        low = (rest - mid.astype(f32)).astype(bf16)
        held["g_class"] = outer(high, hot) + outer(mid, hot) + outer(low, hot)
        add_shared(held["g_class"])

    def first_gradient():
        third.wait()
        d_first = (jnp.sum(first_land[...].astype(f32), axis=0)[:, :cols] * swish_slope(first_t_ref[...])).astype(bf16)
        held["g_first"] = outer(d_first, tf_ref[...].astype(bf16))
        add_shared(held["g_first"])
        held["columns"] = [column_sum(d_first.astype(f32)), column_sum(held["d_second"].astype(f32))]
        for i, s in enumerate(held["columns"]):
            add_shared(s)
            columns_own[i : i + 1, :cols] = s
        fifth.start()

    def totals():
        for p in fourth:
            p.wait()
        small = jnp.sum(small_mp[...], axis=0)[:, :cols]
        add_shared(small)
        small = small.T
        g_head_ref[:, fmod_all.shape[1] :] = small[:, PATCH_VALUES:]
        g_cond_ref[...] = jnp.concatenate(
            [small[:, :PATCH_VALUES], held["g_first"], held["g_second"], held["g_class"]], axis=1
        )
        side = jnp.sum(side_mp[...], axis=0)
        side_ref[...] = side
        held["every"] = square(side[: side.shape[0] - 8]) + square(held["mod"])

    steps = (LAYERS - 1) * late
    places = [
        (0, lambda: run_late(3)),
        (3, lambda: run_late(2)),
        (12, lambda: run_late(1)),
        (22, signal_back),
        (25, second_back),
        (30, bias_sums),
        (35, fada_gradient),
        (40, second_gradient),
        (45, class_gradient),
        (57, first_gradient),
        (63, totals),
    ]
    in_parts(0, steps, step, [(-(-t * steps // 72), work) for t, work in places])

    for k in range(late, count):
        j = k - late
        other_buf[z, j] = x_ref[slot(z, 1 - y, k)]

        @pl.when(z > 0)
        def _():
            upward_other(z, k).wait_recv()
            other_buf[z, j] = (other_buf[z, j].astype(f32) + up_other[z, j].astype(f32)).astype(bf16)

        @pl.when(z < LAYERS - 1)
        def _():
            downward_other(z, k).wait_recv()
            other_buf[z, j] = (other_buf[z, j].astype(f32) + down_other[z, j].astype(f32)).astype(bf16)

        cross_late(k).start()

    last_own[...] = jnp.zeros_like(last_own)

    def final(k, _):
        issue(steps + k + AHEAD)
        out_ref[k] = pair_sum(z, k)

        @pl.when(z > 0)
        def _():
            upward(z, k).wait_recv()
            out_ref[k] += up_buf[z, k].astype(f32)

        @pl.when(z < LAYERS - 1)
        def _():
            downward(z, k).wait_recv()
            out_ref[k] += down_buf[z, k].astype(f32)

        total = out_ref[k]
        last_own[...] += column_sum(total * total)
        return 0

    lax.fori_loop(0, count, final, 0)
    squares = held["shared"] / mp + held["slice"] / ways + held["every"] / (ways * mp)
    squares += jnp.sum(last_own[...], axis=1, keepdims=True)
    last_own[...] = jnp.broadcast_to(squares, (1, 128))
    sixth = push_all(1, last_own, last_all)
    sixth.start()

    def sent(k, _):
        for layer in range(LAYERS):

            @pl.when(k < late)
            def _():
                across(layer, k).wait_send()

            @pl.when(layer > z)
            def _():
                upward(layer, k).wait_send()

            @pl.when(layer < z)
            def _():
                downward(layer, k).wait_send()

        return 0

    lax.fori_loop(0, count, sent, 0)
    for k in range(late, count):
        cross_late(k).wait_send()
        for layer in range(LAYERS):

            @pl.when(layer > z)
            def _():
                upward_other(layer, k).wait_send()

            @pl.when(layer < z)
            def _():
                downward_other(layer, k).wait_send()

    fifth.wait()
    sixth.wait()


def tail(slots, d_fmod, d_signal, small, bias, w_fada, tables, cond, first_t, signal, first_s, tf, facts, slice_rows):
    ways, mp, f32, bf16 = LAYERS * COLUMNS, lax.axis_size("mp"), jnp.float32, jnp.bfloat16
    piece = (PACK_ROWS // SPLIT, LANES // 2)
    slots = slots.reshape((-1,) + piece)
    count = slots.shape[0] // ways
    batch, cols = d_signal.shape[1:]
    rows, fada = batch * ways, w_fada.shape[1]
    side_rows = bias.shape[0] - slice_rows
    wide = ((0, 0), (0, 0), (0, LANES - cols))
    d_signal = jnp.pad(d_signal, wide).reshape(ways, batch, 2, 128).transpose(0, 2, 1, 3)
    d_fmod = jnp.pad(d_fmod.reshape(fada // 128, 128), ((0, 24 - fada // 128), (0, 0)))
    early = jnp.concatenate(
        [jnp.broadcast_to(d_fmod, (ways, 24, 128)), d_signal.reshape(ways, 2 * batch, 128)], 1
    ).astype(bf16)
    small = jnp.pad(small, wide).astype(bf16)
    bias = bias.astype(bf16)
    dma, vmem = pltpu.SemaphoreType.DMA, pl.BlockSpec(memory_space=pltpu.VMEM)
    shape, scratch = jax.ShapeDtypeStruct, pltpu.VMEM
    landing = scratch((LAYERS, count) + piece, bf16)
    few = scratch((LAYERS, CROSS_LATE) + piece, bf16)
    out_shape = [
        shape((count,) + piece, f32),
        shape(tables.shape, f32),
        shape((cols, fada + small.shape[1] - PATCH_VALUES), f32),
        shape((slice_rows, 128), f32),
        shape((side_rows, 128), f32),
        shape((1, fada), f32),
        shape((ways, 8, LANES), f32),
        shape((ways * mp, 1, 128), f32),
    ]
    out = pl.pallas_call(
        tail_body,
        in_specs=[vmem] * 12,
        out_specs=[vmem] * len(out_shape),
        out_shape=out_shape,
        scratch_shapes=[landing] * 3
        + [few] * 3
        + [
            scratch((ways * mp,) + early.shape[1:], bf16),
            scratch(small.shape, bf16),
            scratch((ways,) + bias.shape, bf16),
            scratch((rows, LANES), f32),
            scratch((ways, rows, LANES), bf16),
            scratch((ways, rows, LANES), bf16),
            scratch(small.shape[1:], f32),
            scratch((mp,) + small.shape[1:], f32),
            scratch((side_rows, 128), f32),
            scratch((mp, side_rows, 128), f32),
            scratch((rows, fada), f32),
            scratch((8, LANES), f32),
            scratch((1, 128), f32),
            scratch((rows, CLASSES), f32),
        ]
        + [dma((LAYERS, count))] * 5
        + [dma((LAYERS, CROSS_LATE))] * 3
        + [dma((2, ways * mp))] * 2
        + [dma((4, ways))] * 2
        + [dma((2, mp))] * 2,
        compiler_params=pltpu.CompilerParams(
            collective_id=1, has_side_effects=True, vmem_limit_bytes=58 * 2**20
        ),
        name="tail",
    )(slots, early, small, bias, w_fada, tables, cond, first_t, signal, first_s, tf, facts)
    return [out[0].reshape(-1, PACK_ROWS, LANES // 2)] + list(out[1:])


def halves(x):
    high = x.astype(jnp.bfloat16)
    return high, (x - high.astype(jnp.float32)).astype(jnp.bfloat16)


def left_form(main, tail):
    mh, ml = halves(main)
    th, tl = halves(tail)
    return jnp.concatenate([mh, mh, ml, th, th, tl], axis=1)


def right_form(x):
    h, l = halves(x)
    return jnp.concatenate(
        [h[:LANES], l[:LANES], h[:LANES], h[LANES:], l[LANES:], h[LANES:]], axis=0
    )


def product(left, right):
    return jnp.dot(left, right, preferred_element_type=jnp.float32)


def symmetric_product(left, right_main, right_tail):
    main = product(left, right_main)
    corner = product(left[LANES:], right_tail)
    return main, jnp.concatenate([main[LANES:].T, corner], axis=0)


def inverse_roots(pairs, eye_main, eye_tail):
    contracted, scales = [], []
    for main, tail in pairs:
        trace = jnp.sum(main * eye_main) + jnp.sum(tail * eye_tail)
        shift = 0.0001 * trace / BLOCK_SIDE
        main = main + shift * eye_main
        tail = tail + shift * eye_tail
        square = jnp.sum(main * main, axis=(0, 1), keepdims=True) + jnp.sum(
            tail * tail, axis=(0, 1), keepdims=True
        )
        factor_z = 2.5 / jnp.sqrt(square)
        contracted.append((main * factor_z, tail * factor_z))
        scales.append(jnp.sqrt(jnp.sqrt(factor_z)))
    estimates = None
    for newton_step in range(NEWTON):
        more = newton_step < NEWTON - 1
        factors = [((5.0 * eye_main - m) * 0.25, (5.0 * eye_tail - t) * 0.25) for m, t in contracted]
        rights = [(right_form(m), right_form(t)) for m, t in factors]
        lefts = [left_form(m, t) for m, t in factors]
        if more:
            powers = [symmetric_product(l, *r) for l, r in zip(lefts, rights)]
        if estimates is None:
            estimates = [(m * s, t * s) for (m, t), s in zip(factors, scales)]
        else:
            estimates = [
                symmetric_product(left_form(*e), *r) for e, r in zip(estimates, rights)
            ]
        if more:
            powers = [
                symmetric_product(left_form(*q), right_form(q[0]), right_form(q[1])) for q in powers
            ]
            contracted = [
                symmetric_product(left_form(*q), right_form(m), right_form(t))
                for q, (m, t) in zip(powers, contracted)
            ]
    return estimates


def shampoo_body(clip_ref, g_ref, stat_ref, old_ref, clipped_ref, new_stat_ref, new_ref, low_ref):
    side = BLOCK_SIDE

    def unit(width, offset):
        row = lax.broadcasted_iota(jnp.int32, (side, width), 0)
        col = lax.broadcasted_iota(jnp.int32, (side, width), 1) + offset
        return (row == col).astype(jnp.float32)

    eye_main, eye_tail = unit(LANES, 0), unit(TAIL, LANES)
    pairs, g_rights = [], []
    for j in range(g_ref.shape[0]):
        g_main, g_tail = unpack(g_ref[j] * clip_ref[0])
        clipped_ref[j, :, :LANES] = g_main
        clipped_ref[j, :, LANES:] = g_tail
        flipped = jnp.concatenate([g_main, g_tail], axis=1).T
        g_right = (right_form(g_main), right_form(g_tail))
        f_right = (right_form(flipped[:, :LANES]), right_form(flipped[:, LANES:]))
        g_left = left_form(g_main, g_tail)
        f_left = left_form(flipped[:, :LANES], flipped[:, LANES:])
        g_rights.append(g_right)
        for k, (left, right) in enumerate(((g_left, f_right), (f_left, g_right))):
            main, tail = symmetric_product(left, *right)
            main = 0.5 * stat_ref[j, k, :, :LANES] + 0.5 * main
            tail = 0.5 * stat_ref[j, k, :, LANES:] + 0.5 * tail
            new_stat_ref[j, k, :, :LANES] = main
            new_stat_ref[j, k, :, LANES:] = tail
            pairs.append((main, tail))
    roots = inverse_roots(pairs, eye_main, eye_tail)
    for j, g_right in enumerate(g_rights):
        root_left = left_form(*roots[2 * j])
        half = left_form(product(root_left, g_right[0]), product(root_left, g_right[1]))
        for part, (a, b) in zip(roots[2 * j + 1], ((0, LANES), (LANES, side))):
            direction = product(half, right_form(part))
            old = old_ref[j, :, a:b]
            new = old - shampoo_rate * (direction + decay_rate * old)
            new_ref[j, :, a:b] = new
            low_ref[j, :, a:b] = new.astype(jnp.bfloat16)


def shampoo(clip_factor, gradients, stats, old_blocks):
    count, side = gradients.shape[0], BLOCK_SIDE
    group = next(g for g in (3, 2, 1) if count % g == 0)
    one = pl.BlockSpec((group, side, side), lambda i: (i, 0, 0))
    two = pl.BlockSpec((group, 2, side, side), lambda i: (i, 0, 0, 0))
    block = jax.ShapeDtypeStruct((count, side, side), jnp.float32)
    return pl.pallas_call(
        shampoo_body,
        grid=(count // group,),
        in_specs=[
            pl.BlockSpec(memory_space=pltpu.SMEM),
            pl.BlockSpec((group, PACK_ROWS, LANES // 2), lambda i: (i, 0, 0)),
            two,
            one,
        ],
        out_specs=[one, two, one, one],
        out_shape=[
            block,
            jax.ShapeDtypeStruct((count, 2, side, side), jnp.float32),
            block,
            jax.ShapeDtypeStruct((count, side, side), jnp.bfloat16),
        ],
        compiler_params=pltpu.CompilerParams(vmem_limit_bytes=60 * 2**20),
        cost_estimate=pl.CostEstimate(
            flops=count * 44 * 6 * side**3, bytes_accessed=count * 34 * side * side, transcendentals=0
        ),
        name="shampoo",
    )(clip_factor.reshape(1), gradients, stats, old_blocks)


def adam_update(weight, gradient, moment_one, second):
    moment_one = 0.5 * moment_one + 0.5 * gradient
    second = 0.5 * second + 0.5 * gradient * gradient
    correct = 1.0 - 0.5**STEP
    updated = weight - adam_rate * (
        moment_one / correct / (jnp.sqrt(second / correct) + 1e-08) + decay_rate * weight
    )
    return (moment_one, second, updated)


def per_device(
    latents,
    noise,
    timesteps,
    labels,
    loss_weights,
    slotted_block_weights,
    statistics,
    slot_of_block,
    cond_tables,
    head_tables,
    slice_bias,
    side_bias,
    cond_m,
    cond_v,
    head_m,
    head_v,
    slice_m,
    slice_v,
    side_m,
    side_v,
):
    bf16, f32 = jnp.bfloat16, jnp.float32
    width = MODEL_WIDTH
    mp, dp = lax.axis_size("mp"), lax.axis_size("dp")
    my_mp, my_dp = lax.axis_index("mp"), lax.axis_index("dp")
    query_width, ff_width, ada_width = HEADS * HD // mp, FF // mp, 6 * width // mp
    ada_column = 3 * query_width + ff_width
    row_blocks = width // BLOCK_SIDE
    col_blocks = (ada_column + ada_width) // BLOCK_SIDE
    out_blocks = (query_width + ff_width) // BLOCK_SIDE
    first_out = row_blocks * col_blocks
    t2_row = PATCH_VALUES + FREQ
    class_row = t2_row + width
    local_heads = query_width // HD
    score_scale = HD ** (-0.5)
    batch = latents.shape[0]
    own_n = batch // mp
    cols = cond_tables.shape[1]
    samples = batch * dp

    def own(x):
        return lax.dynamic_slice_in_dim(x, my_mp * own_n, own_n, 0)

    def my_cols(x):
        return lax.dynamic_slice_in_dim(x, my_dp * cols, cols, x.ndim - 1)

    def all_columns(x):
        return x.transpose(1, 0, 2).reshape(x.shape[1], -1)

    def by_columns(x):
        return x.reshape(x.shape[0], dp, cols).transpose(1, 0, 2)

    def share_rows(x):
        return lax.all_gather(x, "mp", axis=0, tiled=True)

    tuned = dp == COLUMNS * LAYERS
    tables, head_low = cond_tables.T.astype(bf16), head_tables.astype(bf16)
    w_fada = head_low[:, : 2 * width]
    b_first = my_cols(side_bias[width : 2 * width])
    b_second = my_cols(side_bias[2 * width : 3 * width])
    time_freq = time_features(timesteps, FREQ).astype(bf16).astype(f32)
    facts = jnp.pad(jnp.stack([labels.astype(f32), loss_weights], 1), ((0, 0), (0, 126)))
    shared = jnp.concatenate([tables[:, :PATCH_VALUES], head_low[:, 2 * width :]], 1)
    if tuned:
        (
            blocks, time_freq, facts, shared, first_t, first_s, cond_vec, signal_cols, signal, final_mod,
        ) = head(
            slotted_block_weights[0], time_freq, facts, shared, tables, w_fada, b_first[None],
            b_second[None],
        )
    else:
        w_first, w_second = tables[:, PATCH_VALUES:t2_row].T, tables[:, t2_row:class_row].T
        blocks = lax.all_gather(pack_blocks(slotted_block_weights[0]), "dp", axis=0, tiled=True)
        time_freq, facts, shared = exchange(
            [(time_freq, "gather"), (facts, "gather"), (shared, "gather")], "dp", 2
        )
        time_freq = time_freq.reshape(samples, FREQ)
        first_t = dense(time_freq.astype(bf16), w_first) + b_first
        (first_s,) = exchange([(swish_unit(first_t).astype(bf16), "gather")], "dp", 3)
        labels_all = facts[:, :, 0].reshape(samples, 1).astype(jnp.int32)
        onehot = labels_all == jnp.arange(CLASSES, dtype=jnp.int32)[None, :]
        first_s = all_columns(first_s)
        cond_vec = (
            dense(first_s, w_second) + b_second + dense(onehot.astype(bf16), tables[:, class_row:].T)
        )
        signal_cols = swish_unit(cond_vec).astype(bf16)
        signal, final_mod = exchange(
            [
                (signal_cols.astype(f32).reshape(dp, batch, cols), "scatter"),
                (dense(signal_cols, w_fada).reshape(dp, batch, 2 * width), "scatter"),
            ],
            "dp",
            4,
        )
        final_mod = jnp.sum(final_mod, 0)
    weight_total = jnp.sum(facts[:, :, 1])
    shared = shared.reshape(width, -1)
    w_patch, w_head = shared[:, :PATCH_VALUES].T, shared[:, PATCH_VALUES:]
    signal = all_columns(signal).astype(bf16)
    final_mod = own(final_mod + side_bias[5 * width : 7 * width])

    w_qkv, w_up, w_ada = assemble(
        blocks,
        slot_of_block,
        0,
        row_blocks,
        [3 * query_width // BLOCK_SIDE, ff_width // BLOCK_SIDE, ada_width // BLOCK_SIDE],
    )
    (w_o,) = assemble(blocks, slot_of_block, first_out, query_width // BLOCK_SIDE, [row_blocks])
    (w_down,) = assemble(
        blocks,
        slot_of_block,
        first_out + query_width // BLOCK_SIDE * row_blocks,
        ff_width // BLOCK_SIDE,
        [row_blocks],
    )
    own_bias = slice_bias[0]
    modul = lax.all_gather(
        dense(signal, w_ada) + own_bias[2 * query_width + ff_width :],
        "mp",
        axis=1,
        tiled=True,
    )
    own_modul = own(modul)

    def part(position):
        return modul[:, None, position * width : (position + 1) * width]

    def heads_of(inputs):
        return inputs.reshape(batch, -1, local_heads, HD)

    keep_rate, noise_rate, upper_log, lower_log, mean_gap = coefficients(timesteps)
    noisy = keep_rate[:, None, None, None] * latents + noise_rate[:, None, None, None] * noise
    patches = patchify(noisy).astype(bf16)
    seq_len = patches.shape[1]
    initial = (
        dense(patches, w_patch) + side_bias[:width] + position_embedding(LATENT_SIDE // 2, width)
    )
    normed_all, _ = layer_norm(initial)
    attn_in = (normed_all * (1.0 + part(1)) + part(0)).astype(bf16)
    start = own(initial)[0]
    own_patches = own(patches)
    target = patchify(own(noise))[0]

    projected = dense(attn_in, w_qkv)
    queries = heads_of((projected[..., :query_width] + own_bias[:query_width]).astype(bf16))
    keys = heads_of(projected[..., query_width : 2 * query_width].astype(bf16))
    values = heads_of(
        (projected[..., 2 * query_width :] + own_bias[query_width : 2 * query_width]).astype(bf16)
    )
    scores = (
        jnp.einsum("slhe,smhe->shlm", queries, keys, preferred_element_type=f32) * score_scale
    )
    row_peak = jnp.max(scores, -1, keepdims=True)
    shifted = jnp.exp(scores - row_peak)
    row_total = jnp.sum(shifted, -1, keepdims=True)
    probs = shifted / row_total
    log_total = row_peak + jnp.log(row_total)
    mixed = (
        jnp.einsum("shlm,smhe->slhe", probs.astype(bf16), values, preferred_element_type=f32)
        .reshape(batch, seq_len, query_width)
        .astype(bf16)
    )

    def rows_of(*rows):
        return jnp.concatenate([r.reshape(1, width) for r in rows], 0)

    shift1, scale1, gate1, shift2, scale2, gate2 = (own_modul[0, i * width : (i + 1) * width] for i in range(6))
    attn, middle, hidden, active, mlp_in = attention_out_stage(
        mixed,
        w_o,
        w_up,
        start,
        rows_of(side_bias[3 * width : 4 * width], gate1, scale2, shift2),
        own_bias[2 * query_width : 2 * query_width + ff_width].reshape(1, ff_width),
    )

    def halves_of(x):
        x = x.reshape(x.shape[:-1] + (4, 8))
        return x[..., :4].reshape(x.shape[:-2] + (16,)), x[..., 4:].reshape(x.shape[:-2] + (16,))

    w_pred, w_raw = halves_of(w_head)
    own_weight = own(loss_weights)
    loss_facts = [own(upper_log), own(lower_log), own(mean_gap), own_weight, own_weight / weight_total]
    d_final, head_in, d_pred, d_raw, sums_f, loss_part, d_hidden, up_sum, d_branch = loss_stage(
        active,
        w_down,
        hidden,
        middle,
        rows_of(side_bias[4 * width : 5 * width], gate2, final_mod[0, width:], final_mod[0, :width]),
        target,
        w_pred,
        w_raw,
        jnp.stack(halves_of(side_bias[7 * width :])),
        jnp.broadcast_to(jnp.stack(loss_facts), (5, 16)),
    )
    loss_part = jnp.sum(loss_part)
    d_fmod = sums_f[:2].reshape(1, 2 * width).astype(bf16)
    g_down = weight_grad(active, d_branch).astype(bf16)
    d_middle, sums_m, d_mixed, d_attn = middle_back_stage(
        d_hidden, w_up, w_o, middle, d_final, attn, rows_of(scale2, gate1)
    )
    g_up = weight_grad(mlp_in, d_hidden).astype(bf16)
    g_outp = weight_grad(mixed, d_attn).astype(bf16)
    d_mixed = heads_of(d_mixed)
    probs = jnp.exp(
        jnp.einsum("slhe,smhe->shlm", queries, keys, preferred_element_type=f32) * score_scale
        - log_total
    )
    d_values = jnp.einsum(
        "shlm,slhe->smhe", probs.astype(bf16), d_mixed, preferred_element_type=f32
    ).astype(bf16)
    d_probs = jnp.einsum("slhe,smhe->shlm", d_mixed, values, preferred_element_type=f32)
    d_scores = (probs * (d_probs - jnp.sum(d_probs * probs, -1, keepdims=True))).astype(bf16)
    d_query = (
        jnp.einsum("shlm,smhe->slhe", d_scores, keys, preferred_element_type=f32) * score_scale
    ).astype(bf16)
    d_keys = (
        jnp.einsum("shlm,slhe->smhe", d_scores, queries, preferred_element_type=f32) * score_scale
    ).astype(bf16)
    flat_q = d_query.reshape(batch, seq_len, query_width)
    flat_v = d_values.reshape(batch, seq_len, query_width)
    d_proj = jnp.concatenate([flat_q, d_keys.reshape(batch, seq_len, query_width), flat_v], 2)
    g_qkv = weight_grad(attn_in, d_proj).astype(bf16)
    d_start, sums_a = start_back_stage(d_proj, w_qkv, start, d_middle, scale1.reshape(1, width))
    d_mod_own = jnp.concatenate(
        [sums_a[0], sums_a[1], sums_m[2], sums_m[0], sums_m[1], sums_f[2]]
    ).reshape(1, 6 * width)
    d_modul = lax.dynamic_slice_in_dim(
        share_rows(d_mod_own.astype(bf16)), my_mp * ada_width, ada_width, 1
    )

    slot_grad = to_slots(
        [g_qkv, g_up], signal, d_modul, [g_outp, g_down], slot_of_block, slot_of_block.shape[0]
    )
    d_signal = by_columns(back_dense(d_modul, w_ada))

    def interleave(p, r):
        parts = [x.reshape(x.shape[:-1] + (4, 4)) for x in (p, r)]
        return jnp.concatenate(parts, -1).reshape(p.shape[:-1] + (32,))

    def thirds(x):
        high = x.astype(bf16).astype(f32)
        mid = (x - high).astype(bf16).astype(f32)
        return [high, mid, x - high - mid]

    def lanes(x, rows):
        return jnp.pad(x, (0, rows * 128 - x.shape[0])).reshape(rows, 128)

    d_out = interleave(d_pred, d_raw)
    small = by_columns(
        jnp.concatenate([weight_grad(own_patches[0], d_start), weight_grad(d_out, head_in)], 0)
    )
    slice_part = jnp.concatenate([total_of(flat_q), total_of(flat_v), up_sum[0], total_of(d_modul)])
    side_part = jnp.concatenate([sums_a[2], sums_m[3], sums_f[3], total_of(d_out)])
    slice_rows, side_rows = (-(-x.shape[0] // 1024) * 8 for x in (slice_part, side_part))
    bias_part = jnp.concatenate(
        [lanes(slice_part, slice_rows), lanes(side_part, side_rows), lanes(jnp.stack(thirds(loss_part)), 8)], 0
    )
    if tuned:
        red_blocks, red_cond, red_head, red_slice, side_sum, side_mod, columns, last = tail(
            slot_grad, d_fmod.astype(f32), d_signal, small, bias_part, w_fada, tables, cond_vec,
            first_t, signal_cols, first_s, time_freq, facts, slice_rows,
        )
    else:
        red_blocks = lax.psum_scatter(slot_grad, "dp", scatter_dimension=0, tiled=True).astype(f32)
        d_fmod_all, d_signal = exchange(
            [(d_fmod.astype(f32), "gather"), (d_signal, "scatter")], EVERY, 5
        )
        d_fmod_all = d_fmod_all.reshape(samples, 2 * width).astype(bf16)
        d_signal = jnp.sum(d_signal.reshape(dp, mp, batch, cols), 1).reshape(samples, cols)
        d_signal = d_signal + back_dense(d_fmod_all, w_fada)
        d_cond = d_signal * swish_slope(cond_vec)
        d_second = d_cond.astype(bf16)
        d_first, small, bias_part = exchange(
            [
                (by_columns(back_dense(d_second, w_second)), "scatter"),
                (small, "scatter"),
                (bias_part, "gather"),
            ],
            "dp",
            6,
        )
        d_first = (jnp.sum(d_first, 0) * swish_slope(first_t)).astype(bf16)
        bias_part = jnp.sum(bias_part, 0)
        red_slice = bias_part[:slice_rows]
        small, side_sum = exchange(
            [(jnp.sum(small, 0), "gather"), (bias_part[slice_rows:], "gather")], "mp", 7
        )
        small, side_sum = jnp.sum(small, 0), jnp.sum(side_sum, 0)
        side_mod = total_of(d_fmod_all)
        g_class = jnp.einsum(
            "sc,sd->cd", onehot.astype(f32), d_cond, precision=exact_precision_flag
        )
        red_cond = jnp.concatenate(
            [
                small[:PATCH_VALUES],
                weight_grad(time_freq.astype(bf16), d_first),
                weight_grad(first_s, d_second),
                g_class,
            ],
            0,
        ).T
        red_head = jnp.concatenate([weight_grad(signal_cols, d_fmod_all), small[PATCH_VALUES:].T], 1)
        side_cols = jnp.stack([total_of(d_first), total_of(d_second)])
        local_squares = (
            jnp.sum(red_blocks * red_blocks)
            + (
                jnp.sum(red_cond * red_cond)
                + jnp.sum(red_head * red_head)
                + jnp.sum(side_cols * side_cols)
            )
            / mp
            + jnp.sum(red_slice * red_slice) / dp
            + (jnp.sum(side_sum[:-8] * side_sum[:-8]) + jnp.sum(side_mod * side_mod)) / (dp * mp)
        )
        last = jnp.pad(side_cols, ((0, 6), (0, LANES - cols)))
        last = jnp.where(jnp.arange(8)[:, None] == 2, local_squares, last)
        (last,) = exchange([(last, "gather")], EVERY, 8)
        columns, last = last.reshape(dp, mp, 8, LANES)[:, 0], last[:, 2:3]
    grad_norm = jnp.sqrt(jnp.sum(last[:, 0, 0]))
    loss_sum = jnp.sum(side_sum[side_rows, :3])
    side_sum = side_sum[:side_rows].reshape(-1)[: side_part.shape[0]]
    red_slice = red_slice.reshape(-1)[: slice_part.shape[0]]
    side_cols = columns[:, :2, :cols].transpose(1, 0, 2).reshape(2 * width)
    red_side = jnp.concatenate(
        [
            side_sum[:width],
            side_cols,
            side_sum[width : 3 * width],
            side_mod.reshape(2 * width),
            side_sum[3 * width :],
        ]
    )
    clip_factor = 1.0 / jnp.maximum(grad_norm, 1.0)
    clipped, new_stats, new_blocks, new_low = shampoo(
        clip_factor, red_blocks, statistics[0], slotted_block_weights[0]
    )
    cond_one, cond_two, new_cond = adam_update(
        cond_tables.T, red_cond * clip_factor, cond_m.T, cond_v.T
    )
    cond_one, cond_two, new_cond = cond_one.T, cond_two.T, new_cond.T
    head_one, head_two, new_head = adam_update(head_tables, red_head * clip_factor, head_m, head_v)
    slice_one, slice_two, new_slice = adam_update(
        slice_bias[0], red_slice * clip_factor, slice_m[0], slice_v[0]
    )
    side_one, side_two, new_side = adam_update(side_bias, red_side * clip_factor, side_m, side_v)
    return (
        loss_sum,
        weight_total,
        grad_norm,
        clipped[None],
        new_stats[None],
        new_blocks[None],
        new_low[None],
        cond_one,
        cond_two,
        new_cond,
        new_cond.astype(bf16),
        head_one,
        head_two,
        new_head,
        new_head.astype(bf16),
        slice_one[None],
        slice_two[None],
        new_slice[None],
        side_one,
        side_two,
        new_side,
    )


def solution(mesh):
    return jax.shard_map(
        per_device,
        mesh=mesh,
        in_specs=(
            P("dp", None, None, None),
            P("dp", None, None, None),
            P("dp"),
            P("dp"),
            P("dp"),
            P("mp", "dp", None, None),
            P("mp", "dp", None, None, None),
            P(),
            P(None, "dp"),
            P("dp", None),
            P("mp", None),
            P(),
            P(None, "dp"),
            P(None, "dp"),
            P("dp", None),
            P("dp", None),
            P("mp", None),
            P("mp", None),
            P(),
            P(),
        ),
        out_specs=(
            P(),
            P(),
            P(),
            P("mp", "dp", None, None),
            P("mp", "dp", None, None, None),
            P("mp", "dp", None, None),
            P("mp", "dp", None, None),
            P(None, "dp"),
            P(None, "dp"),
            P(None, "dp"),
            P(None, "dp"),
            P("dp", None),
            P("dp", None),
            P("dp", None),
            P("dp", None),
            P("mp", None),
            P("mp", None),
            P("mp", None),
            P(),
            P(),
            P(),
        ),
        check_vma=False,
    )
```

```python
import math

import jax
import jax.numpy as jnp
from jax import lax
from jax.experimental import pallas as pl
from jax.experimental.pallas import tpu as pltpu
from jax.sharding import PartitionSpec as P

MODEL_WIDTH = 1152
HEADS = 16
HD = 72
FF = 4608
FREQ = 256
CLASSES = 1001
LATENT_SIDE = 32
PATCH_VALUES = 16
BLOCK_SIDE = 288
NEWTON = 6
STEP = 5
LANES = 256
TAIL = BLOCK_SIDE - LANES


exact_precision_flag = lax.Precision.HIGHEST
shampoo_rate = 0.5
adam_rate = 0.05
decay_rate = 0.01


def dense(operand, weight):
    return jnp.dot(operand, weight, preferred_element_type=jnp.float32)


def back_dense(gradient, weight):
    return jnp.einsum("...j,ij->...i", gradient, weight, preferred_element_type=jnp.float32)


def weight_grad(operand, gradient):
    return jnp.einsum("...i,...j->ij", operand, gradient, preferred_element_type=jnp.float32)


def total_of(inputs):
    return jnp.sum(inputs.astype(jnp.float32), axis=tuple(range(inputs.ndim - 1)))


def swish_unit(inputs):
    return inputs / (1.0 + jnp.exp(-inputs))


def swish_slope(inputs):
    sigmoid = 1.0 / (1.0 + jnp.exp(-inputs))
    return sigmoid * (1.0 + inputs * (1.0 - sigmoid))


def tanh_gelu_activation(inputs):
    return (
        0.5
        * inputs
        * (1.0 + jnp.tanh(0.7978845608028654 * (inputs + 0.044715 * inputs * inputs * inputs)))
    )


def gelu_slope(inputs):
    inner = jnp.tanh(0.7978845608028654 * (inputs + 0.044715 * inputs * inputs * inputs))
    return 0.5 * (1.0 + inner) + 0.5 * inputs * (1.0 - inner * inner) * 0.7978845608028654 * (
        1.0 + 3.0 * 0.044715 * inputs * inputs
    )


def layer_norm(inputs):
    centred = inputs - jnp.mean(inputs, -1, keepdims=True)
    inv_std = lax.rsqrt(jnp.mean(centred * centred, -1, keepdims=True) + 1e-06)
    return (centred * inv_std, inv_std)


def norm_back(gradient, normed, inv_std):
    return inv_std * (
        gradient
        - jnp.mean(gradient, -1, keepdims=True)
        - normed * jnp.mean(gradient * normed, -1, keepdims=True)
    )


def coefficients(step_ids):
    grid = jnp.arange(1000).astype(jnp.float32)
    betas = 0.0001 + (0.02 - 0.0001) * grid / 999.0
    logs = jnp.log(1.0 - betas)[None, :]
    index = jnp.arange(1000, dtype=jnp.int32)[None, :]
    beta_t = 0.0001 + (0.02 - 0.0001) * step_ids.astype(jnp.float32) / 999.0
    cumul_t = jnp.exp(jnp.sum(jnp.where(index <= step_ids[:, None], logs, 0.0), 1))
    before_t = jnp.exp(jnp.sum(jnp.where(index < step_ids[:, None], logs, 0.0), 1))
    keep_rate = jnp.sqrt(cumul_t)
    noise_rate = jnp.sqrt(1.0 - cumul_t)
    upper_log = jnp.log(beta_t)
    lower_log = jnp.log(beta_t * (1.0 - before_t) / (1.0 - cumul_t))
    mean_gap = beta_t * jnp.sqrt(before_t) / (1.0 - cumul_t) * jnp.sqrt(1.0 / cumul_t - 1.0)
    return (keep_rate, noise_rate, upper_log, lower_log, mean_gap)


def time_features(step_ids, feat_width):
    half_width = feat_width // 2
    frequencies = jnp.exp(
        -math.log(10000.0) * jnp.arange(half_width).astype(jnp.float32) / half_width
    )
    phases = step_ids.astype(jnp.float32)[:, None] * frequencies[None, :]
    return jnp.concatenate([jnp.cos(phases), jnp.sin(phases)], 1)


def position_embedding(grid_side, feat_width):
    quarter = feat_width // 4
    omegas = jnp.exp(-math.log(10000.0) * jnp.arange(quarter).astype(jnp.float32) / quarter)
    coords = jnp.arange(grid_side).astype(jnp.float32)
    angles = coords[:, None] * omegas[None, :]
    waves = jnp.concatenate([jnp.sin(angles), jnp.cos(angles)], 1)
    half_width = feat_width // 2
    rows_part = jnp.broadcast_to(waves[:, None, :], (grid_side, grid_side, half_width))
    cols_part = jnp.broadcast_to(waves[None, :, :], (grid_side, grid_side, half_width))
    return jnp.concatenate([rows_part, cols_part], 2).reshape(grid_side * grid_side, feat_width)


def patchify(latent):
    samples_n, channels, height, breadth = latent.shape
    shaped = latent.reshape(samples_n, channels, height // 2, 2, breadth // 2, 2).transpose(
        0, 2, 4, 3, 5, 1
    )
    return shaped.reshape(samples_n, height // 2 * (breadth // 2), 4 * channels)


PACK_ROWS = 656
SPLIT = 1


def pack(x):
    quarter = BLOCK_SIDE // 4
    tail = x[:, LANES:].astype(jnp.float32)
    tail = jnp.concatenate([tail[i * quarter : (i + 1) * quarter] for i in range(4)], axis=1)
    fill = jnp.zeros((PACK_ROWS - 2 * BLOCK_SIDE - quarter, LANES // 2), jnp.float32)
    tail = jnp.concatenate([tail, fill], axis=0)
    half = LANES // 2
    return x[:, :half], x[:, half:LANES], tail.astype(x.dtype)


def unpack(x):
    side, quarter = BLOCK_SIDE, BLOCK_SIDE // 4
    tail = x[2 * side :].astype(jnp.float32)[:quarter]
    tail = jnp.concatenate([tail[:, i * TAIL : (i + 1) * TAIL] for i in range(4)], axis=0)
    main = jnp.concatenate([x[:side], x[side : 2 * side]], axis=1)
    return main, tail.astype(x.dtype)


def store_packed(ref, index, x):
    a, b, c = pack(x)
    side = BLOCK_SIDE
    ref[index + (slice(0, side),)] = a
    ref[index + (slice(side, 2 * side),)] = b
    ref[index + (slice(2 * side, PACK_ROWS),)] = c


def store_pieces(ref, first, x):
    rows = [part for part in pack(x)]
    size, at, piece = PACK_ROWS // SPLIT, 0, 0
    for part in rows:
        done = 0
        while done < part.shape[0]:
            step = min(size - at, part.shape[0] - done)
            ref[first + piece, at : at + step] = part[done : done + step]
            done, at = done + step, at + step
            if at == size:
                piece, at = piece + 1, 0


def pack_blocks(blocks):
    count, side = blocks.shape[0], BLOCK_SIDE

    def body(x_ref, out_ref):
        store_packed(out_ref, (0,), x_ref[0].astype(jnp.bfloat16))

    return pl.pallas_call(
        body,
        grid=(count,),
        in_specs=[pl.BlockSpec((1, side, side), lambda i: (i, 0, 0))],
        out_specs=pl.BlockSpec((1, PACK_ROWS, LANES // 2), lambda i: (i, 0, 0)),
        out_shape=jax.ShapeDtypeStruct((count, PACK_ROWS, LANES // 2), jnp.bfloat16),
        name="pack_blocks",
    )(blocks)


def remote(source, target, send, receive, place):
    return pltpu.make_async_remote_copy(
        src_ref=source,
        dst_ref=target,
        send_sem=send,
        recv_sem=receive,
        device_id=place,
        device_id_type=pl.DeviceIdType.MESH,
    )


def signal_to(semaphore, place):
    pl.semaphore_signal(semaphore, inc=1, device_id=place, device_id_type=pl.DeviceIdType.MESH)


COLUMNS = 2
LAYERS = 4


def grid_place():
    me = lax.axis_index("dp")
    return me // COLUMNS, me % COLUMNS


EVERY = ("dp", "mp")


def exchange(items, axes, number):
    mp, dp = lax.axis_size("mp"), lax.axis_size("dp")
    n = {"dp": dp, "mp": mp, EVERY: dp * mp}[axes]

    def place(i):
        return {"dp": i // mp, "mp": i % mp} if axes == EVERY else {axes: i}

    def row(i):
        return i // mp if axes == EVERY else i

    def body(*refs):
        m = len(items)
        sources, outs, send, receive = refs[:m], refs[m : 2 * m], refs[-2], refs[-1]
        me = lax.axis_index("dp") * mp + lax.axis_index("mp") if axes == EVERY else lax.axis_index(axes)
        barrier = pltpu.get_barrier_semaphore()

        def greet(i, _):
            signal_to(barrier, place(lax.rem(me + i, n)))
            return 0

        lax.fori_loop(1, n, greet, 0)
        pl.semaphore_wait(barrier, n - 1)

        def piece(j, to):
            return sources[j].at[row(to)] if items[j][1] == "scatter" else sources[j]

        def start(i, _):
            to = lax.rem(me + i, n)
            for j in range(m):
                remote(piece(j, to), outs[j].at[me], send.at[j, i], receive.at[j, me], place(to)).start()
            return 0

        lax.fori_loop(1, n, start, 0)
        for j in range(m):
            outs[j][me] = sources[j][row(me)] if items[j][1] == "scatter" else sources[j][...]

        def finish(i, _):
            to = lax.rem(me + i, n)
            for j in range(m):
                copy = remote(piece(j, to), outs[j].at[to], send.at[j, i], receive.at[j, to], place(to))
                copy.wait_recv()
                copy.wait_send()
            return 0

        lax.fori_loop(1, n, finish, 0)

    arrays = [a for a, _ in items]
    shapes = [
        jax.ShapeDtypeStruct((n,) + (a.shape[1:] if kind == "scatter" else a.shape), a.dtype)
        for a, kind in items
    ]
    vmem = pl.BlockSpec(memory_space=pltpu.VMEM)
    return pl.pallas_call(
        body,
        in_specs=[vmem] * len(arrays),
        out_specs=[vmem] * len(arrays),
        out_shape=shapes,
        scratch_shapes=[pltpu.SemaphoreType.DMA((len(arrays), n))] * 2,
        compiler_params=pltpu.CompilerParams(
            collective_id=number, has_side_effects=True, vmem_limit_bytes=40 * 2**20
        ),
        name=f"exchange_{number}",
    )(*arrays)


def assemble(blocks, slots, first, rows, widths):
    side, cols = BLOCK_SIDE, sum(widths)

    def body(ids, *refs):
        base = 0
        for out, width in zip(refs[cols:], widths):
            parts = [part for r in refs[base : base + width] for part in unpack(r[0])]
            out[...] = jnp.concatenate(parts, axis=1)
            base += width

    def spec(c):
        return pl.BlockSpec(
            (1, PACK_ROWS, LANES // 2), lambda r, ids: (ids[first + r * cols + c], 0, 0)
        )

    return pl.pallas_call(
        body,
        grid_spec=pltpu.PrefetchScalarGridSpec(
            num_scalar_prefetch=1,
            grid=(rows,),
            in_specs=[spec(c) for c in range(cols)],
            out_specs=[pl.BlockSpec((side, side * w), lambda r, ids: (r, 0)) for w in widths],
        ),
        out_shape=[jax.ShapeDtypeStruct((rows * side, w * side), jnp.bfloat16) for w in widths],
        compiler_params=pltpu.CompilerParams(vmem_limit_bytes=40 * 2**20),
        cost_estimate=pl.CostEstimate(
            flops=0, bytes_accessed=4 * rows * cols * side * side, transcendentals=0
        ),
        name="assemble",
    )(slots, *([blocks] * cols))


def to_slots(inner, signal, d_modul, lower, slots, total):
    side = BLOCK_SIDE
    ri, widths = inner[0].shape[0] // side, [g.shape[1] // side for g in inner]
    wide = d_modul.shape[1] // side
    ci, co = sum(widths) + wide, lower[0].shape[1] // side
    heights = [g.shape[0] // side for g in lower]
    ro = sum(heights)
    steps = ri + ro
    n = len(inner) + 2 + len(lower)
    batch = signal.shape[0]
    signal = signal.reshape(batch, ri, side).transpose(1, 0, 2)

    def body(ids, *refs):
        sources, (out, buf, sem) = refs[:n], refs[-3:]
        s = pl.program_id(0)
        half = lax.rem(s, 2)

        def drain(which, count):
            for c in range(count):
                pltpu.make_async_copy(buf.at[which, c], out.at[0], sem.at[which, c]).wait()

        def send(source, count, base, first=0):
            for c in range(count):
                store_packed(buf, (half, first + c), source[:, c * side : (c + 1) * side])
                pltpu.make_async_copy(
                    buf.at[half, first + c], out.at[ids[base + c]], sem.at[half, first + c]
                ).start()

        @pl.when(jnp.logical_and(s >= 2, s - 2 < ri))
        def _():
            drain(half, ci)

        @pl.when(s - 2 >= ri)
        def _():
            drain(half, co)

        @pl.when(s < ri)
        def _():
            first = 0
            for source, width in zip(sources, widths):
                send(source, width, s * ci + first, first)
                first += width
            send(outer(refs[len(inner)][0], refs[len(inner) + 1][...]).astype(jnp.bfloat16), wide, s * ci + first, first)

        base = ri
        for source, height in zip(sources[len(inner) + 2 :], heights):

            @pl.when(jnp.logical_and(s >= base, s < base + height))
            def _():
                send(source, co, ri * ci + (s - ri) * co)

            base += height

        @pl.when(s == steps - 1)
        def _():
            drain(1 - half, co)
            drain(half, co)

    extra, aliases = [], {}
    if total != ri * ci + ro * co:
        extra = [jnp.zeros((total, PACK_ROWS, LANES // 2), jnp.bfloat16)]
        aliases = {1 + n: 0}
    specs = [
        pl.BlockSpec((side, w * side), lambda s, ids: (jnp.minimum(s, ri - 1), 0)) for w in widths
    ]
    specs += [
        pl.BlockSpec((1, batch, side), lambda s, ids: (jnp.minimum(s, ri - 1), 0, 0)),
        pl.BlockSpec(d_modul.shape, lambda s, ids: (0, 0)),
    ]
    base = ri
    for height in heights:
        specs.append(
            pl.BlockSpec(
                (side, co * side),
                lambda s, ids, base=base, height=height: (jnp.clip(s - base, 0, height - 1), 0),
            )
        )
        base += height
    return pl.pallas_call(
        body,
        grid_spec=pltpu.PrefetchScalarGridSpec(
            num_scalar_prefetch=1,
            grid=(steps,),
            in_specs=specs + [pl.BlockSpec(memory_space=pl.ANY)] * len(extra),
            out_specs=pl.BlockSpec(memory_space=pl.ANY),
            scratch_shapes=[
                pltpu.VMEM((2, max(ci, co), PACK_ROWS, LANES // 2), jnp.bfloat16),
                pltpu.SemaphoreType.DMA((2, max(ci, co))),
            ],
        ),
        out_shape=jax.ShapeDtypeStruct((total, PACK_ROWS, LANES // 2), jnp.bfloat16),
        compiler_params=pltpu.CompilerParams(vmem_limit_bytes=40 * 2**20),
        cost_estimate=pl.CostEstimate(
            flops=0, bytes_accessed=4 * (ri * ci + ro * co) * side * side, transcendentals=0
        ),
        input_output_aliases=aliases,
        name="to_slots",
    )(slots, *inner, signal, d_modul, *lower, *extra)


CHUNK = 64


def mean_of(x):
    return jnp.sum(x, axis=-1, keepdims=True) * (1.0 / x.shape[-1])


def norm_rows(x):
    centred = x - mean_of(x)
    inv_std = lax.rsqrt(mean_of(centred * centred) + 1e-06)
    return centred * inv_std, inv_std


def norm_rows_back(gradient, normed, inv_std):
    return inv_std * (gradient - mean_of(gradient) - normed * mean_of(gradient * normed))


def column_sum(x):
    return jnp.sum(x, axis=0, keepdims=True)


def times(a, b):
    return jnp.dot(a, b, preferred_element_type=jnp.float32)


def times_flipped(a, b):
    return lax.dot_general(a, b, (((1,), (1,)), ((), ())), preferred_element_type=jnp.float32)


def stage(number, inputs, outputs, shared, make):
    rows, width = inputs[0].shape[1], MODEL_WIDTH
    pieces = rows // CHUNK
    n_in, n_out = len(inputs), len(outputs)

    def body(*refs):
        ins, outs = refs[:n_in], refs[n_in : n_in + n_out]
        rest = refs[n_in + n_out :]
        share = None
        if shared:
            share, rest = rest[0], rest[1:]
        a_out, a_in, b_out, b_in, c_out, c_in, total, near, far = rest
        me = lax.axis_index("mp")
        core = me + 1 - 2 * lax.rem(me, 2)
        across = lax.rem(me + 2, 4)
        other = lax.rem(core + 2, 4)
        to_core, to_across = {"mp": core}, {"mp": across}
        partial, own, after, side = make(ins, outs, share)
        barrier = pltpu.get_barrier_semaphore()
        signal_to(barrier, to_core)
        signal_to(barrier, to_across)
        pl.semaphore_wait(barrier, 2)

        copy_a = remote(a_out, a_in, near.at[0, 0], near.at[1, 0], to_core)
        copy_c = remote(c_out, c_in, near.at[0, 1], near.at[1, 1], to_core)

        def piece(i):
            return pl.ds(i * CHUNK, CHUNK)

        def copy_b(i):
            return remote(
                b_out.at[piece(i)], b_in.at[piece(i)], far.at[0, i], far.at[1, i], to_across
            )

        def share_far(group, i):
            part = share.at[group, piece(i)]
            return remote(part, part, far.at[2, i], far.at[3, i], to_across)

        def share_near(group, i):
            part = share.at[group, piece(i)]
            return remote(part, part, near.at[2, i], near.at[3, i], to_core)

        def pass_near(group, i):
            part = share.at[group, piece(i)]
            return remote(part, part, near.at[4, i], near.at[5, i], to_core)

        a_out[...] = partial(other).astype(jnp.bfloat16)
        copy_a.start()
        total[...] = partial(across)
        copy_a.wait_recv()
        for i in range(pieces):
            at = piece(i)
            b_out[at] = (total[at] + a_in[at].astype(jnp.float32)).astype(jnp.bfloat16)
            copy_b(i).start()
        c_out[...] = partial(core).astype(jnp.bfloat16)
        copy_c.start()
        total[...] = partial(me)
        copy_c.wait_recv()
        for i in range(pieces):
            at = piece(i)
            if side and not shared:
                side(i)
            copy_b(i).wait_recv()
            result = own(
                i * CHUNK, total[at] + c_in[at].astype(jnp.float32) + b_in[at].astype(jnp.float32)
            )
            if shared:
                share[me, at] = result
                share_far(me, i).start()
                share_near(me, i).start()
                if side:
                    side(i)
        if shared:
            for i in range(pieces):
                after(me, i * CHUNK)
            for i in range(pieces):
                share_near(core, i).wait_recv()
                after(core, i * CHUNK)
            for i in range(pieces):
                share_far(across, i).wait_recv()
                pass_near(across, i).start()
                after(across, i * CHUNK)
                if i > 0:
                    pass_near(other, i - 1).wait_recv()
                    after(other, (i - 1) * CHUNK)
            pass_near(other, pieces - 1).wait_recv()
            after(other, (pieces - 1) * CHUNK)
        copy_a.wait_send()
        copy_c.wait_send()
        for i in range(pieces):
            copy_b(i).wait_send()
            if shared:
                share_far(me, i).wait_send()
                share_near(me, i).wait_send()
                pass_near(across, i).wait_send()

    vmem = pl.BlockSpec(memory_space=pltpu.VMEM)
    out_shape = [jax.ShapeDtypeStruct(shape, dtype) for shape, dtype in outputs]
    if shared:
        out_shape.append(jax.ShapeDtypeStruct((4, rows, width), jnp.bfloat16))
    landing = pltpu.VMEM((rows, width), jnp.bfloat16)
    return pl.pallas_call(
        body,
        in_specs=[vmem] * n_in,
        out_specs=[vmem] * len(out_shape),
        out_shape=out_shape,
        scratch_shapes=[landing] * 6
        + [
            pltpu.VMEM((rows, width), jnp.float32),
            pltpu.SemaphoreType.DMA((6, max(pieces, 2))),
            pltpu.SemaphoreType.DMA((4, pieces)),
        ],
        compiler_params=pltpu.CompilerParams(
            collective_id=number, has_side_effects=True, vmem_limit_bytes=56 * 2**20
        ),
        name=f"stage_{number}",
    )(*inputs)


def attention_out_stage(mixed, w_o, w_up, start, rows, up_bias):
    n, width, f32 = mixed.shape[1], MODEL_WIDTH, jnp.float32

    def make(ins, outs, share):
        mixed_ref, w_o_ref, w_up_ref, start_ref, rows_ref, up_ref = ins
        attn_ref, middle_ref, hidden_ref, active_ref = outs

        def partial(group):
            return times(mixed_ref[group], w_o_ref[...])

        def own(at, total):
            at = slice(at, at + CHUNK)
            attn = total + rows_ref[0:1]
            middle = start_ref[at] + rows_ref[1:2] * attn
            attn_ref[at] = attn
            middle_ref[at] = middle
            normed, _ = norm_rows(middle)
            return (normed * (1.0 + rows_ref[2:3]) + rows_ref[3:4]).astype(jnp.bfloat16)

        def after(group, at):
            at = slice(at, at + CHUNK)
            hidden = times(share[group, at], w_up_ref[...]) + up_ref[...]
            hidden_ref[group, at] = hidden
            active_ref[group, at] = tanh_gelu_activation(hidden).astype(jnp.bfloat16)

        return partial, own, after, None

    inner = w_up.shape[1]
    return stage(
        9,
        [mixed, w_o, w_up, start, rows, up_bias],
        [((n, width), f32), ((n, width), f32), ((4, n, inner), f32), ((4, n, inner), jnp.bfloat16)],
        True,
        make,
    )


def loss_stage(active, w_down, hidden, middle, rows, target, w_pred, w_raw, head_bias, facts):
    n, width, f32, bf16 = active.shape[1], MODEL_WIDTH, jnp.float32, jnp.bfloat16
    inner = active.shape[2]

    def make(ins, outs, share):
        active_ref, w_ref, hidden_ref, middle_ref, rows_ref, target_ref, wp_ref, wr_ref, bias_ref, facts_ref = ins
        d_final_ref, head_in_ref, d_pred_ref, d_raw_ref, sums_ref, loss_ref, d_hidden_ref, up_sum_ref = outs
        sums_ref[...] = jnp.zeros_like(sums_ref)
        loss_ref[...] = jnp.zeros_like(loss_ref)
        up_sum_ref[...] = jnp.zeros_like(up_sum_ref)

        def partial(group):
            return times(active_ref[group], w_ref[...])

        def own(at, total):
            at = slice(at, at + CHUNK)
            branch = total + rows_ref[0:1]
            gate, fscale = rows_ref[1:2], 1.0 + rows_ref[2:3]
            normed, inv_std = norm_rows(middle_ref[at] + gate * branch)
            head_in = (normed * fscale + rows_ref[3:4]).astype(bf16)
            head_in_ref[at] = head_in
            upper, lower, gap = facts_ref[0:1], facts_ref[1:2], facts_ref[2:3]
            weight, share_of = facts_ref[3:4], facts_ref[4:5]
            error = times(head_in, wp_ref[...]) + bias_ref[0:1] - target_ref[at]
            fraction = (times(head_in, wr_ref[...]) + bias_ref[1:2] + 1.0) / 2.0
            log_var = fraction * upper + (1.0 - fraction) * lower
            gap = gap * error
            ratio = jnp.exp(lower - log_var)
            spread = gap * gap * jnp.exp(-log_var)
            diverge = 0.5 * (-1.0 + log_var - lower + ratio + spread)
            cells = 1.0 / (n * error.shape[1])
            per_bit = cells / math.log(2.0)
            loss_ref[...] += weight * column_sum(error * error * cells + diverge * per_bit)
            d_pred = (share_of * (2.0 * cells) * error).astype(bf16)
            d_raw = (
                share_of * per_bit * 0.25 * (upper - lower) * (1.0 - ratio - spread)
            ).astype(bf16)
            d_pred_ref[at] = d_pred
            d_raw_ref[at] = d_raw
            d_head = times_flipped(d_pred, wp_ref[...]) + times_flipped(d_raw, wr_ref[...])
            d_final = norm_rows_back(d_head * fscale, normed, inv_std)
            d_final_ref[at] = d_final
            d_branch = (gate * d_final).astype(bf16)
            sums_ref[0:1] += column_sum(d_head)
            sums_ref[1:2] += column_sum(d_head * normed)
            sums_ref[2:3] += column_sum(d_final * branch)
            sums_ref[3:4] += column_sum(d_branch.astype(f32))
            return d_branch

        def after(group, at):
            at = slice(at, at + CHUNK)
            d_active = times_flipped(share[group, at], w_ref[...])
            d_hidden = (d_active * gelu_slope(hidden_ref[group, at])).astype(bf16)
            d_hidden_ref[group, at] = d_hidden
            up_sum_ref[...] += column_sum(d_hidden.astype(f32))

        return partial, own, after, None

    half = w_pred.shape[1]
    return stage(
        10,
        [active, w_down, hidden, middle, rows, target, w_pred, w_raw, head_bias, facts],
        [
            ((n, width), f32),
            ((n, width), bf16),
            ((n, half), bf16),
            ((n, half), bf16),
            ((4, width), f32),
            ((1, half), f32),
            ((4, n, inner), bf16),
            ((1, inner), f32),
        ],
        True,
        make,
    )


def gradient_part(out_ref, a_ref, b_ref, i):
    width = a_ref.shape[2]
    step = max(width // 512, 1) * 128
    at = slice(min(i * step, width), width if i == 3 else min((i + 1) * step, width))
    if at.start < at.stop:
        tokens = a_ref.shape[0] * a_ref.shape[1]
        a = a_ref[:, :, at].reshape(tokens, at.stop - at.start)
        b = b_ref[...].reshape(tokens, b_ref.shape[2])
        out_ref[at] = outer(a, b).astype(jnp.bfloat16)


def middle_back_stage(d_hidden, w_up, w_o, middle, d_final, attn, rows, active, d_branch):
    n, width, f32, bf16 = d_hidden.shape[1], MODEL_WIDTH, jnp.float32, jnp.bfloat16

    def make(ins, outs, share):
        (
            d_hidden_ref, w_up_ref, w_o_ref, middle_ref, d_final_ref, attn_ref, rows_ref, active_ref,
            d_branch_ref,
        ) = ins
        d_middle_ref, sums_ref, d_mixed_ref, g_down_ref = outs
        sums_ref[...] = jnp.zeros_like(sums_ref)

        def partial(group):
            return times_flipped(d_hidden_ref[group], w_up_ref[...])

        def own(at, total):
            at = slice(at, at + CHUNK)
            normed, inv_std = norm_rows(middle_ref[at])
            d_middle = d_final_ref[at] + norm_rows_back(total * (1.0 + rows_ref[0:1]), normed, inv_std)
            d_middle_ref[at] = d_middle
            d_attn = (rows_ref[1:2] * d_middle).astype(bf16)
            sums_ref[0:1] += column_sum(total)
            sums_ref[1:2] += column_sum(total * normed)
            sums_ref[2:3] += column_sum(d_middle * attn_ref[at])
            sums_ref[3:4] += column_sum(d_attn.astype(f32))
            return d_attn

        def after(group, at):
            at = slice(at, at + CHUNK)
            d_mixed_ref[group, at] = times_flipped(share[group, at], w_o_ref[...]).astype(bf16)

        def side(i):
            gradient_part(g_down_ref, active_ref, d_branch_ref, i)

        return partial, own, after, side

    return stage(
        11,
        [d_hidden, w_up, w_o, middle, d_final, attn, rows, active, d_branch],
        [
            ((n, width), f32),
            ((4, width), f32),
            ((4, n, w_o.shape[0]), bf16),
            ((active.shape[2], width), bf16),
        ],
        True,
        make,
    )


def start_back_stage(d_proj, w_qkv, start, d_middle, rows, attn_in, mlp_in, d_hidden, mixed, d_attn):
    n, width, f32, bf16 = d_proj.shape[1], MODEL_WIDTH, jnp.float32, jnp.bfloat16

    def make(ins, outs, share):
        d_proj_ref, w_ref, start_ref, d_middle_ref, rows_ref = ins[:5]
        attn_in_ref, mlp_in_ref, d_hidden_ref, mixed_ref, d_attn_ref = ins[5:]
        d_start_ref, sums_ref, g_qkv_ref, g_up_ref, g_outp_ref = outs
        sums_ref[...] = jnp.zeros_like(sums_ref)

        def partial(group):
            return times_flipped(d_proj_ref[group], w_ref[...])

        def own(at, total):
            at = slice(at, at + CHUNK)
            normed, inv_std = norm_rows(start_ref[at])
            d_start = d_middle_ref[at] + norm_rows_back(total * (1.0 + rows_ref[0:1]), normed, inv_std)
            d_start = d_start.astype(bf16)
            d_start_ref[at] = d_start
            sums_ref[0:1] += column_sum(total)
            sums_ref[1:2] += column_sum(total * normed)
            sums_ref[2:3] += column_sum(d_start.astype(f32))

        def side(i):
            gradient_part(g_up_ref, mlp_in_ref, d_hidden_ref, i)
            gradient_part(g_qkv_ref, attn_in_ref, d_proj_ref, i)
            gradient_part(g_outp_ref, mixed_ref, d_attn_ref, i)

        return partial, own, None, side

    return stage(
        12,
        [d_proj, w_qkv, start, d_middle, rows, attn_in, mlp_in, d_hidden, mixed, d_attn],
        [
            ((n, width), bf16),
            ((3, width), f32),
            ((width, d_proj.shape[2]), bf16),
            ((width, d_hidden.shape[2]), bf16),
            ((mixed.shape[2], width), bf16),
        ],
        False,
        make,
    )


AHEAD = 4
CROSS_LATE = 1


class Push:
    def __init__(self, source, landing, send, receive, n, me, place, row=None):
        self.source, self.landing, self.send, self.receive = source, landing, send, receive
        self.n, self.me, self.place, self.row = n, me, place, row

    def _copy(self, i, sender, to):
        source = self.source if self.row is None else self.source.at[self.row(to)]
        return remote(
            source, self.landing.at[sender], self.send.at[i], self.receive.at[sender], self.place(to)
        )

    def start(self):
        def one(i, _):
            self._copy(i, self.me, lax.rem(self.me + i, self.n)).start()
            return 0

        lax.fori_loop(1, self.n, one, 0)
        own = self.source[...] if self.row is None else self.source[self.row(self.me)]
        self.landing[self.me] = own

    def wait(self):
        def one(i, _):
            to = lax.rem(self.me + i, self.n)
            copy = self._copy(i, to, to)
            copy.wait_recv()
            copy.wait_send()
            return 0

        lax.fori_loop(1, self.n, one, 0)


def in_parts(first, last, step, between):
    for at, work in between:
        lax.fori_loop(first, at, step, 0)
        work()
        first = at
    lax.fori_loop(first, last, step, 0)


def head_body(
    x_ref, tf_ref, facts_ref, shared_ref, tables_ref, fada_ref, b1_ref, b2_ref,
    out_ref, tf_all, facts_all, shared_all, first_t_ref, first_s_ref, cond_ref, signal_ref,
    signal_all, mod_ref,
    packed, tf_land, hot_buf, first_s, first_s_all, signal_own, mod_own, mod_land, local_sem, up_sem, down_sem, side_sem,
    up_other, down_other, recv_sem, send, receive,
):
    count, ways, f32, bf16 = packed.shape[0], LAYERS * COLUMNS, jnp.float32, jnp.bfloat16
    batch, cols = mod_ref.shape[0], tables_ref.shape[0]
    late = count - CROSS_LATE
    z, y = grid_place()
    me = lax.axis_index("dp")

    def place(i):
        return {"dp": i}

    barrier = pltpu.get_barrier_semaphore()

    def greet(i, _):
        signal_to(barrier, place(lax.rem(me + i, ways)))
        return 0

    lax.fori_loop(1, ways, greet, 0)
    pl.semaphore_wait(barrier, ways - 1)

    def push(j, source, landing, row=None):
        return Push(source, landing, send.at[j], receive.at[j], ways, me, place, row)

    first = [
        push(0, tf_ref, tf_land),
        push(1, facts_ref, facts_all),
        push(2, shared_ref, shared_all),
    ]
    for p in first:
        p.start()

    peer = {"dp": z * COLUMNS + 1 - y}
    above = {"dp": jnp.minimum(z + 1, LAYERS - 1) * COLUMNS + y}
    below = {"dp": jnp.maximum(z - 1, 0) * COLUMNS + y}

    def block(layer, column, k):
        return out_ref.at[(layer * COLUMNS + column) * count + k]

    def move(source, layer, k, sem, to):
        return remote(source, block(layer, y, k), sem.at[layer, k], recv_sem.at[layer, y, k], to)

    def move_other(layer, k, sem, to):
        here = block(layer, 1 - y, k)
        return remote(here, here, sem.at[layer, k - late], recv_sem.at[layer, 1 - y, k], to)

    def arrival(layer, column, k):
        here = block(layer, column, k)
        return remote(here, here, side_sem.at[0, 0], recv_sem.at[layer, column, k], peer)

    def send_own(i, _):
        base = count - SPLIT * (i + 1)
        store_pieces(packed, base, x_ref[x_ref.shape[0] - 1 - i].astype(bf16))
        for j in range(SPLIT - 1, -1, -1):
            k = base + j
            own = packed.at[k]
            move(own, z, k, side_sem, peer).start()

            @pl.when(z < LAYERS - 1)
            def _():
                move(own, z, k, up_sem, above).start()

            @pl.when(z > 0)
            def _():
                move(own, z, k, down_sem, below).start()

            pltpu.make_async_copy(own, block(z, y, k), local_sem.at[k]).start()
        return 0

    def pass_own(k):
        arrival(z, 1 - y, k).wait_recv()

        @pl.when(z < LAYERS - 1)
        def _():
            move_other(z, k, up_other, above).start()

        @pl.when(z > 0)
        def _():
            move_other(z, k, down_other, below).start()

    def run_hop(hop):
        def pass_on(i, _):
            k = count - 1 - i

            @pl.when(z >= hop)
            def _():
                layer = z - hop
                arrival(layer, y, k).wait_recv()

                @pl.when(z < LAYERS - 1)
                def _():
                    move(block(layer, y, k), layer, k, up_sem, above).start()

                @pl.when(k < late)
                def _():
                    move(block(layer, y, k), layer, k, side_sem, peer).start()

            @pl.when(z + hop < LAYERS)
            def _():
                layer = z + hop
                arrival(layer, y, k).wait_recv()

                @pl.when(z > 0)
                def _():
                    move(block(layer, y, k), layer, k, down_sem, below).start()

                @pl.when(k < late)
                def _():
                    move(block(layer, y, k), layer, k, side_sem, peer).start()

            return 0

        lax.fori_loop(0, count, pass_on, 0)
        for k in range(late, count):

            @pl.when(z >= hop)
            def _():
                layer = z - hop
                arrival(layer, 1 - y, k).wait_recv()

                @pl.when(z < LAYERS - 1)
                def _():
                    move_other(layer, k, up_other, above).start()

            @pl.when(z + hop < LAYERS)
            def _():
                layer = z + hop
                arrival(layer, 1 - y, k).wait_recv()

                @pl.when(z > 0)
                def _():
                    move_other(layer, k, down_other, below).start()

    t2_row = PATCH_VALUES + FREQ
    class_row = t2_row + MODEL_WIDTH
    second = push(3, first_s, first_s_all)
    third = [
        push(4, signal_own, signal_all, lambda to: to),
        push(5, mod_own, mod_land, lambda to: to),
    ]

    def first_row():
        for p in first:
            p.wait()
        for i in range(ways):
            tf_all[i * batch : (i + 1) * batch] = tf_land[i][:batch]
        first_t = times_flipped(tf_all[...].astype(bf16), tables_ref[:, PATCH_VALUES:t2_row]) + b1_ref[...]
        first_t_ref[...] = first_t
        first_s[:, :cols] = swish_unit(first_t).astype(bf16)
        second.start()

    def class_part():
        for i in range(ways):
            row = lax.broadcasted_iota(jnp.int32, (batch, CLASSES), 1)
            hot = (row == facts_all[i][:batch, 0:1].astype(jnp.int32)).astype(f32)
            hot_buf[i * batch : (i + 1) * batch] = hot
        cond_ref[...] = (
            times_flipped(hot_buf[...].astype(bf16), tables_ref[:, class_row:]) + b2_ref[...]
        )

    def second_row():
        second.wait()
        first_s_ref[...] = jnp.concatenate([first_s_all[i][:, :cols] for i in range(ways)], axis=1)
        cond = cond_ref[...] + times_flipped(first_s_ref[...], tables_ref[:, t2_row:class_row])
        cond_ref[...] = cond
        signal = swish_unit(cond).astype(bf16)
        signal_ref[...] = signal
        signal = signal.astype(f32)
        for i in range(ways):
            signal_own[i, :batch, :cols] = signal[i * batch : (i + 1) * batch]
        third[0].start()

    def modulation():
        mod = times(signal_ref[...], fada_ref[...])
        half = mod.shape[1] // 2
        for i in range(ways):
            mod_own[i, :batch] = mod[i * batch : (i + 1) * batch, :half]
            mod_own[i, batch:] = mod[i * batch : (i + 1) * batch, half:]
        third[1].start()

    own_count = x_ref.shape[0]
    third_of = -(-own_count // 3)
    in_parts(0, own_count, send_own, [(third_of, first_row), (2 * third_of, class_part)])
    second_row()
    modulation()
    for k in range(late, count):
        pass_own(k)
    run_hop(1)
    run_hop(2)
    for p in third:
        p.wait()
    mod = jnp.sum(mod_land[...], axis=0)
    mod_ref[...] = jnp.concatenate([mod[:batch], mod[batch:]], axis=1)
    run_hop(3)

    def finish(k, _):
        pltpu.make_async_copy(packed.at[k], block(z, y, k), local_sem.at[k]).wait()
        for layer in range(LAYERS):

            @pl.when(k < late)
            def _():
                arrival(layer, 1 - y, k).wait_recv()

            @pl.when((k < late) | (layer == z))
            def _():
                move(block(layer, y, k), layer, k, side_sem, peer).wait_send()

            @pl.when((z < LAYERS - 1) & (layer <= z))
            def _():
                move(block(layer, y, k), layer, k, up_sem, above).wait_send()

            @pl.when((z > 0) & (layer >= z))
            def _():
                move(block(layer, y, k), layer, k, down_sem, below).wait_send()

        return 0

    lax.fori_loop(0, count, finish, 0)
    for k in range(late, count):
        for layer in range(LAYERS):

            @pl.when((z < LAYERS - 1) & (layer <= z))
            def _():
                move_other(layer, k, up_other, above).wait_send()

            @pl.when((z > 0) & (layer >= z))
            def _():
                move_other(layer, k, down_other, below).wait_send()


def head(blocks, time_freq, facts, shared, tables, w_fada, b1, b2):
    ways, f32, bf16 = LAYERS * COLUMNS, jnp.float32, jnp.bfloat16
    count = blocks.shape[0] * SPLIT
    batch, cols, rows = time_freq.shape[0], tables.shape[0], time_freq.shape[0] * ways
    fada = w_fada.shape[1]
    piece = (PACK_ROWS // SPLIT, LANES // 2)
    time_freq = jnp.pad(time_freq, ((0, 8 - batch), (0, 0)))
    facts = jnp.pad(facts, ((0, 8 - batch), (0, 0)))
    shared = jnp.pad(shared.T, ((0, 0), (0, LANES - cols)))
    dma = pltpu.SemaphoreType.DMA
    vmem, anywhere = pl.BlockSpec(memory_space=pltpu.VMEM), pl.BlockSpec(memory_space=pl.ANY)
    shape = jax.ShapeDtypeStruct
    out = pl.pallas_call(
        head_body,
        in_specs=[vmem] * 8,
        out_specs=[anywhere] + [vmem] * 9,
        out_shape=[
            shape((count * ways,) + piece, bf16),
            shape((rows, time_freq.shape[1]), f32),
            shape((ways,) + facts.shape, f32),
            shape((ways,) + shared.shape, bf16),
            shape((rows, cols), f32),
            shape((rows, ways * cols), bf16),
            shape((rows, cols), f32),
            shape((rows, cols), bf16),
            shape((ways, 8, LANES), f32),
            shape((batch, fada), f32),
        ],
        scratch_shapes=[
            pltpu.VMEM((count,) + piece, bf16),
            pltpu.VMEM((ways,) + time_freq.shape, f32),
            pltpu.VMEM((rows, CLASSES), f32),
            pltpu.VMEM((rows, LANES), bf16),
            pltpu.VMEM((ways, rows, LANES), bf16),
            pltpu.VMEM((ways, 8, LANES), f32),
            pltpu.VMEM((ways, 2 * batch, fada // 2), f32),
            pltpu.VMEM((ways, 2 * batch, fada // 2), f32),
            dma((count,)),
            dma((LAYERS, count)),
            dma((LAYERS, count)),
            dma((LAYERS, count)),
            dma((LAYERS, CROSS_LATE)),
            dma((LAYERS, CROSS_LATE)),
            dma((LAYERS, COLUMNS, count)),
            dma((6, ways)),
            dma((6, ways)),
        ],
        compiler_params=pltpu.CompilerParams(
            collective_id=0, has_side_effects=True, vmem_limit_bytes=48 * 2**20
        ),
        name="head",
    )(blocks, time_freq, facts, shared, tables, w_fada, b1, b2)
    blocks, time_freq, facts, shared, first_t, first_s, cond, signal, signal_all, mod = out
    blocks = blocks.reshape(-1, PACK_ROWS, LANES // 2)
    return (
        blocks, time_freq, facts[:, :batch], shared[:, :, :cols].transpose(0, 2, 1), first_t, first_s, cond, signal,
        signal_all[:, :batch, :cols], mod,
    )


def outer(a, b):
    return lax.dot_general(a, b, (((0,), (0,)), ((), ())), preferred_element_type=jnp.float32)


def tail_body(
    x_ref, early_ref, small_ref, bias_ref, fada_ref, tables_ref, cond_ref, first_t_ref,
    signal_ref, first_s_ref, tf_ref, facts_ref,
    out_ref, g_cond_ref, g_head_ref, slice_ref, side_ref, mod_sum_ref, columns_all, last_all,
    side_buf, up_buf, down_buf, other_buf, up_other, down_other, early_land, early_mp, small_land,
    bias_land, dsig_all, first_own, first_land, small_own, small_mp, side_own, side_mp, fmod_all, columns_own,
    last_own, hot_buf,
    side_send, line_send, side_recv, up_recv, down_recv, other_send, other_up, other_down,
    send_all, recv_all, send_dp, recv_dp, send_mp, recv_mp,
):
    f32, bf16 = jnp.float32, jnp.bfloat16
    count, ways, mp = out_ref.shape[0], LAYERS * COLUMNS, lax.axis_size("mp")
    batch, cols = facts_ref.shape[1], tables_ref.shape[0]
    everyone = ways * mp
    late = count - CROSS_LATE
    z, y = grid_place()
    my_dp, my_mp = lax.axis_index("dp"), lax.axis_index("mp")
    me = my_dp * mp + my_mp

    def place_all(i):
        return {"dp": i // mp, "mp": lax.rem(i, mp)}

    barrier = pltpu.get_barrier_semaphore()

    def greet(i, _):
        signal_to(barrier, place_all(lax.rem(me + i, everyone)))
        return 0

    lax.fori_loop(1, everyone, greet, 0)
    pl.semaphore_wait(barrier, everyone - 1)

    def push_all(j, source, landing, row=None):
        return Push(source, landing, send_all.at[j], recv_all.at[j], everyone, me, place_all, row)

    def push_dp(j, source, landing, row=None):
        return Push(
            source, landing, send_dp.at[j], recv_dp.at[j], ways, my_dp, lambda i: {"dp": i}, row
        )

    def push_mp(j, source, landing):
        return Push(source, landing, send_mp.at[j], recv_mp.at[j], mp, my_mp, lambda i: {"mp": i})

    first = [push_dp(4, early_ref, early_land, lambda to: to)]
    early_pass = push_mp(2, early_land, early_mp)
    second = [push_dp(0, small_ref, small_land, lambda to: to), push_dp(1, bias_ref, bias_land)]
    third = push_dp(2, first_own, first_land, lambda to: to)
    fifth = push_dp(3, columns_own, columns_all)
    fourth = [push_mp(0, small_own, small_mp), push_mp(1, side_own, side_mp)]

    peer = {"dp": z * COLUMNS + 1 - y}
    above = {"dp": jnp.minimum(z + 1, LAYERS - 1) * COLUMNS + y}
    below = {"dp": jnp.maximum(z - 1, 0) * COLUMNS + y}

    def slot(layer, column, k):
        return (layer * COLUMNS + column) * count + k

    def across(layer, k):
        return remote(
            x_ref.at[slot(layer, 1 - y, k)],
            side_buf.at[layer, k],
            side_send.at[layer, k],
            side_recv.at[layer, k],
            peer,
        )

    def cross_late(k):
        return remote(
            other_buf.at[z, k - late],
            side_buf.at[z, k],
            side_send.at[z, k],
            side_recv.at[z, k],
            peer,
        )

    def upward(layer, k):
        return remote(
            side_buf.at[layer, k], up_buf.at[layer, k], line_send.at[layer, k], up_recv.at[layer, k], above
        )

    def downward(layer, k):
        return remote(
            side_buf.at[layer, k], down_buf.at[layer, k], line_send.at[layer, k], down_recv.at[layer, k], below
        )

    def upward_other(layer, k):
        j = k - late
        return remote(
            other_buf.at[layer, j], up_other.at[layer, j], other_send.at[layer, j], other_up.at[layer, j], above
        )

    def downward_other(layer, k):
        j = k - late
        return remote(
            other_buf.at[layer, j], down_other.at[layer, j], other_send.at[layer, j], other_down.at[layer, j], below
        )

    def own_part(layer, k):
        return x_ref[slot(layer, y, k)].astype(f32)

    def pair_sum(layer, k):
        across(layer, k).wait_recv()
        return own_part(layer, k) + side_buf[layer, k].astype(f32)

    at_end = (z == 0) | (z == LAYERS - 1)

    def turn(t):
        part, within = t // late, lax.rem(t, late)
        end_layer = jnp.where(z == 0, LAYERS - 1 - part, part)
        pair = t - late
        near = jnp.where(lax.rem(pair, 2) == 0, z + 1, z - 1)
        inner_layer = jnp.where(part == 0, jnp.where(z == 1, LAYERS - 1, 0), jnp.where(part == 3, z, near))
        inner_k = jnp.where((part == 0) | (part == 3), within, pair // 2)
        return jnp.where(at_end, end_layer, inner_layer), jnp.where(at_end, within, inner_k)

    def issue(t):
        @pl.when(t < LAYERS * late)
        def _():
            across(*turn(t)).start()

    for t in range(AHEAD):
        issue(jnp.int32(t))
    for p in first + second:
        p.start()

    def along(total, stage_ref, layer, k, copy, landed, begins):
        @pl.when(jnp.logical_not(begins))
        def _():
            copy(layer, k).wait_recv()
            stage_ref[...] = (total + landed[...].astype(f32)).astype(bf16)

        @pl.when(begins)
        def _():
            stage_ref[...] = total.astype(bf16)

        copy(layer, k).start()

    bottom, top = z == 0, z == LAYERS - 1

    def run_late(hop):
        for k in range(late, count):
            j = k - late

            @pl.when(z + hop < LAYERS)
            def _():
                layer = z + hop
                along(
                    own_part(layer, k), side_buf.at[layer, k], layer, k, upward, up_buf.at[layer, k], bottom
                )
                along(
                    x_ref[slot(layer, 1 - y, k)].astype(f32),
                    other_buf.at[layer, j], layer, k, upward_other, up_other.at[layer, j], bottom,
                )

            @pl.when(z >= hop)
            def _():
                layer = z - hop
                along(
                    own_part(layer, k), side_buf.at[layer, k], layer, k, downward, down_buf.at[layer, k], top
                )
                along(
                    x_ref[slot(layer, 1 - y, k)].astype(f32),
                    other_buf.at[layer, j], layer, k, downward_other, down_other.at[layer, j], top,
                )

    def step(t, _):
        issue(t + AHEAD)
        layer, k = turn(t)

        @pl.when(layer > z)
        def _():
            along(
                pair_sum(layer, k), side_buf.at[layer, k], layer, k, upward, up_buf.at[layer, k], bottom
            )

        @pl.when(layer < z)
        def _():
            along(
                pair_sum(layer, k), side_buf.at[layer, k], layer, k, downward, down_buf.at[layer, k], top
            )

        return 0

    t2_row = PATCH_VALUES + FREQ
    class_row = t2_row + MODEL_WIDTH
    held = {"shared": jnp.zeros((1, 1), f32)}

    def square(x):
        return jnp.sum(jnp.sum(x * x, axis=1, keepdims=True), axis=0, keepdims=True)

    def add_shared(x):
        held["shared"] = held["shared"] + square(x)

    def pass_early():
        for p in first:
            p.wait()
        early_pass.start()

    def signal_back():
        early_pass.wait()
        lines = fmod_all.shape[1] // 128
        for i in range(everyone):
            here = early_mp[i % mp, i // mp].astype(f32)
            for j in range(lines):
                fmod_all[i : i + 1, j * 128 : (j + 1) * 128] = here[j : j + 1]
        for i in range(ways):
            here = early_mp[0, i].astype(f32)[24:]
            for j in range(1, mp):
                here = here + early_mp[j, i].astype(f32)[24:]
            dsig_all[i * batch : (i + 1) * batch, :128] = here[:batch]
            dsig_all[i * batch : (i + 1) * batch, 128:] = here[batch:]
        d_signal = dsig_all[:, :cols] + times_flipped(fmod_all[...].astype(bf16), fada_ref[...])
        held["d_cond"] = d_signal * swish_slope(cond_ref[...])
        held["d_second"] = held["d_cond"].astype(bf16)

    def second_back():
        back = times(held["d_second"], tables_ref[:, t2_row:class_row])
        for i in range(ways):
            first_own[i, :, :cols] = back[:, i * cols : (i + 1) * cols].astype(bf16)
        third.start()

    def bias_sums():
        for p in second:
            p.wait()
        small_own[...] = jnp.sum(small_land[...].astype(f32), axis=0)
        bias = jnp.sum(bias_land[...].astype(f32), axis=0)
        slice_rows = slice_ref.shape[0]
        slice_ref[...] = bias[:slice_rows]
        held["slice"] = square(bias[:slice_rows])
        side_own[...] = bias[slice_rows:]
        for p in fourth:
            p.start()

    def fada_gradient():
        g_fada = outer(signal_ref[...], fmod_all[...].astype(bf16))
        g_head_ref[:, : g_fada.shape[1]] = g_fada
        add_shared(g_fada)
        held["mod"] = column_sum(fmod_all[...])
        mod_sum_ref[...] = held["mod"]

    def second_gradient():
        held["g_second"] = outer(held["d_second"], first_s_ref[...])
        add_shared(held["g_second"])

    def class_gradient():
        for i in range(ways):
            row = lax.broadcasted_iota(jnp.int32, (batch, CLASSES), 1)
            hot = (row == facts_ref[i][:, 0:1].astype(jnp.int32)).astype(f32)
            hot_buf[i * batch : (i + 1) * batch] = hot
        hot = hot_buf[...].astype(bf16)
        high = held["d_cond"].astype(bf16)
        rest = held["d_cond"] - high.astype(f32)
        mid = rest.astype(bf16)
        low = (rest - mid.astype(f32)).astype(bf16)
        held["g_class"] = outer(high, hot) + outer(mid, hot) + outer(low, hot)
        add_shared(held["g_class"])

    def first_gradient():
        third.wait()
        d_first = (jnp.sum(first_land[...].astype(f32), axis=0)[:, :cols] * swish_slope(first_t_ref[...])).astype(bf16)
        held["g_first"] = outer(d_first, tf_ref[...].astype(bf16))
        add_shared(held["g_first"])
        held["columns"] = [column_sum(d_first.astype(f32)), column_sum(held["d_second"].astype(f32))]
        for i, s in enumerate(held["columns"]):
            add_shared(s)
            columns_own[i : i + 1, :cols] = s
        fifth.start()

    def totals():
        for p in fourth:
            p.wait()
        small = jnp.sum(small_mp[...], axis=0)[:, :cols]
        add_shared(small)
        small = small.T
        g_head_ref[:, fmod_all.shape[1] :] = small[:, PATCH_VALUES:]
        g_cond_ref[...] = jnp.concatenate(
            [small[:, :PATCH_VALUES], held["g_first"], held["g_second"], held["g_class"]], axis=1
        )
        side = jnp.sum(side_mp[...], axis=0)
        side_ref[...] = side
        held["every"] = square(side[: side.shape[0] - 8]) + square(held["mod"])

    steps = (LAYERS - 1) * late
    places = [
        (0, lambda: run_late(3)),
        (3, lambda: run_late(2)),
        (12, lambda: run_late(1)),
        (20, pass_early),
        (29, signal_back),
        (31, second_back),
        (35, bias_sums),
        (38, fada_gradient),
        (40, second_gradient),
        (45, class_gradient),
        (57, first_gradient),
        (63, totals),
    ]
    in_parts(0, steps, step, [(-(-t * steps // 72), work) for t, work in places])

    for k in range(late, count):
        j = k - late
        other_buf[z, j] = x_ref[slot(z, 1 - y, k)]

        @pl.when(z > 0)
        def _():
            upward_other(z, k).wait_recv()
            other_buf[z, j] = (other_buf[z, j].astype(f32) + up_other[z, j].astype(f32)).astype(bf16)

        @pl.when(z < LAYERS - 1)
        def _():
            downward_other(z, k).wait_recv()
            other_buf[z, j] = (other_buf[z, j].astype(f32) + down_other[z, j].astype(f32)).astype(bf16)

        cross_late(k).start()

    last_own[...] = jnp.zeros_like(last_own)

    def final(k, _):
        issue(steps + k + AHEAD)
        out_ref[k] = pair_sum(z, k)

        @pl.when(z > 0)
        def _():
            upward(z, k).wait_recv()
            out_ref[k] += up_buf[z, k].astype(f32)

        @pl.when(z < LAYERS - 1)
        def _():
            downward(z, k).wait_recv()
            out_ref[k] += down_buf[z, k].astype(f32)

        total = out_ref[k]
        last_own[...] += column_sum(total * total)
        return 0

    lax.fori_loop(0, count, final, 0)
    squares = held["shared"] / mp + held["slice"] / ways + held["every"] / (ways * mp)
    squares += jnp.sum(last_own[...], axis=1, keepdims=True)
    last_own[...] = jnp.broadcast_to(squares, (1, 128))
    sixth = push_all(0, last_own, last_all)
    sixth.start()

    def sent(k, _):
        for layer in range(LAYERS):

            @pl.when(k < late)
            def _():
                across(layer, k).wait_send()

            @pl.when(layer > z)
            def _():
                upward(layer, k).wait_send()

            @pl.when(layer < z)
            def _():
                downward(layer, k).wait_send()

        return 0

    lax.fori_loop(0, count, sent, 0)
    for k in range(late, count):
        cross_late(k).wait_send()
        for layer in range(LAYERS):

            @pl.when(layer > z)
            def _():
                upward_other(layer, k).wait_send()

            @pl.when(layer < z)
            def _():
                downward_other(layer, k).wait_send()

    fifth.wait()
    sixth.wait()


def tail(slots, d_fmod, d_signal, small, bias, w_fada, tables, cond, first_t, signal, first_s, tf, facts, slice_rows):
    ways, mp, f32, bf16 = LAYERS * COLUMNS, lax.axis_size("mp"), jnp.float32, jnp.bfloat16
    piece = (PACK_ROWS // SPLIT, LANES // 2)
    slots = slots.reshape((-1,) + piece)
    count = slots.shape[0] // ways
    batch, cols = d_signal.shape[1:]
    rows, fada = batch * ways, w_fada.shape[1]
    side_rows = bias.shape[0] - slice_rows
    wide = ((0, 0), (0, 0), (0, LANES - cols))
    d_signal = jnp.pad(d_signal, wide).reshape(ways, batch, 2, 128).transpose(0, 2, 1, 3)
    d_fmod = jnp.pad(d_fmod.reshape(fada // 128, 128), ((0, 24 - fada // 128), (0, 0)))
    early = jnp.concatenate(
        [jnp.broadcast_to(d_fmod, (ways, 24, 128)), d_signal.reshape(ways, 2 * batch, 128)], 1
    ).astype(bf16)
    small = jnp.pad(small, wide).astype(bf16)
    bias = bias.astype(bf16)
    dma, vmem = pltpu.SemaphoreType.DMA, pl.BlockSpec(memory_space=pltpu.VMEM)
    shape, scratch = jax.ShapeDtypeStruct, pltpu.VMEM
    landing = scratch((LAYERS, count) + piece, bf16)
    few = scratch((LAYERS, CROSS_LATE) + piece, bf16)
    out_shape = [
        shape((count,) + piece, f32),
        shape(tables.shape, f32),
        shape((cols, fada + small.shape[1] - PATCH_VALUES), f32),
        shape((slice_rows, 128), f32),
        shape((side_rows, 128), f32),
        shape((1, fada), f32),
        shape((ways, 8, LANES), f32),
        shape((ways * mp, 1, 128), f32),
    ]
    out = pl.pallas_call(
        tail_body,
        in_specs=[vmem] * 12,
        out_specs=[vmem] * len(out_shape),
        out_shape=out_shape,
        scratch_shapes=[landing] * 3
        + [few] * 3
        + [
            scratch(early.shape, bf16),
            scratch((mp,) + early.shape, bf16),
            scratch(small.shape, bf16),
            scratch((ways,) + bias.shape, bf16),
            scratch((rows, LANES), f32),
            scratch((ways, rows, LANES), bf16),
            scratch((ways, rows, LANES), bf16),
            scratch(small.shape[1:], f32),
            scratch((mp,) + small.shape[1:], f32),
            scratch((side_rows, 128), f32),
            scratch((mp, side_rows, 128), f32),
            scratch((rows, fada), f32),
            scratch((8, LANES), f32),
            scratch((1, 128), f32),
            scratch((rows, CLASSES), f32),
        ]
        + [dma((LAYERS, count))] * 5
        + [dma((LAYERS, CROSS_LATE))] * 3
        + [dma((1, ways * mp))] * 2
        + [dma((5, ways))] * 2
        + [dma((3, mp))] * 2,
        compiler_params=pltpu.CompilerParams(
            collective_id=1, has_side_effects=True, vmem_limit_bytes=58 * 2**20
        ),
        name="tail",
    )(slots, early, small, bias, w_fada, tables, cond, first_t, signal, first_s, tf, facts)
    return [out[0].reshape(-1, PACK_ROWS, LANES // 2)] + list(out[1:])


def halves(x):
    high = x.astype(jnp.bfloat16)
    return high, (x - high.astype(jnp.float32)).astype(jnp.bfloat16)


def left_form(main, tail):
    mh, ml = halves(main)
    th, tl = halves(tail)
    return jnp.concatenate([mh, mh, ml, th, th, tl], axis=1)


def right_form(x):
    h, l = halves(x)
    return jnp.concatenate(
        [h[:LANES], l[:LANES], h[:LANES], h[LANES:], l[LANES:], h[LANES:]], axis=0
    )


def product(left, right):
    return jnp.dot(left, right, preferred_element_type=jnp.float32)


def symmetric_product(left, right_main, right_tail):
    main = product(left, right_main)
    corner = product(left[LANES:], right_tail)
    return main, jnp.concatenate([main[LANES:].T, corner], axis=0)


def inverse_roots(pairs, eye_main, eye_tail):
    contracted, scales = [], []
    for main, tail in pairs:
        trace = jnp.sum(main * eye_main) + jnp.sum(tail * eye_tail)
        shift = 0.0001 * trace / BLOCK_SIDE
        main = main + shift * eye_main
        tail = tail + shift * eye_tail
        square = jnp.sum(main * main, axis=(0, 1), keepdims=True) + jnp.sum(
            tail * tail, axis=(0, 1), keepdims=True
        )
        factor_z = 2.5 / jnp.sqrt(square)
        contracted.append((main * factor_z, tail * factor_z))
        scales.append(jnp.sqrt(jnp.sqrt(factor_z)))
    estimates = None
    for newton_step in range(NEWTON):
        more = newton_step < NEWTON - 1
        factors = [((5.0 * eye_main - m) * 0.25, (5.0 * eye_tail - t) * 0.25) for m, t in contracted]
        rights = [(right_form(m), right_form(t)) for m, t in factors]
        lefts = [left_form(m, t) for m, t in factors] if more else None
        if more:
            powers = [symmetric_product(l, *r) for l, r in zip(lefts, rights)]
        if estimates is None:
            estimates = [(m * s, t * s) for (m, t), s in zip(factors, scales)]
        else:
            estimates = [
                symmetric_product(left_form(*e), *r) for e, r in zip(estimates, rights)
            ]
        if more:
            powers = [
                symmetric_product(left_form(*q), right_form(q[0]), right_form(q[1])) for q in powers
            ]
            contracted = [
                symmetric_product(left_form(*q), right_form(m), right_form(t))
                for q, (m, t) in zip(powers, contracted)
            ]
    return estimates


def shampoo_body(clip_ref, g_ref, stat_ref, old_ref, clipped_ref, new_stat_ref, new_ref, low_ref):
    side = BLOCK_SIDE

    def unit(width, offset):
        row = lax.broadcasted_iota(jnp.int32, (side, width), 0)
        col = lax.broadcasted_iota(jnp.int32, (side, width), 1) + offset
        return (row == col).astype(jnp.float32)

    eye_main, eye_tail = unit(LANES, 0), unit(TAIL, LANES)
    pairs, g_rights = [], []
    for j in range(g_ref.shape[0]):
        g_main, g_tail = unpack(g_ref[j] * clip_ref[0])
        clipped_ref[j, :, :LANES] = g_main
        clipped_ref[j, :, LANES:] = g_tail
        flipped = jnp.concatenate([g_main, g_tail], axis=1).T
        g_right = (right_form(g_main), right_form(g_tail))
        f_right = (right_form(flipped[:, :LANES]), right_form(flipped[:, LANES:]))
        g_left = left_form(g_main, g_tail)
        f_left = left_form(flipped[:, :LANES], flipped[:, LANES:])
        g_rights.append(g_right)
        for k, (left, right) in enumerate(((g_left, f_right), (f_left, g_right))):
            main, tail = symmetric_product(left, *right)
            main = 0.5 * stat_ref[j, k, :, :LANES] + 0.5 * main
            tail = 0.5 * stat_ref[j, k, :, LANES:] + 0.5 * tail
            new_stat_ref[j, k, :, :LANES] = main
            new_stat_ref[j, k, :, LANES:] = tail
            pairs.append((main, tail))
    roots = inverse_roots(pairs, eye_main, eye_tail)
    for j, g_right in enumerate(g_rights):
        root_left = left_form(*roots[2 * j])
        half = left_form(product(root_left, g_right[0]), product(root_left, g_right[1]))
        for part, (a, b) in zip(roots[2 * j + 1], ((0, LANES), (LANES, side))):
            direction = product(half, right_form(part))
            old = old_ref[j, :, a:b]
            new = old - shampoo_rate * (direction + decay_rate * old)
            new_ref[j, :, a:b] = new
            low_ref[j, :, a:b] = new.astype(jnp.bfloat16)


def shampoo(clip_factor, gradients, stats, old_blocks):
    count, side = gradients.shape[0], BLOCK_SIDE
    group = next(g for g in (3, 2, 1) if count % g == 0)
    one = pl.BlockSpec((group, side, side), lambda i: (i, 0, 0))
    two = pl.BlockSpec((group, 2, side, side), lambda i: (i, 0, 0, 0))
    block = jax.ShapeDtypeStruct((count, side, side), jnp.float32)
    return pl.pallas_call(
        shampoo_body,
        grid=(count // group,),
        in_specs=[
            pl.BlockSpec(memory_space=pltpu.SMEM),
            pl.BlockSpec((group, PACK_ROWS, LANES // 2), lambda i: (i, 0, 0)),
            two,
            one,
        ],
        out_specs=[one, two, one, one],
        out_shape=[
            block,
            jax.ShapeDtypeStruct((count, 2, side, side), jnp.float32),
            block,
            jax.ShapeDtypeStruct((count, side, side), jnp.bfloat16),
        ],
        compiler_params=pltpu.CompilerParams(vmem_limit_bytes=60 * 2**20),
        cost_estimate=pl.CostEstimate(
            flops=count * 44 * 6 * side**3, bytes_accessed=count * 34 * side * side, transcendentals=0
        ),
        name="shampoo",
    )(clip_factor.reshape(1), gradients, stats, old_blocks)


def adam_update(weight, gradient, moment_one, second):
    moment_one = 0.5 * moment_one + 0.5 * gradient
    second = 0.5 * second + 0.5 * gradient * gradient
    correct = 1.0 - 0.5**STEP
    updated = weight - adam_rate * (
        moment_one / correct / (jnp.sqrt(second / correct) + 1e-08) + decay_rate * weight
    )
    return (moment_one, second, updated)


def per_device(
    latents,
    noise,
    timesteps,
    labels,
    loss_weights,
    slotted_block_weights,
    statistics,
    slot_of_block,
    cond_tables,
    head_tables,
    slice_bias,
    side_bias,
    cond_m,
    cond_v,
    head_m,
    head_v,
    slice_m,
    slice_v,
    side_m,
    side_v,
):
    bf16, f32 = jnp.bfloat16, jnp.float32
    width = MODEL_WIDTH
    mp, dp = lax.axis_size("mp"), lax.axis_size("dp")
    my_mp, my_dp = lax.axis_index("mp"), lax.axis_index("dp")
    query_width, ff_width, ada_width = HEADS * HD // mp, FF // mp, 6 * width // mp
    ada_column = 3 * query_width + ff_width
    row_blocks = width // BLOCK_SIDE
    col_blocks = (ada_column + ada_width) // BLOCK_SIDE
    out_blocks = (query_width + ff_width) // BLOCK_SIDE
    first_out = row_blocks * col_blocks
    t2_row = PATCH_VALUES + FREQ
    class_row = t2_row + width
    local_heads = query_width // HD
    score_scale = HD ** (-0.5)
    batch = latents.shape[0]
    own_n = batch // mp
    cols = cond_tables.shape[1]
    samples = batch * dp

    def own(x):
        return lax.dynamic_slice_in_dim(x, my_mp * own_n, own_n, 0)

    def my_cols(x):
        return lax.dynamic_slice_in_dim(x, my_dp * cols, cols, x.ndim - 1)

    def all_columns(x):
        return x.transpose(1, 0, 2).reshape(x.shape[1], -1)

    def by_columns(x):
        return x.reshape(x.shape[0], dp, cols).transpose(1, 0, 2)

    def share_rows(x):
        return lax.all_gather(x, "mp", axis=0, tiled=True)

    tuned = dp == COLUMNS * LAYERS
    tables, head_low = cond_tables.T.astype(bf16), head_tables.astype(bf16)
    w_fada = head_low[:, : 2 * width]
    b_first = my_cols(side_bias[width : 2 * width])
    b_second = my_cols(side_bias[2 * width : 3 * width])
    time_freq = time_features(timesteps, FREQ).astype(bf16).astype(f32)
    facts = jnp.pad(jnp.stack([labels.astype(f32), loss_weights], 1), ((0, 0), (0, 126)))
    shared = jnp.concatenate([tables[:, :PATCH_VALUES], head_low[:, 2 * width :]], 1)
    if tuned:
        (
            blocks, time_freq, facts, shared, first_t, first_s, cond_vec, signal_cols, signal, final_mod,
        ) = head(
            slotted_block_weights[0], time_freq, facts, shared, tables, w_fada, b_first[None],
            b_second[None],
        )
    else:
        w_first, w_second = tables[:, PATCH_VALUES:t2_row].T, tables[:, t2_row:class_row].T
        blocks = lax.all_gather(pack_blocks(slotted_block_weights[0]), "dp", axis=0, tiled=True)
        time_freq, facts, shared = exchange(
            [(time_freq, "gather"), (facts, "gather"), (shared, "gather")], "dp", 2
        )
        time_freq = time_freq.reshape(samples, FREQ)
        first_t = dense(time_freq.astype(bf16), w_first) + b_first
        (first_s,) = exchange([(swish_unit(first_t).astype(bf16), "gather")], "dp", 3)
        labels_all = facts[:, :, 0].reshape(samples, 1).astype(jnp.int32)
        onehot = labels_all == jnp.arange(CLASSES, dtype=jnp.int32)[None, :]
        first_s = all_columns(first_s)
        cond_vec = (
            dense(first_s, w_second) + b_second + dense(onehot.astype(bf16), tables[:, class_row:].T)
        )
        signal_cols = swish_unit(cond_vec).astype(bf16)
        signal, final_mod = exchange(
            [
                (signal_cols.astype(f32).reshape(dp, batch, cols), "scatter"),
                (dense(signal_cols, w_fada).reshape(dp, batch, 2 * width), "scatter"),
            ],
            "dp",
            4,
        )
        final_mod = jnp.sum(final_mod, 0)
    weight_total = jnp.sum(facts[:, :, 1])
    shared = shared.reshape(width, -1)
    w_patch, w_head = shared[:, :PATCH_VALUES].T, shared[:, PATCH_VALUES:]
    signal = all_columns(signal).astype(bf16)
    final_mod = own(final_mod + side_bias[5 * width : 7 * width])

    w_qkv, w_up, w_ada = assemble(
        blocks,
        slot_of_block,
        0,
        row_blocks,
        [3 * query_width // BLOCK_SIDE, ff_width // BLOCK_SIDE, ada_width // BLOCK_SIDE],
    )
    (w_o,) = assemble(blocks, slot_of_block, first_out, query_width // BLOCK_SIDE, [row_blocks])
    (w_down,) = assemble(
        blocks,
        slot_of_block,
        first_out + query_width // BLOCK_SIDE * row_blocks,
        ff_width // BLOCK_SIDE,
        [row_blocks],
    )
    own_bias = slice_bias[0]
    modul = lax.all_gather(
        dense(signal, w_ada) + own_bias[2 * query_width + ff_width :],
        "mp",
        axis=1,
        tiled=True,
    )
    own_modul = own(modul)

    def part(position):
        return modul[:, None, position * width : (position + 1) * width]

    def heads_of(inputs):
        return inputs.reshape(batch, -1, local_heads, HD)

    keep_rate, noise_rate, upper_log, lower_log, mean_gap = coefficients(timesteps)
    noisy = keep_rate[:, None, None, None] * latents + noise_rate[:, None, None, None] * noise
    patches = patchify(noisy).astype(bf16)
    seq_len = patches.shape[1]
    initial = (
        dense(patches, w_patch) + side_bias[:width] + position_embedding(LATENT_SIDE // 2, width)
    )
    normed_all, _ = layer_norm(initial)
    attn_in = (normed_all * (1.0 + part(1)) + part(0)).astype(bf16)
    start = own(initial)[0]
    own_patches = own(patches)
    target = patchify(own(noise))[0]

    projected = dense(attn_in, w_qkv)
    queries = heads_of((projected[..., :query_width] + own_bias[:query_width]).astype(bf16))
    keys = heads_of(projected[..., query_width : 2 * query_width].astype(bf16))
    values = heads_of(
        (projected[..., 2 * query_width :] + own_bias[query_width : 2 * query_width]).astype(bf16)
    )
    scores = (
        jnp.einsum("slhe,smhe->shlm", queries, keys, preferred_element_type=f32) * score_scale
    )
    row_peak = jnp.max(scores, -1, keepdims=True)
    shifted = jnp.exp(scores - row_peak)
    row_total = jnp.sum(shifted, -1, keepdims=True)
    probs = shifted / row_total
    log_total = row_peak + jnp.log(row_total)
    mixed = (
        jnp.einsum("shlm,smhe->slhe", probs.astype(bf16), values, preferred_element_type=f32)
        .reshape(batch, seq_len, query_width)
        .astype(bf16)
    )

    def rows_of(*rows):
        return jnp.concatenate([r.reshape(1, width) for r in rows], 0)

    shift1, scale1, gate1, shift2, scale2, gate2 = (own_modul[0, i * width : (i + 1) * width] for i in range(6))
    attn, middle, hidden, active, mlp_in = attention_out_stage(
        mixed,
        w_o,
        w_up,
        start,
        rows_of(side_bias[3 * width : 4 * width], gate1, scale2, shift2),
        own_bias[2 * query_width : 2 * query_width + ff_width].reshape(1, ff_width),
    )

    def halves_of(x):
        x = x.reshape(x.shape[:-1] + (4, 8))
        return x[..., :4].reshape(x.shape[:-2] + (16,)), x[..., 4:].reshape(x.shape[:-2] + (16,))

    w_pred, w_raw = halves_of(w_head)
    own_weight = own(loss_weights)
    loss_facts = [own(upper_log), own(lower_log), own(mean_gap), own_weight, own_weight / weight_total]
    d_final, head_in, d_pred, d_raw, sums_f, loss_part, d_hidden, up_sum, d_branch = loss_stage(
        active,
        w_down,
        hidden,
        middle,
        rows_of(side_bias[4 * width : 5 * width], gate2, final_mod[0, width:], final_mod[0, :width]),
        target,
        w_pred,
        w_raw,
        jnp.stack(halves_of(side_bias[7 * width :])),
        jnp.broadcast_to(jnp.stack(loss_facts), (5, 16)),
    )
    loss_part = jnp.sum(loss_part)
    d_fmod = sums_f[:2].reshape(1, 2 * width).astype(bf16)
    d_middle, sums_m, d_mixed, g_down, d_attn = middle_back_stage(
        d_hidden, w_up, w_o, middle, d_final, attn, rows_of(scale2, gate1), active, d_branch
    )
    d_mixed = heads_of(d_mixed)
    probs = jnp.exp(
        jnp.einsum("slhe,smhe->shlm", queries, keys, preferred_element_type=f32) * score_scale
        - log_total
    )
    d_values = jnp.einsum(
        "shlm,slhe->smhe", probs.astype(bf16), d_mixed, preferred_element_type=f32
    ).astype(bf16)
    d_probs = jnp.einsum("slhe,smhe->shlm", d_mixed, values, preferred_element_type=f32)
    d_scores = (probs * (d_probs - jnp.sum(d_probs * probs, -1, keepdims=True))).astype(bf16)
    d_query = (
        jnp.einsum("shlm,smhe->slhe", d_scores, keys, preferred_element_type=f32) * score_scale
    ).astype(bf16)
    d_keys = (
        jnp.einsum("shlm,slhe->smhe", d_scores, queries, preferred_element_type=f32) * score_scale
    ).astype(bf16)
    flat_q = d_query.reshape(batch, seq_len, query_width)
    flat_v = d_values.reshape(batch, seq_len, query_width)
    d_proj = jnp.concatenate([flat_q, d_keys.reshape(batch, seq_len, query_width), flat_v], 2)
    d_start, sums_a, g_qkv, g_up, g_outp = start_back_stage(
        d_proj, w_qkv, start, d_middle, scale1.reshape(1, width), attn_in, mlp_in, d_hidden, mixed, d_attn
    )
    d_mod_own = jnp.concatenate(
        [sums_a[0], sums_a[1], sums_m[2], sums_m[0], sums_m[1], sums_f[2]]
    ).reshape(1, 6 * width)
    d_modul = lax.dynamic_slice_in_dim(
        share_rows(d_mod_own.astype(bf16)), my_mp * ada_width, ada_width, 1
    )

    slot_grad = to_slots(
        [g_qkv, g_up], signal, d_modul, [g_outp, g_down], slot_of_block, slot_of_block.shape[0]
    )
    d_signal = by_columns(back_dense(d_modul, w_ada))

    def interleave(p, r):
        parts = [x.reshape(x.shape[:-1] + (4, 4)) for x in (p, r)]
        return jnp.concatenate(parts, -1).reshape(p.shape[:-1] + (32,))

    def thirds(x):
        high = x.astype(bf16).astype(f32)
        mid = (x - high).astype(bf16).astype(f32)
        return [high, mid, x - high - mid]

    def lanes(x, rows):
        return jnp.pad(x, (0, rows * 128 - x.shape[0])).reshape(rows, 128)

    d_out = interleave(d_pred, d_raw)
    small = by_columns(
        jnp.concatenate([weight_grad(own_patches[0], d_start), weight_grad(d_out, head_in)], 0)
    )
    slice_part = jnp.concatenate([total_of(flat_q), total_of(flat_v), up_sum[0], total_of(d_modul)])
    side_part = jnp.concatenate([sums_a[2], sums_m[3], sums_f[3], total_of(d_out)])
    slice_rows, side_rows = (-(-x.shape[0] // 1024) * 8 for x in (slice_part, side_part))
    bias_part = jnp.concatenate(
        [lanes(slice_part, slice_rows), lanes(side_part, side_rows), lanes(jnp.stack(thirds(loss_part)), 8)], 0
    )
    if tuned:
        red_blocks, red_cond, red_head, red_slice, side_sum, side_mod, columns, last = tail(
            slot_grad, d_fmod.astype(f32), d_signal, small, bias_part, w_fada, tables, cond_vec,
            first_t, signal_cols, first_s, time_freq, facts, slice_rows,
        )
    else:
        red_blocks = lax.psum_scatter(slot_grad, "dp", scatter_dimension=0, tiled=True).astype(f32)
        d_fmod_all, d_signal = exchange(
            [(d_fmod.astype(f32), "gather"), (d_signal, "scatter")], EVERY, 5
        )
        d_fmod_all = d_fmod_all.reshape(samples, 2 * width).astype(bf16)
        d_signal = jnp.sum(d_signal.reshape(dp, mp, batch, cols), 1).reshape(samples, cols)
        d_signal = d_signal + back_dense(d_fmod_all, w_fada)
        d_cond = d_signal * swish_slope(cond_vec)
        d_second = d_cond.astype(bf16)
        d_first, small, bias_part = exchange(
            [
                (by_columns(back_dense(d_second, w_second)), "scatter"),
                (small, "scatter"),
                (bias_part, "gather"),
            ],
            "dp",
            6,
        )
        d_first = (jnp.sum(d_first, 0) * swish_slope(first_t)).astype(bf16)
        bias_part = jnp.sum(bias_part, 0)
        red_slice = bias_part[:slice_rows]
        small, side_sum = exchange(
            [(jnp.sum(small, 0), "gather"), (bias_part[slice_rows:], "gather")], "mp", 7
        )
        small, side_sum = jnp.sum(small, 0), jnp.sum(side_sum, 0)
        side_mod = total_of(d_fmod_all)
        g_class = jnp.einsum(
            "sc,sd->cd", onehot.astype(f32), d_cond, precision=exact_precision_flag
        )
        red_cond = jnp.concatenate(
            [
                small[:PATCH_VALUES],
                weight_grad(time_freq.astype(bf16), d_first),
                weight_grad(first_s, d_second),
                g_class,
            ],
            0,
        ).T
        red_head = jnp.concatenate([weight_grad(signal_cols, d_fmod_all), small[PATCH_VALUES:].T], 1)
        side_cols = jnp.stack([total_of(d_first), total_of(d_second)])
        local_squares = (
            jnp.sum(red_blocks * red_blocks)
            + (
                jnp.sum(red_cond * red_cond)
                + jnp.sum(red_head * red_head)
                + jnp.sum(side_cols * side_cols)
            )
            / mp
            + jnp.sum(red_slice * red_slice) / dp
            + (jnp.sum(side_sum[:-8] * side_sum[:-8]) + jnp.sum(side_mod * side_mod)) / (dp * mp)
        )
        last = jnp.pad(side_cols, ((0, 6), (0, LANES - cols)))
        last = jnp.where(jnp.arange(8)[:, None] == 2, local_squares, last)
        (last,) = exchange([(last, "gather")], EVERY, 8)
        columns, last = last.reshape(dp, mp, 8, LANES)[:, 0], last[:, 2:3]
    grad_norm = jnp.sqrt(jnp.sum(last[:, 0, 0]))
    loss_sum = jnp.sum(side_sum[side_rows, :3])
    side_sum = side_sum[:side_rows].reshape(-1)[: side_part.shape[0]]
    red_slice = red_slice.reshape(-1)[: slice_part.shape[0]]
    side_cols = columns[:, :2, :cols].transpose(1, 0, 2).reshape(2 * width)
    red_side = jnp.concatenate(
        [
            side_sum[:width],
            side_cols,
            side_sum[width : 3 * width],
            side_mod.reshape(2 * width),
            side_sum[3 * width :],
        ]
    )
    clip_factor = 1.0 / jnp.maximum(grad_norm, 1.0)
    clipped, new_stats, new_blocks, new_low = shampoo(
        clip_factor, red_blocks, statistics[0], slotted_block_weights[0]
    )
    cond_one, cond_two, new_cond = adam_update(
        cond_tables.T, red_cond * clip_factor, cond_m.T, cond_v.T
    )
    cond_short = new_cond.astype(bf16)
    head_one, head_two, new_head = adam_update(head_tables, red_head * clip_factor, head_m, head_v)
    head_short = new_head.astype(bf16)
    slice_one, slice_two, new_slice = adam_update(
        slice_bias[0], red_slice * clip_factor, slice_m[0], slice_v[0]
    )
    side_one, side_two, new_side = adam_update(side_bias, red_side * clip_factor, side_m, side_v)
    return (
        loss_sum,
        weight_total,
        grad_norm,
        clipped[None],
        new_stats[None],
        new_blocks[None],
        new_low[None],
        cond_one.T,
        cond_two.T,
        new_cond.T,
        cond_short.T,
        head_one,
        head_two,
        new_head,
        head_short,
        slice_one[None],
        slice_two[None],
        new_slice[None],
        side_one,
        side_two,
        new_side,
    )


def solution(mesh):
    return jax.shard_map(
        per_device,
        mesh=mesh,
        in_specs=(
            P("dp", None, None, None),
            P("dp", None, None, None),
            P("dp"),
            P("dp"),
            P("dp"),
            P("mp", "dp", None, None),
            P("mp", "dp", None, None, None),
            P(),
            P(None, "dp"),
            P("dp", None),
            P("mp", None),
            P(),
            P(None, "dp"),
            P(None, "dp"),
            P("dp", None),
            P("dp", None),
            P("mp", None),
            P("mp", None),
            P(),
            P(),
        ),
        out_specs=(
            P(),
            P(),
            P(),
            P("mp", "dp", None, None),
            P("mp", "dp", None, None, None),
            P("mp", "dp", None, None),
            P("mp", "dp", None, None),
            P(None, "dp"),
            P(None, "dp"),
            P(None, "dp"),
            P(None, "dp"),
            P("dp", None),
            P("dp", None),
            P("dp", None),
            P("dp", None),
            P("mp", None),
            P("mp", None),
            P("mp", None),
            P(),
            P(),
            P(),
        ),
        check_vma=False,
    )
```

```python
import math

import jax
import jax.numpy as jnp
from jax import lax
from jax.experimental import pallas as pl
from jax.experimental.pallas import tpu as pltpu
from jax.sharding import PartitionSpec as P

MODEL_WIDTH = 1152
HEADS = 16
HD = 72
FF = 4608
FREQ = 256
CLASSES = 1001
LATENT_SIDE = 32
PATCH_VALUES = 16
BLOCK_SIDE = 288
NEWTON = 6
STEP = 5
LANES = 256
TAIL = BLOCK_SIDE - LANES


exact_precision_flag = lax.Precision.HIGHEST
shampoo_rate = 0.5
adam_rate = 0.05
decay_rate = 0.01


def dense(operand, weight):
    return jnp.dot(operand, weight, preferred_element_type=jnp.float32)


def back_dense(gradient, weight):
    return jnp.einsum("...j,ij->...i", gradient, weight, preferred_element_type=jnp.float32)


def weight_grad(operand, gradient):
    return jnp.einsum("...i,...j->ij", operand, gradient, preferred_element_type=jnp.float32)


def total_of(inputs):
    return jnp.sum(inputs.astype(jnp.float32), axis=tuple(range(inputs.ndim - 1)))


def swish_unit(inputs):
    return inputs / (1.0 + jnp.exp(-inputs))


def swish_slope(inputs):
    sigmoid = 1.0 / (1.0 + jnp.exp(-inputs))
    return sigmoid * (1.0 + inputs * (1.0 - sigmoid))


def tanh_gelu_activation(inputs):
    return (
        0.5
        * inputs
        * (1.0 + jnp.tanh(0.7978845608028654 * (inputs + 0.044715 * inputs * inputs * inputs)))
    )


def gelu_slope(inputs):
    inner = jnp.tanh(0.7978845608028654 * (inputs + 0.044715 * inputs * inputs * inputs))
    return 0.5 * (1.0 + inner) + 0.5 * inputs * (1.0 - inner * inner) * 0.7978845608028654 * (
        1.0 + 3.0 * 0.044715 * inputs * inputs
    )


def layer_norm(inputs):
    centred = inputs - jnp.mean(inputs, -1, keepdims=True)
    inv_std = lax.rsqrt(jnp.mean(centred * centred, -1, keepdims=True) + 1e-06)
    return (centred * inv_std, inv_std)


def norm_back(gradient, normed, inv_std):
    return inv_std * (
        gradient
        - jnp.mean(gradient, -1, keepdims=True)
        - normed * jnp.mean(gradient * normed, -1, keepdims=True)
    )


def coefficients(step_ids):
    grid = jnp.arange(1000).astype(jnp.float32)
    betas = 0.0001 + (0.02 - 0.0001) * grid / 999.0
    logs = jnp.log(1.0 - betas)[None, :]
    index = jnp.arange(1000, dtype=jnp.int32)[None, :]
    beta_t = 0.0001 + (0.02 - 0.0001) * step_ids.astype(jnp.float32) / 999.0
    cumul_t = jnp.exp(jnp.sum(jnp.where(index <= step_ids[:, None], logs, 0.0), 1))
    before_t = jnp.exp(jnp.sum(jnp.where(index < step_ids[:, None], logs, 0.0), 1))
    keep_rate = jnp.sqrt(cumul_t)
    noise_rate = jnp.sqrt(1.0 - cumul_t)
    upper_log = jnp.log(beta_t)
    lower_log = jnp.log(beta_t * (1.0 - before_t) / (1.0 - cumul_t))
    mean_gap = beta_t * jnp.sqrt(before_t) / (1.0 - cumul_t) * jnp.sqrt(1.0 / cumul_t - 1.0)
    return (keep_rate, noise_rate, upper_log, lower_log, mean_gap)


def time_features(step_ids, feat_width):
    half_width = feat_width // 2
    frequencies = jnp.exp(
        -math.log(10000.0) * jnp.arange(half_width).astype(jnp.float32) / half_width
    )
    phases = step_ids.astype(jnp.float32)[:, None] * frequencies[None, :]
    return jnp.concatenate([jnp.cos(phases), jnp.sin(phases)], 1)


def position_embedding(grid_side, feat_width):
    quarter = feat_width // 4
    omegas = jnp.exp(-math.log(10000.0) * jnp.arange(quarter).astype(jnp.float32) / quarter)
    coords = jnp.arange(grid_side).astype(jnp.float32)
    angles = coords[:, None] * omegas[None, :]
    waves = jnp.concatenate([jnp.sin(angles), jnp.cos(angles)], 1)
    half_width = feat_width // 2
    rows_part = jnp.broadcast_to(waves[:, None, :], (grid_side, grid_side, half_width))
    cols_part = jnp.broadcast_to(waves[None, :, :], (grid_side, grid_side, half_width))
    return jnp.concatenate([rows_part, cols_part], 2).reshape(grid_side * grid_side, feat_width)


def patchify(latent):
    samples_n, channels, height, breadth = latent.shape
    shaped = latent.reshape(samples_n, channels, height // 2, 2, breadth // 2, 2).transpose(
        0, 2, 4, 3, 5, 1
    )
    return shaped.reshape(samples_n, height // 2 * (breadth // 2), 4 * channels)


PACK_ROWS = 656
SPLIT = 1


def pack(x):
    quarter = BLOCK_SIDE // 4
    tail = x[:, LANES:].astype(jnp.float32)
    tail = jnp.concatenate([tail[i * quarter : (i + 1) * quarter] for i in range(4)], axis=1)
    fill = jnp.zeros((PACK_ROWS - 2 * BLOCK_SIDE - quarter, LANES // 2), jnp.float32)
    tail = jnp.concatenate([tail, fill], axis=0)
    half = LANES // 2
    return x[:, :half], x[:, half:LANES], tail.astype(x.dtype)


def unpack(x):
    side, quarter = BLOCK_SIDE, BLOCK_SIDE // 4
    tail = x[2 * side :].astype(jnp.float32)[:quarter]
    tail = jnp.concatenate([tail[:, i * TAIL : (i + 1) * TAIL] for i in range(4)], axis=0)
    main = jnp.concatenate([x[:side], x[side : 2 * side]], axis=1)
    return main, tail.astype(x.dtype)


def store_packed(ref, index, x):
    a, b, c = pack(x)
    side = BLOCK_SIDE
    ref[index + (slice(0, side),)] = a
    ref[index + (slice(side, 2 * side),)] = b
    ref[index + (slice(2 * side, PACK_ROWS),)] = c


def store_pieces(ref, first, x):
    rows = [part for part in pack(x)]
    size, at, piece = PACK_ROWS // SPLIT, 0, 0
    for part in rows:
        done = 0
        while done < part.shape[0]:
            step = min(size - at, part.shape[0] - done)
            ref[first + piece, at : at + step] = part[done : done + step]
            done, at = done + step, at + step
            if at == size:
                piece, at = piece + 1, 0


def pack_blocks(blocks):
    count, side = blocks.shape[0], BLOCK_SIDE

    def body(x_ref, out_ref):
        store_packed(out_ref, (0,), x_ref[0].astype(jnp.bfloat16))

    return pl.pallas_call(
        body,
        grid=(count,),
        in_specs=[pl.BlockSpec((1, side, side), lambda i: (i, 0, 0))],
        out_specs=pl.BlockSpec((1, PACK_ROWS, LANES // 2), lambda i: (i, 0, 0)),
        out_shape=jax.ShapeDtypeStruct((count, PACK_ROWS, LANES // 2), jnp.bfloat16),
        name="pack_blocks",
    )(blocks)


def remote(source, target, send, receive, place):
    return pltpu.make_async_remote_copy(
        src_ref=source,
        dst_ref=target,
        send_sem=send,
        recv_sem=receive,
        device_id=place,
        device_id_type=pl.DeviceIdType.MESH,
    )


def signal_to(semaphore, place):
    pl.semaphore_signal(semaphore, inc=1, device_id=place, device_id_type=pl.DeviceIdType.MESH)


COLUMNS = 2
LAYERS = 4


def grid_place():
    me = lax.axis_index("dp")
    return me // COLUMNS, me % COLUMNS


EVERY = ("dp", "mp")


def exchange(items, axes, number):
    mp, dp = lax.axis_size("mp"), lax.axis_size("dp")
    n = {"dp": dp, "mp": mp, EVERY: dp * mp}[axes]

    def place(i):
        return {"dp": i // mp, "mp": i % mp} if axes == EVERY else {axes: i}

    def row(i):
        return i // mp if axes == EVERY else i

    def body(*refs):
        m = len(items)
        sources, outs, send, receive = refs[:m], refs[m : 2 * m], refs[-2], refs[-1]
        me = lax.axis_index("dp") * mp + lax.axis_index("mp") if axes == EVERY else lax.axis_index(axes)
        barrier = pltpu.get_barrier_semaphore()

        def greet(i, _):
            signal_to(barrier, place(lax.rem(me + i, n)))
            return 0

        lax.fori_loop(1, n, greet, 0)
        pl.semaphore_wait(barrier, n - 1)

        def piece(j, to):
            return sources[j].at[row(to)] if items[j][1] == "scatter" else sources[j]

        def start(i, _):
            to = lax.rem(me + i, n)
            for j in range(m):
                remote(piece(j, to), outs[j].at[me], send.at[j, i], receive.at[j, me], place(to)).start()
            return 0

        lax.fori_loop(1, n, start, 0)
        for j in range(m):
            outs[j][me] = sources[j][row(me)] if items[j][1] == "scatter" else sources[j][...]

        def finish(i, _):
            to = lax.rem(me + i, n)
            for j in range(m):
                copy = remote(piece(j, to), outs[j].at[to], send.at[j, i], receive.at[j, to], place(to))
                copy.wait_recv()
                copy.wait_send()
            return 0

        lax.fori_loop(1, n, finish, 0)

    arrays = [a for a, _ in items]
    shapes = [
        jax.ShapeDtypeStruct((n,) + (a.shape[1:] if kind == "scatter" else a.shape), a.dtype)
        for a, kind in items
    ]
    vmem = pl.BlockSpec(memory_space=pltpu.VMEM)
    return pl.pallas_call(
        body,
        in_specs=[vmem] * len(arrays),
        out_specs=[vmem] * len(arrays),
        out_shape=shapes,
        scratch_shapes=[pltpu.SemaphoreType.DMA((len(arrays), n))] * 2,
        compiler_params=pltpu.CompilerParams(
            collective_id=number, has_side_effects=True, vmem_limit_bytes=40 * 2**20
        ),
        name=f"exchange_{number}",
    )(*arrays)


def assemble(blocks, slots, first, rows, widths):
    side, cols = BLOCK_SIDE, sum(widths)

    def body(ids, *refs):
        base = 0
        for out, width in zip(refs[cols:], widths):
            parts = [part for r in refs[base : base + width] for part in unpack(r[0])]
            out[...] = jnp.concatenate(parts, axis=1)
            base += width

    def spec(c):
        return pl.BlockSpec(
            (1, PACK_ROWS, LANES // 2), lambda r, ids: (ids[first + r * cols + c], 0, 0)
        )

    return pl.pallas_call(
        body,
        grid_spec=pltpu.PrefetchScalarGridSpec(
            num_scalar_prefetch=1,
            grid=(rows,),
            in_specs=[spec(c) for c in range(cols)],
            out_specs=[pl.BlockSpec((side, side * w), lambda r, ids: (r, 0)) for w in widths],
        ),
        out_shape=[jax.ShapeDtypeStruct((rows * side, w * side), jnp.bfloat16) for w in widths],
        compiler_params=pltpu.CompilerParams(vmem_limit_bytes=40 * 2**20),
        cost_estimate=pl.CostEstimate(
            flops=0, bytes_accessed=4 * rows * cols * side * side, transcendentals=0
        ),
        name="assemble",
    )(slots, *([blocks] * cols))


def to_slots(inner, signal, d_modul, lower, slots, total):
    side = BLOCK_SIDE
    ri, widths = inner[0].shape[0] // side, [g.shape[1] // side for g in inner]
    wide = d_modul.shape[1] // side
    ci, co = sum(widths) + wide, lower[0].shape[1] // side
    heights = [g.shape[0] // side for g in lower]
    ro = sum(heights)
    steps = ri + ro
    n = len(inner) + 2 + len(lower)
    batch = signal.shape[0]
    signal = signal.reshape(batch, ri, side).transpose(1, 0, 2)

    def body(ids, *refs):
        sources, (out, buf, sem) = refs[:n], refs[-3:]
        s = pl.program_id(0)
        half = lax.rem(s, 2)

        def drain(which, count):
            for c in range(count):
                pltpu.make_async_copy(buf.at[which, c], out.at[0], sem.at[which, c]).wait()

        def send(source, count, base, first=0):
            for c in range(count):
                store_packed(buf, (half, first + c), source[:, c * side : (c + 1) * side])
                pltpu.make_async_copy(
                    buf.at[half, first + c], out.at[ids[base + c]], sem.at[half, first + c]
                ).start()

        @pl.when(jnp.logical_and(s >= 2, s - 2 < ri))
        def _():
            drain(half, ci)

        @pl.when(s - 2 >= ri)
        def _():
            drain(half, co)

        @pl.when(s < ri)
        def _():
            first = 0
            for source, width in zip(sources, widths):
                send(source, width, s * ci + first, first)
                first += width
            send(outer(refs[len(inner)][0], refs[len(inner) + 1][...]).astype(jnp.bfloat16), wide, s * ci + first, first)

        base = ri
        for source, height in zip(sources[len(inner) + 2 :], heights):

            @pl.when(jnp.logical_and(s >= base, s < base + height))
            def _():
                send(source, co, ri * ci + (s - ri) * co)

            base += height

        @pl.when(s == steps - 1)
        def _():
            drain(1 - half, co)
            drain(half, co)

    extra, aliases = [], {}
    if total != ri * ci + ro * co:
        extra = [jnp.zeros((total, PACK_ROWS, LANES // 2), jnp.bfloat16)]
        aliases = {1 + n: 0}
    specs = [
        pl.BlockSpec((side, w * side), lambda s, ids: (jnp.minimum(s, ri - 1), 0)) for w in widths
    ]
    specs += [
        pl.BlockSpec((1, batch, side), lambda s, ids: (jnp.minimum(s, ri - 1), 0, 0)),
        pl.BlockSpec(d_modul.shape, lambda s, ids: (0, 0)),
    ]
    base = ri
    for height in heights:
        specs.append(
            pl.BlockSpec(
                (side, co * side),
                lambda s, ids, base=base, height=height: (jnp.clip(s - base, 0, height - 1), 0),
            )
        )
        base += height
    return pl.pallas_call(
        body,
        grid_spec=pltpu.PrefetchScalarGridSpec(
            num_scalar_prefetch=1,
            grid=(steps,),
            in_specs=specs + [pl.BlockSpec(memory_space=pl.ANY)] * len(extra),
            out_specs=pl.BlockSpec(memory_space=pl.ANY),
            scratch_shapes=[
                pltpu.VMEM((2, max(ci, co), PACK_ROWS, LANES // 2), jnp.bfloat16),
                pltpu.SemaphoreType.DMA((2, max(ci, co))),
            ],
        ),
        out_shape=jax.ShapeDtypeStruct((total, PACK_ROWS, LANES // 2), jnp.bfloat16),
        compiler_params=pltpu.CompilerParams(vmem_limit_bytes=40 * 2**20),
        cost_estimate=pl.CostEstimate(
            flops=0, bytes_accessed=4 * (ri * ci + ro * co) * side * side, transcendentals=0
        ),
        input_output_aliases=aliases,
        name="to_slots",
    )(slots, *inner, signal, d_modul, *lower, *extra)


CHUNK = 64


def mean_of(x):
    return jnp.sum(x, axis=-1, keepdims=True) * (1.0 / x.shape[-1])


def norm_rows(x):
    centred = x - mean_of(x)
    inv_std = lax.rsqrt(mean_of(centred * centred) + 1e-06)
    return centred * inv_std, inv_std


def norm_rows_back(gradient, normed, inv_std):
    return inv_std * (gradient - mean_of(gradient) - normed * mean_of(gradient * normed))


def column_sum(x):
    return jnp.sum(x, axis=0, keepdims=True)


def times(a, b):
    return jnp.dot(a, b, preferred_element_type=jnp.float32)


def times_flipped(a, b):
    return lax.dot_general(a, b, (((1,), (1,)), ((), ())), preferred_element_type=jnp.float32)


def stage(number, inputs, outputs, shared, make):
    rows, width = inputs[0].shape[1], MODEL_WIDTH
    pieces = rows // CHUNK
    n_in, n_out = len(inputs), len(outputs)

    def body(*refs):
        ins, outs = refs[:n_in], refs[n_in : n_in + n_out]
        rest = refs[n_in + n_out :]
        share = None
        if shared:
            share, rest = rest[0], rest[1:]
        a_out, a_in, b_out, b_in, c_out, c_in, total, near, far = rest
        me = lax.axis_index("mp")
        core = me + 1 - 2 * lax.rem(me, 2)
        across = lax.rem(me + 2, 4)
        other = lax.rem(core + 2, 4)
        to_core, to_across = {"mp": core}, {"mp": across}
        partial, own, after, side = make(ins, outs, share)
        barrier = pltpu.get_barrier_semaphore()
        signal_to(barrier, to_core)
        signal_to(barrier, to_across)
        pl.semaphore_wait(barrier, 2)

        copy_a = remote(a_out, a_in, near.at[0, 0], near.at[1, 0], to_core)
        copy_c = remote(c_out, c_in, near.at[0, 1], near.at[1, 1], to_core)

        def piece(i):
            return pl.ds(i * CHUNK, CHUNK)

        def copy_b(i):
            return remote(
                b_out.at[piece(i)], b_in.at[piece(i)], far.at[0, i], far.at[1, i], to_across
            )

        def share_far(group, i):
            part = share.at[group, piece(i)]
            return remote(part, part, far.at[2, i], far.at[3, i], to_across)

        def share_near(group, i):
            part = share.at[group, piece(i)]
            return remote(part, part, near.at[2, i], near.at[3, i], to_core)

        def pass_near(group, i):
            part = share.at[group, piece(i)]
            return remote(part, part, near.at[4, i], near.at[5, i], to_core)

        a_out[...] = partial(other).astype(jnp.bfloat16)
        copy_a.start()
        total[...] = partial(across)
        copy_a.wait_recv()
        for i in range(pieces):
            at = piece(i)
            b_out[at] = (total[at] + a_in[at].astype(jnp.float32)).astype(jnp.bfloat16)
            copy_b(i).start()
        c_out[...] = partial(core).astype(jnp.bfloat16)
        copy_c.start()
        total[...] = partial(me)
        copy_c.wait_recv()
        for i in range(pieces):
            at = piece(i)
            if side and not shared:
                side(i)
            copy_b(i).wait_recv()
            result = own(
                i * CHUNK, total[at] + c_in[at].astype(jnp.float32) + b_in[at].astype(jnp.float32)
            )
            if shared:
                share[me, at] = result
                share_far(me, i).start()
                share_near(me, i).start()
                if side:
                    side(i)
        if shared:
            for i in range(pieces):
                after(me, i * CHUNK)
            for i in range(pieces):
                share_near(core, i).wait_recv()
                after(core, i * CHUNK)
            for i in range(pieces):
                share_far(across, i).wait_recv()
                pass_near(across, i).start()
                after(across, i * CHUNK)
                if i > 0:
                    pass_near(other, i - 1).wait_recv()
                    after(other, (i - 1) * CHUNK)
            pass_near(other, pieces - 1).wait_recv()
            after(other, (pieces - 1) * CHUNK)
        copy_a.wait_send()
        copy_c.wait_send()
        for i in range(pieces):
            copy_b(i).wait_send()
            if shared:
                share_far(me, i).wait_send()
                share_near(me, i).wait_send()
                pass_near(across, i).wait_send()

    vmem = pl.BlockSpec(memory_space=pltpu.VMEM)
    out_shape = [jax.ShapeDtypeStruct(shape, dtype) for shape, dtype in outputs]
    if shared:
        out_shape.append(jax.ShapeDtypeStruct((4, rows, width), jnp.bfloat16))
    landing = pltpu.VMEM((rows, width), jnp.bfloat16)
    return pl.pallas_call(
        body,
        in_specs=[vmem] * n_in,
        out_specs=[vmem] * len(out_shape),
        out_shape=out_shape,
        scratch_shapes=[landing] * 6
        + [
            pltpu.VMEM((rows, width), jnp.float32),
            pltpu.SemaphoreType.DMA((6, max(pieces, 2))),
            pltpu.SemaphoreType.DMA((4, pieces)),
        ],
        compiler_params=pltpu.CompilerParams(
            collective_id=number, has_side_effects=True, vmem_limit_bytes=56 * 2**20
        ),
        name=f"stage_{number}",
    )(*inputs)


def attention_out_stage(mixed, w_o, w_up, start, rows, up_bias):
    n, width, f32 = mixed.shape[1], MODEL_WIDTH, jnp.float32

    def make(ins, outs, share):
        mixed_ref, w_o_ref, w_up_ref, start_ref, rows_ref, up_ref = ins
        attn_ref, middle_ref, hidden_ref, active_ref = outs

        def partial(group):
            return times(mixed_ref[group], w_o_ref[...])

        def own(at, total):
            at = slice(at, at + CHUNK)
            attn = total + rows_ref[0:1]
            middle = start_ref[at] + rows_ref[1:2] * attn
            attn_ref[at] = attn
            middle_ref[at] = middle
            normed, _ = norm_rows(middle)
            return (normed * (1.0 + rows_ref[2:3]) + rows_ref[3:4]).astype(jnp.bfloat16)

        def after(group, at):
            at = slice(at, at + CHUNK)
            hidden = times(share[group, at], w_up_ref[...]) + up_ref[...]
            hidden_ref[group, at] = hidden
            active_ref[group, at] = tanh_gelu_activation(hidden).astype(jnp.bfloat16)

        return partial, own, after, None

    inner = w_up.shape[1]
    return stage(
        9,
        [mixed, w_o, w_up, start, rows, up_bias],
        [((n, width), f32), ((n, width), f32), ((4, n, inner), f32), ((4, n, inner), jnp.bfloat16)],
        True,
        make,
    )


def loss_stage(active, w_down, hidden, middle, rows, target, w_pred, w_raw, head_bias, facts):
    n, width, f32, bf16 = active.shape[1], MODEL_WIDTH, jnp.float32, jnp.bfloat16
    inner = active.shape[2]

    def make(ins, outs, share):
        active_ref, w_ref, hidden_ref, middle_ref, rows_ref, target_ref, wp_ref, wr_ref, bias_ref, facts_ref = ins
        d_final_ref, head_in_ref, d_pred_ref, d_raw_ref, sums_ref, loss_ref, d_hidden_ref, up_sum_ref = outs
        sums_ref[...] = jnp.zeros_like(sums_ref)
        loss_ref[...] = jnp.zeros_like(loss_ref)
        up_sum_ref[...] = jnp.zeros_like(up_sum_ref)

        def partial(group):
            return times(active_ref[group], w_ref[...])

        def own(at, total):
            at = slice(at, at + CHUNK)
            branch = total + rows_ref[0:1]
            gate, fscale = rows_ref[1:2], 1.0 + rows_ref[2:3]
            normed, inv_std = norm_rows(middle_ref[at] + gate * branch)
            head_in = (normed * fscale + rows_ref[3:4]).astype(bf16)
            head_in_ref[at] = head_in
            upper, lower, gap = facts_ref[0:1], facts_ref[1:2], facts_ref[2:3]
            weight = facts_ref[3:4]
            share_of = weight / facts_ref[4:5]
            error = times_flipped(head_in, wp_ref[...]) + bias_ref[0:1] - target_ref[at]
            fraction = (times_flipped(head_in, wr_ref[...]) + bias_ref[1:2] + 1.0) / 2.0
            log_var = fraction * upper + (1.0 - fraction) * lower
            gap = gap * error
            ratio = jnp.exp(lower - log_var)
            spread = gap * gap * jnp.exp(-log_var)
            diverge = 0.5 * (-1.0 + log_var - lower + ratio + spread)
            cells = 1.0 / (n * error.shape[1])
            per_bit = cells / math.log(2.0)
            loss_ref[...] += weight * column_sum(error * error * cells + diverge * per_bit)
            d_pred = (share_of * (2.0 * cells) * error).astype(bf16)
            d_raw = (
                share_of * per_bit * 0.25 * (upper - lower) * (1.0 - ratio - spread)
            ).astype(bf16)
            d_pred_ref[at] = d_pred
            d_raw_ref[at] = d_raw
            d_head = times(d_pred, wp_ref[...]) + times(d_raw, wr_ref[...])
            d_final = norm_rows_back(d_head * fscale, normed, inv_std)
            d_final_ref[at] = d_final
            d_branch = (gate * d_final).astype(bf16)
            sums_ref[0:1] += column_sum(d_head)
            sums_ref[1:2] += column_sum(d_head * normed)
            sums_ref[2:3] += column_sum(d_final * branch)
            sums_ref[3:4] += column_sum(d_branch.astype(f32))
            return d_branch

        def after(group, at):
            at = slice(at, at + CHUNK)
            d_active = times_flipped(share[group, at], w_ref[...])
            d_hidden = (d_active * gelu_slope(hidden_ref[group, at])).astype(bf16)
            d_hidden_ref[group, at] = d_hidden
            up_sum_ref[...] += column_sum(d_hidden.astype(f32))

        return partial, own, after, None

    half = w_pred.shape[0]
    return stage(
        10,
        [active, w_down, hidden, middle, rows, target, w_pred, w_raw, head_bias, facts],
        [
            ((n, width), f32),
            ((n, width), bf16),
            ((n, half), bf16),
            ((n, half), bf16),
            ((4, width), f32),
            ((1, half), f32),
            ((4, n, inner), bf16),
            ((1, inner), f32),
        ],
        True,
        make,
    )


def gradient_part(out_ref, a_ref, b_ref, i):
    width = a_ref.shape[2]
    step = max(width // 512, 1) * 128
    at = slice(min(i * step, width), width if i == 3 else min((i + 1) * step, width))
    if at.start < at.stop:
        tokens = a_ref.shape[0] * a_ref.shape[1]
        a = a_ref[:, :, at].reshape(tokens, at.stop - at.start)
        b = b_ref[...].reshape(tokens, b_ref.shape[2])
        out_ref[at] = outer(a, b).astype(jnp.bfloat16)


def middle_back_stage(d_hidden, w_up, w_o, middle, d_final, attn, rows, active, d_branch):
    n, width, f32, bf16 = d_hidden.shape[1], MODEL_WIDTH, jnp.float32, jnp.bfloat16

    def make(ins, outs, share):
        (
            d_hidden_ref, w_up_ref, w_o_ref, middle_ref, d_final_ref, attn_ref, rows_ref, active_ref,
            d_branch_ref,
        ) = ins
        d_middle_ref, sums_ref, d_mixed_ref, g_down_ref = outs
        sums_ref[...] = jnp.zeros_like(sums_ref)

        def partial(group):
            return times_flipped(d_hidden_ref[group], w_up_ref[...])

        def own(at, total):
            at = slice(at, at + CHUNK)
            normed, inv_std = norm_rows(middle_ref[at])
            d_middle = d_final_ref[at] + norm_rows_back(total * (1.0 + rows_ref[0:1]), normed, inv_std)
            d_middle_ref[at] = d_middle
            d_attn = (rows_ref[1:2] * d_middle).astype(bf16)
            sums_ref[0:1] += column_sum(total)
            sums_ref[1:2] += column_sum(total * normed)
            sums_ref[2:3] += column_sum(d_middle * attn_ref[at])
            sums_ref[3:4] += column_sum(d_attn.astype(f32))
            return d_attn

        def after(group, at):
            at = slice(at, at + CHUNK)
            d_mixed_ref[group, at] = times_flipped(share[group, at], w_o_ref[...]).astype(bf16)

        def side(i):
            gradient_part(g_down_ref, active_ref, d_branch_ref, i)

        return partial, own, after, side

    return stage(
        11,
        [d_hidden, w_up, w_o, middle, d_final, attn, rows, active, d_branch],
        [
            ((n, width), f32),
            ((4, width), f32),
            ((4, n, w_o.shape[0]), bf16),
            ((active.shape[2], width), bf16),
        ],
        True,
        make,
    )


def start_back_stage(d_proj, w_qkv, start, d_middle, rows, attn_in, mlp_in, d_hidden, mixed, d_attn):
    n, width, f32, bf16 = d_proj.shape[1], MODEL_WIDTH, jnp.float32, jnp.bfloat16

    def make(ins, outs, share):
        d_proj_ref, w_ref, start_ref, d_middle_ref, rows_ref = ins[:5]
        attn_in_ref, mlp_in_ref, d_hidden_ref, mixed_ref, d_attn_ref = ins[5:]
        d_start_ref, sums_ref, g_qkv_ref, g_up_ref, g_outp_ref = outs
        sums_ref[...] = jnp.zeros_like(sums_ref)

        def partial(group):
            return times_flipped(d_proj_ref[group], w_ref[...])

        def own(at, total):
            at = slice(at, at + CHUNK)
            normed, inv_std = norm_rows(start_ref[at])
            d_start = d_middle_ref[at] + norm_rows_back(total * (1.0 + rows_ref[0:1]), normed, inv_std)
            d_start = d_start.astype(bf16)
            d_start_ref[at] = d_start
            sums_ref[0:1] += column_sum(total)
            sums_ref[1:2] += column_sum(total * normed)
            sums_ref[2:3] += column_sum(d_start.astype(f32))

        def side(i):
            gradient_part(g_up_ref, mlp_in_ref, d_hidden_ref, i)
            gradient_part(g_qkv_ref, attn_in_ref, d_proj_ref, i)
            gradient_part(g_outp_ref, mixed_ref, d_attn_ref, i)

        return partial, own, None, side

    return stage(
        12,
        [d_proj, w_qkv, start, d_middle, rows, attn_in, mlp_in, d_hidden, mixed, d_attn],
        [
            ((n, width), bf16),
            ((3, width), f32),
            ((width, d_proj.shape[2]), bf16),
            ((width, d_hidden.shape[2]), bf16),
            ((mixed.shape[2], width), bf16),
        ],
        False,
        make,
    )


AHEAD = 4
CROSS_LATE = 1


class Push:
    def __init__(self, source, landing, send, receive, n, me, place, row=None):
        self.source, self.landing, self.send, self.receive = source, landing, send, receive
        self.n, self.me, self.place, self.row = n, me, place, row

    def _copy(self, i, sender, to):
        source = self.source if self.row is None else self.source.at[self.row(to)]
        return remote(
            source, self.landing.at[sender], self.send.at[i], self.receive.at[sender], self.place(to)
        )

    def start(self):
        def one(i, _):
            self._copy(i, self.me, lax.rem(self.me + i, self.n)).start()
            return 0

        lax.fori_loop(1, self.n, one, 0)
        own = self.source[...] if self.row is None else self.source[self.row(self.me)]
        self.landing[self.me] = own

    def wait(self):
        def one(i, _):
            to = lax.rem(self.me + i, self.n)
            copy = self._copy(i, to, to)
            copy.wait_recv()
            copy.wait_send()
            return 0

        lax.fori_loop(1, self.n, one, 0)


def in_parts(first, last, step, between):
    for at, work in between:
        lax.fori_loop(first, at, step, 0)
        work()
        first = at
    lax.fori_loop(first, last, step, 0)


def head_body(
    x_ref, tf_ref, facts_ref, shared_ref, tables_ref, fada_ref, b1_ref, b2_ref,
    out_ref, tf_all, facts_all, shared_out, first_t_ref, first_s_ref, cond_ref, signal_ref,
    signal_out, mod_ref,
    packed, shared_all, signal_all, tf_land, hot_buf, first_s, first_s_all, signal_own, mod_own, mod_land, local_sem, up_sem, down_sem, side_sem,
    up_other, down_other, recv_sem, send, receive,
):
    count, ways, f32, bf16 = packed.shape[0], LAYERS * COLUMNS, jnp.float32, jnp.bfloat16
    batch, cols = mod_ref.shape[0], tables_ref.shape[0]
    late = count - CROSS_LATE
    z, y = grid_place()
    me = lax.axis_index("dp")

    def place(i):
        return {"dp": i}

    barrier = pltpu.get_barrier_semaphore()

    def greet(i, _):
        signal_to(barrier, place(lax.rem(me + i, ways)))
        return 0

    lax.fori_loop(1, ways, greet, 0)
    pl.semaphore_wait(barrier, ways - 1)

    def push(j, source, landing, row=None):
        return Push(source, landing, send.at[j], receive.at[j], ways, me, place, row)

    first = [
        push(0, tf_ref, tf_land),
        push(1, facts_ref, facts_all),
        push(2, shared_ref, shared_all),
    ]
    for p in first:
        p.start()

    peer = {"dp": z * COLUMNS + 1 - y}
    above = {"dp": jnp.minimum(z + 1, LAYERS - 1) * COLUMNS + y}
    below = {"dp": jnp.maximum(z - 1, 0) * COLUMNS + y}

    def block(layer, column, k):
        return out_ref.at[(layer * COLUMNS + column) * count + k]

    def move(source, layer, k, sem, to):
        return remote(source, block(layer, y, k), sem.at[layer, k], recv_sem.at[layer, y, k], to)

    def move_other(layer, k, sem, to):
        here = block(layer, 1 - y, k)
        return remote(here, here, sem.at[layer, k - late], recv_sem.at[layer, 1 - y, k], to)

    def arrival(layer, column, k):
        here = block(layer, column, k)
        return remote(here, here, side_sem.at[0, 0], recv_sem.at[layer, column, k], peer)

    def send_own(i, _):
        base = count - SPLIT * (i + 1)
        store_pieces(packed, base, x_ref[x_ref.shape[0] - 1 - i].astype(bf16))
        for j in range(SPLIT - 1, -1, -1):
            k = base + j
            own = packed.at[k]
            move(own, z, k, side_sem, peer).start()

            @pl.when(z < LAYERS - 1)
            def _():
                move(own, z, k, up_sem, above).start()

            @pl.when(z > 0)
            def _():
                move(own, z, k, down_sem, below).start()

            pltpu.make_async_copy(own, block(z, y, k), local_sem.at[k]).start()
        return 0

    def pass_own(k):
        arrival(z, 1 - y, k).wait_recv()

        @pl.when(z < LAYERS - 1)
        def _():
            move_other(z, k, up_other, above).start()

        @pl.when(z > 0)
        def _():
            move_other(z, k, down_other, below).start()

    def run_hop(hop):
        def pass_on(i, _):
            k = count - 1 - i

            @pl.when(z >= hop)
            def _():
                layer = z - hop
                arrival(layer, y, k).wait_recv()

                @pl.when(z < LAYERS - 1)
                def _():
                    move(block(layer, y, k), layer, k, up_sem, above).start()

                @pl.when(k < late)
                def _():
                    move(block(layer, y, k), layer, k, side_sem, peer).start()

            @pl.when(z + hop < LAYERS)
            def _():
                layer = z + hop
                arrival(layer, y, k).wait_recv()

                @pl.when(z > 0)
                def _():
                    move(block(layer, y, k), layer, k, down_sem, below).start()

                @pl.when(k < late)
                def _():
                    move(block(layer, y, k), layer, k, side_sem, peer).start()

            return 0

        lax.fori_loop(0, count, pass_on, 0)
        for k in range(late, count):

            @pl.when(z >= hop)
            def _():
                layer = z - hop
                arrival(layer, 1 - y, k).wait_recv()

                @pl.when(z < LAYERS - 1)
                def _():
                    move_other(layer, k, up_other, above).start()

            @pl.when(z + hop < LAYERS)
            def _():
                layer = z + hop
                arrival(layer, 1 - y, k).wait_recv()

                @pl.when(z > 0)
                def _():
                    move_other(layer, k, down_other, below).start()

    t2_row = PATCH_VALUES + FREQ
    class_row = t2_row + MODEL_WIDTH
    second = push(3, first_s, first_s_all)
    third = [
        push(4, signal_own, signal_all, lambda to: to),
        push(5, mod_own, mod_land, lambda to: to),
    ]

    def first_row():
        for p in first:
            p.wait()
        for i in range(ways):
            tf_all[i * batch : (i + 1) * batch] = tf_land[i][:batch]
        first_t = times_flipped(tf_all[...].astype(bf16), tables_ref[:, PATCH_VALUES:t2_row]) + b1_ref[...]
        first_t_ref[...] = first_t
        first_s[:, :cols] = swish_unit(first_t).astype(bf16)
        second.start()

    def class_part():
        for i in range(ways):
            row = lax.broadcasted_iota(jnp.int32, (batch, CLASSES), 1)
            hot = (row == facts_all[i][:batch, 0:1].astype(jnp.int32)).astype(f32)
            hot_buf[i * batch : (i + 1) * batch] = hot
        cond_ref[...] = (
            times_flipped(hot_buf[...].astype(bf16), tables_ref[:, class_row:]) + b2_ref[...]
        )

    def second_row():
        second.wait()
        first_s_ref[...] = jnp.concatenate([first_s_all[i][:, :cols] for i in range(ways)], axis=1)
        cond = cond_ref[...] + times_flipped(first_s_ref[...], tables_ref[:, t2_row:class_row])
        cond_ref[...] = cond
        signal = swish_unit(cond).astype(bf16)
        signal_ref[...] = signal
        signal = signal.astype(f32)
        for i in range(ways):
            signal_own[i, :batch, :cols] = signal[i * batch : (i + 1) * batch]
        third[0].start()

    def modulation():
        mod = times(signal_ref[...], fada_ref[...])
        half = mod.shape[1] // 2
        for i in range(ways):
            mod_own[i, :batch] = mod[i * batch : (i + 1) * batch, :half]
            mod_own[i, batch:] = mod[i * batch : (i + 1) * batch, half:]
        third[1].start()

    own_count = x_ref.shape[0]
    third_of = -(-own_count // 3)
    in_parts(0, own_count, send_own, [(third_of, first_row), (2 * third_of, class_part)])
    second_row()
    modulation()
    for k in range(late, count):
        pass_own(k)
    run_hop(1)
    run_hop(2)
    for p in third:
        p.wait()
    mod = jnp.sum(mod_land[...], axis=0)
    mod_ref[...] = jnp.concatenate([mod[:batch], mod[batch:]], axis=1)
    signal_out[...] = jnp.concatenate(
        [signal_all[i][:batch, :cols] for i in range(ways)], axis=1
    ).astype(bf16)
    rows = jnp.concatenate([shared_all[i].astype(f32)[:, :cols] for i in range(ways)], axis=1)
    shared_out[:PATCH_VALUES] = rows[:PATCH_VALUES].astype(bf16)
    for i in range(2):
        picked = [rows[PATCH_VALUES + 8 * p + 4 * i :][:4] for p in range(4)]
        shared_out[16 * i + PATCH_VALUES : 16 * i + PATCH_VALUES + 16] = jnp.concatenate(
            picked, axis=0
        ).astype(bf16)
    run_hop(3)

    def finish(k, _):
        pltpu.make_async_copy(packed.at[k], block(z, y, k), local_sem.at[k]).wait()
        for layer in range(LAYERS):

            @pl.when(k < late)
            def _():
                arrival(layer, 1 - y, k).wait_recv()

            @pl.when((k < late) | (layer == z))
            def _():
                move(block(layer, y, k), layer, k, side_sem, peer).wait_send()

            @pl.when((z < LAYERS - 1) & (layer <= z))
            def _():
                move(block(layer, y, k), layer, k, up_sem, above).wait_send()

            @pl.when((z > 0) & (layer >= z))
            def _():
                move(block(layer, y, k), layer, k, down_sem, below).wait_send()

        return 0

    lax.fori_loop(0, count, finish, 0)
    for k in range(late, count):
        for layer in range(LAYERS):

            @pl.when((z < LAYERS - 1) & (layer <= z))
            def _():
                move_other(layer, k, up_other, above).wait_send()

            @pl.when((z > 0) & (layer >= z))
            def _():
                move_other(layer, k, down_other, below).wait_send()


def head(blocks, time_freq, facts, shared, tables, w_fada, b1, b2):
    ways, f32, bf16 = LAYERS * COLUMNS, jnp.float32, jnp.bfloat16
    count = blocks.shape[0] * SPLIT
    batch, cols, rows = time_freq.shape[0], tables.shape[0], time_freq.shape[0] * ways
    fada = w_fada.shape[1]
    piece = (PACK_ROWS // SPLIT, LANES // 2)
    time_freq = jnp.pad(time_freq, ((0, 8 - batch), (0, 0)))
    facts = jnp.pad(facts, ((0, 8 - batch), (0, 0)))
    shared = jnp.pad(shared.T, ((0, 0), (0, LANES - cols)))
    dma = pltpu.SemaphoreType.DMA
    vmem, anywhere = pl.BlockSpec(memory_space=pltpu.VMEM), pl.BlockSpec(memory_space=pl.ANY)
    shape = jax.ShapeDtypeStruct
    out = pl.pallas_call(
        head_body,
        in_specs=[vmem] * 8,
        out_specs=[anywhere] + [vmem] * 9,
        out_shape=[
            shape((count * ways,) + piece, bf16),
            shape((rows, time_freq.shape[1]), f32),
            shape((ways,) + facts.shape, f32),
            shape((shared.shape[0], ways * cols), bf16),
            shape((rows, cols), f32),
            shape((rows, ways * cols), bf16),
            shape((rows, cols), f32),
            shape((rows, cols), bf16),
            shape((batch, ways * cols), bf16),
            shape((batch, fada), f32),
        ],
        scratch_shapes=[
            pltpu.VMEM((count,) + piece, bf16),
            pltpu.VMEM((ways,) + shared.shape, bf16),
            pltpu.VMEM((ways, 8, LANES), f32),
            pltpu.VMEM((ways,) + time_freq.shape, f32),
            pltpu.VMEM((rows, CLASSES), f32),
            pltpu.VMEM((rows, LANES), bf16),
            pltpu.VMEM((ways, rows, LANES), bf16),
            pltpu.VMEM((ways, 8, LANES), f32),
            pltpu.VMEM((ways, 2 * batch, fada // 2), f32),
            pltpu.VMEM((ways, 2 * batch, fada // 2), f32),
            dma((count,)),
            dma((LAYERS, count)),
            dma((LAYERS, count)),
            dma((LAYERS, count)),
            dma((LAYERS, CROSS_LATE)),
            dma((LAYERS, CROSS_LATE)),
            dma((LAYERS, COLUMNS, count)),
            dma((6, ways)),
            dma((6, ways)),
        ],
        compiler_params=pltpu.CompilerParams(
            collective_id=0, has_side_effects=True, vmem_limit_bytes=48 * 2**20
        ),
        name="head",
    )(blocks, time_freq, facts, shared, tables, w_fada, b1, b2)
    blocks, time_freq, facts, shared, first_t, first_s, cond, signal, signal_all, mod = out
    blocks = blocks.reshape(-1, PACK_ROWS, LANES // 2)
    return (
        blocks, time_freq, facts[:, :batch], shared, first_t, first_s, cond, signal, signal_all, mod,
    )


def outer(a, b):
    return lax.dot_general(a, b, (((0,), (0,)), ((), ())), preferred_element_type=jnp.float32)


def tail_body(
    x_ref, early_ref, small_ref, bias_ref, fada_ref, tables_ref, cond_ref, first_t_ref,
    signal_ref, first_s_ref, tf_ref, facts_ref,
    out_ref, g_cond_ref, g_head_ref, slice_ref, side_ref, mod_sum_ref, columns_all, last_all,
    side_buf, up_buf, down_buf, other_buf, up_other, down_other, early_land, early_mp, small_land,
    bias_land, dsig_all, first_own, first_land, small_own, small_mp, side_own, side_mp, fmod_all, columns_own,
    last_own, hot_buf,
    side_send, line_send, side_recv, up_recv, down_recv, other_send, other_up, other_down,
    send_all, recv_all, send_dp, recv_dp, send_mp, recv_mp,
):
    f32, bf16 = jnp.float32, jnp.bfloat16
    count, ways, mp = out_ref.shape[0], LAYERS * COLUMNS, lax.axis_size("mp")
    batch, cols = facts_ref.shape[1], tables_ref.shape[0]
    everyone = ways * mp
    late = count - CROSS_LATE
    z, y = grid_place()
    my_dp, my_mp = lax.axis_index("dp"), lax.axis_index("mp")
    me = my_dp * mp + my_mp

    def place_all(i):
        return {"dp": i // mp, "mp": lax.rem(i, mp)}

    barrier = pltpu.get_barrier_semaphore()

    def greet(i, _):
        signal_to(barrier, place_all(lax.rem(me + i, everyone)))
        return 0

    lax.fori_loop(1, everyone, greet, 0)
    pl.semaphore_wait(barrier, everyone - 1)

    def push_all(j, source, landing, row=None):
        return Push(source, landing, send_all.at[j], recv_all.at[j], everyone, me, place_all, row)

    def push_dp(j, source, landing, row=None):
        return Push(
            source, landing, send_dp.at[j], recv_dp.at[j], ways, my_dp, lambda i: {"dp": i}, row
        )

    def push_mp(j, source, landing):
        return Push(source, landing, send_mp.at[j], recv_mp.at[j], mp, my_mp, lambda i: {"mp": i})

    first = [push_dp(4, early_ref, early_land, lambda to: to)]
    early_pass = push_mp(2, early_land, early_mp)
    second = [push_dp(0, small_ref, small_land, lambda to: to), push_dp(1, bias_ref, bias_land)]
    third = push_dp(2, first_own, first_land, lambda to: to)
    fifth = push_dp(3, columns_own, columns_all)
    fourth = [push_mp(0, small_own, small_mp), push_mp(1, side_own, side_mp)]

    peer = {"dp": z * COLUMNS + 1 - y}
    above = {"dp": jnp.minimum(z + 1, LAYERS - 1) * COLUMNS + y}
    below = {"dp": jnp.maximum(z - 1, 0) * COLUMNS + y}

    def slot(layer, column, k):
        return (layer * COLUMNS + column) * count + k

    def across(layer, k):
        return remote(
            x_ref.at[slot(layer, 1 - y, k)],
            side_buf.at[layer, k],
            side_send.at[layer, k],
            side_recv.at[layer, k],
            peer,
        )

    def cross_late(k):
        return remote(
            other_buf.at[z, k - late],
            side_buf.at[z, k],
            side_send.at[z, k],
            side_recv.at[z, k],
            peer,
        )

    def upward(layer, k):
        return remote(
            side_buf.at[layer, k], up_buf.at[layer, k], line_send.at[layer, k], up_recv.at[layer, k], above
        )

    def downward(layer, k):
        return remote(
            side_buf.at[layer, k], down_buf.at[layer, k], line_send.at[layer, k], down_recv.at[layer, k], below
        )

    def upward_other(layer, k):
        j = k - late
        return remote(
            other_buf.at[layer, j], up_other.at[layer, j], other_send.at[layer, j], other_up.at[layer, j], above
        )

    def downward_other(layer, k):
        j = k - late
        return remote(
            other_buf.at[layer, j], down_other.at[layer, j], other_send.at[layer, j], other_down.at[layer, j], below
        )

    def own_part(layer, k):
        return x_ref[slot(layer, y, k)].astype(f32)

    def pair_sum(layer, k):
        across(layer, k).wait_recv()
        return own_part(layer, k) + side_buf[layer, k].astype(f32)

    at_end = (z == 0) | (z == LAYERS - 1)

    def turn(t):
        part, within = t // late, lax.rem(t, late)
        end_layer = jnp.where(z == 0, LAYERS - 1 - part, part)
        pair = t - late
        near = jnp.where(lax.rem(pair, 2) == 0, z + 1, z - 1)
        inner_layer = jnp.where(part == 0, jnp.where(z == 1, LAYERS - 1, 0), jnp.where(part == 3, z, near))
        inner_k = jnp.where((part == 0) | (part == 3), within, pair // 2)
        return jnp.where(at_end, end_layer, inner_layer), jnp.where(at_end, within, inner_k)

    def issue(t):
        @pl.when(t < LAYERS * late)
        def _():
            across(*turn(t)).start()

    for t in range(AHEAD):
        issue(jnp.int32(t))
    for p in first + second:
        p.start()

    def along(total, stage_ref, layer, k, copy, landed, begins):
        @pl.when(jnp.logical_not(begins))
        def _():
            copy(layer, k).wait_recv()
            stage_ref[...] = (total + landed[...].astype(f32)).astype(bf16)

        @pl.when(begins)
        def _():
            stage_ref[...] = total.astype(bf16)

        copy(layer, k).start()

    bottom, top = z == 0, z == LAYERS - 1

    def run_late(hop):
        for k in range(late, count):
            j = k - late

            @pl.when(z + hop < LAYERS)
            def _():
                layer = z + hop
                along(
                    own_part(layer, k), side_buf.at[layer, k], layer, k, upward, up_buf.at[layer, k], bottom
                )
                along(
                    x_ref[slot(layer, 1 - y, k)].astype(f32),
                    other_buf.at[layer, j], layer, k, upward_other, up_other.at[layer, j], bottom,
                )

            @pl.when(z >= hop)
            def _():
                layer = z - hop
                along(
                    own_part(layer, k), side_buf.at[layer, k], layer, k, downward, down_buf.at[layer, k], top
                )
                along(
                    x_ref[slot(layer, 1 - y, k)].astype(f32),
                    other_buf.at[layer, j], layer, k, downward_other, down_other.at[layer, j], top,
                )

    def step(t, _):
        issue(t + AHEAD)
        layer, k = turn(t)

        @pl.when(layer > z)
        def _():
            along(
                pair_sum(layer, k), side_buf.at[layer, k], layer, k, upward, up_buf.at[layer, k], bottom
            )

        @pl.when(layer < z)
        def _():
            along(
                pair_sum(layer, k), side_buf.at[layer, k], layer, k, downward, down_buf.at[layer, k], top
            )

        return 0

    t2_row = PATCH_VALUES + FREQ
    class_row = t2_row + MODEL_WIDTH
    held = {"shared": jnp.zeros((1, 1), f32)}

    def square(x):
        return jnp.sum(jnp.sum(x * x, axis=1, keepdims=True), axis=0, keepdims=True)

    def add_shared(x):
        held["shared"] = held["shared"] + square(x)

    def pass_early():
        for p in first:
            p.wait()
        early_pass.start()

    def signal_back():
        early_pass.wait()
        lines = fmod_all.shape[1] // 128
        for i in range(everyone):
            here = early_mp[i % mp, i // mp].astype(f32)
            for j in range(lines):
                fmod_all[i : i + 1, j * 128 : (j + 1) * 128] = here[j : j + 1]
        for i in range(ways):
            here = early_mp[0, i].astype(f32)[24:]
            for j in range(1, mp):
                here = here + early_mp[j, i].astype(f32)[24:]
            dsig_all[i * batch : (i + 1) * batch, :128] = here[:batch]
            dsig_all[i * batch : (i + 1) * batch, 128:] = here[batch:]
        d_signal = dsig_all[:, :cols] + times_flipped(fmod_all[...].astype(bf16), fada_ref[...])
        held["d_cond"] = d_signal * swish_slope(cond_ref[...])
        held["d_second"] = held["d_cond"].astype(bf16)

    def second_back():
        back = times(held["d_second"], tables_ref[:, t2_row:class_row])
        for i in range(ways):
            first_own[i, :, :cols] = back[:, i * cols : (i + 1) * cols].astype(bf16)
        third.start()

    def bias_sums():
        for p in second:
            p.wait()
        small_own[...] = jnp.sum(small_land[...].astype(f32), axis=0)
        bias = jnp.sum(bias_land[...].astype(f32), axis=0)
        slice_rows = slice_ref.shape[0]
        slice_ref[...] = bias[:slice_rows]
        held["slice"] = square(bias[:slice_rows])
        side_own[...] = bias[slice_rows:]
        for p in fourth:
            p.start()

    def fada_gradient():
        g_fada = outer(signal_ref[...], fmod_all[...].astype(bf16))
        g_head_ref[:, : g_fada.shape[1]] = g_fada
        add_shared(g_fada)
        held["mod"] = column_sum(fmod_all[...])
        mod_sum_ref[...] = held["mod"]

    def second_gradient():
        held["g_second"] = outer(held["d_second"], first_s_ref[...])
        add_shared(held["g_second"])

    def class_gradient():
        for i in range(ways):
            row = lax.broadcasted_iota(jnp.int32, (batch, CLASSES), 1)
            hot = (row == facts_ref[i][:, 0:1].astype(jnp.int32)).astype(f32)
            hot_buf[i * batch : (i + 1) * batch] = hot
        hot = hot_buf[...].astype(bf16)
        high = held["d_cond"].astype(bf16)
        rest = held["d_cond"] - high.astype(f32)
        mid = rest.astype(bf16)
        low = (rest - mid.astype(f32)).astype(bf16)
        held["g_class"] = outer(high, hot) + outer(mid, hot) + outer(low, hot)
        add_shared(held["g_class"])

    def first_gradient():
        third.wait()
        d_first = (jnp.sum(first_land[...].astype(f32), axis=0)[:, :cols] * swish_slope(first_t_ref[...])).astype(bf16)
        held["g_first"] = outer(d_first, tf_ref[...].astype(bf16))
        add_shared(held["g_first"])
        held["columns"] = [column_sum(d_first.astype(f32)), column_sum(held["d_second"].astype(f32))]
        for i, s in enumerate(held["columns"]):
            add_shared(s)
            columns_own[i : i + 1, :cols] = s
        fifth.start()

    def totals():
        for p in fourth:
            p.wait()
        small = jnp.sum(small_mp[...], axis=0)[:, :cols]
        add_shared(small)
        small = small.T
        g_head_ref[:, fmod_all.shape[1] :] = small[:, PATCH_VALUES:]
        g_cond_ref[...] = jnp.concatenate(
            [small[:, :PATCH_VALUES], held["g_first"], held["g_second"], held["g_class"]], axis=1
        )
        side = jnp.sum(side_mp[...], axis=0)
        side_ref[...] = side
        held["every"] = square(side[: side.shape[0] - 8]) + square(held["mod"])

    steps = (LAYERS - 1) * late
    places = [
        (0, lambda: run_late(3)),
        (3, lambda: run_late(2)),
        (12, lambda: run_late(1)),
        (20, pass_early),
        (29, signal_back),
        (31, second_back),
        (35, bias_sums),
        (38, fada_gradient),
        (40, second_gradient),
        (45, class_gradient),
        (57, first_gradient),
        (63, totals),
    ]
    in_parts(0, steps, step, [(-(-t * steps // 72), work) for t, work in places])

    for k in range(late, count):
        j = k - late
        other_buf[z, j] = x_ref[slot(z, 1 - y, k)]

        @pl.when(z > 0)
        def _():
            upward_other(z, k).wait_recv()
            other_buf[z, j] = (other_buf[z, j].astype(f32) + up_other[z, j].astype(f32)).astype(bf16)

        @pl.when(z < LAYERS - 1)
        def _():
            downward_other(z, k).wait_recv()
            other_buf[z, j] = (other_buf[z, j].astype(f32) + down_other[z, j].astype(f32)).astype(bf16)

        cross_late(k).start()

    last_own[...] = jnp.zeros_like(last_own)

    def final(k, _):
        issue(steps + k + AHEAD)
        out_ref[k] = pair_sum(z, k)

        @pl.when(z > 0)
        def _():
            upward(z, k).wait_recv()
            out_ref[k] += up_buf[z, k].astype(f32)

        @pl.when(z < LAYERS - 1)
        def _():
            downward(z, k).wait_recv()
            out_ref[k] += down_buf[z, k].astype(f32)

        total = out_ref[k]
        last_own[...] += column_sum(total * total)
        return 0

    lax.fori_loop(0, count, final, 0)
    squares = held["shared"] / mp + held["slice"] / ways + held["every"] / (ways * mp)
    squares += jnp.sum(last_own[...], axis=1, keepdims=True)
    last_own[...] = jnp.broadcast_to(squares, (1, 128))
    sixth = push_all(0, last_own, last_all)
    sixth.start()

    def sent(k, _):
        for layer in range(LAYERS):

            @pl.when(k < late)
            def _():
                across(layer, k).wait_send()

            @pl.when(layer > z)
            def _():
                upward(layer, k).wait_send()

            @pl.when(layer < z)
            def _():
                downward(layer, k).wait_send()

        return 0

    lax.fori_loop(0, count, sent, 0)
    for k in range(late, count):
        cross_late(k).wait_send()
        for layer in range(LAYERS):

            @pl.when(layer > z)
            def _():
                upward_other(layer, k).wait_send()

            @pl.when(layer < z)
            def _():
                downward_other(layer, k).wait_send()

    fifth.wait()
    sixth.wait()


def tail(slots, d_fmod, d_signal, small, bias, w_fada, tables, cond, first_t, signal, first_s, tf, facts, slice_rows):
    ways, mp, f32, bf16 = LAYERS * COLUMNS, lax.axis_size("mp"), jnp.float32, jnp.bfloat16
    piece = (PACK_ROWS // SPLIT, LANES // 2)
    slots = slots.reshape((-1,) + piece)
    count = slots.shape[0] // ways
    batch, cols = d_signal.shape[1:]
    rows, fada = batch * ways, w_fada.shape[1]
    side_rows = bias.shape[0] - slice_rows
    wide = ((0, 0), (0, 0), (0, LANES - cols))
    d_signal = jnp.pad(d_signal, wide).reshape(ways, batch, 2, 128).transpose(0, 2, 1, 3)
    d_fmod = jnp.pad(d_fmod.reshape(fada // 128, 128), ((0, 24 - fada // 128), (0, 0)))
    early = jnp.concatenate(
        [jnp.broadcast_to(d_fmod, (ways, 24, 128)), d_signal.reshape(ways, 2 * batch, 128)], 1
    ).astype(bf16)
    small = jnp.pad(small, wide).astype(bf16)
    bias = bias.astype(bf16)
    dma, vmem = pltpu.SemaphoreType.DMA, pl.BlockSpec(memory_space=pltpu.VMEM)
    shape, scratch = jax.ShapeDtypeStruct, pltpu.VMEM
    landing = scratch((LAYERS, count) + piece, bf16)
    few = scratch((LAYERS, CROSS_LATE) + piece, bf16)
    out_shape = [
        shape((count,) + piece, f32),
        shape(tables.shape, f32),
        shape((cols, fada + small.shape[1] - PATCH_VALUES), f32),
        shape((slice_rows, 128), f32),
        shape((side_rows, 128), f32),
        shape((1, fada), f32),
        shape((ways, 8, LANES), f32),
        shape((ways * mp, 1, 128), f32),
    ]
    out = pl.pallas_call(
        tail_body,
        in_specs=[vmem] * 12,
        out_specs=[vmem] * len(out_shape),
        out_shape=out_shape,
        scratch_shapes=[landing] * 3
        + [few] * 3
        + [
            scratch(early.shape, bf16),
            scratch((mp,) + early.shape, bf16),
            scratch(small.shape, bf16),
            scratch((ways,) + bias.shape, bf16),
            scratch((rows, LANES), f32),
            scratch((ways, rows, LANES), bf16),
            scratch((ways, rows, LANES), bf16),
            scratch(small.shape[1:], f32),
            scratch((mp,) + small.shape[1:], f32),
            scratch((side_rows, 128), f32),
            scratch((mp, side_rows, 128), f32),
            scratch((rows, fada), f32),
            scratch((8, LANES), f32),
            scratch((1, 128), f32),
            scratch((rows, CLASSES), f32),
        ]
        + [dma((LAYERS, count))] * 5
        + [dma((LAYERS, CROSS_LATE))] * 3
        + [dma((1, ways * mp))] * 2
        + [dma((5, ways))] * 2
        + [dma((3, mp))] * 2,
        compiler_params=pltpu.CompilerParams(
            collective_id=1, has_side_effects=True, vmem_limit_bytes=58 * 2**20
        ),
        name="tail",
    )(slots, early, small, bias, w_fada, tables, cond, first_t, signal, first_s, tf, facts)
    return [out[0].reshape(-1, PACK_ROWS, LANES // 2)] + list(out[1:])


def halves(x):
    high = x.astype(jnp.bfloat16)
    return high, (x - high.astype(jnp.float32)).astype(jnp.bfloat16)


def left_form(main, tail):
    mh, ml = halves(main)
    th, tl = halves(tail)
    return jnp.concatenate([mh, mh, ml, th, th, tl], axis=1)


def right_form(x):
    h, l = halves(x)
    return jnp.concatenate(
        [h[:LANES], l[:LANES], h[:LANES], h[LANES:], l[LANES:], h[LANES:]], axis=0
    )


def product(left, right):
    return jnp.dot(left, right, preferred_element_type=jnp.float32)


def symmetric_product(left, right_main, right_tail):
    main = product(left, right_main)
    corner = product(left[LANES:], right_tail)
    return main, jnp.concatenate([main[LANES:].T, corner], axis=0)


def inverse_roots(pairs, eye_main, eye_tail):
    contracted, scales = [], []
    for main, tail in pairs:
        trace = jnp.sum(main * eye_main) + jnp.sum(tail * eye_tail)
        shift = 0.0001 * trace / BLOCK_SIDE
        main = main + shift * eye_main
        tail = tail + shift * eye_tail
        square = jnp.sum(main * main, axis=(0, 1), keepdims=True) + jnp.sum(
            tail * tail, axis=(0, 1), keepdims=True
        )
        factor_z = 2.5 / jnp.sqrt(square)
        contracted.append((main * factor_z, tail * factor_z))
        scales.append(jnp.sqrt(jnp.sqrt(factor_z)))
    estimates = None
    for newton_step in range(NEWTON):
        more = newton_step < NEWTON - 1
        factors = [((5.0 * eye_main - m) * 0.25, (5.0 * eye_tail - t) * 0.25) for m, t in contracted]
        rights = [(right_form(m), right_form(t)) for m, t in factors]
        lefts = [left_form(m, t) for m, t in factors] if more else None
        if more:
            powers = [symmetric_product(l, *r) for l, r in zip(lefts, rights)]
        if estimates is None:
            estimates = [(m * s, t * s) for (m, t), s in zip(factors, scales)]
        else:
            estimates = [
                symmetric_product(left_form(*e), *r) for e, r in zip(estimates, rights)
            ]
        if more:
            powers = [
                symmetric_product(left_form(*q), right_form(q[0]), right_form(q[1])) for q in powers
            ]
            contracted = [
                symmetric_product(left_form(*q), right_form(m), right_form(t))
                for q, (m, t) in zip(powers, contracted)
            ]
    return estimates


def shampoo_body(clip_ref, g_ref, stat_ref, old_ref, clipped_ref, new_stat_ref, new_ref, low_ref):
    side = BLOCK_SIDE

    def unit(width, offset):
        row = lax.broadcasted_iota(jnp.int32, (side, width), 0)
        col = lax.broadcasted_iota(jnp.int32, (side, width), 1) + offset
        return (row == col).astype(jnp.float32)

    eye_main, eye_tail = unit(LANES, 0), unit(TAIL, LANES)
    pairs, g_rights = [], []
    for j in range(g_ref.shape[0]):
        g_main, g_tail = unpack(g_ref[j] * clip_ref[0])
        clipped_ref[j, :, :LANES] = g_main
        clipped_ref[j, :, LANES:] = g_tail
        flipped = jnp.concatenate([g_main, g_tail], axis=1).T
        g_right = (right_form(g_main), right_form(g_tail))
        f_right = (right_form(flipped[:, :LANES]), right_form(flipped[:, LANES:]))
        g_left = left_form(g_main, g_tail)
        f_left = left_form(flipped[:, :LANES], flipped[:, LANES:])
        g_rights.append(g_right)
        for k, (left, right) in enumerate(((g_left, f_right), (f_left, g_right))):
            main, tail = symmetric_product(left, *right)
            main = 0.5 * stat_ref[j, k, :, :LANES] + 0.5 * main
            tail = 0.5 * stat_ref[j, k, :, LANES:] + 0.5 * tail
            new_stat_ref[j, k, :, :LANES] = main
            new_stat_ref[j, k, :, LANES:] = tail
            pairs.append((main, tail))
    roots = inverse_roots(pairs, eye_main, eye_tail)
    for j, g_right in enumerate(g_rights):
        root_left = left_form(*roots[2 * j])
        half = left_form(product(root_left, g_right[0]), product(root_left, g_right[1]))
        for part, (a, b) in zip(roots[2 * j + 1], ((0, LANES), (LANES, side))):
            direction = product(half, right_form(part))
            old = old_ref[j, :, a:b]
            new = old - shampoo_rate * (direction + decay_rate * old)
            new_ref[j, :, a:b] = new
            low_ref[j, :, a:b] = new.astype(jnp.bfloat16)


def shampoo(clip_factor, gradients, stats, old_blocks):
    count, side = gradients.shape[0], BLOCK_SIDE
    group = next(g for g in (3, 2, 1) if count % g == 0)
    one = pl.BlockSpec((group, side, side), lambda i: (i, 0, 0))
    two = pl.BlockSpec((group, 2, side, side), lambda i: (i, 0, 0, 0))
    block = jax.ShapeDtypeStruct((count, side, side), jnp.float32)
    return pl.pallas_call(
        shampoo_body,
        grid=(count // group,),
        in_specs=[
            pl.BlockSpec(memory_space=pltpu.SMEM),
            pl.BlockSpec((group, PACK_ROWS, LANES // 2), lambda i: (i, 0, 0)),
            two,
            one,
        ],
        out_specs=[one, two, one, one],
        out_shape=[
            block,
            jax.ShapeDtypeStruct((count, 2, side, side), jnp.float32),
            block,
            jax.ShapeDtypeStruct((count, side, side), jnp.bfloat16),
        ],
        compiler_params=pltpu.CompilerParams(vmem_limit_bytes=60 * 2**20),
        cost_estimate=pl.CostEstimate(
            flops=count * 44 * 6 * side**3, bytes_accessed=count * 34 * side * side, transcendentals=0
        ),
        name="shampoo",
    )(clip_factor.reshape(1), gradients, stats, old_blocks)


def adam_update(weight, gradient, moment_one, second):
    moment_one = 0.5 * moment_one + 0.5 * gradient
    second = 0.5 * second + 0.5 * gradient * gradient
    correct = 1.0 - 0.5**STEP
    updated = weight - adam_rate * (
        moment_one / correct / (jnp.sqrt(second / correct) + 1e-08) + decay_rate * weight
    )
    return (moment_one, second, updated)


def per_device(
    latents,
    noise,
    timesteps,
    labels,
    loss_weights,
    slotted_block_weights,
    statistics,
    slot_of_block,
    cond_tables,
    head_tables,
    slice_bias,
    side_bias,
    cond_m,
    cond_v,
    head_m,
    head_v,
    slice_m,
    slice_v,
    side_m,
    side_v,
):
    bf16, f32 = jnp.bfloat16, jnp.float32
    width = MODEL_WIDTH
    mp, dp = lax.axis_size("mp"), lax.axis_size("dp")
    my_mp, my_dp = lax.axis_index("mp"), lax.axis_index("dp")
    query_width, ff_width, ada_width = HEADS * HD // mp, FF // mp, 6 * width // mp
    ada_column = 3 * query_width + ff_width
    row_blocks = width // BLOCK_SIDE
    col_blocks = (ada_column + ada_width) // BLOCK_SIDE
    out_blocks = (query_width + ff_width) // BLOCK_SIDE
    first_out = row_blocks * col_blocks
    t2_row = PATCH_VALUES + FREQ
    class_row = t2_row + width
    local_heads = query_width // HD
    score_scale = HD ** (-0.5)
    batch = latents.shape[0]
    own_n = batch // mp
    cols = cond_tables.shape[1]
    samples = batch * dp

    def own(x):
        return lax.dynamic_slice_in_dim(x, my_mp * own_n, own_n, 0)

    def my_cols(x):
        return lax.dynamic_slice_in_dim(x, my_dp * cols, cols, x.ndim - 1)

    def all_columns(x):
        return x.transpose(1, 0, 2).reshape(x.shape[1], -1)

    def by_columns(x):
        return x.reshape(x.shape[0], dp, cols).transpose(1, 0, 2)

    def share_rows(x):
        return lax.all_gather(x, "mp", axis=0, tiled=True)

    tuned = dp == COLUMNS * LAYERS
    tables, head_low = cond_tables.T.astype(bf16), head_tables.astype(bf16)
    w_fada = head_low[:, : 2 * width]
    b_first = my_cols(side_bias[width : 2 * width])
    b_second = my_cols(side_bias[2 * width : 3 * width])
    time_freq = time_features(timesteps, FREQ).astype(bf16).astype(f32)
    facts = jnp.pad(jnp.stack([labels.astype(f32), loss_weights], 1), ((0, 0), (0, 126)))
    shared = jnp.concatenate([tables[:, :PATCH_VALUES], head_low[:, 2 * width :]], 1)
    if tuned:
        (
            blocks, time_freq, facts, shared, first_t, first_s, cond_vec, signal_cols, signal, final_mod,
        ) = head(
            slotted_block_weights[0], time_freq, facts, shared, tables, w_fada, b_first[None],
            b_second[None],
        )
    else:
        w_first, w_second = tables[:, PATCH_VALUES:t2_row].T, tables[:, t2_row:class_row].T
        blocks = lax.all_gather(pack_blocks(slotted_block_weights[0]), "dp", axis=0, tiled=True)
        time_freq, facts, shared = exchange(
            [(time_freq, "gather"), (facts, "gather"), (shared, "gather")], "dp", 2
        )
        time_freq = time_freq.reshape(samples, FREQ)
        first_t = dense(time_freq.astype(bf16), w_first) + b_first
        (first_s,) = exchange([(swish_unit(first_t).astype(bf16), "gather")], "dp", 3)
        labels_all = facts[:, :, 0].reshape(samples, 1).astype(jnp.int32)
        onehot = labels_all == jnp.arange(CLASSES, dtype=jnp.int32)[None, :]
        first_s = all_columns(first_s)
        cond_vec = (
            dense(first_s, w_second) + b_second + dense(onehot.astype(bf16), tables[:, class_row:].T)
        )
        signal_cols = swish_unit(cond_vec).astype(bf16)
        signal, final_mod = exchange(
            [
                (signal_cols.astype(f32).reshape(dp, batch, cols), "scatter"),
                (dense(signal_cols, w_fada).reshape(dp, batch, 2 * width), "scatter"),
            ],
            "dp",
            4,
        )
        final_mod = jnp.sum(final_mod, 0)
        signal = all_columns(signal).astype(bf16)
        shared = shared.reshape(width, -1).T
        of_head = shared[PATCH_VALUES:].reshape(4, 2, 4, width).transpose(1, 0, 2, 3)
        shared = jnp.concatenate([shared[:PATCH_VALUES], of_head.reshape(32, width)], 0)
    weight_total = jnp.sum(facts[:, :, 1])
    w_patch, w_pred, w_raw = shared[:PATCH_VALUES], shared[PATCH_VALUES:32], shared[32:]
    final_mod = own(final_mod + side_bias[5 * width : 7 * width])

    w_qkv, w_up, w_ada = assemble(
        blocks,
        slot_of_block,
        0,
        row_blocks,
        [3 * query_width // BLOCK_SIDE, ff_width // BLOCK_SIDE, ada_width // BLOCK_SIDE],
    )
    (w_o,) = assemble(blocks, slot_of_block, first_out, query_width // BLOCK_SIDE, [row_blocks])
    (w_down,) = assemble(
        blocks,
        slot_of_block,
        first_out + query_width // BLOCK_SIDE * row_blocks,
        ff_width // BLOCK_SIDE,
        [row_blocks],
    )
    own_bias = slice_bias[0]
    modul = lax.all_gather(
        dense(signal, w_ada) + own_bias[2 * query_width + ff_width :],
        "mp",
        axis=1,
        tiled=True,
    )
    own_modul = own(modul)

    def part(position):
        return modul[:, None, position * width : (position + 1) * width]

    def heads_of(inputs):
        return inputs.reshape(batch, -1, local_heads, HD)

    keep_rate, noise_rate, upper_log, lower_log, mean_gap = coefficients(timesteps)
    noisy = keep_rate[:, None, None, None] * latents + noise_rate[:, None, None, None] * noise
    patches = patchify(noisy).astype(bf16)
    seq_len = patches.shape[1]
    initial = (
        dense(patches, w_patch) + side_bias[:width] + position_embedding(LATENT_SIDE // 2, width)
    )
    normed_all, _ = layer_norm(initial)
    attn_in = (normed_all * (1.0 + part(1)) + part(0)).astype(bf16)
    start = own(initial)[0]
    own_patches = own(patches)
    target = patchify(own(noise))[0]

    projected = dense(attn_in, w_qkv)
    queries = heads_of((projected[..., :query_width] + own_bias[:query_width]).astype(bf16))
    keys = heads_of(projected[..., query_width : 2 * query_width].astype(bf16))
    values = heads_of(
        (projected[..., 2 * query_width :] + own_bias[query_width : 2 * query_width]).astype(bf16)
    )
    scores = (
        jnp.einsum("slhe,smhe->shlm", queries, keys, preferred_element_type=f32) * score_scale
    )
    row_peak = jnp.max(scores, -1, keepdims=True)
    shifted = jnp.exp(scores - row_peak)
    row_total = jnp.sum(shifted, -1, keepdims=True)
    probs = shifted / row_total
    log_total = row_peak + jnp.log(row_total)
    mixed = (
        jnp.einsum("shlm,smhe->slhe", probs.astype(bf16), values, preferred_element_type=f32)
        .reshape(batch, seq_len, query_width)
        .astype(bf16)
    )

    def rows_of(*rows):
        return jnp.concatenate([r.reshape(1, width) for r in rows], 0)

    shift1, scale1, gate1, shift2, scale2, gate2 = (own_modul[0, i * width : (i + 1) * width] for i in range(6))
    attn, middle, hidden, active, mlp_in = attention_out_stage(
        mixed,
        w_o,
        w_up,
        start,
        rows_of(side_bias[3 * width : 4 * width], gate1, scale2, shift2),
        own_bias[2 * query_width : 2 * query_width + ff_width].reshape(1, ff_width),
    )

    def halves_of(x):
        x = x.reshape(x.shape[:-1] + (4, 8))
        return x[..., :4].reshape(x.shape[:-2] + (16,)), x[..., 4:].reshape(x.shape[:-2] + (16,))

    own_facts = [own(x) for x in (upper_log, lower_log, mean_gap, loss_weights)]
    loss_facts = jnp.stack(own_facts + [weight_total[None]])
    loss_facts = jnp.broadcast_to(loss_facts, (5, 16))
    d_final, head_in, d_pred, d_raw, sums_f, loss_part, d_hidden, up_sum, d_branch = loss_stage(
        active,
        w_down,
        hidden,
        middle,
        rows_of(side_bias[4 * width : 5 * width], gate2, final_mod[0, width:], final_mod[0, :width]),
        target,
        w_pred,
        w_raw,
        jnp.stack(halves_of(side_bias[7 * width :])),
        loss_facts,
    )
    loss_part = jnp.sum(loss_part)
    d_fmod = sums_f[:2].reshape(1, 2 * width).astype(bf16)
    d_middle, sums_m, d_mixed, g_down, d_attn = middle_back_stage(
        d_hidden, w_up, w_o, middle, d_final, attn, rows_of(scale2, gate1), active, d_branch
    )
    d_mixed = heads_of(d_mixed)
    probs = jnp.exp(
        jnp.einsum("slhe,smhe->shlm", queries, keys, preferred_element_type=f32) * score_scale
        - log_total
    )
    d_values = jnp.einsum(
        "shlm,slhe->smhe", probs.astype(bf16), d_mixed, preferred_element_type=f32
    ).astype(bf16)
    d_probs = jnp.einsum("slhe,smhe->shlm", d_mixed, values, preferred_element_type=f32)
    d_scores = (probs * (d_probs - jnp.sum(d_probs * probs, -1, keepdims=True))).astype(bf16)
    d_query = (
        jnp.einsum("shlm,smhe->slhe", d_scores, keys, preferred_element_type=f32) * score_scale
    ).astype(bf16)
    d_keys = (
        jnp.einsum("shlm,slhe->smhe", d_scores, queries, preferred_element_type=f32) * score_scale
    ).astype(bf16)
    flat_q = d_query.reshape(batch, seq_len, query_width)
    flat_v = d_values.reshape(batch, seq_len, query_width)
    d_proj = jnp.concatenate([flat_q, d_keys.reshape(batch, seq_len, query_width), flat_v], 2)
    d_start, sums_a, g_qkv, g_up, g_outp = start_back_stage(
        d_proj, w_qkv, start, d_middle, scale1.reshape(1, width), attn_in, mlp_in, d_hidden, mixed, d_attn
    )
    d_mod_own = jnp.concatenate(
        [sums_a[0], sums_a[1], sums_m[2], sums_m[0], sums_m[1], sums_f[2]]
    ).reshape(1, 6 * width)
    d_modul = lax.dynamic_slice_in_dim(
        share_rows(d_mod_own.astype(bf16)), my_mp * ada_width, ada_width, 1
    )

    slot_grad = to_slots(
        [g_qkv, g_up], signal, d_modul, [g_outp, g_down], slot_of_block, slot_of_block.shape[0]
    )
    d_signal = by_columns(back_dense(d_modul, w_ada))

    def interleave(p, r):
        parts = [x.reshape(x.shape[:-1] + (4, 4)) for x in (p, r)]
        return jnp.concatenate(parts, -1).reshape(p.shape[:-1] + (32,))

    def thirds(x):
        high = x.astype(bf16).astype(f32)
        mid = (x - high).astype(bf16).astype(f32)
        return [high, mid, x - high - mid]

    def lanes(x, rows):
        return jnp.pad(x, (0, rows * 128 - x.shape[0])).reshape(rows, 128)

    d_out = interleave(d_pred, d_raw)
    small = by_columns(
        jnp.concatenate([weight_grad(own_patches[0], d_start), weight_grad(d_out, head_in)], 0)
    )
    slice_part = jnp.concatenate([total_of(flat_q), total_of(flat_v), up_sum[0], total_of(d_modul)])
    side_part = jnp.concatenate([sums_a[2], sums_m[3], sums_f[3], total_of(d_out)])
    slice_rows, side_rows = (-(-x.shape[0] // 1024) * 8 for x in (slice_part, side_part))
    bias_part = jnp.concatenate(
        [lanes(slice_part, slice_rows), lanes(side_part, side_rows), lanes(jnp.stack(thirds(loss_part)), 8)], 0
    )
    if tuned:
        red_blocks, red_cond, red_head, red_slice, side_sum, side_mod, columns, last = tail(
            slot_grad, d_fmod.astype(f32), d_signal, small, bias_part, w_fada, tables, cond_vec,
            first_t, signal_cols, first_s, time_freq, facts, slice_rows,
        )
    else:
        red_blocks = lax.psum_scatter(slot_grad, "dp", scatter_dimension=0, tiled=True).astype(f32)
        d_fmod_all, d_signal = exchange(
            [(d_fmod.astype(f32), "gather"), (d_signal, "scatter")], EVERY, 5
        )
        d_fmod_all = d_fmod_all.reshape(samples, 2 * width).astype(bf16)
        d_signal = jnp.sum(d_signal.reshape(dp, mp, batch, cols), 1).reshape(samples, cols)
        d_signal = d_signal + back_dense(d_fmod_all, w_fada)
        d_cond = d_signal * swish_slope(cond_vec)
        d_second = d_cond.astype(bf16)
        d_first, small, bias_part = exchange(
            [
                (by_columns(back_dense(d_second, w_second)), "scatter"),
                (small, "scatter"),
                (bias_part, "gather"),
            ],
            "dp",
            6,
        )
        d_first = (jnp.sum(d_first, 0) * swish_slope(first_t)).astype(bf16)
        bias_part = jnp.sum(bias_part, 0)
        red_slice = bias_part[:slice_rows]
        small, side_sum = exchange(
            [(jnp.sum(small, 0), "gather"), (bias_part[slice_rows:], "gather")], "mp", 7
        )
        small, side_sum = jnp.sum(small, 0), jnp.sum(side_sum, 0)
        side_mod = total_of(d_fmod_all)
        g_class = jnp.einsum(
            "sc,sd->cd", onehot.astype(f32), d_cond, precision=exact_precision_flag
        )
        red_cond = jnp.concatenate(
            [
                small[:PATCH_VALUES],
                weight_grad(time_freq.astype(bf16), d_first),
                weight_grad(first_s, d_second),
                g_class,
            ],
            0,
        ).T
        red_head = jnp.concatenate([weight_grad(signal_cols, d_fmod_all), small[PATCH_VALUES:].T], 1)
        side_cols = jnp.stack([total_of(d_first), total_of(d_second)])
        local_squares = (
            jnp.sum(red_blocks * red_blocks)
            + (
                jnp.sum(red_cond * red_cond)
                + jnp.sum(red_head * red_head)
                + jnp.sum(side_cols * side_cols)
            )
            / mp
            + jnp.sum(red_slice * red_slice) / dp
            + (jnp.sum(side_sum[:-8] * side_sum[:-8]) + jnp.sum(side_mod * side_mod)) / (dp * mp)
        )
        last = jnp.pad(side_cols, ((0, 6), (0, LANES - cols)))
        last = jnp.where(jnp.arange(8)[:, None] == 2, local_squares, last)
        (last,) = exchange([(last, "gather")], EVERY, 8)
        columns, last = last.reshape(dp, mp, 8, LANES)[:, 0], last[:, 2:3]
    grad_norm = jnp.sqrt(jnp.sum(last[:, 0, 0]))
    loss_sum = jnp.sum(side_sum[side_rows, :3])
    side_sum = side_sum[:side_rows].reshape(-1)[: side_part.shape[0]]
    red_slice = red_slice.reshape(-1)[: slice_part.shape[0]]
    side_cols = columns[:, :2, :cols].transpose(1, 0, 2).reshape(2 * width)
    red_side = jnp.concatenate(
        [
            side_sum[:width],
            side_cols,
            side_sum[width : 3 * width],
            side_mod.reshape(2 * width),
            side_sum[3 * width :],
        ]
    )
    clip_factor = 1.0 / jnp.maximum(grad_norm, 1.0)
    clipped, new_stats, new_blocks, new_low = shampoo(
        clip_factor, red_blocks, statistics[0], slotted_block_weights[0]
    )
    cond_one, cond_two, new_cond = adam_update(
        cond_tables.T, red_cond * clip_factor, cond_m.T, cond_v.T
    )
    cond_short = new_cond.astype(bf16)
    head_one, head_two, new_head = adam_update(head_tables, red_head * clip_factor, head_m, head_v)
    head_short = new_head.astype(bf16)
    slice_one, slice_two, new_slice = adam_update(
        slice_bias[0], red_slice * clip_factor, slice_m[0], slice_v[0]
    )
    side_one, side_two, new_side = adam_update(side_bias, red_side * clip_factor, side_m, side_v)
    return (
        loss_sum,
        weight_total,
        grad_norm,
        clipped[None],
        new_stats[None],
        new_blocks[None],
        new_low[None],
        cond_one.T,
        cond_two.T,
        new_cond.T,
        cond_short.T,
        head_one,
        head_two,
        new_head,
        head_short,
        slice_one[None],
        slice_two[None],
        new_slice[None],
        side_one,
        side_two,
        new_side,
    )


def solution(mesh):
    return jax.shard_map(
        per_device,
        mesh=mesh,
        in_specs=(
            P("dp", None, None, None),
            P("dp", None, None, None),
            P("dp"),
            P("dp"),
            P("dp"),
            P("mp", "dp", None, None),
            P("mp", "dp", None, None, None),
            P(),
            P(None, "dp"),
            P("dp", None),
            P("mp", None),
            P(),
            P(None, "dp"),
            P(None, "dp"),
            P("dp", None),
            P("dp", None),
            P("mp", None),
            P("mp", None),
            P(),
            P(),
        ),
        out_specs=(
            P(),
            P(),
            P(),
            P("mp", "dp", None, None),
            P("mp", "dp", None, None, None),
            P("mp", "dp", None, None),
            P("mp", "dp", None, None),
            P(None, "dp"),
            P(None, "dp"),
            P(None, "dp"),
            P(None, "dp"),
            P("dp", None),
            P("dp", None),
            P("dp", None),
            P("dp", None),
            P("mp", None),
            P("mp", None),
            P("mp", None),
            P(),
            P(),
            P(),
        ),
        check_vma=False,
    )
```
